32 devices in a mesh: ifg: 8 (over z, x), grp: 4 (over y, core).
Axes of the slice: x: 2, y: 2, z: 4, core: 2. Of those that a mesh axis runs over, the one named last changes fastest.
Arguments:
- phases: bfloat16 [1024, 4, 32768], P('ifg', 'grp'), may hold values from -6 to 6
- date_pairs: int32 [2, 1024], replicated, may hold values from 0 to 199, as said below
- pair_counts: int32 [16], replicated, may hold values from 128 to 1024, as said below
- group_ids: int32 [4, 128], P(None, 'ifg'), may hold values from 0 to 15, as said below
Outputs:
- series: float32 [4, 200, 32768], P('grp', None, 'ifg')
The draws below stay inside these ranges and needn't reach their ends.
Inputs may be any that keep to these rules, and one draw needn't show every extreme that they name: date_pairs[0, k] < date_pairs[1, k]; the baseline date_pairs[1, k] - date_pairs[0, k] lies in 1 to 25 and never falls as k grows. `pair_counts`: each count is 128 times a power of two; some class has all 1024 interferograms and some has 128. `group_ids`: constant over each aligned run of 8 blocks of a sub-strip.
All inputs are finite; a program needn't handle non-finite values.
Results may differ from the reference program's by a relative error of at most 0.0003.
Values may be sent and summed in bfloat16 or wider, within the bound.
No kernel may reach another device: no remote copies, remote signals or barrier semaphores. Data moves between devices by JAX's collectives and lax.ppermute only.
A program may use at most 128 MiB of HBM per device.

```python
import jax
import jax.numpy as jnp
from jax import lax

K = 1024
M = 200
NG = 16
BLOCK = 256
RUN = 8
SLAB = 128
STRIPS = 4
SBLK = 128
SPIX = 32768


def draw_date_pairs(key, part):
    first_key, second_key = jax.random.split(jax.random.fold_in(key, 11))
    baseline = jnp.sort(jax.random.randint(first_key, (K,), 1, M // 8 + 1))
    earlier = jax.random.randint(second_key, (K,), 0, M - baseline)
    return jnp.stack([earlier, earlier + baseline]).astype(jnp.int32)


def draw_pair_counts(key, part):
    levels = jax.random.randint(jax.random.fold_in(key, 23), (NG,), 0, 4)
    counts = K // 8 * jnp.left_shift(jnp.ones((NG,), jnp.int32), levels)
    counts = counts.at[0].set(K).at[1].set(K // 8)
    return counts.astype(jnp.int32)


def draw_group_ids(key, part):
    run_groups = jax.random.randint(jax.random.fold_in(key, 37), (STRIPS, SBLK // RUN), 0, NG)
    return jnp.repeat(run_groups, RUN, axis=1).astype(jnp.int32)


def shard_levels(key, dims, cuts, smallest, top_value):
    loudness = 1.0
    for axis_at, blocks in cuts:
        draws = jax.random.uniform(jax.random.fold_in(jax.random.fold_in(key, 6), axis_at), (blocks,), jnp.float32, smallest / len(cuts), top_value / len(cuts))
        loudness = loudness * jnp.repeat(jnp.exp(draws), dims[axis_at] // blocks).reshape((-1,) + (1,) * (len(dims) - 1 - axis_at))
    return loudness


def noise(stream_key, extent, width, bound, cuts=(), held_as=jnp.bfloat16):
    factor_of = shard_levels(stream_key, extent, cuts, -0.22, 0.18) if cuts else 1.0
    values = jax.random.normal(stream_key, extent, jnp.float32) * width * factor_of
    return jnp.minimum(jnp.maximum(values, -bound), bound).astype(held_as)


def setup_inputs(seed: int = 0) -> dict:
    arg_keys = jax.random.split(jax.random.key(seed), 5)
    phases = noise(arg_keys[0], (K, STRIPS, SPIX), 1.0, 6.0, ((0, 8), (1, 4)))
    date_pairs = draw_date_pairs(jax.random.fold_in(arg_keys[4], 71), 0)
    pair_counts = draw_pair_counts(jax.random.fold_in(arg_keys[4], 71), 0)
    group_ids = draw_group_ids(jax.random.fold_in(arg_keys[4], 71), 0)
    return {"phases": phases, "date_pairs": date_pairs, "pair_counts": pair_counts, "group_ids": group_ids}


damping = 1.0

def reference(phases, date_pairs, pair_counts, group_ids):
    date_index = jnp.arange(M, dtype=jnp.int32)
    design = (date_index[None, :] == date_pairs[1][:, None]).astype(jnp.float32) - (date_index[None, :] == date_pairs[0][:, None]).astype(jnp.float32)
    row_index = jnp.arange(K, dtype=jnp.int32)
    keep_mask = (row_index[None, :] < pair_counts[:, None]).astype(jnp.float32)
    identity = jnp.eye(M, dtype=jnp.float32)

    def class_gram(mask_row):
        return jnp.dot((design * mask_row[:, None]).T, design, precision=lax.Precision.HIGHEST) + damping * identity
    gram_sums = lax.map(class_gram, keep_mask)
    factors = jnp.linalg.cholesky(gram_sums)

    def strip_solve(strip_index):
        strip_data = lax.dynamic_index_in_dim(phases, strip_index, 1, keepdims=False)
        block_groups = lax.dynamic_index_in_dim(group_ids, strip_index, 0, keepdims=False)
        slab_count = pair_counts[block_groups] // SLAB

        def add_slab(slab_index, running):
            data_slab = lax.dynamic_slice_in_dim(strip_data, slab_index * SLAB, SLAB, 0).astype(jnp.float32)
            design_slab = lax.dynamic_slice_in_dim(design, slab_index * SLAB, SLAB, 0)
            slab_term = jnp.dot(design_slab.T, data_slab, precision=lax.Precision.HIGHEST)
            weight = jnp.repeat((slab_index < slab_count).astype(jnp.float32), BLOCK)
            return running + slab_term * weight[None, :]
        right_side = lax.fori_loop(0, K // SLAB, add_slab, jnp.zeros((M, SPIX), jnp.float32))
        per_block = right_side.reshape(M, SBLK, BLOCK).transpose(1, 0, 2)

        def solve_block(pieces):
            block_rhs, group = pieces
            return jax.scipy.linalg.cho_solve((factors[group], True), block_rhs)
        solved = lax.map(solve_block, (per_block, block_groups))
        return solved.transpose(1, 0, 2).reshape(M, SPIX)
    return lax.map(strip_solve, jnp.arange(STRIPS, dtype=jnp.int32))
```

```python
import functools

import jax
import jax.numpy as jnp
from jax import lax
from jax.experimental import pallas as pl
from jax.experimental.pallas import tpu as pltpu
from jax.sharding import PartitionSpec as P

M = 200
RUN = 8
PAD = 256
SLABS = 8
DAMPING = 1.0
VMEM_BYTES = 48 * 1024 * 1024
F32 = jnp.float32
HIGHEST = lax.Precision.HIGHEST


def incidence(earlier, later, rows):
    shape = (rows, earlier.shape[1])
    date = lax.broadcasted_iota(jnp.int32, shape, 0)
    return (date == later).astype(F32) - (date == earlier).astype(F32)


def inverse_kernel(counts_ref, pairs_ref, out_ref):
    run = pl.program_id(0)
    earlier, later = pairs_ref[0:1, :], pairs_ref[1:2, :]
    design = incidence(earlier, later, PAD)
    pair = lax.broadcasted_iota(jnp.int32, design.shape, 1)
    kept = jnp.where(pair < counts_ref[run], design, 0.0).astype(jnp.bfloat16)
    contract_last = (((1,), (1,)), ((), ()))
    gram = lax.dot_general(kept, kept, contract_last, preferred_element_type=F32)
    row = lax.broadcasted_iota(jnp.int32, gram.shape, 0)
    col = lax.broadcasted_iota(jnp.int32, gram.shape, 1)
    identity = (row == col).astype(F32)
    gram = gram + DAMPING * identity
    low = DAMPING
    high = 2.0 * jnp.max(gram) - DAMPING
    total, width = high + low, high - low
    scale = 2.0 * total * total - width * width
    start = (8.0 * total / scale) * identity - (8.0 / scale) * gram
    needed = 18.0 * scale / (8.0 * high * low)
    steps = jnp.int32(1)
    for power in range(1, 16):
        steps += (needed > float(2**power)).astype(jnp.int32)

    def step(_, guess):
        product = jnp.dot(gram, guess, precision=HIGHEST, preferred_element_type=F32)
        return 2.0 * guess - jnp.dot(guess, product, precision=HIGHEST, preferred_element_type=F32)

    out_ref[0] = lax.fori_loop(0, steps, step, start)


def invert_classes(date_pairs, run_counts):
    runs = run_counts.shape[0]
    return pl.pallas_call(
        inverse_kernel,
        out_shape=jax.ShapeDtypeStruct((runs, PAD, PAD), F32),
        grid_spec=pltpu.PrefetchScalarGridSpec(
            num_scalar_prefetch=1,
            grid=(runs,),
            in_specs=[pl.BlockSpec(date_pairs.shape, lambda r, c: (0, 0))],
            out_specs=pl.BlockSpec((1, PAD, PAD), lambda r, c: (r, 0, 0)),
        ),
        compiler_params=pltpu.CompilerParams(vmem_limit_bytes=VMEM_BYTES),
        cost_estimate=pl.CostEstimate(flops=runs * 20 * 12 * PAD**3, bytes_accessed=runs * PAD * PAD * 4, transcendentals=0),
        name="invert_classes",
    )(run_counts, date_pairs)


def sum_solve_kernel(tiles, counts_ref, pairs_ref, data_ref, inverse_ref, out_ref):
    run = pl.program_id(0) // tiles
    design = incidence(pairs_ref[0:1, :], pairs_ref[1:2, :], PAD)
    pair = lax.broadcasted_iota(jnp.int32, design.shape, 1)
    kept = jnp.where(pair < counts_ref[run], design, 0.0).astype(jnp.bfloat16)
    sums = jnp.dot(kept, data_ref[...], preferred_element_type=F32)
    out_ref[...] = jnp.dot(inverse_ref[0, :M, :], sums, precision=HIGHEST, preferred_element_type=F32)


def sum_solve(run_counts, date_pairs, received, inverse):
    runs = run_counts.shape[0]
    total_pairs, pixels = received.shape
    run_pixels = pixels // runs
    tile = run_pixels // 2
    tiles = run_pixels // tile
    return pl.pallas_call(
        functools.partial(sum_solve_kernel, tiles),
        out_shape=jax.ShapeDtypeStruct((M, pixels), F32),
        grid_spec=pltpu.PrefetchScalarGridSpec(
            num_scalar_prefetch=1,
            grid=(runs * tiles,),
            in_specs=[
                pl.BlockSpec(date_pairs.shape, lambda i, c: (0, 0)),
                pl.BlockSpec((total_pairs, tile), lambda i, c: (0, i)),
                pl.BlockSpec((1, PAD, PAD), lambda i, c: (i // tiles, 0, 0)),
            ],
            out_specs=pl.BlockSpec((M, tile), lambda i, c: (0, i)),
        ),
        compiler_params=pltpu.CompilerParams(vmem_limit_bytes=VMEM_BYTES),
        name="sum_solve",
    )(run_counts, date_pairs, received, inverse)


def local(phases, date_pairs, pair_counts, group_ids):
    owner_count = lax.axis_size("ifg")
    total_pairs = date_pairs.shape[1]
    local_pairs, _, pixels = phases.shape
    owner_pixels = pixels // owner_count
    strip_groups = lax.dynamic_index_in_dim(group_ids, lax.axis_index("grp"), 0, keepdims=False)
    run_counts = jnp.take(pair_counts, strip_groups[::RUN])
    outgoing = phases.reshape(local_pairs, owner_count, owner_pixels).transpose(1, 0, 2)
    received = lax.all_to_all(outgoing, "ifg", split_axis=0, concat_axis=0, tiled=True)
    inverse = invert_classes(date_pairs, run_counts)
    solved = sum_solve(run_counts, date_pairs, received.reshape(total_pairs, owner_pixels), inverse)
    return solved[None, :, :]


def solution(mesh):
    in_specs = (P("ifg", "grp", None), P(), P(), P(None, "ifg"))
    out_specs = P("grp", None, "ifg")
    return jax.shard_map(local, mesh=mesh, in_specs=in_specs, out_specs=out_specs, check_vma=False)
```

```python
import functools

import jax
import jax.numpy as jnp
from jax import lax
from jax.experimental import pallas as pl
from jax.experimental.pallas import tpu as pltpu
from jax.sharding import PartitionSpec as P

M = 200
RUN = 8
PAD = 256
SLABS = 8
DAMPING = 1.0
VMEM_BYTES = 48 * 1024 * 1024
F32 = jnp.float32
HIGHEST = lax.Precision.HIGHEST
CODE_ROWS = 8
ROWS = M + CODE_ROWS
LEVELS = 32700.0
CODES_PER_OCTAVE = 128.0
SMALLEST = 2.0**-110
CHUNK_ORDER = ((3, 2, 1, 0), (0, 3, 2, 1), (3, 0, 1, 2), (0, 1, 2, 3))
SENDS = (
    (((0, 1), (1, 0), (2, 3), (3, 2)),),
    (((0, 1), (1, 3), (2, 0), (3, 2)),),
    (((0, 1), (1, 2)), ((3, 2), (2, 1))),
)


def incidence(earlier, later, rows):
    shape = (rows, earlier.shape[1])
    date = lax.broadcasted_iota(jnp.int32, shape, 0)
    return (date == later).astype(F32) - (date == earlier).astype(F32)


def inverse_kernel(counts_ref, pairs_ref, *rest):
    out_ref = rest[-1]
    run = pl.program_id(0)
    earlier, later = pairs_ref[0:1, :], pairs_ref[1:2, :]
    design = incidence(earlier, later, PAD)
    pair = lax.broadcasted_iota(jnp.int32, design.shape, 1)
    kept = jnp.where(pair < counts_ref[run], design, 0.0).astype(jnp.bfloat16)
    contract_last = (((1,), (1,)), ((), ()))
    gram = lax.dot_general(kept, kept, contract_last, preferred_element_type=F32)
    row = lax.broadcasted_iota(jnp.int32, gram.shape, 0)
    col = lax.broadcasted_iota(jnp.int32, gram.shape, 1)
    identity = (row == col).astype(F32)
    gram = gram + DAMPING * identity
    low = DAMPING
    high = 2.0 * jnp.max(gram) - DAMPING
    total, width = high + low, high - low
    scale = 2.0 * total * total - width * width
    start = (8.0 * total / scale) * identity - (8.0 / scale) * gram
    needed = 18.0 * scale / (8.0 * high * low)
    steps = jnp.int32(1)
    for power in range(1, 16):
        steps += (needed > float(2**power)).astype(jnp.int32)

    def step(_, guess):
        product = jnp.dot(gram, guess, precision=HIGHEST, preferred_element_type=F32)
        return 2.0 * guess - jnp.dot(guess, product, precision=HIGHEST, preferred_element_type=F32)

    out_ref[0] = lax.fori_loop(0, steps, step, start)


def invert_classes(date_pairs, run_counts, after):
    runs = run_counts.shape[0]
    waits = [] if after is None else [after]
    return pl.pallas_call(
        inverse_kernel,
        out_shape=jax.ShapeDtypeStruct((runs, PAD, PAD), F32),
        grid_spec=pltpu.PrefetchScalarGridSpec(
            num_scalar_prefetch=1,
            grid=(runs,),
            in_specs=[pl.BlockSpec(date_pairs.shape, lambda r, c: (0, 0))]
            + [pl.BlockSpec(memory_space=pl.ANY)] * len(waits),
            out_specs=pl.BlockSpec((1, PAD, PAD), lambda r, c: (r, 0, 0)),
        ),
        compiler_params=pltpu.CompilerParams(vmem_limit_bytes=VMEM_BYTES),
        cost_estimate=pl.CostEstimate(flops=runs * 20 * 12 * PAD**3, bytes_accessed=runs * PAD * PAD * 4, transcendentals=0),
        name="invert_classes",
    )(run_counts, date_pairs, *waits)


def sum_solve_kernel(tiles, counts_ref, pairs_ref, data_ref, inverse_ref, out_ref):
    run = pl.program_id(0) // tiles
    design = incidence(pairs_ref[0:1, :], pairs_ref[1:2, :], PAD)
    pair = lax.broadcasted_iota(jnp.int32, design.shape, 1)
    kept = jnp.where(pair < counts_ref[run], design, 0.0).astype(jnp.bfloat16)
    sums = jnp.dot(kept, data_ref[...], preferred_element_type=F32)
    out_ref[...] = jnp.dot(inverse_ref[0, :M, :], sums, precision=HIGHEST, preferred_element_type=F32)


def sum_solve(run_counts, date_pairs, received, inverse):
    runs = run_counts.shape[0]
    total_pairs, pixels = received.shape
    run_pixels = pixels // runs
    tile = run_pixels // 2
    tiles = run_pixels // tile
    return pl.pallas_call(
        functools.partial(sum_solve_kernel, tiles),
        out_shape=jax.ShapeDtypeStruct((M, pixels), F32),
        grid_spec=pltpu.PrefetchScalarGridSpec(
            num_scalar_prefetch=1,
            grid=(runs * tiles,),
            in_specs=[
                pl.BlockSpec(date_pairs.shape, lambda i, c: (0, 0)),
                pl.BlockSpec((total_pairs, tile), lambda i, c: (0, i)),
                pl.BlockSpec((1, PAD, PAD), lambda i, c: (i // tiles, 0, 0)),
            ],
            out_specs=pl.BlockSpec((M, tile), lambda i, c: (0, i)),
        ),
        compiler_params=pltpu.CompilerParams(vmem_limit_bytes=VMEM_BYTES),
        name="sum_solve",
    )(run_counts, date_pairs, received, inverse)


def decode(coded):
    values = coded.astype(jnp.int32).astype(F32)
    scale = jnp.exp2(values[M : M + 1, :] * (1.0 / CODES_PER_OCTAVE)) * (1.0 / LEVELS)
    return values, scale


def encode(sums):
    largest = jnp.max(jnp.abs(sums[:M, :]), axis=0, keepdims=True)
    code = jnp.ceil(jnp.log2(jnp.maximum(largest, SMALLEST)) * CODES_PER_OCTAVE)
    inverse_scale = LEVELS / jnp.exp2(code * (1.0 / CODES_PER_OCTAVE))
    scaled = jnp.round(sums * inverse_scale)
    row = lax.broadcasted_iota(jnp.int32, sums.shape, 0)
    return jnp.where(row < M, scaled, code).astype(jnp.int32).astype(jnp.int16)


def pair_sums(count, pairs_ref, own, partner):
    design = incidence(pairs_ref[0:1, :], pairs_ref[1:2, :], ROWS)
    kept = jnp.where(pairs_ref[2:3, :] < count, design, 0.0).astype(jnp.bfloat16)
    width = own.shape[0]
    sums = jnp.dot(kept[:, :width], own, preferred_element_type=F32)
    return sums + jnp.dot(kept[:, width:], partner, preferred_element_type=F32)


def step_kernel(has_earlier, scalars, pairs_ref, own_ref, partner_ref, next_ref, *rest):
    if has_earlier:
        earlier_ref, coded_ref, outgoing_ref = rest
    else:
        coded_ref, outgoing_ref = rest
    sums = pair_sums(scalars[2], pairs_ref, own_ref[...], partner_ref[...])
    if has_earlier:
        values, scale = decode(earlier_ref[...])
        sums = sums + values * (scale * scalars[3].astype(F32))
    coded_ref[...] = encode(sums)
    outgoing_ref[...] = next_ref[...]


def step(scalars, pairs, phases, partner, earlier, piece, tile, next_pixels):
    local_pairs = phases.shape[0]
    tiles = piece // tile
    next_tile = next_pixels // tiles
    in_specs = [
        pl.BlockSpec(pairs.shape, lambda i, s: (0, 0)),
        pl.BlockSpec((local_pairs, tile), lambda i, s: (0, s[0] * tiles + i)),
        pl.BlockSpec((local_pairs, tile), lambda i, s: (0, i)),
        pl.BlockSpec((local_pairs, next_tile), lambda i, s: (0, s[1] * tiles + i)),
    ]
    operands = [pairs, phases, partner, phases]
    if earlier is not None:
        in_specs.append(pl.BlockSpec((ROWS, tile), lambda i, s: (0, i)))
        operands.append(earlier)
    return pl.pallas_call(
        functools.partial(step_kernel, earlier is not None),
        out_shape=(
            jax.ShapeDtypeStruct((ROWS, piece), jnp.int16),
            jax.ShapeDtypeStruct((local_pairs, next_pixels), phases.dtype),
        ),
        grid_spec=pltpu.PrefetchScalarGridSpec(
            num_scalar_prefetch=1,
            grid=(tiles,),
            in_specs=in_specs,
            out_specs=(
                pl.BlockSpec((ROWS, tile), lambda i, s: (0, i)),
                pl.BlockSpec((local_pairs, next_tile), lambda i, s: (0, i)),
            ),
        ),
        compiler_params=pltpu.CompilerParams(vmem_limit_bytes=VMEM_BYTES),
        name="sum_step",
    )(scalars, *operands)


def own_kernel(scalars, pairs_ref, own_ref, partner_ref, *rest):
    earlier_refs, sums_ref = rest[:-1], rest[-1]
    sums = pair_sums(scalars[2], pairs_ref, own_ref[...], partner_ref[...])
    for earlier_ref in earlier_refs:
        values, scale = decode(earlier_ref[...])
        sums = sums + values * (scale * scalars[3].astype(F32))
    sums_ref[...] = sums[:M, :]


def own_sums(scalars, pairs, phases, partner, arrived, piece, tile):
    local_pairs = phases.shape[0]
    tiles = piece // tile
    return pl.pallas_call(
        own_kernel,
        out_shape=jax.ShapeDtypeStruct((M, piece), F32),
        grid_spec=pltpu.PrefetchScalarGridSpec(
            num_scalar_prefetch=1,
            grid=(tiles,),
            in_specs=[
                pl.BlockSpec(pairs.shape, lambda i, s: (0, 0)),
                pl.BlockSpec((local_pairs, tile), lambda i, s: (0, s[0] * tiles + i)),
                pl.BlockSpec((local_pairs, tile), lambda i, s: (0, s[1] * tiles + i)),
            ]
            + [pl.BlockSpec((ROWS, tile), lambda i, s: (0, i))] * len(arrived),
            out_specs=pl.BlockSpec((M, tile), lambda i, s: (0, i)),
        ),
        compiler_params=pltpu.CompilerParams(vmem_limit_bytes=VMEM_BYTES),
        name="own_sums",
    )(scalars, pairs, phases, partner, *arrived)


def finish_kernel(arrivals, sums_ref, inverse_ref, *rest):
    sums = sums_ref[...]
    for earlier_ref in rest[:arrivals]:
        values, scale = decode(earlier_ref[...])
        sums = sums + (values * scale)[:M, :]
    rest[-1][...] = jnp.dot(inverse_ref[0, :M, :M], sums, precision=HIGHEST, preferred_element_type=F32)


def finish(run, sums, inverse, arrived, series, pixels, tile):
    piece = sums.shape[1]
    tiles = piece // tile
    in_specs = [
        pl.BlockSpec((M, tile), lambda i: (0, i)),
        pl.BlockSpec((1, PAD, PAD), lambda i: (run, 0, 0)),
    ] + [pl.BlockSpec((ROWS, tile), lambda i: (0, i))] * len(arrived)
    operands = [sums, inverse, *arrived]
    aliases = {}
    if series is not None:
        in_specs.append(pl.BlockSpec(memory_space=pl.ANY))
        aliases = {len(operands): 0}
        operands.append(series)
    return pl.pallas_call(
        functools.partial(finish_kernel, len(arrived)),
        out_shape=jax.ShapeDtypeStruct((M, pixels), F32),
        grid=(tiles,),
        in_specs=in_specs,
        out_specs=pl.BlockSpec((M, tile), lambda i: (0, run * tiles + i)),
        input_output_aliases=aliases,
        compiler_params=pltpu.CompilerParams(vmem_limit_bytes=VMEM_BYTES),
        name="finish",
    )(*operands)


def line_permutation(links):
    return [(2 * source + side, 2 * target + side) for source, target in links for side in range(2)]


def solve_by_sums(phases, date_pairs, run_counts):
    owner_count = lax.axis_size("ifg")
    line = owner_count // 2
    local_pairs, pixels = phases.shape
    owner_pixels = pixels // owner_count
    runs = run_counts.shape[0]
    piece = owner_pixels // runs
    tile = piece // 4
    me = lax.axis_index("ifg")
    place, side = me // 2, me % 2

    chunks = jnp.repeat(jnp.asarray(CHUNK_ORDER, jnp.int32)[place], runs)
    run_of = jnp.tile(jnp.arange(runs, dtype=jnp.int32), line)
    blocks = (chunks * 2 + side) * runs + run_of
    away_blocks = (chunks * 2 + 1 - side) * runs + run_of
    first_away = lax.dynamic_slice(phases, (0, away_blocks[0] * piece), (local_pairs, piece))
    swap = [(i, i ^ 1) for i in range(owner_count)]
    partner = lax.ppermute(first_away, "ifg", swap)

    counts = [run_counts]
    for shift in range(1, line):
        links = [(i, (i + shift) % line) for i in range(line)]
        counts.append(lax.ppermute(run_counts, "ifg", line_permutation(links)))
    piece_counts = jnp.stack(counts)[(place - chunks) % line, run_of]
    inner = ((place > 0) & (place < line - 1)).astype(jnp.int32)

    index = jnp.arange(local_pairs, dtype=jnp.int32)
    own_index, partner_index = me * local_pairs + index, (me ^ 1) * local_pairs + index
    pair_index = jnp.concatenate([own_index, partner_index])
    own_pairs = lax.dynamic_slice(date_pairs, (0, me * local_pairs), (2, local_pairs))
    partner_pairs = lax.dynamic_slice(date_pairs, (0, (me ^ 1) * local_pairs), (2, local_pairs))
    pairs = jnp.concatenate([jnp.concatenate([own_pairs, partner_pairs], axis=1), pair_index[None, :]])

    steps = (line - 1) * runs
    received = []
    for at in range(steps):
        earlier = received[at - runs][0] if at >= runs else None
        last = at == steps - 1
        next_pixels = owner_pixels if last else piece
        next_block = away_blocks[at + 1] // runs if last else away_blocks[at + 1]
        scalars = jnp.stack([blocks[at], next_block, piece_counts[at], inner])
        coded, next_away = step(scalars, pairs, phases, partner, earlier, piece, tile, next_pixels)
        partner = lax.ppermute(next_away, "ifg", swap)
        received.append([lax.ppermute(coded, "ifg", line_permutation(links)) for links in SENDS[at // runs]])

    inverse = invert_classes(date_pairs, run_counts, coded)
    sums = []
    for run in range(runs):
        scalars = jnp.stack([blocks[steps + run], jnp.int32(run), piece_counts[steps + run], 1 - inner])
        arrived = [part for place_at in range(line - 2) for part in received[place_at * runs + run]]
        sums.append(own_sums(scalars, pairs, phases, partner, arrived, piece, tile))
    series = None
    for run in range(runs):
        series = finish(run, sums[run], inverse, received[(line - 2) * runs + run], series, owner_pixels, tile)
    return series


def solve_by_blocks(phases, date_pairs, run_counts):
    owner_count = lax.axis_size("ifg")
    local_pairs, pixels = phases.shape
    owner_pixels = pixels // owner_count
    outgoing = phases.reshape(local_pairs, owner_count, owner_pixels).transpose(1, 0, 2)
    received = lax.all_to_all(outgoing, "ifg", split_axis=0, concat_axis=0, tiled=True)
    inverse = invert_classes(date_pairs, run_counts, None)
    return sum_solve(run_counts, date_pairs, received.reshape(-1, owner_pixels), inverse)


def local(phases, date_pairs, pair_counts, group_ids):
    local_pairs, _, pixels = phases.shape
    strip_groups = lax.dynamic_index_in_dim(group_ids, lax.axis_index("grp"), 0, keepdims=False)
    run_counts = jnp.take(pair_counts, strip_groups[::RUN])
    by_sums = lax.axis_size("ifg") == 2 * len(CHUNK_ORDER) and 2 * local_pairs > ROWS
    solve = solve_by_sums if by_sums else solve_by_blocks
    return solve(phases.reshape(local_pairs, pixels), date_pairs, run_counts)[None, :, :]


def solution(mesh):
    in_specs = (P("ifg", "grp", None), P(), P(), P(None, "ifg"))
    out_specs = P("grp", None, "ifg")
    return jax.shard_map(local, mesh=mesh, in_specs=in_specs, out_specs=out_specs, check_vma=False)
```

```python
import functools

import jax
import jax.numpy as jnp
import numpy as np
from jax import lax
from jax.experimental import pallas as pl
from jax.experimental.pallas import tpu as pltpu
from jax.sharding import PartitionSpec as P

M = 200
RUN = 8
PAD = 256
SLABS = 8
DAMPING = 1.0
VMEM_BYTES = 48 * 1024 * 1024
F32 = jnp.float32
HIGHEST = lax.Precision.HIGHEST
STEADY = pl.CostEstimate(flops=10_000_000_000, bytes_accessed=30_000_000, transcendentals=0)
LITTLE = pl.CostEstimate(flops=1024, bytes_accessed=1024, transcendentals=0)
CUTS = 2
FLIGHT = 2
FIRST_SWAPS = ((0, 1), (1, 1))
SWAPS = {0: (2, 2), 2: (4, 2), 3: (6, 2), 5: (8, 2), 6: (10, 2), 8: (12, 4)}
SWAP_WAITS = {8: 11}
ME, PARTNER, INNER, FIXED = 0, 1, 2, 3
CODE_ROWS = 8
ROWS = M + CODE_ROWS
LEVELS = 32700.0
CODES_PER_OCTAVE = 128.0
SMALLEST = 2.0**-110
CHUNK_ORDER = ((3, 2, 1, 0), (0, 3, 2, 1), (3, 0, 1, 2), (0, 1, 2, 3))
SENDS = (
    (((0, 1), (1, 0), (2, 3), (3, 2)),),
    (((0, 1), (1, 3), (2, 0), (3, 2)),),
    (((0, 1), (1, 2)), ((3, 2), (2, 1))),
)


def incidence(earlier, later, rows):
    shape = (rows, earlier.shape[1])
    date = lax.broadcasted_iota(jnp.int32, shape, 0)
    return (date == later).astype(F32) - (date == earlier).astype(F32)


def split_product(left, right):
    def halves(value):
        high = value.astype(jnp.bfloat16)
        return high, (value - high.astype(F32)).astype(jnp.bfloat16)

    left_high, left_low = halves(left)
    right_high, right_low = halves(right)
    small = jnp.dot(left_high, right_low, preferred_element_type=F32) + jnp.dot(left_low, right_high, preferred_element_type=F32)
    return jnp.dot(left_high, right_high, preferred_element_type=F32) + small


def full_product(left, right):
    return jnp.dot(left, right, precision=HIGHEST, preferred_element_type=F32)


def inverse_kernel(run, counts_ref, pairs_ref, *rest):
    out_ref = rest[-1]
    earlier, later = pairs_ref[0:1, :], pairs_ref[1:2, :]
    design = incidence(earlier, later, PAD)
    pair = lax.broadcasted_iota(jnp.int32, design.shape, 1)
    kept = jnp.where(pair < counts_ref[run], design, 0.0).astype(jnp.bfloat16)
    contract_last = (((1,), (1,)), ((), ()))
    gram = lax.dot_general(kept, kept, contract_last, preferred_element_type=F32)
    row = lax.broadcasted_iota(jnp.int32, gram.shape, 0)
    col = lax.broadcasted_iota(jnp.int32, gram.shape, 1)
    identity = (row == col).astype(F32)
    gram = gram + DAMPING * identity
    low = DAMPING
    high = 2.0 * jnp.max(gram) - DAMPING
    total, width = high + low, high - low
    scale = 2.0 * total * total - width * width
    start = (8.0 * total / scale) * identity - (8.0 / scale) * gram
    needed = 18.0 * scale / (8.0 * high * low)
    steps = jnp.int32(0)
    for power in range(1, 16):
        steps += (needed > float(2**power)).astype(jnp.int32)

    def newton(product, guess):
        return 2.0 * guess - product(guess, product(gram, guess))

    guess = lax.fori_loop(0, steps - 1, lambda _, guess: newton(split_product, guess), start)
    out_ref[...] = newton(full_product, newton(full_product, guess))


def invert_class(run, date_pairs, run_counts, after):
    return pl.pallas_call(
        functools.partial(inverse_kernel, run),
        out_shape=jax.ShapeDtypeStruct((PAD, PAD), F32),
        grid_spec=pltpu.PrefetchScalarGridSpec(
            num_scalar_prefetch=1,
            grid=(1,),
            in_specs=[pl.BlockSpec(date_pairs.shape, lambda i, c: (0, 0))] + [pl.BlockSpec(memory_space=pl.ANY)] * len(after),
            out_specs=pl.BlockSpec((PAD, PAD), lambda i, c: (0, 0)),
        ),
        compiler_params=pltpu.CompilerParams(vmem_limit_bytes=VMEM_BYTES),
        cost_estimate=LITTLE,
        name=f"invert_class_{run}",
    )(run_counts, date_pairs, *after)


def sum_solve_kernel(tiles, counts_ref, pairs_ref, data_ref, inverse_ref, out_ref):
    run = pl.program_id(0) // tiles
    design = incidence(pairs_ref[0:1, :], pairs_ref[1:2, :], PAD)
    pair = lax.broadcasted_iota(jnp.int32, design.shape, 1)
    kept = jnp.where(pair < counts_ref[run], design, 0.0).astype(jnp.bfloat16)
    sums = jnp.dot(kept, data_ref[...], preferred_element_type=F32)
    out_ref[...] = jnp.dot(inverse_ref[0, :M, :], sums, precision=HIGHEST, preferred_element_type=F32)


def sum_solve(run_counts, date_pairs, received, inverse):
    runs = run_counts.shape[0]
    total_pairs, pixels = received.shape
    run_pixels = pixels // runs
    tile = run_pixels // 2
    tiles = run_pixels // tile
    return pl.pallas_call(
        functools.partial(sum_solve_kernel, tiles),
        out_shape=jax.ShapeDtypeStruct((M, pixels), F32),
        grid_spec=pltpu.PrefetchScalarGridSpec(
            num_scalar_prefetch=1,
            grid=(runs * tiles,),
            in_specs=[
                pl.BlockSpec(date_pairs.shape, lambda i, c: (0, 0)),
                pl.BlockSpec((total_pairs, tile), lambda i, c: (0, i)),
                pl.BlockSpec((1, PAD, PAD), lambda i, c: (i // tiles, 0, 0)),
            ],
            out_specs=pl.BlockSpec((M, tile), lambda i, c: (0, i)),
        ),
        compiler_params=pltpu.CompilerParams(vmem_limit_bytes=VMEM_BYTES),
        name="sum_solve",
    )(run_counts, date_pairs, received, inverse)


def decode(coded):
    values = coded.astype(jnp.int32).astype(F32)
    scale = jnp.exp2(values[M : M + 1, :] * (1.0 / CODES_PER_OCTAVE)) * (1.0 / LEVELS)
    return values, scale


def encode(sums):
    largest = jnp.max(jnp.abs(sums[:M, :]), axis=0, keepdims=True)
    code = jnp.ceil(jnp.log2(jnp.maximum(largest, SMALLEST)) * CODES_PER_OCTAVE)
    inverse_scale = LEVELS / jnp.exp2(code * (1.0 / CODES_PER_OCTAVE))
    scaled = jnp.round(sums * inverse_scale)
    row = lax.broadcasted_iota(jnp.int32, sums.shape, 0)
    return jnp.where(row < M, scaled, code).astype(jnp.int32).astype(jnp.int16)


def piece_count(at, layout, table, counts):
    parts, _, _, shifts = layout
    run = at % parts // CUTS
    return counts[table[shifts + at] * (parts // CUTS) + run]


def pair_sums(count, table, pairs_ref, partner_pairs_ref, own_ref, partner_ref):
    width = own_ref.shape[0]
    sums = jnp.zeros((ROWS, own_ref.shape[1]), F32)
    lane = lax.broadcasted_iota(jnp.int32, (1, width), 1)
    for member, dates, data in ((ME, pairs_ref, own_ref), (PARTNER, partner_pairs_ref, partner_ref)):
        design = incidence(dates[0:1, :], dates[1:2, :], ROWS)
        kept = jnp.where(table[member] * width + lane < count, design, 0.0).astype(jnp.bfloat16)
        sums = sums + jnp.dot(kept, data[...], preferred_element_type=F32)
    return sums


def pair_specs(date_pairs, width):
    return [pl.BlockSpec((2, width), lambda i, t, c: (0, t[ME])), pl.BlockSpec((2, width), lambda i, t, c: (0, t[PARTNER]))]


def step_kernel(at, layout, adds, swaps, table, counts, *rest):
    pair, rest = rest[:4], rest[4:]
    if swaps:
        rest[-1][...] = rest[0][...]
        coded_ref, rest = rest[-2], rest[1:]
    else:
        coded_ref = rest[-1]
    sums = pair_sums(piece_count(at, layout, table, counts), table, *pair)
    if adds:
        values, scale = decode(rest[0][...])
        sums = sums + values * (scale * table[INNER].astype(F32))
    coded_ref[...] = encode(sums)


def step(at, swap, layout, scalars, date_pairs, phases, partner, earlier, after, piece):
    partner, place_in = partner
    local_pairs = phases.shape[0]
    _, blocks, away, _ = layout
    tiles = 2
    tile = piece // tiles
    in_specs = pair_specs(date_pairs, local_pairs) + [
        pl.BlockSpec((local_pairs, tile), lambda i, t, c: (0, t[blocks + at] * tiles + i)),
        pl.BlockSpec((local_pairs, tile), lambda i, t, c: (0, place_in * tiles + i)),
    ]
    operands = [date_pairs, date_pairs, phases, partner]
    out_shape = [jax.ShapeDtypeStruct((ROWS, piece), jnp.int16)]
    out_specs = [pl.BlockSpec((ROWS, tile), lambda i, t, c: (0, i))]
    if swap is not None:
        first, count = swap
        wide = tile * count
        in_specs.append(pl.BlockSpec((local_pairs, wide), lambda i, t, c: (0, t[away + first] // count * tiles + i)))
        operands.append(phases)
        out_shape.append(jax.ShapeDtypeStruct((local_pairs, piece * count), phases.dtype))
        out_specs.append(pl.BlockSpec((local_pairs, wide), lambda i, t, c: (0, i)))
    if earlier is not None:
        in_specs.append(pl.BlockSpec((ROWS, tile), lambda i, t, c: (0, i)))
        operands.append(earlier)
    in_specs += [pl.BlockSpec(memory_space=pl.ANY)] * len(after)
    results = pl.pallas_call(
        functools.partial(step_kernel, at, layout, earlier is not None, swap is not None),
        out_shape=out_shape,
        grid_spec=pltpu.PrefetchScalarGridSpec(
            num_scalar_prefetch=2,
            grid=(tiles,),
            in_specs=in_specs,
            out_specs=out_specs,
        ),
        compiler_params=pltpu.CompilerParams(vmem_limit_bytes=VMEM_BYTES),
        cost_estimate=STEADY,
        name=f"sum_step_{at:02d}",
    )(*scalars, *operands, *after)
    return results if swap is not None else (results[0], None)


def own_kernel(at, layout, table, counts, *rest):
    sums = pair_sums(piece_count(at, layout, table, counts), table, *rest[:4])
    for earlier_ref in rest[4:-1]:
        values, scale = decode(earlier_ref[...])
        sums = sums + values * (scale * (1 - table[INNER]).astype(F32))
    rest[-1][...] = sums[:M, :]


def own_sums(at, layout, scalars, date_pairs, phases, partner, arrived, piece):
    partner, place_in = partner
    local_pairs = phases.shape[0]
    blocks = layout[1]
    tiles = 2
    tile = piece // tiles
    return pl.pallas_call(
        functools.partial(own_kernel, at, layout),
        out_shape=jax.ShapeDtypeStruct((M, piece), F32),
        grid_spec=pltpu.PrefetchScalarGridSpec(
            num_scalar_prefetch=2,
            grid=(tiles,),
            in_specs=pair_specs(date_pairs, local_pairs)
            + [
                pl.BlockSpec((local_pairs, tile), lambda i, t, c: (0, t[blocks + at] * tiles + i)),
                pl.BlockSpec((local_pairs, tile), lambda i, t, c: (0, place_in * tiles + i)),
            ]
            + [pl.BlockSpec((ROWS, tile), lambda i, t, c: (0, i))] * len(arrived),
            out_specs=pl.BlockSpec((M, tile), lambda i, t, c: (0, i)),
        ),
        compiler_params=pltpu.CompilerParams(vmem_limit_bytes=VMEM_BYTES),
        cost_estimate=LITTLE,
        name=f"own_sums_{at:02d}",
    )(*scalars, date_pairs, date_pairs, phases, partner, *arrived)


def finish_kernel(arrivals, sums_ref, inverse_ref, *rest):
    sums = sums_ref[...]
    for earlier_ref in rest[:arrivals]:
        values, scale = decode(earlier_ref[...])
        sums = sums + (values * scale)[:M, :]
    rest[-1][...] = full_product(inverse_ref[:M, :M], sums)


def finish(part, sums, inverse, arrived, series, pixels):
    piece = sums.shape[1]
    tiles = 2
    tile = piece // tiles
    in_specs = [
        pl.BlockSpec((M, tile), lambda i: (0, i)),
        pl.BlockSpec((PAD, PAD), lambda i: (0, 0)),
    ] + [pl.BlockSpec((ROWS, tile), lambda i: (0, i))] * len(arrived)
    operands = [sums, inverse, *arrived]
    aliases = {}
    if series is not None:
        in_specs.append(pl.BlockSpec(memory_space=pl.ANY))
        aliases = {len(operands): 0}
        operands.append(series)
    return pl.pallas_call(
        functools.partial(finish_kernel, len(arrived)),
        out_shape=jax.ShapeDtypeStruct((M, pixels), F32),
        grid=(tiles,),
        in_specs=in_specs,
        out_specs=pl.BlockSpec((M, tile), lambda i: (0, part * tiles + i)),
        input_output_aliases=aliases,
        compiler_params=pltpu.CompilerParams(vmem_limit_bytes=VMEM_BYTES),
        cost_estimate=LITTLE,
        name=f"finish_{part}",
    )(*operands)


def line_permutation(links):
    return [(2 * source + side, 2 * target + side) for source, target in links for side in range(2)]


def solve_by_sums(phases, date_pairs, counts_of):
    owner_count = lax.axis_size("ifg")
    line = owner_count // 2
    local_pairs, pixels = phases.shape
    owner_pixels = pixels // owner_count
    runs = counts_of(None).shape[0]
    parts = runs * CUTS
    piece = owner_pixels // parts
    steps = (line - 1) * parts
    me = lax.axis_index("ifg")

    places = np.repeat(np.array(CHUNK_ORDER), parts, axis=1)
    part_of = np.tile(np.arange(parts), line)
    rows = []
    for device in range(owner_count):
        place, side = device // 2, device % 2
        own = (places[place] * 2 + side) * parts + part_of
        away = (places[place] * 2 + 1 - side) * parts + part_of
        shift = (place - places[place]) % line
        rows.append(np.concatenate([[device, device ^ 1, int(0 < place < line - 1)], own, away, shift]))
    row = lax.dynamic_index_in_dim(jnp.asarray(np.stack(rows), jnp.int32), me, 0, keepdims=False)
    head, pieces = FIXED, line * parts
    layout = (parts, head, head + pieces, head + 2 * pieces)

    swap = [(i, i ^ 1) for i in range(owner_count)]
    partner_of = {}

    def swapped(away, first, count):
        here = lax.ppermute(away, "ifg", swap)
        partner_of.update({first + place: (here, place) for place in range(count)})

    counts = None
    for first, count in FIRST_SWAPS:
        block = row[head + pieces + first]
        if counts is not None:
            block, _ = lax.optimization_barrier((block, counts))
        away = lax.dynamic_slice(phases, (0, block * piece), (local_pairs, piece * count))
        swapped(away, first, count)
        if counts is None:
            run_counts = counts_of(away)
            counts = [run_counts]
            for distance in range(1, line):
                links = [(i, (i + distance) % line) for i in range(line)]
                counts.append(lax.ppermute(run_counts, "ifg", line_permutation(links)))
            counts = jnp.concatenate(counts)
    scalars = (row, counts)

    received, inverses, coded = [], [], None
    for at in range(steps):
        earlier = received[at - parts][0] if at >= parts else None
        after = [coded] if at else []
        after += received[at - FLIGHT] if at >= FLIGHT else []
        if at in SWAP_WAITS:
            after.append(partner_of[SWAP_WAITS[at]][0])
        if at >= parts and at % 2 == 0 and len(inverses) < runs:
            inverses.append(invert_class(len(inverses), date_pairs, run_counts, received[at - FLIGHT]))
            after.append(inverses[-1])
        coded, away = step(at, SWAPS.get(at), layout, scalars, date_pairs, phases, partner_of[at], earlier, after, piece)
        received.append([lax.ppermute(coded, "ifg", line_permutation(links)) for links in SENDS[at // parts]])
        if at in SWAPS:
            swapped(away, *SWAPS[at])

    sums = []
    for part in range(parts):
        arrived = [each for place in range(line - 2) for each in received[place * parts + part]]
        sums.append(own_sums(steps + part, layout, scalars, date_pairs, phases, partner_of[steps + part], arrived, piece))
    series = None
    for part in range(parts):
        series = finish(part, sums[part], inverses[part // CUTS], received[(line - 2) * parts + part], series, owner_pixels)
    return series


def solve_by_blocks(phases, date_pairs, counts_of):
    owner_count = lax.axis_size("ifg")
    local_pairs, pixels = phases.shape
    owner_pixels = pixels // owner_count
    run_counts = counts_of(None)
    outgoing = phases.reshape(local_pairs, owner_count, owner_pixels).transpose(1, 0, 2)
    received = lax.all_to_all(outgoing, "ifg", split_axis=0, concat_axis=0, tiled=True)
    inverse = jnp.stack([invert_class(run, date_pairs, run_counts, []) for run in range(run_counts.shape[0])])
    return sum_solve(run_counts, date_pairs, received.reshape(-1, owner_pixels), inverse)


def local(phases, date_pairs, pair_counts, group_ids):
    local_pairs, _, pixels = phases.shape

    def counts_of(after):
        groups = group_ids if after is None else lax.optimization_barrier((group_ids, after))[0]
        strip_groups = lax.dynamic_index_in_dim(groups, lax.axis_index("grp"), 0, keepdims=False)[::RUN]
        chosen = strip_groups[:, None] == jnp.arange(pair_counts.shape[0], dtype=jnp.int32)
        return jnp.sum(jnp.where(chosen, pair_counts, 0), axis=1)

    line = lax.axis_size("ifg") == 2 * len(CHUNK_ORDER) and group_ids.shape[1] == 2 * RUN
    by_sums = line and 2 * local_pairs > ROWS and local_pairs % 128 == 0
    solve = solve_by_sums if by_sums else solve_by_blocks
    return solve(phases.reshape(local_pairs, pixels), date_pairs, counts_of)[None, :, :]


def solution(mesh):
    in_specs = (P("ifg", "grp", None), P(), P(), P(None, "ifg"))
    out_specs = P("grp", None, "ifg")
    return jax.shard_map(local, mesh=mesh, in_specs=in_specs, out_specs=out_specs, check_vma=False)
```

```python
import functools

import jax
import jax.numpy as jnp
import numpy as np
from jax import lax
from jax.experimental import pallas as pl
from jax.experimental.pallas import tpu as pltpu
from jax.sharding import PartitionSpec as P

M = 200
RUN = 8
PAD = 256
SLABS = 8
DAMPING = 1.0
VMEM_BYTES = 48 * 1024 * 1024
F32 = jnp.float32
HIGHEST = lax.Precision.HIGHEST
STEADY = pl.CostEstimate(flops=10_000_000_000, bytes_accessed=30_000_000, transcendentals=0)
LITTLE = pl.CostEstimate(flops=1024, bytes_accessed=1024, transcendentals=0)
CUTS = 2
FLIGHT = 2
FIRST_SWAPS = ((0, 1), (1, 1))
SWAPS = {0: (2, 2), 2: (4, 2), 3: (6, 2), 4: (8, 2), 5: (10, 2), 7: (12, 4)}
SWAP_WAITS = {7: 9, 8: 11}
OWN_STEPS = {10: (0, 1), 11: (2, 3)}
ME, PARTNER, INNER, FIXED = 0, 1, 2, 3
CODE_ROWS = 8
ROWS = M + CODE_ROWS
LEVELS = 32700.0
CODES_PER_OCTAVE = 128.0
SMALLEST = 2.0**-110
CHUNK_ORDER = ((3, 2, 1, 0), (0, 3, 2, 1), (3, 0, 1, 2), (0, 1, 2, 3))
SENDS = (
    (((0, 1), (1, 0), (2, 3), (3, 2)),),
    (((0, 1), (1, 3), (2, 0), (3, 2)),),
    (((0, 1), (3, 2)), ((1, 2), (2, 1))),
)


def incidence(earlier, later, rows):
    shape = (rows, earlier.shape[1])
    date = lax.broadcasted_iota(jnp.int32, shape, 0)
    return (date == later).astype(F32) - (date == earlier).astype(F32)


def split_product(left, right):
    def halves(value):
        high = value.astype(jnp.bfloat16)
        return high, (value - high.astype(F32)).astype(jnp.bfloat16)

    left_high, left_low = halves(left)
    right_high, right_low = halves(right)
    small = jnp.dot(left_high, right_low, preferred_element_type=F32) + jnp.dot(left_low, right_high, preferred_element_type=F32)
    return jnp.dot(left_high, right_high, preferred_element_type=F32) + small


def full_product(left, right):
    return jnp.dot(left, right, precision=HIGHEST, preferred_element_type=F32)


def inverse_kernel(counts_ref, pairs_ref, *rest):
    out_ref = rest[-1]
    runs = out_ref.shape[0]
    design = incidence(pairs_ref[0:1, :], pairs_ref[1:2, :], PAD)
    pair = lax.broadcasted_iota(jnp.int32, design.shape, 1)
    contract_last = (((1,), (1,)), ((), ()))
    row = lax.broadcasted_iota(jnp.int32, (PAD, PAD), 0)
    col = lax.broadcasted_iota(jnp.int32, (PAD, PAD), 1)
    identity = (row == col).astype(F32)
    grams = []
    for run in range(runs):
        kept = jnp.where(pair < counts_ref[run], design, 0.0).astype(jnp.bfloat16)
        gram = lax.dot_general(kept, kept, contract_last, preferred_element_type=F32)
        grams.append(gram + DAMPING * identity)
    low = DAMPING
    high = 2.0 * functools.reduce(jnp.maximum, [jnp.max(gram) for gram in grams]) - DAMPING
    total, width = high + low, high - low
    scale = 2.0 * total * total - width * width
    starts = tuple((8.0 * total / scale) * identity - (8.0 / scale) * gram for gram in grams)
    needed = 18.0 * scale / (8.0 * high * low)
    steps = jnp.int32(0)
    for power in range(1, 16):
        steps += (needed > float(2**power)).astype(jnp.int32)

    def newton(product, guesses):
        products = [product(gram, guess) for gram, guess in zip(grams, guesses)]
        return tuple(2.0 * guess - product(guess, each) for guess, each in zip(guesses, products))

    guesses = lax.fori_loop(0, steps - 1, lambda _, guesses: newton(split_product, guesses), starts)
    for run, guess in enumerate(newton(full_product, newton(full_product, guesses))):
        out_ref[run] = guess


def invert_classes(date_pairs, run_counts, after):
    shape = (run_counts.shape[0], PAD, PAD)
    return pl.pallas_call(
        inverse_kernel,
        out_shape=jax.ShapeDtypeStruct(shape, F32),
        grid_spec=pltpu.PrefetchScalarGridSpec(
            num_scalar_prefetch=1,
            grid=(1,),
            in_specs=[pl.BlockSpec(date_pairs.shape, lambda i, c: (0, 0))] + [pl.BlockSpec(memory_space=pl.ANY)] * len(after),
            out_specs=pl.BlockSpec(shape, lambda i, c: (0, 0, 0)),
        ),
        compiler_params=pltpu.CompilerParams(vmem_limit_bytes=VMEM_BYTES),
        cost_estimate=LITTLE,
        name="invert_classes_0",
    )(run_counts, date_pairs, *after)


def sum_solve_kernel(tiles, counts_ref, pairs_ref, data_ref, inverse_ref, out_ref):
    run = pl.program_id(0) // tiles
    design = incidence(pairs_ref[0:1, :], pairs_ref[1:2, :], PAD)
    pair = lax.broadcasted_iota(jnp.int32, design.shape, 1)
    kept = jnp.where(pair < counts_ref[run], design, 0.0).astype(jnp.bfloat16)
    sums = jnp.dot(kept, data_ref[...], preferred_element_type=F32)
    out_ref[...] = jnp.dot(inverse_ref[0, :M, :], sums, precision=HIGHEST, preferred_element_type=F32)


def sum_solve(run_counts, date_pairs, received, inverse):
    runs = run_counts.shape[0]
    total_pairs, pixels = received.shape
    run_pixels = pixels // runs
    tile = run_pixels // 2
    tiles = run_pixels // tile
    return pl.pallas_call(
        functools.partial(sum_solve_kernel, tiles),
        out_shape=jax.ShapeDtypeStruct((M, pixels), F32),
        grid_spec=pltpu.PrefetchScalarGridSpec(
            num_scalar_prefetch=1,
            grid=(runs * tiles,),
            in_specs=[
                pl.BlockSpec(date_pairs.shape, lambda i, c: (0, 0)),
                pl.BlockSpec((total_pairs, tile), lambda i, c: (0, i)),
                pl.BlockSpec((1, PAD, PAD), lambda i, c: (i // tiles, 0, 0)),
            ],
            out_specs=pl.BlockSpec((M, tile), lambda i, c: (0, i)),
        ),
        compiler_params=pltpu.CompilerParams(vmem_limit_bytes=VMEM_BYTES),
        name="sum_solve",
    )(run_counts, date_pairs, received, inverse)


def decode(coded):
    values = coded.astype(jnp.int32).astype(F32)
    scale = jnp.exp2(values[M : M + 1, :] * (1.0 / CODES_PER_OCTAVE)) * (1.0 / LEVELS)
    return values, scale


def encode(sums):
    largest = jnp.max(jnp.abs(sums[:M, :]), axis=0, keepdims=True)
    code = jnp.ceil(jnp.log2(jnp.maximum(largest, SMALLEST)) * CODES_PER_OCTAVE)
    inverse_scale = LEVELS / jnp.exp2(code * (1.0 / CODES_PER_OCTAVE))
    scaled = jnp.round(sums * inverse_scale)
    row = lax.broadcasted_iota(jnp.int32, sums.shape, 0)
    return jnp.where(row < M, scaled, code).astype(jnp.int32).astype(jnp.int16)


def piece_count(at, layout, table, counts):
    parts, _, _, shifts = layout
    run = at % parts // CUTS
    return counts[table[shifts + at] * (parts // CUTS) + run]


def pair_sums(count, table, pairs_ref, own_ref, partner_ref):
    width = own_ref.shape[0]
    sums = jnp.zeros((ROWS, own_ref.shape[1]), F32)
    lane = lax.broadcasted_iota(jnp.int32, (1, width), 1)
    for member, dates, data in ((ME, pairs_ref[:, :width], own_ref), (PARTNER, pairs_ref[:, width:], partner_ref)):
        design = incidence(dates[0:1, :], dates[1:2, :], ROWS)
        kept = jnp.where(table[member] * width + lane < count, design, 0.0).astype(jnp.bfloat16)
        sums = sums + jnp.dot(kept, data[...], preferred_element_type=F32)
    return sums


def copy_kernel(table, source_ref, _, target_ref):
    target_ref[...] = source_ref[...]


def give_out(swap, layout, table, phases, after, piece):
    first, count = swap
    away = layout[2]
    shape = (phases.shape[0], piece * count)
    return pl.pallas_call(
        copy_kernel,
        out_shape=jax.ShapeDtypeStruct(shape, phases.dtype),
        grid_spec=pltpu.PrefetchScalarGridSpec(
            num_scalar_prefetch=1,
            grid=(1,),
            in_specs=[
                pl.BlockSpec(shape, lambda i, t: (0, t[away + first] // count)),
                pl.BlockSpec(memory_space=pl.ANY),
            ],
            out_specs=pl.BlockSpec(shape, lambda i, t: (0, 0)),
        ),
        compiler_params=pltpu.CompilerParams(vmem_limit_bytes=VMEM_BYTES),
        cost_estimate=LITTLE,
        name="give_out",
    )(table, phases, after)


def step_kernel(at, layout, adds, swaps, table, counts, *rest):
    pair, rest = rest[:3], rest[3:]
    if swaps:
        rest[-1][...] = rest[0][...]
        coded_ref, rest = rest[-2], rest[1:]
    else:
        coded_ref = rest[-1]
    sums = pair_sums(piece_count(at, layout, table, counts), table, *pair)
    if adds:
        values, scale = decode(rest[0][...])
        sums = sums + values * (scale * table[INNER].astype(F32))
    coded_ref[...] = encode(sums)


def step(at, swap, layout, scalars, pairs, phases, partner, earlier, after, piece):
    partner, place_in = partner
    local_pairs = phases.shape[0]
    _, blocks, away, _ = layout
    tiles = 2
    tile = piece // tiles
    in_specs = [
        pl.BlockSpec(pairs.shape, lambda i, t, c: (0, 0)),
        pl.BlockSpec((local_pairs, tile), lambda i, t, c: (0, t[blocks + at] * tiles + i)),
        pl.BlockSpec((local_pairs, tile), lambda i, t, c: (0, place_in * tiles + i)),
    ]
    operands = [pairs, phases, partner]
    out_shape = [jax.ShapeDtypeStruct((ROWS, piece), jnp.int16)]
    out_specs = [pl.BlockSpec((ROWS, tile), lambda i, t, c: (0, i))]
    if swap is not None:
        first, count = swap
        wide = tile * count
        in_specs.append(pl.BlockSpec((local_pairs, wide), lambda i, t, c: (0, t[away + first] // count * tiles + i)))
        operands.append(phases)
        out_shape.append(jax.ShapeDtypeStruct((local_pairs, piece * count), phases.dtype))
        out_specs.append(pl.BlockSpec((local_pairs, wide), lambda i, t, c: (0, i)))
    if earlier is not None:
        in_specs.append(pl.BlockSpec((ROWS, tile), lambda i, t, c: (0, i)))
        operands.append(earlier)
    in_specs += [pl.BlockSpec(memory_space=pl.ANY)] * len(after)
    results = pl.pallas_call(
        functools.partial(step_kernel, at, layout, earlier is not None, swap is not None),
        out_shape=out_shape,
        grid_spec=pltpu.PrefetchScalarGridSpec(
            num_scalar_prefetch=2,
            grid=(tiles,),
            in_specs=in_specs,
            out_specs=out_specs,
        ),
        compiler_params=pltpu.CompilerParams(vmem_limit_bytes=VMEM_BYTES),
        cost_estimate=STEADY,
        name=f"sum_step_{at:02d}",
    )(*scalars, *operands, *after)
    return results if swap is not None else (results[0], None)


def own_kernel(at, layout, table, counts, *rest):
    sums = pair_sums(piece_count(at, layout, table, counts), table, *rest[:3])
    for earlier_ref in rest[3:-1]:
        values, scale = decode(earlier_ref[...])
        sums = sums + values * (scale * (1 - table[INNER]).astype(F32))
    rest[-1][...] = sums[:M, :]


def own_sums(at, layout, scalars, pairs, phases, partner, arrived, piece):
    partner, place_in = partner
    local_pairs = phases.shape[0]
    blocks = layout[1]
    tiles = 2
    tile = piece // tiles
    return pl.pallas_call(
        functools.partial(own_kernel, at, layout),
        out_shape=jax.ShapeDtypeStruct((M, piece), F32),
        grid_spec=pltpu.PrefetchScalarGridSpec(
            num_scalar_prefetch=2,
            grid=(tiles,),
            in_specs=[
                pl.BlockSpec(pairs.shape, lambda i, t, c: (0, 0)),
                pl.BlockSpec((local_pairs, tile), lambda i, t, c: (0, t[blocks + at] * tiles + i)),
                pl.BlockSpec((local_pairs, tile), lambda i, t, c: (0, place_in * tiles + i)),
            ]
            + [pl.BlockSpec((ROWS, tile), lambda i, t, c: (0, i))] * len(arrived),
            out_specs=pl.BlockSpec((M, tile), lambda i, t, c: (0, i)),
        ),
        compiler_params=pltpu.CompilerParams(vmem_limit_bytes=VMEM_BYTES),
        cost_estimate=LITTLE,
        name=f"own_sums_{at:02d}",
    )(*scalars, pairs, phases, partner, *arrived)


def finish_kernel(arrivals, sums_ref, inverse_ref, *rest):
    sums = sums_ref[...]
    for earlier_ref in rest[:arrivals]:
        values, scale = decode(earlier_ref[...])
        sums = sums + (values * scale)[:M, :]
    rest[-1][...] = full_product(inverse_ref[0, :M, :M], sums)


def finish(part, sums, inverse, arrived, series, pixels):
    piece = sums.shape[1]
    tiles = 2
    tile = piece // tiles
    in_specs = [
        pl.BlockSpec((M, tile), lambda i: (0, i)),
        pl.BlockSpec((1, PAD, PAD), lambda i: (part // CUTS, 0, 0)),
    ] + [pl.BlockSpec((ROWS, tile), lambda i: (0, i))] * len(arrived)
    operands = [sums, inverse, *arrived]
    aliases = {}
    if series is not None:
        in_specs.append(pl.BlockSpec(memory_space=pl.ANY))
        aliases = {len(operands): 0}
        operands.append(series)
    return pl.pallas_call(
        functools.partial(finish_kernel, len(arrived)),
        out_shape=jax.ShapeDtypeStruct((M, pixels), F32),
        grid=(tiles,),
        in_specs=in_specs,
        out_specs=pl.BlockSpec((M, tile), lambda i: (0, part * tiles + i)),
        input_output_aliases=aliases,
        compiler_params=pltpu.CompilerParams(vmem_limit_bytes=VMEM_BYTES),
        cost_estimate=LITTLE,
        name=f"finish_{part}",
    )(*operands)


def line_permutation(links):
    return [(2 * source + side, 2 * target + side) for source, target in links for side in range(2)]


def solve_by_sums(phases, date_pairs, counts_of):
    owner_count = lax.axis_size("ifg")
    line = owner_count // 2
    local_pairs, pixels = phases.shape
    owner_pixels = pixels // owner_count
    runs = counts_of().shape[0]
    parts = runs * CUTS
    piece = owner_pixels // parts
    steps = (line - 1) * parts
    me = lax.axis_index("ifg")

    places = np.repeat(np.array(CHUNK_ORDER), parts, axis=1)
    part_of = np.tile(np.arange(parts), line)
    rows = []
    for device in range(owner_count):
        place, side = device // 2, device % 2
        own = (places[place] * 2 + side) * parts + part_of
        away = (places[place] * 2 + 1 - side) * parts + part_of
        shift = (place - places[place]) % line
        rows.append(np.concatenate([[device, device ^ 1, int(0 < place < line - 1)], own, away, shift]))
    row = lax.dynamic_index_in_dim(jnp.asarray(np.stack(rows), jnp.int32), me, 0, keepdims=False)
    head, pieces = FIXED, line * parts
    layout = (parts, head, head + pieces, head + 2 * pieces)

    swap = [(i, i ^ 1) for i in range(owner_count)]
    partner_of = {}

    def swapped(away, first, count):
        here = lax.ppermute(away, "ifg", swap)
        partner_of.update({first + place: (here, place) for place in range(count)})

    run_counts = counts_of()
    counts = [run_counts]
    for distance in range(1, line):
        links = [(i, (i + distance) % line) for i in range(line)]
        counts.append(lax.ppermute(run_counts, "ifg", line_permutation(links)))
    counts = jnp.concatenate(counts)
    (first, count), second = FIRST_SWAPS
    block, _ = lax.optimization_barrier((row[head + pieces + first], run_counts))
    swapped(lax.dynamic_slice(phases, (0, block * piece), (local_pairs, piece * count)), first, count)
    swapped(give_out(second, layout, row, phases, counts, piece), *second)
    pairs = jnp.concatenate([lax.dynamic_slice(date_pairs, (0, row[at] * local_pairs), (2, local_pairs)) for at in (ME, PARTNER)], axis=1)
    scalars = (row, counts)

    received, sums, coded = [], [], None
    for at in range(steps):
        earlier = received[at - parts][0] if at >= parts else None
        after = [coded] if at else []
        after += received[at - FLIGHT] if at >= FLIGHT else []
        if at in SWAP_WAITS:
            after.append(partner_of[SWAP_WAITS[at]][0])
        for part in OWN_STEPS.get(at, ()):
            arrived = [each for place in range(line - 2) for each in received[place * parts + part]]
            sums.append(own_sums(steps + part, layout, scalars, pairs, phases, partner_of[steps + part], arrived, piece))
            after.append(sums[-1])
        coded, away = step(at, SWAPS.get(at), layout, scalars, pairs, phases, partner_of[at], earlier, after, piece)
        received.append([lax.ppermute(coded, "ifg", line_permutation(links)) for links in SENDS[at // parts]])
        if at in SWAPS:
            swapped(away, *SWAPS[at])

    inverse = invert_classes(date_pairs, run_counts, [coded])
    series = None
    for part in range(parts):
        series = finish(part, sums[part], inverse, received[(line - 2) * parts + part], series, owner_pixels)
    return series


def solve_by_blocks(phases, date_pairs, counts_of):
    owner_count = lax.axis_size("ifg")
    local_pairs, pixels = phases.shape
    owner_pixels = pixels // owner_count
    run_counts = counts_of()
    outgoing = phases.reshape(local_pairs, owner_count, owner_pixels).transpose(1, 0, 2)
    received = lax.all_to_all(outgoing, "ifg", split_axis=0, concat_axis=0, tiled=True)
    inverse = invert_classes(date_pairs, run_counts, [])
    return sum_solve(run_counts, date_pairs, received.reshape(-1, owner_pixels), inverse)


def local(phases, date_pairs, pair_counts, group_ids):
    local_pairs, _, pixels = phases.shape

    def counts_of():
        strip_groups = lax.dynamic_index_in_dim(group_ids, lax.axis_index("grp"), 0, keepdims=False)[::RUN]
        chosen = strip_groups[:, None] == jnp.arange(pair_counts.shape[0], dtype=jnp.int32)
        return jnp.sum(jnp.where(chosen, pair_counts, 0), axis=1)

    line = lax.axis_size("ifg") == 2 * len(CHUNK_ORDER) and group_ids.shape[1] == 2 * RUN
    by_sums = line and 2 * local_pairs > ROWS and local_pairs % 128 == 0
    solve = solve_by_sums if by_sums else solve_by_blocks
    return solve(phases.reshape(local_pairs, pixels), date_pairs, counts_of)[None, :, :]


def solution(mesh):
    in_specs = (P("ifg", "grp", None), P(), P(), P(None, "ifg"))
    out_specs = P("grp", None, "ifg")
    return jax.shard_map(local, mesh=mesh, in_specs=in_specs, out_specs=out_specs, check_vma=False)
```

```python
import functools

import jax
import jax.numpy as jnp
import numpy as np
from jax import lax
from jax.experimental import pallas as pl
from jax.experimental.pallas import tpu as pltpu
from jax.sharding import PartitionSpec as P

M = 200
RUN = 8
PAD = 256
SLABS = 8
DAMPING = 1.0
VMEM_BYTES = 48 * 1024 * 1024
F32 = jnp.float32
HIGHEST = lax.Precision.HIGHEST
STEADY = pl.CostEstimate(flops=10_000_000_000, bytes_accessed=30_000_000, transcendentals=0)
LITTLE = pl.CostEstimate(flops=1024, bytes_accessed=1024, transcendentals=0)
CUTS = 2
HALVES = 2
FLIGHT = 2
FIRST_SWAPS = ((0, 1), (1, 1), (2, 2))
SWAPS = {1: (4, 2), 3: (6, 2), 4: (8, 2), 5: (10, 2), 6: (12, 2), 7: (14, 2)}
SWAP_WAITS = {5: 6, 6: 8, 7: 10, 8: 12, 9: 14}
INVERSE_STEP = 6
OWN_STEPS = {10: (0, 1), 11: (2, 3)}
ME, PARTNER, INNER, FIXED = 0, 1, 2, 3
LANES = 128
CODE_ROWS = 16
LEVELS = 32700.0
CODES_PER_OCTAVE = 128.0
SMALLEST = 2.0**-110
CHUNK_ORDER = ((3, 2, 1, 0), (0, 3, 2, 1), (3, 0, 1, 2), (0, 1, 2, 3))
SENDS = (
    (((0, 1), (1, 0), (2, 3), (3, 2)),),
    (((0, 1), (1, 3), (2, 0), (3, 2)),),
    (((0, 1), (3, 2)), ((1, 2), (2, 1))),
)


def incidence(earlier, later, rows):
    shape = (rows, earlier.shape[1])
    date = lax.broadcasted_iota(jnp.int32, shape, 0)
    return (date == later).astype(F32) - (date == earlier).astype(F32)


def split_product(left, right):
    def halves(value):
        high = value.astype(jnp.bfloat16)
        return high, (value - high.astype(F32)).astype(jnp.bfloat16)

    left_high, left_low = halves(left)
    right_high, right_low = halves(right)
    small = jnp.dot(left_high, right_low, preferred_element_type=F32) + jnp.dot(left_low, right_high, preferred_element_type=F32)
    return jnp.dot(left_high, right_high, preferred_element_type=F32) + small


def full_product(left, right):
    return jnp.dot(left, right, precision=HIGHEST, preferred_element_type=F32)


def inverse_kernel(counts_ref, pairs_ref, *rest):
    out_ref = rest[-1]
    runs = out_ref.shape[0]
    design = incidence(pairs_ref[0:1, :], pairs_ref[1:2, :], PAD)
    pair = lax.broadcasted_iota(jnp.int32, design.shape, 1)
    contract_last = (((1,), (1,)), ((), ()))
    row = lax.broadcasted_iota(jnp.int32, (PAD, PAD), 0)
    col = lax.broadcasted_iota(jnp.int32, (PAD, PAD), 1)
    identity = (row == col).astype(F32)
    grams = []
    for run in range(runs):
        kept = jnp.where(pair < counts_ref[run], design, 0.0).astype(jnp.bfloat16)
        gram = lax.dot_general(kept, kept, contract_last, preferred_element_type=F32)
        grams.append(gram + DAMPING * identity)
    low = DAMPING
    high = 2.0 * functools.reduce(jnp.maximum, [jnp.max(gram) for gram in grams]) - DAMPING
    total, width = high + low, high - low
    scale = 2.0 * total * total - width * width
    starts = tuple((8.0 * total / scale) * identity - (8.0 / scale) * gram for gram in grams)
    needed = 18.0 * scale / (8.0 * high * low)
    steps = jnp.int32(0)
    for power in range(1, 16):
        steps += (needed > float(2**power)).astype(jnp.int32)

    def newton(product, guesses):
        products = [product(gram, guess) for gram, guess in zip(grams, guesses)]
        return tuple(2.0 * guess - product(guess, each) for guess, each in zip(guesses, products))

    guesses = lax.fori_loop(0, steps - 1, lambda _, guesses: newton(split_product, guesses), starts)
    for run, guess in enumerate(newton(full_product, newton(full_product, guesses))):
        out_ref[run] = guess


def invert_classes(date_pairs, run_counts, after):
    shape = (run_counts.shape[0], PAD, PAD)
    return pl.pallas_call(
        inverse_kernel,
        out_shape=jax.ShapeDtypeStruct(shape, F32),
        grid_spec=pltpu.PrefetchScalarGridSpec(
            num_scalar_prefetch=1,
            grid=(1,),
            in_specs=[pl.BlockSpec(date_pairs.shape, lambda i, c: (0, 0))] + [pl.BlockSpec(memory_space=pl.ANY)] * len(after),
            out_specs=pl.BlockSpec(shape, lambda i, c: (0, 0, 0)),
        ),
        compiler_params=pltpu.CompilerParams(vmem_limit_bytes=VMEM_BYTES),
        cost_estimate=LITTLE,
        name="invert_classes_0",
    )(run_counts, date_pairs, *after)


def sum_solve_kernel(tiles, counts_ref, pairs_ref, data_ref, inverse_ref, out_ref):
    run = pl.program_id(0) // tiles
    design = incidence(pairs_ref[0:1, :], pairs_ref[1:2, :], PAD)
    pair = lax.broadcasted_iota(jnp.int32, design.shape, 1)
    kept = jnp.where(pair < counts_ref[run], design, 0.0).astype(jnp.bfloat16)
    sums = jnp.dot(kept, data_ref[...], preferred_element_type=F32)
    out_ref[...] = jnp.dot(inverse_ref[0, :M, :], sums, precision=HIGHEST, preferred_element_type=F32)


def sum_solve(run_counts, date_pairs, received, inverse):
    runs = run_counts.shape[0]
    total_pairs, pixels = received.shape
    run_pixels = pixels // runs
    tile = run_pixels // 2
    tiles = run_pixels // tile
    return pl.pallas_call(
        functools.partial(sum_solve_kernel, tiles),
        out_shape=jax.ShapeDtypeStruct((M, pixels), F32),
        grid_spec=pltpu.PrefetchScalarGridSpec(
            num_scalar_prefetch=1,
            grid=(runs * tiles,),
            in_specs=[
                pl.BlockSpec(date_pairs.shape, lambda i, c: (0, 0)),
                pl.BlockSpec((total_pairs, tile), lambda i, c: (0, i)),
                pl.BlockSpec((1, PAD, PAD), lambda i, c: (i // tiles, 0, 0)),
            ],
            out_specs=pl.BlockSpec((M, tile), lambda i, c: (0, i)),
        ),
        compiler_params=pltpu.CompilerParams(vmem_limit_bytes=VMEM_BYTES),
        name="sum_solve",
    )(run_counts, date_pairs, received, inverse)


def coded_rows(piece):
    return M * (piece // LANES) + CODE_ROWS


def decode(coded_ref, codes_ref, lots, first):
    coded = coded_ref[...].astype(jnp.int32).astype(F32)
    values = jnp.concatenate([coded[lot * M : (lot + 1) * M, :] for lot in range(lots)], axis=1)
    codes = codes_ref[...].astype(jnp.int32).astype(F32)
    codes = jnp.concatenate([codes[first + lot : first + lot + 1, :] for lot in range(lots)], axis=1)
    return values, jnp.exp2(codes * (1.0 / CODES_PER_OCTAVE)) * (1.0 / LEVELS)


def encode(sums):
    largest = jnp.max(jnp.abs(sums), axis=0, keepdims=True)
    code = jnp.ceil(jnp.log2(jnp.maximum(largest, SMALLEST)) * CODES_PER_OCTAVE)
    scaled = jnp.round(sums * (LEVELS / jnp.exp2(code * (1.0 / CODES_PER_OCTAVE))))
    lots = sums.shape[1] // LANES
    return jnp.concatenate([scaled[:, lot * LANES : (lot + 1) * LANES] for lot in range(lots)], axis=0), code


def whole(values):
    return values.astype(jnp.int32).astype(jnp.int16)


def piece_count(at, layout, table, counts):
    parts, _, _, shifts = layout
    run = at % parts // CUTS
    return counts[table[shifts + at] * (parts // CUTS) + run]


def pair_sums(count, table, pairs_ref, own_ref, partner_ref):
    width = own_ref.shape[0]
    sums = jnp.zeros((M, own_ref.shape[1]), F32)
    lane = lax.broadcasted_iota(jnp.int32, (1, width), 1)
    for member, dates, data in ((ME, pairs_ref[:, :width], own_ref), (PARTNER, pairs_ref[:, width:], partner_ref)):
        design = incidence(dates[0:1, :], dates[1:2, :], M)
        kept = jnp.where(table[member] * width + lane < count, design, 0.0).astype(jnp.bfloat16)
        sums = sums + jnp.dot(kept, data[...], preferred_element_type=F32)
    return sums


def copy_kernel(table, source_ref, _, target_ref):
    target_ref[...] = source_ref[...]


def give_out(swap, layout, table, phases, after, piece):
    first, count = swap
    away = layout[2]
    shape = (phases.shape[0], piece * count)
    return pl.pallas_call(
        copy_kernel,
        out_shape=jax.ShapeDtypeStruct(shape, phases.dtype),
        grid_spec=pltpu.PrefetchScalarGridSpec(
            num_scalar_prefetch=1,
            grid=(1,),
            in_specs=[
                pl.BlockSpec(shape, lambda i, t: (0, t[away + first] // count)),
                pl.BlockSpec(memory_space=pl.ANY),
            ],
            out_specs=pl.BlockSpec(shape, lambda i, t: (0, 0)),
        ),
        compiler_params=pltpu.CompilerParams(vmem_limit_bytes=VMEM_BYTES),
        cost_estimate=LITTLE,
        name="give_out",
    )(table, phases, after)


def step_kernel(at, layout, adds, swaps, halves, table, counts, pairs_ref, own_ref, partner_ref, *rest):
    if swaps:
        rest[-1][...] = rest[0][...]
        coded_ref, rest = rest[-2], rest[1:]
    else:
        coded_ref = rest[-1]
    count = piece_count(at, layout, table, counts)
    width = own_ref.shape[1] // halves
    lots = width // LANES
    codes = []
    for half in range(halves):
        part = pl.ds(half * width, width)
        sums = pair_sums(count, table, pairs_ref, own_ref.at[:, part], partner_ref.at[:, part])
        if adds:
            rows = pl.ds(half * lots * M, lots * M)
            values, scale = decode(rest[0].at[rows, :], rest[0].at[halves * lots * M :, :], lots, half * lots)
            sums = sums + values * (scale * table[INNER].astype(F32))
        scaled, code = encode(sums)
        coded_ref[half * lots * M : (half + 1) * lots * M, :] = whole(scaled)
        codes += [code[:, lot * LANES : (lot + 1) * LANES] for lot in range(lots)]
    codes += [jnp.zeros((CODE_ROWS - len(codes), LANES), F32)]
    coded_ref[halves * lots * M :, :] = whole(jnp.concatenate(codes, axis=0))


def step(at, swap, layout, scalars, pairs, phases, partner, earlier, after, piece):
    partner, place_in = partner
    local_pairs = phases.shape[0]
    _, blocks, away, _ = layout
    coded_shape = (coded_rows(piece), LANES)
    in_specs = [
        pl.BlockSpec(pairs.shape, lambda i, t, c: (0, 0)),
        pl.BlockSpec((local_pairs, piece), lambda i, t, c: (0, t[blocks + at])),
        pl.BlockSpec((local_pairs, piece), lambda i, t, c: (0, place_in)),
    ]
    operands = [pairs, phases, partner]
    out_shape = [jax.ShapeDtypeStruct(coded_shape, jnp.int16)]
    out_specs = [pl.BlockSpec(coded_shape, lambda i, t, c: (0, 0))]
    if swap is not None:
        first, count = swap
        wide = piece * count
        in_specs.append(pl.BlockSpec((local_pairs, wide), lambda i, t, c: (0, t[away + first] // count)))
        operands.append(phases)
        out_shape.append(jax.ShapeDtypeStruct((local_pairs, wide), phases.dtype))
        out_specs.append(pl.BlockSpec((local_pairs, wide), lambda i, t, c: (0, 0)))
    if earlier is not None:
        in_specs.append(pl.BlockSpec(coded_shape, lambda i, t, c: (0, 0)))
        operands.append(earlier)
    in_specs += [pl.BlockSpec(memory_space=pl.ANY)] * len(after)
    results = pl.pallas_call(
        functools.partial(step_kernel, at, layout, earlier is not None, swap is not None, HALVES),
        out_shape=out_shape,
        grid_spec=pltpu.PrefetchScalarGridSpec(
            num_scalar_prefetch=2,
            grid=(1,),
            in_specs=in_specs,
            out_specs=out_specs,
        ),
        compiler_params=pltpu.CompilerParams(vmem_limit_bytes=VMEM_BYTES),
        cost_estimate=STEADY,
        name=f"sum_step_{at:02d}",
    )(*scalars, *operands, *after)
    return results if swap is not None else (results[0], None)


def coded_specs(piece, tiles, index):
    lots = piece // LANES
    return [
        pl.BlockSpec((lots // tiles * M, LANES), lambda *at: (at[index], 0)),
        pl.BlockSpec((CODE_ROWS, LANES), lambda *at: (lots * M // CODE_ROWS, 0)),
    ]


def add_arrived(sums, refs, tiles):
    lots = sums.shape[1] // LANES
    for coded_ref, codes_ref in zip(refs[::2], refs[1::2]):
        tile = pl.program_id(0)
        parts = [decode(coded_ref, codes_ref, lots, at * lots) for at in range(tiles)]
        values = parts[0][0]
        scale = functools.reduce(lambda chosen, at: jnp.where(tile == at, parts[at][1], chosen), range(1, tiles), parts[0][1])
        sums = sums + values * scale
    return sums


def own_kernel(at, layout, tiles, table, counts, pairs_ref, own_ref, partner_ref, *rest):
    sums = pair_sums(piece_count(at, layout, table, counts), table, pairs_ref, own_ref, partner_ref)
    arrived = add_arrived(jnp.zeros_like(sums), rest[:-1], tiles)
    rest[-1][...] = sums + arrived * (1 - table[INNER]).astype(F32)


def own_sums(at, layout, scalars, pairs, phases, partner, arrived, piece):
    partner, place_in = partner
    local_pairs = phases.shape[0]
    blocks = layout[1]
    tiles = HALVES
    tile = piece // tiles
    return pl.pallas_call(
        functools.partial(own_kernel, at, layout, tiles),
        out_shape=jax.ShapeDtypeStruct((M, piece), F32),
        grid_spec=pltpu.PrefetchScalarGridSpec(
            num_scalar_prefetch=2,
            grid=(tiles,),
            in_specs=[
                pl.BlockSpec(pairs.shape, lambda i, t, c: (0, 0)),
                pl.BlockSpec((local_pairs, tile), lambda i, t, c: (0, t[blocks + at] * tiles + i)),
                pl.BlockSpec((local_pairs, tile), lambda i, t, c: (0, place_in * tiles + i)),
            ]
            + coded_specs(piece, tiles, 0) * len(arrived),
            out_specs=pl.BlockSpec((M, tile), lambda i, t, c: (0, i)),
        ),
        compiler_params=pltpu.CompilerParams(vmem_limit_bytes=VMEM_BYTES),
        cost_estimate=LITTLE,
        name=f"own_sums_{at:02d}",
    )(*scalars, pairs, phases, partner, *[each for each in arrived for _ in range(2)])


def finish_kernel(tiles, arrivals, sums_ref, inverse_ref, *rest):
    sums = add_arrived(sums_ref[...], rest[: 2 * arrivals], tiles)
    rest[-1][...] = full_product(inverse_ref[0, :M, :M], sums)


def finish(part, sums, inverse, arrived, series, pixels):
    piece = sums.shape[1]
    tiles = HALVES
    tile = piece // tiles
    in_specs = [
        pl.BlockSpec((M, tile), lambda i: (0, i)),
        pl.BlockSpec((1, PAD, PAD), lambda i: (part // CUTS, 0, 0)),
    ] + coded_specs(piece, tiles, 0) * len(arrived)
    operands = [sums, inverse] + [each for each in arrived for _ in range(2)]
    aliases = {}
    if series is not None:
        in_specs.append(pl.BlockSpec(memory_space=pl.ANY))
        aliases = {len(operands): 0}
        operands.append(series)
    return pl.pallas_call(
        functools.partial(finish_kernel, tiles, len(arrived)),
        out_shape=jax.ShapeDtypeStruct((M, pixels), F32),
        grid=(tiles,),
        in_specs=in_specs,
        out_specs=pl.BlockSpec((M, tile), lambda i: (0, part * tiles + i)),
        input_output_aliases=aliases,
        compiler_params=pltpu.CompilerParams(vmem_limit_bytes=VMEM_BYTES),
        cost_estimate=LITTLE,
        name=f"finish_{part}",
    )(*operands)


def line_permutation(links):
    return [(2 * source + side, 2 * target + side) for source, target in links for side in range(2)]


def solve_by_sums(phases, date_pairs, counts_of):
    owner_count = lax.axis_size("ifg")
    line = owner_count // 2
    local_pairs, pixels = phases.shape
    owner_pixels = pixels // owner_count
    runs = counts_of(None).shape[0]
    parts = runs * CUTS
    piece = owner_pixels // parts
    steps = (line - 1) * parts
    me = lax.axis_index("ifg")

    places = np.repeat(np.array(CHUNK_ORDER), parts, axis=1)
    part_of = np.tile(np.arange(parts), line)
    rows = []
    for device in range(owner_count):
        place, side = device // 2, device % 2
        own = (places[place] * 2 + side) * parts + part_of
        away = (places[place] * 2 + 1 - side) * parts + part_of
        known = [place, line - 1 - place, place ^ 1, line - 1 - (place ^ 1)]
        shift = np.array([known.index(chunk) for chunk in places[place]])
        rows.append(np.concatenate([[device, device ^ 1, int(0 < place < line - 1)], own, away, shift]))
    row = lax.dynamic_index_in_dim(jnp.asarray(np.stack(rows), jnp.int32), me, 0, keepdims=False)
    head, pieces = FIXED, line * parts
    layout = (parts, head, head + pieces, head + 2 * pieces)

    swap = [(i, i ^ 1) for i in range(owner_count)]
    partner_of = {}

    def swapped(away, first, count):
        here = lax.ppermute(away, "ifg", swap)
        partner_of.update({first + place: (here, place) for place in range(count)})

    place, side = me // 2, me % 2
    first, count = FIRST_SWAPS[0]
    chunk = jnp.where(place % 2 == 0, line - 1, 0)
    away = lax.dynamic_slice(phases, (0, ((chunk * 2 + 1 - side) * parts + first) * piece), (local_pairs, piece * count))
    swapped(away, first, count)
    run_counts = counts_of(away)
    mirrored = lax.ppermute(run_counts, "ifg", line_permutation([(i, line - 1 - i) for i in range(line)]))
    both = jnp.concatenate([run_counts, mirrored])
    counts = jnp.concatenate([both, lax.ppermute(both, "ifg", line_permutation([(i, i ^ 1) for i in range(line)]))])
    for after, swap_pieces in zip((mirrored, counts), FIRST_SWAPS[1:]):
        swapped(give_out(swap_pieces, layout, row, phases, after, piece), *swap_pieces)
    pairs = jnp.concatenate([lax.dynamic_slice(date_pairs, (0, row[at] * local_pairs), (2, local_pairs)) for at in (ME, PARTNER)], axis=1)
    scalars = (row, counts)

    received, sums, coded = [], [], None
    for at in range(steps):
        earlier = received[at - parts][0] if at >= parts else None
        after = [coded] if at else []
        after += received[at - FLIGHT] if at >= FLIGHT else []
        if at in SWAP_WAITS:
            after.append(partner_of[SWAP_WAITS[at]][0])
        if at == INVERSE_STEP:
            inverse = invert_classes(date_pairs, run_counts, [coded])
            after.append(inverse)
        for part in OWN_STEPS.get(at, ()):
            arrived = [each for place in range(line - 2) for each in received[place * parts + part]]
            sums.append(own_sums(steps + part, layout, scalars, pairs, phases, partner_of[steps + part], arrived, piece))
            after.append(sums[-1])
        coded, away = step(at, SWAPS.get(at), layout, scalars, pairs, phases, partner_of[at], earlier, after, piece)
        received.append([lax.ppermute(coded, "ifg", line_permutation(links)) for links in SENDS[at // parts]])
        if at in SWAPS:
            swapped(away, *SWAPS[at])

    series = None
    for part in range(parts):
        series = finish(part, sums[part], inverse, received[(line - 2) * parts + part], series, owner_pixels)
    return series


def solve_by_blocks(phases, date_pairs, counts_of):
    owner_count = lax.axis_size("ifg")
    local_pairs, pixels = phases.shape
    owner_pixels = pixels // owner_count
    run_counts = counts_of(None)
    outgoing = phases.reshape(local_pairs, owner_count, owner_pixels).transpose(1, 0, 2)
    received = lax.all_to_all(outgoing, "ifg", split_axis=0, concat_axis=0, tiled=True)
    inverse = invert_classes(date_pairs, run_counts, [])
    return sum_solve(run_counts, date_pairs, received.reshape(-1, owner_pixels), inverse)


def local(phases, date_pairs, pair_counts, group_ids):
    local_pairs, _, pixels = phases.shape

    def counts_of(after):
        groups = group_ids if after is None else lax.optimization_barrier((group_ids, after))[0]
        strip_groups = lax.dynamic_index_in_dim(groups, lax.axis_index("grp"), 0, keepdims=False)[::RUN]
        chosen = strip_groups[:, None] == jnp.arange(pair_counts.shape[0], dtype=jnp.int32)
        return jnp.sum(jnp.where(chosen, pair_counts, 0), axis=1)

    line = lax.axis_size("ifg") == 2 * len(CHUNK_ORDER) and group_ids.shape[1] == 2 * RUN
    by_sums = line and 2 * local_pairs > M and local_pairs % LANES == 0
    solve = solve_by_sums if by_sums else solve_by_blocks
    return solve(phases.reshape(local_pairs, pixels), date_pairs, counts_of)[None, :, :]


def solution(mesh):
    in_specs = (P("ifg", "grp", None), P(), P(), P(None, "ifg"))
    out_specs = P("grp", None, "ifg")
    return jax.shard_map(local, mesh=mesh, in_specs=in_specs, out_specs=out_specs, check_vma=False)
```

```python
import functools

import jax
import jax.numpy as jnp
import numpy as np
from jax import lax
from jax.experimental import pallas as pl
from jax.experimental.pallas import tpu as pltpu
from jax.sharding import PartitionSpec as P

M = 200
RUN = 8
PAD = 256
SLABS = 8
DAMPING = 1.0
VMEM_BYTES = 48 * 1024 * 1024
F32 = jnp.float32
HIGHEST = lax.Precision.HIGHEST
STEADY = pl.CostEstimate(flops=10_000_000_000, bytes_accessed=30_000_000, transcendentals=0)
LITTLE = pl.CostEstimate(flops=1024, bytes_accessed=1024, transcendentals=0)
CUTS = 2
HALVES = 2
FLIGHT = 2
FIRST_SWAPS = ((0, 1), (1, 1), (2, 2))
SWAPS = {2: (4, 2), 3: (6, 2), 5: (8, 2), 6: (10, 2), 7: (12, 4)}
SWAP_WAITS = {9: 11}
INVERSE_STEP = 2
ME, PARTNER, INNER, FIXED = 0, 1, 2, 3
LATE = 2
LANES = 128
CODE_ROWS = 16
LEVELS = 32700.0
CODES_PER_OCTAVE = 128.0
SMALLEST = 2.0**-110
CHUNK_ORDER = ((3, 2, 1, 0), (0, 3, 2, 1), (3, 0, 1, 2), (0, 1, 2, 3))
SENDS = (
    (((0, 1), (1, 0), (2, 3), (3, 2)),),
    (((0, 1), (1, 3), (2, 0), (3, 2)),),
    (((0, 1), (3, 2)), ((1, 2), (2, 1))),
)


def incidence(earlier, later, rows):
    shape = (rows, earlier.shape[1])
    date = lax.broadcasted_iota(jnp.int32, shape, 0)
    return (date == later).astype(F32) - (date == earlier).astype(F32)


def split_product(left, right):
    def halves(value):
        high = value.astype(jnp.bfloat16)
        return high, (value - high.astype(F32)).astype(jnp.bfloat16)

    left_high, left_low = halves(left)
    right_high, right_low = halves(right)
    small = jnp.dot(left_high, right_low, preferred_element_type=F32) + jnp.dot(left_low, right_high, preferred_element_type=F32)
    return jnp.dot(left_high, right_high, preferred_element_type=F32) + small


def full_product(left, right):
    return jnp.dot(left, right, precision=HIGHEST, preferred_element_type=F32)


def inverse_kernel(counts_ref, pairs_ref, *rest):
    out_ref = rest[-1]
    runs = out_ref.shape[0]
    design = incidence(pairs_ref[0:1, :], pairs_ref[1:2, :], PAD)
    pair = lax.broadcasted_iota(jnp.int32, design.shape, 1)
    contract_last = (((1,), (1,)), ((), ()))
    row = lax.broadcasted_iota(jnp.int32, (PAD, PAD), 0)
    col = lax.broadcasted_iota(jnp.int32, (PAD, PAD), 1)
    identity = (row == col).astype(F32)
    grams = []
    for run in range(runs):
        kept = jnp.where(pair < counts_ref[run], design, 0.0).astype(jnp.bfloat16)
        gram = lax.dot_general(kept, kept, contract_last, preferred_element_type=F32)
        grams.append(gram + DAMPING * identity)
    low = DAMPING
    high = 2.0 * functools.reduce(jnp.maximum, [jnp.max(gram) for gram in grams]) - DAMPING
    total, width = high + low, high - low
    scale = 2.0 * total * total - width * width
    starts = tuple((8.0 * total / scale) * identity - (8.0 / scale) * gram for gram in grams)
    needed = 18.0 * scale / (8.0 * high * low)
    steps = jnp.int32(0)
    for power in range(1, 16):
        steps += (needed > float(2**power)).astype(jnp.int32)

    def newton(product, guesses):
        products = [product(gram, guess) for gram, guess in zip(grams, guesses)]
        return tuple(2.0 * guess - product(guess, each) for guess, each in zip(guesses, products))

    full_steps = 1 + (high > 100.0).astype(jnp.int32)
    guesses = lax.fori_loop(0, steps + 1 - full_steps, lambda _, guesses: newton(split_product, guesses), starts)
    guesses = lax.fori_loop(0, full_steps, lambda _, guesses: newton(full_product, guesses), guesses)
    for run, guess in enumerate(guesses):
        out_ref[run] = guess


def invert_classes(date_pairs, run_counts, after):
    shape = (run_counts.shape[0], PAD, PAD)
    return pl.pallas_call(
        inverse_kernel,
        out_shape=jax.ShapeDtypeStruct(shape, F32),
        grid_spec=pltpu.PrefetchScalarGridSpec(
            num_scalar_prefetch=1,
            grid=(1,),
            in_specs=[pl.BlockSpec(date_pairs.shape, lambda i, c: (0, 0))] + [pl.BlockSpec(memory_space=pl.ANY)] * len(after),
            out_specs=pl.BlockSpec(shape, lambda i, c: (0, 0, 0)),
        ),
        compiler_params=pltpu.CompilerParams(vmem_limit_bytes=VMEM_BYTES),
        cost_estimate=LITTLE,
        name="invert_classes_0",
    )(run_counts, date_pairs, *after)


def sum_solve_kernel(tiles, counts_ref, pairs_ref, data_ref, inverse_ref, out_ref):
    run = pl.program_id(0) // tiles
    design = incidence(pairs_ref[0:1, :], pairs_ref[1:2, :], PAD)
    pair = lax.broadcasted_iota(jnp.int32, design.shape, 1)
    kept = jnp.where(pair < counts_ref[run], design, 0.0).astype(jnp.bfloat16)
    sums = jnp.dot(kept, data_ref[...], preferred_element_type=F32)
    out_ref[...] = jnp.dot(inverse_ref[0, :M, :], sums, precision=HIGHEST, preferred_element_type=F32)


def sum_solve(run_counts, date_pairs, received, inverse):
    runs = run_counts.shape[0]
    total_pairs, pixels = received.shape
    run_pixels = pixels // runs
    tile = run_pixels // 2
    tiles = run_pixels // tile
    return pl.pallas_call(
        functools.partial(sum_solve_kernel, tiles),
        out_shape=jax.ShapeDtypeStruct((M, pixels), F32),
        grid_spec=pltpu.PrefetchScalarGridSpec(
            num_scalar_prefetch=1,
            grid=(runs * tiles,),
            in_specs=[
                pl.BlockSpec(date_pairs.shape, lambda i, c: (0, 0)),
                pl.BlockSpec((total_pairs, tile), lambda i, c: (0, i)),
                pl.BlockSpec((1, PAD, PAD), lambda i, c: (i // tiles, 0, 0)),
            ],
            out_specs=pl.BlockSpec((M, tile), lambda i, c: (0, i)),
        ),
        compiler_params=pltpu.CompilerParams(vmem_limit_bytes=VMEM_BYTES),
        name="sum_solve",
    )(run_counts, date_pairs, received, inverse)


def coded_rows(piece):
    return M * (piece // LANES) + CODE_ROWS


def decode(coded_ref, codes_ref, lots, first):
    coded = coded_ref[...].astype(jnp.int32).astype(F32)
    values = jnp.concatenate([coded[lot * M : (lot + 1) * M, :] for lot in range(lots)], axis=1)
    codes = codes_ref[...].astype(jnp.int32).astype(F32)
    codes = jnp.concatenate([codes[first + lot : first + lot + 1, :] for lot in range(lots)], axis=1)
    return values, jnp.exp2(codes * (1.0 / CODES_PER_OCTAVE)) * (1.0 / LEVELS)


def encode(sums):
    largest = jnp.max(jnp.abs(sums), axis=0, keepdims=True)
    code = jnp.ceil(jnp.log2(jnp.maximum(largest, SMALLEST)) * CODES_PER_OCTAVE)
    scaled = jnp.round(sums * (LEVELS / jnp.exp2(code * (1.0 / CODES_PER_OCTAVE))))
    lots = sums.shape[1] // LANES
    return jnp.concatenate([scaled[:, lot * LANES : (lot + 1) * LANES] for lot in range(lots)], axis=0), code


def whole(values):
    return values.astype(jnp.int32).astype(jnp.int16)


def piece_count(at, layout, table, counts):
    parts, _, _, shifts = layout
    run = at % parts // CUTS
    return counts[table[shifts + at] * (parts // CUTS) + run]


def pair_sums(count, table, pairs_ref, own_ref, partner_ref):
    width = own_ref.shape[0]
    sums = jnp.zeros((M, own_ref.shape[1]), F32)
    lane = lax.broadcasted_iota(jnp.int32, (1, width), 1)
    for member, dates, data in ((ME, pairs_ref[:, :width], own_ref), (PARTNER, pairs_ref[:, width:], partner_ref)):
        design = incidence(dates[0:1, :], dates[1:2, :], M)
        kept = jnp.where(table[member] * width + lane < count, design, 0.0).astype(jnp.bfloat16)
        sums = sums + jnp.dot(kept, data[...], preferred_element_type=F32)
    return sums


def copy_kernel(table, source_ref, _, target_ref):
    target_ref[...] = source_ref[...]


def give_out(swap, layout, table, phases, after, piece):
    first, count = swap
    away = layout[2]
    shape = (phases.shape[0], piece * count)
    return pl.pallas_call(
        copy_kernel,
        out_shape=jax.ShapeDtypeStruct(shape, phases.dtype),
        grid_spec=pltpu.PrefetchScalarGridSpec(
            num_scalar_prefetch=1,
            grid=(1,),
            in_specs=[
                pl.BlockSpec(shape, lambda i, t: (0, t[away + first] // count)),
                pl.BlockSpec(memory_space=pl.ANY),
            ],
            out_specs=pl.BlockSpec(shape, lambda i, t: (0, 0)),
        ),
        compiler_params=pltpu.CompilerParams(vmem_limit_bytes=VMEM_BYTES),
        cost_estimate=LITTLE,
        name="give_out",
    )(table, phases, after)


def step_kernel(at, layout, adds, swaps, halves, table, counts, pairs_ref, own_ref, partner_ref, *rest):
    if swaps:
        rest[-1][...] = rest[0][...]
        coded_ref, rest = rest[-2], rest[1:]
    else:
        coded_ref = rest[-1]
    count = piece_count(at, layout, table, counts)
    width = own_ref.shape[1] // halves
    lots = width // LANES
    codes = []
    for half in range(halves):
        part = pl.ds(half * width, width)
        sums = pair_sums(count, table, pairs_ref, own_ref.at[:, part], partner_ref.at[:, part])
        if adds:
            rows = pl.ds(half * lots * M, lots * M)
            values, scale = decode(rest[0].at[rows, :], rest[0].at[halves * lots * M :, :], lots, half * lots)
            sums = sums + values * (scale * table[INNER].astype(F32))
        scaled, code = encode(sums)
        coded_ref[half * lots * M : (half + 1) * lots * M, :] = whole(scaled)
        codes += [code[:, lot * LANES : (lot + 1) * LANES] for lot in range(lots)]
    codes += [jnp.zeros((CODE_ROWS - len(codes), LANES), F32)]
    coded_ref[halves * lots * M :, :] = whole(jnp.concatenate(codes, axis=0))


def step(at, swap, layout, scalars, pairs, phases, partner, earlier, after, piece):
    partner, place_in = partner
    local_pairs = phases.shape[0]
    _, blocks, away, _ = layout
    coded_shape = (coded_rows(piece), LANES)
    in_specs = [
        pl.BlockSpec(pairs.shape, lambda i, t, c: (0, 0)),
        pl.BlockSpec((local_pairs, piece), lambda i, t, c: (0, t[blocks + at])),
        pl.BlockSpec((local_pairs, piece), lambda i, t, c: (0, place_in)),
    ]
    operands = [pairs, phases, partner]
    out_shape = [jax.ShapeDtypeStruct(coded_shape, jnp.int16)]
    out_specs = [pl.BlockSpec(coded_shape, lambda i, t, c: (0, 0))]
    if swap is not None:
        first, count = swap
        wide = piece * count
        in_specs.append(pl.BlockSpec((local_pairs, wide), lambda i, t, c: (0, t[away + first] // count)))
        operands.append(phases)
        out_shape.append(jax.ShapeDtypeStruct((local_pairs, wide), phases.dtype))
        out_specs.append(pl.BlockSpec((local_pairs, wide), lambda i, t, c: (0, 0)))
    if earlier is not None:
        in_specs.append(pl.BlockSpec(coded_shape, lambda i, t, c: (0, 0)))
        operands.append(earlier)
    in_specs += [pl.BlockSpec(memory_space=pl.ANY)] * len(after)
    results = pl.pallas_call(
        functools.partial(step_kernel, at, layout, earlier is not None, swap is not None, HALVES),
        out_shape=out_shape,
        grid_spec=pltpu.PrefetchScalarGridSpec(
            num_scalar_prefetch=2,
            grid=(1,),
            in_specs=in_specs,
            out_specs=out_specs,
        ),
        compiler_params=pltpu.CompilerParams(vmem_limit_bytes=VMEM_BYTES),
        cost_estimate=STEADY,
        name=f"sum_step_{at:02d}",
    )(*scalars, *operands, *after)
    return results if swap is not None else (results[0], None)


def coded_specs(piece, tiles, index):
    lots = piece // LANES
    return [
        pl.BlockSpec((lots // tiles * M, LANES), lambda *at: (at[index], 0)),
        pl.BlockSpec((CODE_ROWS, LANES), lambda *at: (lots * M // CODE_ROWS, 0)),
    ]


def add_arrived(sums, refs, tiles):
    lots = sums.shape[1] // LANES
    for coded_ref, codes_ref in zip(refs[::2], refs[1::2]):
        tile = pl.program_id(0)
        parts = [decode(coded_ref, codes_ref, lots, at * lots) for at in range(tiles)]
        values = parts[0][0]
        scale = functools.reduce(lambda chosen, at: jnp.where(tile == at, parts[at][1], chosen), range(1, tiles), parts[0][1])
        sums = sums + values * scale
    return sums


def finish_kernel(at, layout, tiles, early, table, counts, pairs_ref, own_ref, partner_ref, inverse_ref, *rest):
    sums = pair_sums(piece_count(at, layout, table, counts), table, pairs_ref, own_ref, partner_ref)
    from_ends = add_arrived(jnp.zeros_like(sums), rest[: 2 * early], tiles)
    sums = sums + from_ends * (1 - table[INNER]).astype(F32)
    sums = add_arrived(sums, rest[2 * early : 2 * early + 2 * LATE], tiles)
    rest[-1][...] = full_product(inverse_ref[0, :M, :M], sums)


def finish(at, part, layout, scalars, pairs, phases, partner, inverse, early, late, series, pixels, piece):
    partner, place_in = partner
    local_pairs = phases.shape[0]
    blocks = layout[1]
    tiles = HALVES
    tile = piece // tiles
    arrived = early + late
    in_specs = [
        pl.BlockSpec(pairs.shape, lambda i, t, c: (0, 0)),
        pl.BlockSpec((local_pairs, tile), lambda i, t, c: (0, t[blocks + at] * tiles + i)),
        pl.BlockSpec((local_pairs, tile), lambda i, t, c: (0, place_in * tiles + i)),
        pl.BlockSpec((1, PAD, PAD), lambda i, t, c: (part // CUTS, 0, 0)),
    ] + coded_specs(piece, tiles, 0) * len(arrived)
    operands = [*scalars, pairs, phases, partner, inverse] + [each for each in arrived for _ in range(2)]
    aliases = {}
    if series is not None:
        in_specs.append(pl.BlockSpec(memory_space=pl.ANY))
        aliases = {len(operands): 0}
        operands.append(series)
    return pl.pallas_call(
        functools.partial(finish_kernel, at, layout, tiles, len(early)),
        out_shape=jax.ShapeDtypeStruct((M, pixels), F32),
        grid_spec=pltpu.PrefetchScalarGridSpec(
            num_scalar_prefetch=2,
            grid=(tiles,),
            in_specs=in_specs,
            out_specs=pl.BlockSpec((M, tile), lambda i, t, c: (0, part * tiles + i)),
        ),
        input_output_aliases=aliases,
        compiler_params=pltpu.CompilerParams(vmem_limit_bytes=VMEM_BYTES),
        cost_estimate=LITTLE,
        name=f"finish_{part}",
    )(*operands)


def line_permutation(links):
    return [(2 * source + side, 2 * target + side) for source, target in links for side in range(2)]


def solve_by_sums(phases, date_pairs, counts_of):
    owner_count = lax.axis_size("ifg")
    line = owner_count // 2
    local_pairs, pixels = phases.shape
    owner_pixels = pixels // owner_count
    runs = counts_of().shape[0]
    parts = runs * CUTS
    piece = owner_pixels // parts
    steps = (line - 1) * parts
    me = lax.axis_index("ifg")

    places = np.repeat(np.array(CHUNK_ORDER), parts, axis=1)
    part_of = np.tile(np.arange(parts), line)
    rows = []
    for device in range(owner_count):
        place, side = device // 2, device % 2
        own = (places[place] * 2 + side) * parts + part_of
        away = (places[place] * 2 + 1 - side) * parts + part_of
        known = [place, line - 1 - place, place ^ 1, line - 1 - (place ^ 1)]
        shift = np.array([known.index(chunk) for chunk in places[place]])
        rows.append(np.concatenate([[device, device ^ 1, int(0 < place < line - 1)], own, away, shift]))
    row = lax.dynamic_index_in_dim(jnp.asarray(np.stack(rows), jnp.int32), me, 0, keepdims=False)
    head, pieces = FIXED, line * parts
    layout = (parts, head, head + pieces, head + 2 * pieces)

    swap = [(i, i ^ 1) for i in range(owner_count)]
    partner_of = {}

    def swapped(away, first, count):
        here = lax.ppermute(away, "ifg", swap)
        partner_of.update({first + place: (here, place) for place in range(count)})

    place, side = me // 2, me % 2
    run_counts = counts_of()
    mirrored = lax.ppermute(run_counts, "ifg", line_permutation([(i, line - 1 - i) for i in range(line)]))
    first, count = FIRST_SWAPS[0]
    chunk, _ = lax.optimization_barrier((jnp.where(place % 2 == 0, line - 1, 0), run_counts))
    away = lax.dynamic_slice(phases, (0, ((chunk * 2 + 1 - side) * parts + first) * piece), (local_pairs, piece * count))
    swapped(away, first, count)
    both = jnp.concatenate([run_counts, mirrored])
    counts = jnp.concatenate([both, lax.ppermute(both, "ifg", line_permutation([(i, i ^ 1) for i in range(line)]))])
    swapped(give_out(FIRST_SWAPS[1], layout, row, phases, mirrored, piece), *FIRST_SWAPS[1])
    pairs = jnp.concatenate([lax.dynamic_slice(date_pairs, (0, row[at] * local_pairs), (2, local_pairs)) for at in (ME, PARTNER)], axis=1)
    scalars = (row, counts)

    received, coded = [], None
    for at in range(steps):
        earlier = received[at - parts][0] if at >= parts else None
        after = [coded] if at else []
        after += received[at - FLIGHT] if at >= FLIGHT else []
        if at in SWAP_WAITS:
            after.append(partner_of[SWAP_WAITS[at]][0])
        if at == INVERSE_STEP:
            inverse = invert_classes(date_pairs, run_counts, [coded])
            after.append(inverse)
        coded, away = step(at, SWAPS.get(at), layout, scalars, pairs, phases, partner_of[at], earlier, after, piece)
        received.append([lax.ppermute(coded, "ifg", line_permutation(links)) for links in SENDS[at // parts]])
        if at in SWAPS:
            swapped(away, *SWAPS[at])
        if at == 0:
            swapped(give_out(FIRST_SWAPS[2], layout, row, phases, coded, piece), *FIRST_SWAPS[2])

    series = None
    for part in range(parts):
        at = steps + part
        early = [each for place in range(line - 2) for each in received[place * parts + part]]
        late = received[(line - 2) * parts + part]
        series = finish(at, part, layout, scalars, pairs, phases, partner_of[at], inverse, early, late, series, owner_pixels, piece)
    return series


def solve_by_blocks(phases, date_pairs, counts_of):
    owner_count = lax.axis_size("ifg")
    local_pairs, pixels = phases.shape
    owner_pixels = pixels // owner_count
    run_counts = counts_of()
    outgoing = phases.reshape(local_pairs, owner_count, owner_pixels).transpose(1, 0, 2)
    received = lax.all_to_all(outgoing, "ifg", split_axis=0, concat_axis=0, tiled=True)
    inverse = invert_classes(date_pairs, run_counts, [])
    return sum_solve(run_counts, date_pairs, received.reshape(-1, owner_pixels), inverse)


def local(phases, date_pairs, pair_counts, group_ids):
    local_pairs, _, pixels = phases.shape

    def counts_of():
        strip_groups = lax.dynamic_index_in_dim(group_ids, lax.axis_index("grp"), 0, keepdims=False)[::RUN]
        chosen = strip_groups[:, None] == jnp.arange(pair_counts.shape[0], dtype=jnp.int32)
        return jnp.sum(jnp.where(chosen, pair_counts, 0), axis=1)

    line = lax.axis_size("ifg") == 2 * len(CHUNK_ORDER) and group_ids.shape[1] == 2 * RUN
    by_sums = line and 2 * local_pairs > M and local_pairs % LANES == 0
    solve = solve_by_sums if by_sums else solve_by_blocks
    return solve(phases.reshape(local_pairs, pixels), date_pairs, counts_of)[None, :, :]


def solution(mesh):
    in_specs = (P("ifg", "grp", None), P(), P(), P(None, "ifg"))
    out_specs = P("grp", None, "ifg")
    return jax.shard_map(local, mesh=mesh, in_specs=in_specs, out_specs=out_specs, check_vma=False)
```

```python
import functools

import jax
import jax.numpy as jnp
import numpy as np
from jax import lax
from jax.experimental import pallas as pl
from jax.experimental.pallas import tpu as pltpu
from jax.sharding import PartitionSpec as P

M = 200
RUN = 8
PAD = 256
SLABS = 8
DAMPING = 1.0
VMEM_BYTES = 48 * 1024 * 1024
F32 = jnp.float32
HIGHEST = lax.Precision.HIGHEST
STEADY = pl.CostEstimate(flops=10_000_000_000, bytes_accessed=30_000_000, transcendentals=0)
LITTLE = pl.CostEstimate(flops=1024, bytes_accessed=1024, transcendentals=0)
CUTS = 2
HALVES = 2
FLIGHT = 2
FIRST_SWAPS = ((0, 1), (1, 1), (2, 2))
SWAPS = {2: (4, 2), 3: (6, 2), 5: (8, 2), 6: (10, 2), 7: (12, 4)}
SWAP_WAITS = {5: 7, 7: 9, 8: 11, 10: 12}
MEETINGS = (1, 3, 5, 7, 8, 10)
INVERSE_STEP = 2
ME, PARTNER, INNER, FIXED = 0, 1, 2, 3
LATE = 2
LANES = 128
CODE_ROWS = 16
LEVELS = 32700.0
ROUNDER = 1.5 * 2.0**23
CODES_PER_OCTAVE = 128.0
SMALLEST = 2.0**-110
CHUNK_ORDER = ((3, 2, 1, 0), (0, 3, 2, 1), (3, 0, 1, 2), (0, 1, 2, 3))
SENDS = (
    (((0, 1), (1, 0), (2, 3), (3, 2)),),
    (((0, 1), (1, 3), (2, 0), (3, 2)),),
    (((0, 1), (3, 2)), ((1, 2), (2, 1))),
)


def incidence(earlier, later, rows):
    shape = (rows, earlier.shape[1])
    date = lax.broadcasted_iota(jnp.int32, shape, 0)
    return (date == later).astype(F32) - (date == earlier).astype(F32)


def split_product(left, right):
    def halves(value):
        high = value.astype(jnp.bfloat16)
        return high, (value - high.astype(F32)).astype(jnp.bfloat16)

    left_high, left_low = halves(left)
    right_high, right_low = halves(right)
    small = jnp.dot(left_high, right_low, preferred_element_type=F32) + jnp.dot(left_low, right_high, preferred_element_type=F32)
    return jnp.dot(left_high, right_high, preferred_element_type=F32) + small


def full_product(left, right):
    return jnp.dot(left, right, precision=HIGHEST, preferred_element_type=F32)


def inverse_kernel(counts_ref, pairs_ref, *rest):
    out_ref = rest[-1]
    runs = out_ref.shape[0]
    design = incidence(pairs_ref[0:1, :], pairs_ref[1:2, :], PAD)
    pair = lax.broadcasted_iota(jnp.int32, design.shape, 1)
    contract_last = (((1,), (1,)), ((), ()))
    row = lax.broadcasted_iota(jnp.int32, (PAD, PAD), 0)
    col = lax.broadcasted_iota(jnp.int32, (PAD, PAD), 1)
    identity = (row == col).astype(F32)
    grams = []
    for run in range(runs):
        kept = jnp.where(pair < counts_ref[run], design, 0.0).astype(jnp.bfloat16)
        gram = lax.dot_general(kept, kept, contract_last, preferred_element_type=F32)
        grams.append(gram + DAMPING * identity)
    low = DAMPING
    high = 2.0 * functools.reduce(jnp.maximum, [jnp.max(gram) for gram in grams]) - DAMPING
    total, width = high + low, high - low
    scale = 2.0 * total * total - width * width
    starts = tuple((8.0 * total / scale) * identity - (8.0 / scale) * gram for gram in grams)
    needed = 18.0 * scale / (8.0 * high * low)
    steps = jnp.int32(0)
    for power in range(1, 16):
        steps += (needed > float(2**power)).astype(jnp.int32)

    def newton(product, guesses):
        products = [product(gram, guess) for gram, guess in zip(grams, guesses)]
        return tuple(2.0 * guess - product(guess, each) for guess, each in zip(guesses, products))

    full_steps = 1 + (high > 100.0).astype(jnp.int32)
    guesses = lax.fori_loop(0, steps + 1 - full_steps, lambda _, guesses: newton(split_product, guesses), starts)
    guesses = lax.fori_loop(0, full_steps, lambda _, guesses: newton(full_product, guesses), guesses)
    for run, guess in enumerate(guesses):
        out_ref[run] = guess


def invert_classes(date_pairs, run_counts, after):
    shape = (run_counts.shape[0], PAD, PAD)
    return pl.pallas_call(
        inverse_kernel,
        out_shape=jax.ShapeDtypeStruct(shape, F32),
        grid_spec=pltpu.PrefetchScalarGridSpec(
            num_scalar_prefetch=1,
            grid=(1,),
            in_specs=[pl.BlockSpec(date_pairs.shape, lambda i, c: (0, 0))] + [pl.BlockSpec(memory_space=pl.ANY)] * len(after),
            out_specs=pl.BlockSpec(shape, lambda i, c: (0, 0, 0)),
        ),
        compiler_params=pltpu.CompilerParams(vmem_limit_bytes=VMEM_BYTES),
        cost_estimate=LITTLE,
        name="invert_classes_0",
    )(run_counts, date_pairs, *after)


def sum_solve_kernel(tiles, counts_ref, pairs_ref, data_ref, inverse_ref, out_ref):
    run = pl.program_id(0) // tiles
    design = incidence(pairs_ref[0:1, :], pairs_ref[1:2, :], PAD)
    pair = lax.broadcasted_iota(jnp.int32, design.shape, 1)
    kept = jnp.where(pair < counts_ref[run], design, 0.0).astype(jnp.bfloat16)
    sums = jnp.dot(kept, data_ref[...], preferred_element_type=F32)
    out_ref[...] = jnp.dot(inverse_ref[0, :M, :], sums, precision=HIGHEST, preferred_element_type=F32)


def sum_solve(run_counts, date_pairs, received, inverse):
    runs = run_counts.shape[0]
    total_pairs, pixels = received.shape
    run_pixels = pixels // runs
    tile = run_pixels // 2
    tiles = run_pixels // tile
    return pl.pallas_call(
        functools.partial(sum_solve_kernel, tiles),
        out_shape=jax.ShapeDtypeStruct((M, pixels), F32),
        grid_spec=pltpu.PrefetchScalarGridSpec(
            num_scalar_prefetch=1,
            grid=(runs * tiles,),
            in_specs=[
                pl.BlockSpec(date_pairs.shape, lambda i, c: (0, 0)),
                pl.BlockSpec((total_pairs, tile), lambda i, c: (0, i)),
                pl.BlockSpec((1, PAD, PAD), lambda i, c: (i // tiles, 0, 0)),
            ],
            out_specs=pl.BlockSpec((M, tile), lambda i, c: (0, i)),
        ),
        compiler_params=pltpu.CompilerParams(vmem_limit_bytes=VMEM_BYTES),
        name="sum_solve",
    )(run_counts, date_pairs, received, inverse)


def coded_rows(piece):
    return M * (piece // LANES) + CODE_ROWS


def decode(coded_ref, codes_ref, lots, first):
    coded = coded_ref[...].astype(jnp.int32).astype(F32)
    values = jnp.concatenate([coded[lot * M : (lot + 1) * M, :] for lot in range(lots)], axis=1)
    codes = codes_ref[...].astype(jnp.int32).astype(F32)
    codes = jnp.concatenate([codes[first + lot : first + lot + 1, :] for lot in range(lots)], axis=1)
    return values, jnp.exp2(codes * (1.0 / CODES_PER_OCTAVE)) * (1.0 / LEVELS)


def encode(sums):
    largest = jnp.max(jnp.abs(sums), axis=0, keepdims=True)
    code = jnp.ceil(jnp.log2(jnp.maximum(largest, SMALLEST)) * CODES_PER_OCTAVE)
    scaled = (sums * (LEVELS / jnp.exp2(code * (1.0 / CODES_PER_OCTAVE))) + ROUNDER) - ROUNDER
    lots = sums.shape[1] // LANES
    return jnp.concatenate([scaled[:, lot * LANES : (lot + 1) * LANES] for lot in range(lots)], axis=0), code


def whole(values):
    return values.astype(jnp.int32).astype(jnp.int16)


def piece_count(at, layout, table, counts):
    parts, _, _, shifts = layout
    run = at % parts // CUTS
    return counts[table[shifts + at] * (parts // CUTS) + run]


def pair_sums(count, table, pairs_ref, own_ref, partner_ref):
    width = own_ref.shape[0]
    lane = lax.broadcasted_iota(jnp.int32, (1, 2 * width), 1)
    pair = jnp.where(lane < width, table[ME] * width + lane, table[PARTNER] * width + lane - width)
    design = incidence(pairs_ref[0:1, :], pairs_ref[1:2, :], M)
    kept = jnp.where(pair < count, design, 0.0).astype(jnp.bfloat16)
    data = jnp.concatenate([own_ref[...], partner_ref[...]], axis=0)
    return jnp.dot(kept, data, preferred_element_type=F32)


def copy_kernel(table, source_ref, _, target_ref):
    target_ref[...] = source_ref[...]


def give_out(swap, layout, table, phases, after, piece):
    first, count = swap
    away = layout[2]
    shape = (phases.shape[0], piece * count)
    return pl.pallas_call(
        copy_kernel,
        out_shape=jax.ShapeDtypeStruct(shape, phases.dtype),
        grid_spec=pltpu.PrefetchScalarGridSpec(
            num_scalar_prefetch=1,
            grid=(1,),
            in_specs=[
                pl.BlockSpec(shape, lambda i, t: (0, t[away + first] // count)),
                pl.BlockSpec(memory_space=pl.ANY),
            ],
            out_specs=pl.BlockSpec(shape, lambda i, t: (0, 0)),
        ),
        compiler_params=pltpu.CompilerParams(vmem_limit_bytes=VMEM_BYTES),
        cost_estimate=LITTLE,
        name="give_out",
    )(table, phases, after)


def step_kernel(at, layout, adds, swaps, tells, halves, table, counts, pairs_ref, own_ref, partner_ref, *rest):
    if tells:
        rest[-1][...] = jnp.zeros_like(rest[-1])
        rest = rest[:-1]
    if swaps:
        rest[-1][...] = rest[0][...]
        coded_ref, rest = rest[-2], rest[1:]
    else:
        coded_ref = rest[-1]
    count = piece_count(at, layout, table, counts)
    width = own_ref.shape[1] // halves
    lots = width // LANES
    codes = []
    for half in range(halves):
        part = pl.ds(half * width, width)
        sums = pair_sums(count, table, pairs_ref, own_ref.at[:, part], partner_ref.at[:, part])
        if adds:
            rows = pl.ds(half * lots * M, lots * M)
            values, scale = decode(rest[0].at[rows, :], rest[0].at[halves * lots * M :, :], lots, half * lots)
            sums = sums + values * (scale * table[INNER].astype(F32))
        scaled, code = encode(sums)
        coded_ref[half * lots * M : (half + 1) * lots * M, :] = whole(scaled)
        codes += [code[:, lot * LANES : (lot + 1) * LANES] for lot in range(lots)]
    codes += [jnp.zeros((CODE_ROWS - len(codes), LANES), F32)]
    coded_ref[halves * lots * M :, :] = whole(jnp.concatenate(codes, axis=0))


def step(at, swap, layout, scalars, pairs, phases, partner, earlier, after, piece):
    partner, place_in = partner
    local_pairs = phases.shape[0]
    _, blocks, away, _ = layout
    coded_shape = (coded_rows(piece), LANES)
    in_specs = [
        pl.BlockSpec(pairs.shape, lambda i, t, c: (0, 0)),
        pl.BlockSpec((local_pairs, piece), lambda i, t, c: (0, t[blocks + at])),
        pl.BlockSpec((local_pairs, piece), lambda i, t, c: (0, place_in)),
    ]
    operands = [pairs, phases, partner]
    out_shape = [jax.ShapeDtypeStruct(coded_shape, jnp.int16)]
    out_specs = [pl.BlockSpec(coded_shape, lambda i, t, c: (0, 0))]
    if swap is not None:
        first, count = swap
        wide = piece * count
        in_specs.append(pl.BlockSpec((local_pairs, wide), lambda i, t, c: (0, t[away + first] // count)))
        operands.append(phases)
        out_shape.append(jax.ShapeDtypeStruct((local_pairs, wide), phases.dtype))
        out_specs.append(pl.BlockSpec((local_pairs, wide), lambda i, t, c: (0, 0)))
    if earlier is not None:
        in_specs.append(pl.BlockSpec(coded_shape, lambda i, t, c: (0, 0)))
        operands.append(earlier)
    if at in MEETINGS:
        out_shape.append(jax.ShapeDtypeStruct((8, LANES), F32))
        out_specs.append(pl.BlockSpec((8, LANES), lambda i, t, c: (0, 0)))
    in_specs += [pl.BlockSpec(memory_space=pl.ANY)] * len(after)
    results = pl.pallas_call(
        functools.partial(step_kernel, at, layout, earlier is not None, swap is not None, at in MEETINGS, HALVES),
        out_shape=out_shape,
        grid_spec=pltpu.PrefetchScalarGridSpec(
            num_scalar_prefetch=2,
            grid=(1,),
            in_specs=in_specs,
            out_specs=out_specs,
        ),
        compiler_params=pltpu.CompilerParams(vmem_limit_bytes=VMEM_BYTES),
        cost_estimate=STEADY,
        name=f"sum_step_{at:02d}",
    )(*scalars, *operands, *after)
    return results[0], results[1] if swap is not None else None, results[-1] if at in MEETINGS else None


def coded_specs(piece, tiles, index):
    lots = piece // LANES
    return [
        pl.BlockSpec((lots // tiles * M, LANES), lambda *at: (at[index], 0)),
        pl.BlockSpec((CODE_ROWS, LANES), lambda *at: (lots * M // CODE_ROWS, 0)),
    ]


def add_arrived(sums_ref, refs, tiles):
    lots = sums_ref.shape[1] // LANES
    tile = pl.program_id(0)
    for coded_ref, codes_ref in zip(refs[::2], refs[1::2]):
        parts = [decode(coded_ref, codes_ref, lots, at * lots) for at in range(tiles)]
        scale = functools.reduce(lambda chosen, at: jnp.where(tile == at, parts[at][1], chosen), range(1, tiles), parts[0][1])
        sums_ref[...] += parts[0][0] * scale


def finish_kernel(at, layout, tiles, early, table, counts, pairs_ref, own_ref, partner_ref, inverse_ref, *rest):
    out_ref, sums_ref = rest[-2:]
    sums_ref[...] = pair_sums(piece_count(at, layout, table, counts), table, pairs_ref, own_ref, partner_ref)

    @pl.when(table[INNER] == 0)
    def _():
        add_arrived(sums_ref, rest[: 2 * early], tiles)

    @pl.when(table[INNER] == 1)
    def _():
        add_arrived(sums_ref, rest[2 * early : 2 * early + 2 * LATE], tiles)

    out_ref[...] = split_product(inverse_ref[0, :M, :M], sums_ref[...])


def finish(at, part, layout, scalars, pairs, phases, partner, inverse, early, late, series, pixels, piece):
    partner, place_in = partner
    local_pairs = phases.shape[0]
    blocks = layout[1]
    tiles = HALVES
    tile = piece // tiles
    arrived = early + late
    in_specs = [
        pl.BlockSpec(pairs.shape, lambda i, t, c: (0, 0)),
        pl.BlockSpec((local_pairs, tile), lambda i, t, c: (0, t[blocks + at] * tiles + i)),
        pl.BlockSpec((local_pairs, tile), lambda i, t, c: (0, place_in * tiles + i)),
        pl.BlockSpec((1, PAD, PAD), lambda i, t, c: (part // CUTS, 0, 0)),
    ] + coded_specs(piece, tiles, 0) * len(arrived)
    operands = [*scalars, pairs, phases, partner, inverse] + [each for each in arrived for _ in range(2)]
    aliases = {}
    if series is not None:
        in_specs.append(pl.BlockSpec(memory_space=pl.ANY))
        aliases = {len(operands): 0}
        operands.append(series)
    return pl.pallas_call(
        functools.partial(finish_kernel, at, layout, tiles, len(early)),
        out_shape=jax.ShapeDtypeStruct((M, pixels), F32),
        grid_spec=pltpu.PrefetchScalarGridSpec(
            num_scalar_prefetch=2,
            grid=(tiles,),
            in_specs=in_specs,
            out_specs=pl.BlockSpec((M, tile), lambda i, t, c: (0, part * tiles + i)),
            scratch_shapes=[pltpu.VMEM((M, tile), F32)],
        ),
        input_output_aliases=aliases,
        compiler_params=pltpu.CompilerParams(vmem_limit_bytes=VMEM_BYTES),
        cost_estimate=LITTLE,
        name=f"finish_{part}",
    )(*operands)


def line_permutation(links):
    return [(2 * source + side, 2 * target + side) for source, target in links for side in range(2)]


def solve_by_sums(phases, date_pairs, counts_of):
    owner_count = lax.axis_size("ifg")
    line = owner_count // 2
    local_pairs, pixels = phases.shape
    owner_pixels = pixels // owner_count
    runs = counts_of().shape[0]
    parts = runs * CUTS
    piece = owner_pixels // parts
    steps = (line - 1) * parts
    me = lax.axis_index("ifg")

    places = np.repeat(np.array(CHUNK_ORDER), parts, axis=1)
    part_of = np.tile(np.arange(parts), line)
    rows = []
    for device in range(owner_count):
        place, side = device // 2, device % 2
        own = (places[place] * 2 + side) * parts + part_of
        away = (places[place] * 2 + 1 - side) * parts + part_of
        known = [place, line - 1 - place, place ^ 1, line - 1 - (place ^ 1)]
        shift = np.array([known.index(chunk) for chunk in places[place]])
        rows.append(np.concatenate([[device, device ^ 1, int(0 < place < line - 1)], own, away, shift]))
    row = lax.dynamic_index_in_dim(jnp.asarray(np.stack(rows), jnp.int32), me, 0, keepdims=False)
    head, pieces = FIXED, line * parts
    layout = (parts, head, head + pieces, head + 2 * pieces)

    swap = [(i, i ^ 1) for i in range(owner_count)]
    partner_of = {}

    def swapped(away, first, count):
        here = lax.ppermute(away, "ifg", swap)
        partner_of.update({first + place: (here, place) for place in range(count)})

    place, side = me // 2, me % 2
    run_counts = counts_of()
    mirrored = lax.ppermute(run_counts, "ifg", line_permutation([(i, line - 1 - i) for i in range(line)]))
    first, count = FIRST_SWAPS[0]
    chunk, _ = lax.optimization_barrier((jnp.where(place % 2 == 0, line - 1, 0), run_counts))
    away = lax.dynamic_slice(phases, (0, ((chunk * 2 + 1 - side) * parts + first) * piece), (local_pairs, piece * count))
    swapped(away, first, count)
    both = jnp.concatenate([run_counts, mirrored])
    counts = jnp.concatenate([both, lax.ppermute(both, "ifg", line_permutation([(i, i ^ 1) for i in range(line)]))])
    swapped(give_out(FIRST_SWAPS[1], layout, row, phases, mirrored, piece), *FIRST_SWAPS[1])
    pairs = jnp.concatenate([lax.dynamic_slice(date_pairs, (0, row[at] * local_pairs), (2, local_pairs)) for at in (ME, PARTNER)], axis=1)
    scalars = (row, counts)

    received, coded = [], None
    for at in range(steps):
        earlier = received[at - parts][0] if at >= parts else None
        after = [coded] if at else []
        after += received[at - FLIGHT] if at >= FLIGHT else []
        if at - 1 in MEETINGS:
            after.append(met)
        if at in SWAP_WAITS:
            after.append(partner_of[SWAP_WAITS[at]][0])
        if at == INVERSE_STEP:
            inverse = invert_classes(date_pairs, run_counts, [coded])
            after.append(inverse)
        coded, away, told = step(at, SWAPS.get(at), layout, scalars, pairs, phases, partner_of[at], earlier, after, piece)
        received.append([lax.ppermute(coded, "ifg", line_permutation(links)) for links in SENDS[at // parts]])
        if at in SWAPS:
            swapped(away, *SWAPS[at])
        if at in MEETINGS:
            met = lax.ppermute(told, "grp", [(i, i ^ 1) for i in range(lax.axis_size("grp"))])
        if at == 0:
            swapped(give_out(FIRST_SWAPS[2], layout, row, phases, coded, piece), *FIRST_SWAPS[2])

    series = None
    for part in range(parts):
        at = steps + part
        early = [each for place in range(line - 2) for each in received[place * parts + part]]
        late = received[(line - 2) * parts + part]
        series = finish(at, part, layout, scalars, pairs, phases, partner_of[at], inverse, early, late, series, owner_pixels, piece)
    return series


def solve_by_blocks(phases, date_pairs, counts_of):
    owner_count = lax.axis_size("ifg")
    local_pairs, pixels = phases.shape
    owner_pixels = pixels // owner_count
    run_counts = counts_of()
    outgoing = phases.reshape(local_pairs, owner_count, owner_pixels).transpose(1, 0, 2)
    received = lax.all_to_all(outgoing, "ifg", split_axis=0, concat_axis=0, tiled=True)
    inverse = invert_classes(date_pairs, run_counts, [])
    return sum_solve(run_counts, date_pairs, received.reshape(-1, owner_pixels), inverse)


def local(phases, date_pairs, pair_counts, group_ids):
    local_pairs, _, pixels = phases.shape

    def counts_of():
        strip_groups = lax.dynamic_index_in_dim(group_ids, lax.axis_index("grp"), 0, keepdims=False)[::RUN]
        chosen = strip_groups[:, None] == jnp.arange(pair_counts.shape[0], dtype=jnp.int32)
        return jnp.sum(jnp.where(chosen, pair_counts, 0), axis=1)

    line = lax.axis_size("ifg") == 2 * len(CHUNK_ORDER) and group_ids.shape[1] == 2 * RUN
    by_sums = line and 2 * local_pairs > M and local_pairs % LANES == 0 and lax.axis_size("grp") % 2 == 0
    solve = solve_by_sums if by_sums else solve_by_blocks
    return solve(phases.reshape(local_pairs, pixels), date_pairs, counts_of)[None, :, :]


def solution(mesh):
    in_specs = (P("ifg", "grp", None), P(), P(), P(None, "ifg"))
    out_specs = P("grp", None, "ifg")
    return jax.shard_map(local, mesh=mesh, in_specs=in_specs, out_specs=out_specs, check_vma=False)
```

```python
import functools

import jax
import jax.numpy as jnp
import numpy as np
from jax import lax
from jax.experimental import pallas as pl
from jax.experimental.pallas import tpu as pltpu
from jax.sharding import PartitionSpec as P

M = 200
RUN = 8
PAD = 256
SLABS = 8
DAMPING = 1.0
VMEM_BYTES = 48 * 1024 * 1024
F32 = jnp.float32
HIGHEST = lax.Precision.HIGHEST
STEADY = pl.CostEstimate(flops=10_000_000_000, bytes_accessed=30_000_000, transcendentals=0)
LITTLE = pl.CostEstimate(flops=1024, bytes_accessed=1024, transcendentals=0)
CUTS = 2
HALVES = 2
FLIGHT = 2
FIRST_SWAPS = ((0, 1), (1, 1), (2, 2))
SWAPS = {2: (4, 2), 3: (6, 2), 5: (8, 4), 8: (12, 4)}
SWAP_WAITS = {5: 6}
MEETINGS = ()
INVERSE_STEP = 2
FINISHED_AHEAD = 1
ME, PARTNER, INNER, FIXED = 0, 1, 2, 3
LANES = 128
CODE_ROWS = 16
LEVELS = 32700.0
ROUNDER = 1.5 * 2.0**23
CODES_PER_OCTAVE = 128.0
SMALLEST = 2.0**-110
CHUNK_ORDER = ((2, 3, 1, 0), (0, 2, 3, 1), (3, 1, 0, 2), (1, 0, 2, 3))
SENDS = (
    (((0, 1), (1, 0), (2, 3), (3, 2)),),
    (((0, 1), (3, 2)), ((1, 2), (2, 1))),
    (((0, 1), (1, 3), (2, 0), (3, 2)),),
)


def incidence(earlier, later, rows):
    shape = (rows, earlier.shape[1])
    date = lax.broadcasted_iota(jnp.int32, shape, 0)
    return (date == later).astype(F32) - (date == earlier).astype(F32)


def split_product(left, right):
    def halves(value):
        high = value.astype(jnp.bfloat16)
        return high, (value - high.astype(F32)).astype(jnp.bfloat16)

    left_high, left_low = halves(left)
    right_high, right_low = halves(right)
    small = jnp.dot(left_high, right_low, preferred_element_type=F32) + jnp.dot(left_low, right_high, preferred_element_type=F32)
    return jnp.dot(left_high, right_high, preferred_element_type=F32) + small


def full_product(left, right):
    return jnp.dot(left, right, precision=HIGHEST, preferred_element_type=F32)


def inverse_kernel(counts_ref, pairs_ref, *rest):
    out_ref = rest[-1]
    runs = out_ref.shape[0]
    design = incidence(pairs_ref[0:1, :], pairs_ref[1:2, :], PAD)
    pair = lax.broadcasted_iota(jnp.int32, design.shape, 1)
    contract_last = (((1,), (1,)), ((), ()))
    row = lax.broadcasted_iota(jnp.int32, (PAD, PAD), 0)
    col = lax.broadcasted_iota(jnp.int32, (PAD, PAD), 1)
    identity = (row == col).astype(F32)
    grams = []
    for run in range(runs):
        kept = jnp.where(pair < counts_ref[run], design, 0.0).astype(jnp.bfloat16)
        gram = lax.dot_general(kept, kept, contract_last, preferred_element_type=F32)
        grams.append(gram + DAMPING * identity)
    low = DAMPING
    high = 2.0 * functools.reduce(jnp.maximum, [jnp.max(gram) for gram in grams]) - DAMPING
    total, width = high + low, high - low
    scale = 2.0 * total * total - width * width
    starts = tuple((8.0 * total / scale) * identity - (8.0 / scale) * gram for gram in grams)
    needed = 18.0 * scale / (8.0 * high * low)
    steps = jnp.int32(0)
    for power in range(1, 16):
        steps += (needed > float(2**power)).astype(jnp.int32)

    def newton(product, guesses):
        products = [product(gram, guess) for gram, guess in zip(grams, guesses)]
        return tuple(2.0 * guess - product(guess, each) for guess, each in zip(guesses, products))

    full_steps = 1 + (high > 100.0).astype(jnp.int32)
    guesses = lax.fori_loop(0, steps + 1 - full_steps, lambda _, guesses: newton(split_product, guesses), starts)
    guesses = lax.fori_loop(0, full_steps, lambda _, guesses: newton(full_product, guesses), guesses)
    for run, guess in enumerate(guesses):
        out_ref[run] = guess


def invert_classes(date_pairs, run_counts, after):
    shape = (run_counts.shape[0], PAD, PAD)
    return pl.pallas_call(
        inverse_kernel,
        out_shape=jax.ShapeDtypeStruct(shape, F32),
        grid_spec=pltpu.PrefetchScalarGridSpec(
            num_scalar_prefetch=1,
            grid=(1,),
            in_specs=[pl.BlockSpec(date_pairs.shape, lambda i, c: (0, 0))] + [pl.BlockSpec(memory_space=pl.ANY)] * len(after),
            out_specs=pl.BlockSpec(shape, lambda i, c: (0, 0, 0)),
        ),
        compiler_params=pltpu.CompilerParams(vmem_limit_bytes=VMEM_BYTES),
        cost_estimate=LITTLE,
        name="invert_classes_0",
    )(run_counts, date_pairs, *after)


def sum_solve_kernel(tiles, counts_ref, pairs_ref, data_ref, inverse_ref, out_ref):
    run = pl.program_id(0) // tiles
    design = incidence(pairs_ref[0:1, :], pairs_ref[1:2, :], PAD)
    pair = lax.broadcasted_iota(jnp.int32, design.shape, 1)
    kept = jnp.where(pair < counts_ref[run], design, 0.0).astype(jnp.bfloat16)
    sums = jnp.dot(kept, data_ref[...], preferred_element_type=F32)
    out_ref[...] = jnp.dot(inverse_ref[0, :M, :], sums, precision=HIGHEST, preferred_element_type=F32)


def sum_solve(run_counts, date_pairs, received, inverse):
    runs = run_counts.shape[0]
    total_pairs, pixels = received.shape
    run_pixels = pixels // runs
    tile = run_pixels // 2
    tiles = run_pixels // tile
    return pl.pallas_call(
        functools.partial(sum_solve_kernel, tiles),
        out_shape=jax.ShapeDtypeStruct((M, pixels), F32),
        grid_spec=pltpu.PrefetchScalarGridSpec(
            num_scalar_prefetch=1,
            grid=(runs * tiles,),
            in_specs=[
                pl.BlockSpec(date_pairs.shape, lambda i, c: (0, 0)),
                pl.BlockSpec((total_pairs, tile), lambda i, c: (0, i)),
                pl.BlockSpec((1, PAD, PAD), lambda i, c: (i // tiles, 0, 0)),
            ],
            out_specs=pl.BlockSpec((M, tile), lambda i, c: (0, i)),
        ),
        compiler_params=pltpu.CompilerParams(vmem_limit_bytes=VMEM_BYTES),
        name="sum_solve",
    )(run_counts, date_pairs, received, inverse)


def coded_rows(piece):
    return M * (piece // LANES) + CODE_ROWS


def decode(coded_ref, codes_ref, lots, first):
    coded = coded_ref[...].astype(jnp.int32).astype(F32)
    values = jnp.concatenate([coded[lot * M : (lot + 1) * M, :] for lot in range(lots)], axis=1)
    codes = codes_ref[...].astype(jnp.int32).astype(F32)
    codes = jnp.concatenate([codes[first + lot : first + lot + 1, :] for lot in range(lots)], axis=1)
    return values, jnp.exp2(codes * (1.0 / CODES_PER_OCTAVE)) * (1.0 / LEVELS)


def encode(sums):
    largest = jnp.max(jnp.abs(sums), axis=0, keepdims=True)
    code = jnp.ceil(jnp.log2(jnp.maximum(largest, SMALLEST)) * CODES_PER_OCTAVE)
    scaled = (sums * (LEVELS / jnp.exp2(code * (1.0 / CODES_PER_OCTAVE))) + ROUNDER) - ROUNDER
    lots = sums.shape[1] // LANES
    return jnp.concatenate([scaled[:, lot * LANES : (lot + 1) * LANES] for lot in range(lots)], axis=0), code


def whole(values):
    return values.astype(jnp.int32).astype(jnp.int16)


def piece_count(at, layout, table, counts):
    parts, _, _, shifts = layout
    run = at % parts // CUTS
    return counts[table[shifts + at] * (parts // CUTS) + run]


def pair_sums(count, table, pairs_ref, own_ref, partner_ref):
    width = own_ref.shape[0]
    lane = lax.broadcasted_iota(jnp.int32, (1, 2 * width), 1)
    pair = jnp.where(lane < width, table[ME] * width + lane, table[PARTNER] * width + lane - width)
    design = incidence(pairs_ref[0:1, :], pairs_ref[1:2, :], M)
    kept = jnp.where(pair < count, design, 0.0).astype(jnp.bfloat16)
    data = jnp.concatenate([own_ref[...], partner_ref[...]], axis=0)
    return jnp.dot(kept, data, preferred_element_type=F32)


def copy_kernel(table, source_ref, _, target_ref):
    target_ref[...] = source_ref[...]


def give_out(swap, layout, table, phases, after, piece):
    first, count = swap
    away = layout[2]
    shape = (phases.shape[0], piece * count)
    return pl.pallas_call(
        copy_kernel,
        out_shape=jax.ShapeDtypeStruct(shape, phases.dtype),
        grid_spec=pltpu.PrefetchScalarGridSpec(
            num_scalar_prefetch=1,
            grid=(1,),
            in_specs=[
                pl.BlockSpec(shape, lambda i, t: (0, t[away + first] // count)),
                pl.BlockSpec(memory_space=pl.ANY),
            ],
            out_specs=pl.BlockSpec(shape, lambda i, t: (0, 0)),
        ),
        compiler_params=pltpu.CompilerParams(vmem_limit_bytes=VMEM_BYTES),
        cost_estimate=LITTLE,
        name="give_out",
    )(table, phases, after)


def step_kernel(at, layout, adds, swaps, tells, halves, table, counts, pairs_ref, own_ref, partner_ref, *rest):
    if tells:
        rest[-1][...] = jnp.zeros_like(rest[-1])
        rest = rest[:-1]
    if swaps:
        rest[-1][...] = rest[0][...]
        coded_ref, rest = rest[-2], rest[1:]
    else:
        coded_ref = rest[-1]
    count = piece_count(at, layout, table, counts)
    width = own_ref.shape[1] // halves
    lots = width // LANES
    codes = []
    for half in range(halves):
        part = pl.ds(half * width, width)
        sums = pair_sums(count, table, pairs_ref, own_ref.at[:, part], partner_ref.at[:, part])
        if adds:
            rows = pl.ds(half * lots * M, lots * M)
            values, scale = decode(rest[0].at[rows, :], rest[0].at[halves * lots * M :, :], lots, half * lots)
            sums = sums + values * (scale * table[INNER].astype(F32))
        scaled, code = encode(sums)
        coded_ref[half * lots * M : (half + 1) * lots * M, :] = whole(scaled)
        codes += [code[:, lot * LANES : (lot + 1) * LANES] for lot in range(lots)]
    codes += [jnp.zeros((CODE_ROWS - len(codes), LANES), F32)]
    coded_ref[halves * lots * M :, :] = whole(jnp.concatenate(codes, axis=0))


def step(at, swap, layout, scalars, pairs, phases, partner, earlier, after, piece):
    partner, place_in = partner
    local_pairs = phases.shape[0]
    _, blocks, away, _ = layout
    coded_shape = (coded_rows(piece), LANES)
    in_specs = [
        pl.BlockSpec(pairs.shape, lambda i, t, c: (0, 0)),
        pl.BlockSpec((local_pairs, piece), lambda i, t, c: (0, t[blocks + at])),
        pl.BlockSpec((local_pairs, piece), lambda i, t, c: (0, place_in)),
    ]
    operands = [pairs, phases, partner]
    out_shape = [jax.ShapeDtypeStruct(coded_shape, jnp.int16)]
    out_specs = [pl.BlockSpec(coded_shape, lambda i, t, c: (0, 0))]
    if swap is not None:
        first, count = swap
        wide = piece * count
        in_specs.append(pl.BlockSpec((local_pairs, wide), lambda i, t, c: (0, t[away + first] // count)))
        operands.append(phases)
        out_shape.append(jax.ShapeDtypeStruct((local_pairs, wide), phases.dtype))
        out_specs.append(pl.BlockSpec((local_pairs, wide), lambda i, t, c: (0, 0)))
    if earlier is not None:
        in_specs.append(pl.BlockSpec(coded_shape, lambda i, t, c: (0, 0)))
        operands.append(earlier)
    if at in MEETINGS:
        out_shape.append(jax.ShapeDtypeStruct((8, LANES), F32))
        out_specs.append(pl.BlockSpec((8, LANES), lambda i, t, c: (0, 0)))
    in_specs += [pl.BlockSpec(memory_space=pl.ANY)] * len(after)
    results = pl.pallas_call(
        functools.partial(step_kernel, at, layout, earlier is not None, swap is not None, at in MEETINGS, HALVES),
        out_shape=out_shape,
        grid_spec=pltpu.PrefetchScalarGridSpec(
            num_scalar_prefetch=2,
            grid=(1,),
            in_specs=in_specs,
            out_specs=out_specs,
        ),
        compiler_params=pltpu.CompilerParams(vmem_limit_bytes=VMEM_BYTES),
        cost_estimate=STEADY,
        name=f"sum_step_{at:02d}",
    )(*scalars, *operands, *after)
    return results[0], results[1] if swap is not None else None, results[-1] if at in MEETINGS else None


def coded_specs(piece, tiles, index):
    lots = piece // LANES
    return [
        pl.BlockSpec((lots // tiles * M, LANES), lambda *at: (at[index], 0)),
        pl.BlockSpec((CODE_ROWS, LANES), lambda *at: (lots * M // CODE_ROWS, 0)),
    ]


def add_arrived(sums_ref, refs, tiles):
    lots = sums_ref.shape[1] // LANES
    tile = pl.program_id(0)
    for coded_ref, codes_ref in zip(refs[::2], refs[1::2]):
        parts = [decode(coded_ref, codes_ref, lots, at * lots) for at in range(tiles)]
        scale = functools.reduce(lambda chosen, at: jnp.where(tile == at, parts[at][1], chosen), range(1, tiles), parts[0][1])
        sums_ref[...] += parts[0][0] * scale


def finish_kernel(at, layout, tiles, table, counts, pairs_ref, own_ref, partner_ref, inverse_ref, *rest):
    first, middle, last = rest[:2], rest[2:4], rest[4:6]
    out_ref, sums_ref = rest[-2:]
    sums_ref[...] = pair_sums(piece_count(at, layout, table, counts), table, pairs_ref, own_ref, partner_ref)

    @pl.when(table[INNER] == 0)
    def _():
        add_arrived(sums_ref, first, tiles)

    @pl.when(table[INNER] == 1)
    def _():
        add_arrived(sums_ref, middle, tiles)

    add_arrived(sums_ref, last, tiles)
    out_ref[...] = split_product(inverse_ref[0, :M, :M], sums_ref[...])


def finish(at, part, layout, scalars, pairs, phases, partner, inverse, arrived, series, pixels, piece):
    partner, place_in = partner
    local_pairs = phases.shape[0]
    blocks = layout[1]
    tiles = HALVES
    tile = piece // tiles
    in_specs = [
        pl.BlockSpec(pairs.shape, lambda i, t, c: (0, 0)),
        pl.BlockSpec((local_pairs, tile), lambda i, t, c: (0, t[blocks + at] * tiles + i)),
        pl.BlockSpec((local_pairs, tile), lambda i, t, c: (0, place_in * tiles + i)),
        pl.BlockSpec((1, PAD, PAD), lambda i, t, c: (part // CUTS, 0, 0)),
    ] + coded_specs(piece, tiles, 0) * len(arrived)
    operands = [*scalars, pairs, phases, partner, inverse] + [each for each in arrived for _ in range(2)]
    aliases = {}
    if series is not None:
        in_specs.append(pl.BlockSpec(memory_space=pl.ANY))
        aliases = {len(operands): 0}
        operands.append(series)
    return pl.pallas_call(
        functools.partial(finish_kernel, at, layout, tiles),
        out_shape=jax.ShapeDtypeStruct((M, pixels), F32),
        grid_spec=pltpu.PrefetchScalarGridSpec(
            num_scalar_prefetch=2,
            grid=(tiles,),
            in_specs=in_specs,
            out_specs=pl.BlockSpec((M, tile), lambda i, t, c: (0, part * tiles + i)),
            scratch_shapes=[pltpu.VMEM((M, tile), F32)],
        ),
        input_output_aliases=aliases,
        compiler_params=pltpu.CompilerParams(vmem_limit_bytes=VMEM_BYTES),
        cost_estimate=LITTLE,
        name=f"finish_{part}",
    )(*operands)


def line_permutation(links):
    return [(2 * source + side, 2 * target + side) for source, target in links for side in range(2)]


def solve_by_sums(phases, date_pairs, counts_of):
    owner_count = lax.axis_size("ifg")
    line = owner_count // 2
    local_pairs, pixels = phases.shape
    owner_pixels = pixels // owner_count
    runs = counts_of().shape[0]
    parts = runs * CUTS
    piece = owner_pixels // parts
    steps = (line - 1) * parts
    me = lax.axis_index("ifg")

    places = np.repeat(np.array(CHUNK_ORDER), parts, axis=1)
    part_of = np.tile(np.arange(parts), line)
    rows = []
    for device in range(owner_count):
        place, side = device // 2, device % 2
        own = (places[place] * 2 + side) * parts + part_of
        away = (places[place] * 2 + 1 - side) * parts + part_of
        known = [place, line - 1 - place, place ^ 1, line - 1 - (place ^ 1)]
        shift = np.array([known.index(chunk) for chunk in places[place]])
        rows.append(np.concatenate([[device, device ^ 1, int(0 < place < line - 1)], own, away, shift]))
    row = lax.dynamic_index_in_dim(jnp.asarray(np.stack(rows), jnp.int32), me, 0, keepdims=False)
    head, pieces = FIXED, line * parts
    layout = (parts, head, head + pieces, head + 2 * pieces)

    swap = [(i, i ^ 1) for i in range(owner_count)]
    partner_of = {}

    def swapped(away, first, count):
        here = lax.ppermute(away, "ifg", swap)
        partner_of.update({first + place: (here, place) for place in range(count)})

    place, side = me // 2, me % 2
    run_counts = counts_of()
    mirrored = lax.ppermute(run_counts, "ifg", line_permutation([(i, line - 1 - i) for i in range(line)]))
    first, count = FIRST_SWAPS[0]
    chunk, _ = lax.optimization_barrier((jnp.where(place < line // 2, 2 - 2 * place, 7 - 2 * place), run_counts))
    away = lax.dynamic_slice(phases, (0, ((chunk * 2 + 1 - side) * parts + first) * piece), (local_pairs, piece * count))
    swapped(away, first, count)
    both = jnp.concatenate([run_counts, mirrored])
    counts = jnp.concatenate([both, lax.ppermute(both, "ifg", line_permutation([(i, i ^ 1) for i in range(line)]))])
    swapped(give_out(FIRST_SWAPS[1], layout, row, phases, mirrored, piece), *FIRST_SWAPS[1])
    pairs = jnp.concatenate([lax.dynamic_slice(date_pairs, (0, row[at] * local_pairs), (2, local_pairs)) for at in (ME, PARTNER)], axis=1)
    scalars = (row, counts)

    received, coded, series = [], None, None

    def finished(part, series):
        at = steps + part
        arrived = [received[place * parts + part][-1] for place in range(line - 1)]
        return finish(at, part, layout, scalars, pairs, phases, partner_of[at], inverse, arrived, series, owner_pixels, piece)

    for at in range(steps):
        earlier = received[at - parts][0] if at >= parts else None
        after = [coded] if at else []
        after += received[at - FLIGHT] if at >= FLIGHT else []
        if at - 1 in MEETINGS:
            after.append(met)
        if at in SWAP_WAITS:
            after.append(partner_of[SWAP_WAITS[at]][0])
        if at == INVERSE_STEP:
            inverse = invert_classes(date_pairs, run_counts, [coded])
            after.append(inverse)
        if at == steps - 1:
            for part in range(FINISHED_AHEAD):
                series = finished(part, series)
                after.append(series)
        coded, away, told = step(at, SWAPS.get(at), layout, scalars, pairs, phases, partner_of[at], earlier, after, piece)
        received.append([lax.ppermute(coded, "ifg", line_permutation(links)) for links in SENDS[at // parts]])
        if at in SWAPS:
            swapped(away, *SWAPS[at])
        if at in MEETINGS:
            met = lax.ppermute(told, "grp", [(i, i ^ 1) for i in range(lax.axis_size("grp"))])
        if at == 0:
            swapped(give_out(FIRST_SWAPS[2], layout, row, phases, coded, piece), *FIRST_SWAPS[2])

    for part in range(FINISHED_AHEAD, parts):
        series = finished(part, series)
    return series


def solve_by_blocks(phases, date_pairs, counts_of):
    owner_count = lax.axis_size("ifg")
    local_pairs, pixels = phases.shape
    owner_pixels = pixels // owner_count
    run_counts = counts_of()
    outgoing = phases.reshape(local_pairs, owner_count, owner_pixels).transpose(1, 0, 2)
    received = lax.all_to_all(outgoing, "ifg", split_axis=0, concat_axis=0, tiled=True)
    inverse = invert_classes(date_pairs, run_counts, [])
    return sum_solve(run_counts, date_pairs, received.reshape(-1, owner_pixels), inverse)


def local(phases, date_pairs, pair_counts, group_ids):
    local_pairs, _, pixels = phases.shape

    def counts_of():
        strip_groups = lax.dynamic_index_in_dim(group_ids, lax.axis_index("grp"), 0, keepdims=False)[::RUN]
        chosen = strip_groups[:, None] == jnp.arange(pair_counts.shape[0], dtype=jnp.int32)
        return jnp.sum(jnp.where(chosen, pair_counts, 0), axis=1)

    line = lax.axis_size("ifg") == 2 * len(CHUNK_ORDER) and group_ids.shape[1] == 2 * RUN
    by_sums = line and 2 * local_pairs > M and local_pairs % LANES == 0 and lax.axis_size("grp") % 2 == 0
    solve = solve_by_sums if by_sums else solve_by_blocks
    return solve(phases.reshape(local_pairs, pixels), date_pairs, counts_of)[None, :, :]


def solution(mesh):
    in_specs = (P("ifg", "grp", None), P(), P(), P(None, "ifg"))
    out_specs = P("grp", None, "ifg")
    return jax.shard_map(local, mesh=mesh, in_specs=in_specs, out_specs=out_specs, check_vma=False)
```

```python
import functools

import jax
import jax.numpy as jnp
import numpy as np
from jax import lax
from jax.experimental import pallas as pl
from jax.experimental.pallas import tpu as pltpu
from jax.sharding import PartitionSpec as P

M = 200
RUN = 8
PAD = 256
SLABS = 8
DAMPING = 1.0
VMEM_BYTES = 48 * 1024 * 1024
F32 = jnp.float32
HIGHEST = lax.Precision.HIGHEST
STEADY = pl.CostEstimate(flops=10_000_000_000, bytes_accessed=30_000_000, transcendentals=0)
LITTLE = pl.CostEstimate(flops=1024, bytes_accessed=1024, transcendentals=0)
CUTS = 2
HALVES = 2
FLIGHT = 2
FIRST_SWAPS = ((0, 1), (1, 1), (2, 2))
SWAPS = {2: (4, 2), 3: (6, 2), 5: (8, 4), 8: (12, 2), 9: (14, 2)}
SWAP_WAITS = {5: 6, 10: 12}
MEETINGS = ()
INVERSE_STEP = 2
FINISHED_AHEAD = 0
ME, PARTNER, INNER, FIXED = 0, 1, 2, 3
LANES = 128
CODE_ROWS = 16
LEVELS = 32700.0
ROUNDER = 1.5 * 2.0**23
CODES_PER_OCTAVE = 128.0
SMALLEST = 2.0**-110
CHUNK_ORDER = ((2, 3, 1, 0), (0, 2, 3, 1), (3, 1, 0, 2), (1, 0, 2, 3))
SENDS = (
    (((0, 1), (1, 0), (2, 3), (3, 2)),),
    (((0, 1), (3, 2)), ((1, 2), (2, 1))),
    (((0, 1), (1, 3), (2, 0), (3, 2)),),
)


def incidence(earlier, later, rows):
    shape = (rows, earlier.shape[1])
    date = lax.broadcasted_iota(jnp.int32, shape, 0)
    return (date == later).astype(F32) - (date == earlier).astype(F32)


def split_product(left, right):
    def halves(value):
        high = value.astype(jnp.bfloat16)
        return high, (value - high.astype(F32)).astype(jnp.bfloat16)

    left_high, left_low = halves(left)
    right_high, right_low = halves(right)
    small = jnp.dot(left_high, right_low, preferred_element_type=F32) + jnp.dot(left_low, right_high, preferred_element_type=F32)
    return jnp.dot(left_high, right_high, preferred_element_type=F32) + small


def full_product(left, right):
    return jnp.dot(left, right, precision=HIGHEST, preferred_element_type=F32)


def inverse_kernel(counts_ref, pairs_ref, *rest):
    out_ref = rest[-1]
    runs = out_ref.shape[0]
    design = incidence(pairs_ref[0:1, :], pairs_ref[1:2, :], PAD)
    pair = lax.broadcasted_iota(jnp.int32, design.shape, 1)
    contract_last = (((1,), (1,)), ((), ()))
    row = lax.broadcasted_iota(jnp.int32, (PAD, PAD), 0)
    col = lax.broadcasted_iota(jnp.int32, (PAD, PAD), 1)
    identity = (row == col).astype(F32)
    grams = []
    for run in range(runs):
        kept = jnp.where(pair < counts_ref[run], design, 0.0).astype(jnp.bfloat16)
        gram = lax.dot_general(kept, kept, contract_last, preferred_element_type=F32)
        grams.append(gram + DAMPING * identity)
    low = DAMPING
    high = 2.0 * functools.reduce(jnp.maximum, [jnp.max(gram) for gram in grams]) - DAMPING
    total, width = high + low, high - low
    scale = 2.0 * total * total - width * width
    starts = tuple((8.0 * total / scale) * identity - (8.0 / scale) * gram for gram in grams)
    needed = 18.0 * scale / (8.0 * high * low)
    steps = jnp.int32(0)
    for power in range(1, 16):
        steps += (needed > float(2**power)).astype(jnp.int32)

    def newton(product, guesses):
        products = [product(gram, guess) for gram, guess in zip(grams, guesses)]
        return tuple(2.0 * guess - product(guess, each) for guess, each in zip(guesses, products))

    full_steps = 1 + (high > 100.0).astype(jnp.int32)
    guesses = lax.fori_loop(0, steps + 1 - full_steps, lambda _, guesses: newton(split_product, guesses), starts)
    guesses = lax.fori_loop(0, full_steps, lambda _, guesses: newton(full_product, guesses), guesses)
    for run, guess in enumerate(guesses):
        out_ref[run] = guess


def invert_classes(date_pairs, run_counts, after):
    shape = (run_counts.shape[0], PAD, PAD)
    return pl.pallas_call(
        inverse_kernel,
        out_shape=jax.ShapeDtypeStruct(shape, F32),
        grid_spec=pltpu.PrefetchScalarGridSpec(
            num_scalar_prefetch=1,
            grid=(1,),
            in_specs=[pl.BlockSpec(date_pairs.shape, lambda i, c: (0, 0))] + [pl.BlockSpec(memory_space=pl.ANY)] * len(after),
            out_specs=pl.BlockSpec(shape, lambda i, c: (0, 0, 0)),
        ),
        compiler_params=pltpu.CompilerParams(vmem_limit_bytes=VMEM_BYTES),
        cost_estimate=LITTLE,
        name="invert_classes_0",
    )(run_counts, date_pairs, *after)


def sum_solve_kernel(tiles, counts_ref, pairs_ref, data_ref, inverse_ref, out_ref):
    run = pl.program_id(0) // tiles
    design = incidence(pairs_ref[0:1, :], pairs_ref[1:2, :], PAD)
    pair = lax.broadcasted_iota(jnp.int32, design.shape, 1)
    kept = jnp.where(pair < counts_ref[run], design, 0.0).astype(jnp.bfloat16)
    sums = jnp.dot(kept, data_ref[...], preferred_element_type=F32)
    out_ref[...] = jnp.dot(inverse_ref[0, :M, :], sums, precision=HIGHEST, preferred_element_type=F32)


def sum_solve(run_counts, date_pairs, received, inverse):
    runs = run_counts.shape[0]
    total_pairs, pixels = received.shape
    run_pixels = pixels // runs
    tile = run_pixels // 2
    tiles = run_pixels // tile
    return pl.pallas_call(
        functools.partial(sum_solve_kernel, tiles),
        out_shape=jax.ShapeDtypeStruct((M, pixels), F32),
        grid_spec=pltpu.PrefetchScalarGridSpec(
            num_scalar_prefetch=1,
            grid=(runs * tiles,),
            in_specs=[
                pl.BlockSpec(date_pairs.shape, lambda i, c: (0, 0)),
                pl.BlockSpec((total_pairs, tile), lambda i, c: (0, i)),
                pl.BlockSpec((1, PAD, PAD), lambda i, c: (i // tiles, 0, 0)),
            ],
            out_specs=pl.BlockSpec((M, tile), lambda i, c: (0, i)),
        ),
        compiler_params=pltpu.CompilerParams(vmem_limit_bytes=VMEM_BYTES),
        name="sum_solve",
    )(run_counts, date_pairs, received, inverse)


def coded_rows(piece):
    return M * (piece // LANES) + CODE_ROWS


def decode(coded_ref, codes_ref, lots, first):
    coded = coded_ref[...].astype(jnp.int32).astype(F32)
    values = jnp.concatenate([coded[lot * M : (lot + 1) * M, :] for lot in range(lots)], axis=1)
    codes = codes_ref[...].astype(jnp.int32).astype(F32)
    codes = jnp.concatenate([codes[first + lot : first + lot + 1, :] for lot in range(lots)], axis=1)
    return values, jnp.exp2(codes * (1.0 / CODES_PER_OCTAVE)) * (1.0 / LEVELS)


def encode(sums):
    largest = jnp.max(jnp.abs(sums), axis=0, keepdims=True)
    code = jnp.ceil(jnp.log2(jnp.maximum(largest, SMALLEST)) * CODES_PER_OCTAVE)
    scaled = (sums * (LEVELS / jnp.exp2(code * (1.0 / CODES_PER_OCTAVE))) + ROUNDER) - ROUNDER
    lots = sums.shape[1] // LANES
    return jnp.concatenate([scaled[:, lot * LANES : (lot + 1) * LANES] for lot in range(lots)], axis=0), code


def whole(values):
    return values.astype(jnp.int32).astype(jnp.int16)


def piece_count(at, layout, table, counts):
    parts, _, _, shifts = layout
    run = at % parts // CUTS
    return counts[table[shifts + at] * (parts // CUTS) + run]


def pair_sums(count, table, pairs_ref, own_ref, partner_ref):
    width = own_ref.shape[0]
    lane = lax.broadcasted_iota(jnp.int32, (1, 2 * width), 1)
    pair = jnp.where(lane < width, table[ME] * width + lane, table[PARTNER] * width + lane - width)
    design = incidence(pairs_ref[0:1, :], pairs_ref[1:2, :], M)
    kept = jnp.where(pair < count, design, 0.0).astype(jnp.bfloat16)
    data = jnp.concatenate([own_ref[...], partner_ref[...]], axis=0)
    return jnp.dot(kept, data, preferred_element_type=F32)


def copy_kernel(table, source_ref, _, target_ref):
    target_ref[...] = source_ref[...]


def give_out(swap, layout, table, phases, after, piece):
    first, count = swap
    away = layout[2]
    shape = (phases.shape[0], piece * count)
    return pl.pallas_call(
        copy_kernel,
        out_shape=jax.ShapeDtypeStruct(shape, phases.dtype),
        grid_spec=pltpu.PrefetchScalarGridSpec(
            num_scalar_prefetch=1,
            grid=(1,),
            in_specs=[
                pl.BlockSpec(shape, lambda i, t: (0, t[away + first] // count)),
                pl.BlockSpec(memory_space=pl.ANY),
            ],
            out_specs=pl.BlockSpec(shape, lambda i, t: (0, 0)),
        ),
        compiler_params=pltpu.CompilerParams(vmem_limit_bytes=VMEM_BYTES),
        cost_estimate=LITTLE,
        name="give_out",
    )(table, phases, after)


def step_kernel(at, layout, adds, swaps, tells, halves, table, counts, pairs_ref, own_ref, partner_ref, *rest):
    if tells:
        rest[-1][...] = jnp.zeros_like(rest[-1])
        rest = rest[:-1]
    if swaps:
        rest[-1][...] = rest[0][...]
        coded_ref, rest = rest[-2], rest[1:]
    else:
        coded_ref = rest[-1]
    count = piece_count(at, layout, table, counts)
    width = own_ref.shape[1] // halves
    lots = width // LANES
    codes = []
    for half in range(halves):
        part = pl.ds(half * width, width)
        sums = pair_sums(count, table, pairs_ref, own_ref.at[:, part], partner_ref.at[:, part])
        if adds:
            rows = pl.ds(half * lots * M, lots * M)
            values, scale = decode(rest[0].at[rows, :], rest[0].at[halves * lots * M :, :], lots, half * lots)
            sums = sums + values * (scale * table[INNER].astype(F32))
        scaled, code = encode(sums)
        coded_ref[half * lots * M : (half + 1) * lots * M, :] = whole(scaled)
        codes += [code[:, lot * LANES : (lot + 1) * LANES] for lot in range(lots)]
    codes += [jnp.zeros((CODE_ROWS - len(codes), LANES), F32)]
    coded_ref[halves * lots * M :, :] = whole(jnp.concatenate(codes, axis=0))


def step(at, swap, layout, scalars, pairs, phases, partner, earlier, after, piece):
    partner, place_in = partner
    local_pairs = phases.shape[0]
    _, blocks, away, _ = layout
    coded_shape = (coded_rows(piece), LANES)
    in_specs = [
        pl.BlockSpec(pairs.shape, lambda i, t, c: (0, 0)),
        pl.BlockSpec((local_pairs, piece), lambda i, t, c: (0, t[blocks + at])),
        pl.BlockSpec((local_pairs, piece), lambda i, t, c: (0, place_in)),
    ]
    operands = [pairs, phases, partner]
    out_shape = [jax.ShapeDtypeStruct(coded_shape, jnp.int16)]
    out_specs = [pl.BlockSpec(coded_shape, lambda i, t, c: (0, 0))]
    if swap is not None:
        first, count = swap
        wide = piece * count
        in_specs.append(pl.BlockSpec((local_pairs, wide), lambda i, t, c: (0, t[away + first] // count)))
        operands.append(phases)
        out_shape.append(jax.ShapeDtypeStruct((local_pairs, wide), phases.dtype))
        out_specs.append(pl.BlockSpec((local_pairs, wide), lambda i, t, c: (0, 0)))
    if earlier is not None:
        in_specs.append(pl.BlockSpec(coded_shape, lambda i, t, c: (0, 0)))
        operands.append(earlier)
    if at in MEETINGS:
        out_shape.append(jax.ShapeDtypeStruct((8, LANES), F32))
        out_specs.append(pl.BlockSpec((8, LANES), lambda i, t, c: (0, 0)))
    in_specs += [pl.BlockSpec(memory_space=pl.ANY)] * len(after)
    results = pl.pallas_call(
        functools.partial(step_kernel, at, layout, earlier is not None, swap is not None, at in MEETINGS, HALVES),
        out_shape=out_shape,
        grid_spec=pltpu.PrefetchScalarGridSpec(
            num_scalar_prefetch=2,
            grid=(1,),
            in_specs=in_specs,
            out_specs=out_specs,
        ),
        compiler_params=pltpu.CompilerParams(vmem_limit_bytes=VMEM_BYTES),
        cost_estimate=STEADY,
        name=f"sum_step_{at:02d}",
    )(*scalars, *operands, *after)
    return results[0], results[1] if swap is not None else None, results[-1] if at in MEETINGS else None


def coded_specs(piece, tiles, index):
    lots = piece // LANES
    return [
        pl.BlockSpec((lots // tiles * M, LANES), lambda *at: (at[index], 0)),
        pl.BlockSpec((CODE_ROWS, LANES), lambda *at: (lots * M // CODE_ROWS, 0)),
    ]


def add_arrived(sums_ref, refs, tiles):
    lots = sums_ref.shape[1] // LANES
    tile = pl.program_id(0)
    for coded_ref, codes_ref in zip(refs[::2], refs[1::2]):
        parts = [decode(coded_ref, codes_ref, lots, at * lots) for at in range(tiles)]
        scale = functools.reduce(lambda chosen, at: jnp.where(tile == at, parts[at][1], chosen), range(1, tiles), parts[0][1])
        sums_ref[...] += parts[0][0] * scale


def finish_kernel(at, layout, tiles, table, counts, pairs_ref, own_ref, partner_ref, inverse_ref, *rest):
    first, middle, last = rest[:2], rest[2:4], rest[4:6]
    out_ref, sums_ref = rest[-2:]
    sums_ref[...] = pair_sums(piece_count(at, layout, table, counts), table, pairs_ref, own_ref, partner_ref)

    @pl.when(table[INNER] == 0)
    def _():
        add_arrived(sums_ref, first, tiles)

    @pl.when(table[INNER] == 1)
    def _():
        add_arrived(sums_ref, middle, tiles)

    add_arrived(sums_ref, last, tiles)
    out_ref[...] = split_product(inverse_ref[0, :M, :M], sums_ref[...])


def finish(at, part, layout, scalars, pairs, phases, partner, inverse, arrived, series, pixels, piece):
    partner, place_in = partner
    local_pairs = phases.shape[0]
    blocks = layout[1]
    tiles = HALVES
    tile = piece // tiles
    in_specs = [
        pl.BlockSpec(pairs.shape, lambda i, t, c: (0, 0)),
        pl.BlockSpec((local_pairs, tile), lambda i, t, c: (0, t[blocks + at] * tiles + i)),
        pl.BlockSpec((local_pairs, tile), lambda i, t, c: (0, place_in * tiles + i)),
        pl.BlockSpec((1, PAD, PAD), lambda i, t, c: (part // CUTS, 0, 0)),
    ] + coded_specs(piece, tiles, 0) * len(arrived)
    operands = [*scalars, pairs, phases, partner, inverse] + [each for each in arrived for _ in range(2)]
    aliases = {}
    if series is not None:
        in_specs.append(pl.BlockSpec(memory_space=pl.ANY))
        aliases = {len(operands): 0}
        operands.append(series)
    return pl.pallas_call(
        functools.partial(finish_kernel, at, layout, tiles),
        out_shape=jax.ShapeDtypeStruct((M, pixels), F32),
        grid_spec=pltpu.PrefetchScalarGridSpec(
            num_scalar_prefetch=2,
            grid=(tiles,),
            in_specs=in_specs,
            out_specs=pl.BlockSpec((M, tile), lambda i, t, c: (0, part * tiles + i)),
            scratch_shapes=[pltpu.VMEM((M, tile), F32)],
        ),
        input_output_aliases=aliases,
        compiler_params=pltpu.CompilerParams(vmem_limit_bytes=VMEM_BYTES),
        cost_estimate=LITTLE,
        name=f"finish_{part}",
    )(*operands)


def line_permutation(links):
    return [(2 * source + side, 2 * target + side) for source, target in links for side in range(2)]


def solve_by_sums(phases, date_pairs, counts_of):
    owner_count = lax.axis_size("ifg")
    line = owner_count // 2
    local_pairs, pixels = phases.shape
    owner_pixels = pixels // owner_count
    runs = counts_of().shape[0]
    parts = runs * CUTS
    piece = owner_pixels // parts
    steps = (line - 1) * parts
    me = lax.axis_index("ifg")

    places = np.repeat(np.array(CHUNK_ORDER), parts, axis=1)
    part_of = np.tile(np.arange(parts), line)
    rows = []
    for device in range(owner_count):
        place, side = device // 2, device % 2
        own = (places[place] * 2 + side) * parts + part_of
        away = (places[place] * 2 + 1 - side) * parts + part_of
        known = [place, line - 1 - place, place ^ 1, line - 1 - (place ^ 1)]
        shift = np.array([known.index(chunk) for chunk in places[place]])
        rows.append(np.concatenate([[device, device ^ 1, int(0 < place < line - 1)], own, away, shift]))
    row = lax.dynamic_index_in_dim(jnp.asarray(np.stack(rows), jnp.int32), me, 0, keepdims=False)
    head, pieces = FIXED, line * parts
    layout = (parts, head, head + pieces, head + 2 * pieces)

    swap = [(i, i ^ 1) for i in range(owner_count)]
    partner_of = {}

    def swapped(away, first, count):
        here = lax.ppermute(away, "ifg", swap)
        partner_of.update({first + place: (here, place) for place in range(count)})

    place, side = me // 2, me % 2
    run_counts = counts_of()
    mirrored = lax.ppermute(run_counts, "ifg", line_permutation([(i, line - 1 - i) for i in range(line)]))
    first, count = FIRST_SWAPS[0]
    chunk, _ = lax.optimization_barrier((jnp.where(place < line // 2, 2 - 2 * place, 7 - 2 * place), run_counts))
    away = lax.dynamic_slice(phases, (0, ((chunk * 2 + 1 - side) * parts + first) * piece), (local_pairs, piece * count))
    swapped(away, first, count)
    both = jnp.concatenate([run_counts, mirrored])
    counts = jnp.concatenate([both, lax.ppermute(both, "ifg", line_permutation([(i, i ^ 1) for i in range(line)]))])
    swapped(give_out(FIRST_SWAPS[1], layout, row, phases, mirrored, piece), *FIRST_SWAPS[1])
    pairs = jnp.concatenate([lax.dynamic_slice(date_pairs, (0, row[at] * local_pairs), (2, local_pairs)) for at in (ME, PARTNER)], axis=1)
    scalars = (row, counts)

    received, coded, series = [], None, None

    def finished(part, series):
        at = steps + part
        arrived = [received[place * parts + part][-1] for place in range(line - 1)]
        return finish(at, part, layout, scalars, pairs, phases, partner_of[at], inverse, arrived, series, owner_pixels, piece)

    for at in range(steps):
        earlier = received[at - parts][0] if at >= parts else None
        after = [coded] if at else []
        after += received[at - FLIGHT] if at >= FLIGHT else []
        if at - 1 in MEETINGS:
            after.append(met)
        if at in SWAP_WAITS:
            after.append(partner_of[SWAP_WAITS[at]][0])
        if at == INVERSE_STEP:
            inverse = invert_classes(date_pairs, run_counts, [coded])
            after.append(inverse)
        if at == steps - 1:
            for part in range(FINISHED_AHEAD):
                series = finished(part, series)
                after.append(series)
        coded, away, told = step(at, SWAPS.get(at), layout, scalars, pairs, phases, partner_of[at], earlier, after, piece)
        received.append([lax.ppermute(coded, "ifg", line_permutation(links)) for links in SENDS[at // parts]])
        if at in SWAPS:
            swapped(away, *SWAPS[at])
        if at in MEETINGS:
            met = lax.ppermute(told, "grp", [(i, i ^ 1) for i in range(lax.axis_size("grp"))])
        if at == 0:
            swapped(give_out(FIRST_SWAPS[2], layout, row, phases, coded, piece), *FIRST_SWAPS[2])

    for part in range(FINISHED_AHEAD, parts):
        series = finished(part, series)
    return series


def solve_by_blocks(phases, date_pairs, counts_of):
    owner_count = lax.axis_size("ifg")
    local_pairs, pixels = phases.shape
    owner_pixels = pixels // owner_count
    run_counts = counts_of()
    outgoing = phases.reshape(local_pairs, owner_count, owner_pixels).transpose(1, 0, 2)
    received = lax.all_to_all(outgoing, "ifg", split_axis=0, concat_axis=0, tiled=True)
    inverse = invert_classes(date_pairs, run_counts, [])
    return sum_solve(run_counts, date_pairs, received.reshape(-1, owner_pixels), inverse)


def local(phases, date_pairs, pair_counts, group_ids):
    local_pairs, _, pixels = phases.shape

    def counts_of():
        strip_groups = lax.dynamic_index_in_dim(group_ids, lax.axis_index("grp"), 0, keepdims=False)[::RUN]
        chosen = strip_groups[:, None] == jnp.arange(pair_counts.shape[0], dtype=jnp.int32)
        return jnp.sum(jnp.where(chosen, pair_counts, 0), axis=1)

    line = lax.axis_size("ifg") == 2 * len(CHUNK_ORDER) and group_ids.shape[1] == 2 * RUN
    by_sums = line and 2 * local_pairs > M and local_pairs % LANES == 0 and lax.axis_size("grp") % 2 == 0
    solve = solve_by_sums if by_sums else solve_by_blocks
    return solve(phases.reshape(local_pairs, pixels), date_pairs, counts_of)[None, :, :]


def solution(mesh):
    in_specs = (P("ifg", "grp", None), P(), P(), P(None, "ifg"))
    out_specs = P("grp", None, "ifg")
    return jax.shard_map(local, mesh=mesh, in_specs=in_specs, out_specs=out_specs, check_vma=False)
```

```python
import functools

import jax
import jax.numpy as jnp
import numpy as np
from jax import lax
from jax.experimental import pallas as pl
from jax.experimental.pallas import tpu as pltpu
from jax.sharding import PartitionSpec as P

M = 200
RUN = 8
PAD = 256
SLABS = 8
DAMPING = 1.0
VMEM_BYTES = 48 * 1024 * 1024
F32 = jnp.float32
HIGHEST = lax.Precision.HIGHEST
STEADY = pl.CostEstimate(flops=10_000_000_000, bytes_accessed=30_000_000, transcendentals=0)
LITTLE = pl.CostEstimate(flops=1024, bytes_accessed=1024, transcendentals=0)
CUTS = 2
HALVES = 2
FLIGHT = 2
FIRST_SWAPS = ((1, 1), (2, 2))
SWAPS = {2: (4, 2), 3: (6, 2), 5: (8, 4), 8: (12, 2), 9: (14, 2)}
SWAP_WAITS = {5: 6, 10: 12}
INVERSE_STEP = 2
FINISHED_AHEAD = 1
ME, PARTNER, NEAR, NEAR_PARTNER, INNER, FIXED = 0, 1, 2, 3, 4, 5
LANES = 128
CODE_ROWS = 16
LEVELS = 32700.0
ROUNDER = 1.5 * 2.0**23
CODES_PER_OCTAVE = 128.0
SMALLEST = 2.0**-110
CHUNK_ORDER = ((2, 3, 1, 0), (0, 2, 3, 1), (3, 1, 0, 2), (1, 0, 2, 3))
SENDS = (
    (((0, 1), (1, 0), (2, 3), (3, 2)),),
    (((0, 1), (3, 2)), ((1, 2), (2, 1))),
    (((0, 1), (1, 3), (2, 0), (3, 2)),),
)


def incidence(earlier, later, rows):
    shape = (rows, earlier.shape[1])
    date = lax.broadcasted_iota(jnp.int32, shape, 0)
    return (date == later).astype(F32) - (date == earlier).astype(F32)


def split_product(left, right):
    def halves(value):
        high = value.astype(jnp.bfloat16)
        return high, (value - high.astype(F32)).astype(jnp.bfloat16)

    left_high, left_low = halves(left)
    right_high, right_low = halves(right)
    small = jnp.dot(left_high, right_low, preferred_element_type=F32) + jnp.dot(left_low, right_high, preferred_element_type=F32)
    return jnp.dot(left_high, right_high, preferred_element_type=F32) + small


def full_product(left, right):
    return jnp.dot(left, right, precision=HIGHEST, preferred_element_type=F32)


def inverse_kernel(counts_ref, pairs_ref, *rest):
    out_ref = rest[-1]
    runs = out_ref.shape[0]
    design = incidence(pairs_ref[0:1, :], pairs_ref[1:2, :], PAD)
    pair = lax.broadcasted_iota(jnp.int32, design.shape, 1)
    contract_last = (((1,), (1,)), ((), ()))
    row = lax.broadcasted_iota(jnp.int32, (PAD, PAD), 0)
    col = lax.broadcasted_iota(jnp.int32, (PAD, PAD), 1)
    identity = (row == col).astype(F32)
    grams = []
    for run in range(runs):
        kept = jnp.where(pair < counts_ref[run], design, 0.0).astype(jnp.bfloat16)
        gram = lax.dot_general(kept, kept, contract_last, preferred_element_type=F32)
        grams.append(gram + DAMPING * identity)
    low = DAMPING
    high = 2.0 * functools.reduce(jnp.maximum, [jnp.max(gram) for gram in grams]) - DAMPING
    total, width = high + low, high - low
    scale = 2.0 * total * total - width * width
    starts = tuple((8.0 * total / scale) * identity - (8.0 / scale) * gram for gram in grams)
    needed = 18.0 * scale / (8.0 * high * low)
    steps = jnp.int32(0)
    for power in range(1, 16):
        steps += (needed > float(2**power)).astype(jnp.int32)

    def newton(product, guesses):
        products = [product(gram, guess) for gram, guess in zip(grams, guesses)]
        return tuple(2.0 * guess - product(guess, each) for guess, each in zip(guesses, products))

    full_steps = 1 + (high > 100.0).astype(jnp.int32)
    guesses = lax.fori_loop(0, steps + 1 - full_steps, lambda _, guesses: newton(split_product, guesses), starts)
    guesses = lax.fori_loop(0, full_steps, lambda _, guesses: newton(full_product, guesses), guesses)
    for run, guess in enumerate(guesses):
        out_ref[run] = guess


def invert_classes(date_pairs, run_counts, after):
    shape = (run_counts.shape[0], PAD, PAD)
    return pl.pallas_call(
        inverse_kernel,
        out_shape=jax.ShapeDtypeStruct(shape, F32),
        grid_spec=pltpu.PrefetchScalarGridSpec(
            num_scalar_prefetch=1,
            grid=(1,),
            in_specs=[pl.BlockSpec(date_pairs.shape, lambda i, c: (0, 0))] + [pl.BlockSpec(memory_space=pl.ANY)] * len(after),
            out_specs=pl.BlockSpec(shape, lambda i, c: (0, 0, 0)),
        ),
        compiler_params=pltpu.CompilerParams(vmem_limit_bytes=VMEM_BYTES),
        cost_estimate=LITTLE,
        name="invert_classes_0",
    )(run_counts, date_pairs, *after)


def sum_solve_kernel(tiles, counts_ref, pairs_ref, data_ref, inverse_ref, out_ref):
    run = pl.program_id(0) // tiles
    design = incidence(pairs_ref[0:1, :], pairs_ref[1:2, :], PAD)
    pair = lax.broadcasted_iota(jnp.int32, design.shape, 1)
    kept = jnp.where(pair < counts_ref[run], design, 0.0).astype(jnp.bfloat16)
    sums = jnp.dot(kept, data_ref[...], preferred_element_type=F32)
    out_ref[...] = jnp.dot(inverse_ref[0, :M, :], sums, precision=HIGHEST, preferred_element_type=F32)


def sum_solve(run_counts, date_pairs, received, inverse):
    runs = run_counts.shape[0]
    total_pairs, pixels = received.shape
    run_pixels = pixels // runs
    tile = run_pixels // 2
    tiles = run_pixels // tile
    return pl.pallas_call(
        functools.partial(sum_solve_kernel, tiles),
        out_shape=jax.ShapeDtypeStruct((M, pixels), F32),
        grid_spec=pltpu.PrefetchScalarGridSpec(
            num_scalar_prefetch=1,
            grid=(runs * tiles,),
            in_specs=[
                pl.BlockSpec(date_pairs.shape, lambda i, c: (0, 0)),
                pl.BlockSpec((total_pairs, tile), lambda i, c: (0, i)),
                pl.BlockSpec((1, PAD, PAD), lambda i, c: (i // tiles, 0, 0)),
            ],
            out_specs=pl.BlockSpec((M, tile), lambda i, c: (0, i)),
        ),
        compiler_params=pltpu.CompilerParams(vmem_limit_bytes=VMEM_BYTES),
        name="sum_solve",
    )(run_counts, date_pairs, received, inverse)


def coded_rows(piece):
    return M * (piece // LANES) + CODE_ROWS


def decode(coded_ref, codes_ref, lots, first):
    coded = coded_ref[...].astype(jnp.int32).astype(F32)
    values = jnp.concatenate([coded[lot * M : (lot + 1) * M, :] for lot in range(lots)], axis=1)
    codes = codes_ref[...].astype(jnp.int32).astype(F32)
    codes = jnp.concatenate([codes[first + lot : first + lot + 1, :] for lot in range(lots)], axis=1)
    return values, jnp.exp2(codes * (1.0 / CODES_PER_OCTAVE)) * (1.0 / LEVELS)


def encode(sums):
    largest = jnp.max(jnp.abs(sums), axis=0, keepdims=True)
    code = jnp.ceil(jnp.log2(jnp.maximum(largest, SMALLEST)) * CODES_PER_OCTAVE)
    scaled = (sums * (LEVELS / jnp.exp2(code * (1.0 / CODES_PER_OCTAVE))) + ROUNDER) - ROUNDER
    lots = sums.shape[1] // LANES
    return jnp.concatenate([scaled[:, lot * LANES : (lot + 1) * LANES] for lot in range(lots)], axis=0), code


def whole(values):
    return values.astype(jnp.int32).astype(jnp.int16)


def piece_count(at, layout, table, counts):
    parts, _, _, shifts = layout
    run = at % parts // CUTS
    return counts[table[shifts + at] * (parts // CUTS) + run]


def pair_sums(count, table, pairs_ref, first_ref, second_ref, members=(ME, PARTNER)):
    width = first_ref.shape[0]
    lane = lax.broadcasted_iota(jnp.int32, (1, 2 * width), 1)
    pair = jnp.where(lane < width, table[members[0]] * width + lane, table[members[1]] * width + lane - width)
    dates = pairs_ref[:, members[0] * width : (members[0] + 2) * width]
    design = incidence(dates[0:1, :], dates[1:2, :], M)
    kept = jnp.where(pair < count, design, 0.0).astype(jnp.bfloat16)
    data = jnp.concatenate([first_ref[...], second_ref[...]], axis=0)
    return jnp.dot(kept, data, preferred_element_type=F32)


def near_sums(wanted, count, table, pairs_ref, raw_refs):
    return pair_sums(jnp.where(wanted, count, 0), table, pairs_ref, *raw_refs, members=(NEAR, NEAR_PARTNER))


def copy_kernel(table, source_ref, _, target_ref):
    target_ref[...] = source_ref[...]


def give_out(swap, layout, table, phases, after, piece):
    first, count = swap
    away = layout[2]
    shape = (phases.shape[0], piece * count)
    return pl.pallas_call(
        copy_kernel,
        out_shape=jax.ShapeDtypeStruct(shape, phases.dtype),
        grid_spec=pltpu.PrefetchScalarGridSpec(
            num_scalar_prefetch=1,
            grid=(1,),
            in_specs=[
                pl.BlockSpec(shape, lambda i, t: (0, t[away + first] // count)),
                pl.BlockSpec(memory_space=pl.ANY),
            ],
            out_specs=pl.BlockSpec(shape, lambda i, t: (0, 0)),
        ),
        compiler_params=pltpu.CompilerParams(vmem_limit_bytes=VMEM_BYTES),
        cost_estimate=LITTLE,
        name="give_out",
    )(table, phases, after)


def step_kernel(at, layout, adds, swaps, halves, table, counts, pairs_ref, own_ref, partner_ref, *rest):
    if swaps:
        rest[-1][...] = rest[0][...]
        coded_ref, rest = rest[-2], rest[1:]
    else:
        coded_ref = rest[-1]
    count = piece_count(at, layout, table, counts)
    width = own_ref.shape[1] // halves
    lots = width // LANES
    codes = []
    for half in range(halves):
        part = pl.ds(half * width, width)
        sums = pair_sums(count, table, pairs_ref, own_ref.at[:, part], partner_ref.at[:, part])
        if adds == 1:
            rows = pl.ds(half * lots * M, lots * M)
            values, scale = decode(rest[0].at[rows, :], rest[0].at[halves * lots * M :, :], lots, half * lots)
            sums = sums + values * (scale * table[INNER].astype(F32))
        if adds == 2:
            sums = sums + near_sums(table[INNER] == 1, count, table, pairs_ref, [raw_ref.at[:, part] for raw_ref in rest[:2]])
        scaled, code = encode(sums)
        coded_ref[half * lots * M : (half + 1) * lots * M, :] = whole(scaled)
        codes += [code[:, lot * LANES : (lot + 1) * LANES] for lot in range(lots)]
    codes += [jnp.zeros((CODE_ROWS - len(codes), LANES), F32)]
    coded_ref[halves * lots * M :, :] = whole(jnp.concatenate(codes, axis=0))


def step(at, swap, layout, scalars, pairs, phases, partner, earlier, after, piece):
    partner, place_in = partner
    local_pairs = phases.shape[0]
    _, blocks, away, _ = layout
    coded_shape = (coded_rows(piece), LANES)
    in_specs = [
        pl.BlockSpec(pairs.shape, lambda i, t, c: (0, 0)),
        pl.BlockSpec((local_pairs, piece), lambda i, t, c: (0, t[blocks + at])),
        pl.BlockSpec((local_pairs, piece), lambda i, t, c: (0, place_in)),
    ]
    operands = [pairs, phases, partner]
    out_shape = [jax.ShapeDtypeStruct(coded_shape, jnp.int16)]
    out_specs = [pl.BlockSpec(coded_shape, lambda i, t, c: (0, 0))]
    if swap is not None:
        first, count = swap
        wide = piece * count
        in_specs.append(pl.BlockSpec((local_pairs, wide), lambda i, t, c: (0, t[away + first] // count)))
        operands.append(phases)
        out_shape.append(jax.ShapeDtypeStruct((local_pairs, wide), phases.dtype))
        out_specs.append(pl.BlockSpec((local_pairs, wide), lambda i, t, c: (0, 0)))
    in_specs += [pl.BlockSpec(each.shape, lambda i, t, c: (0, 0)) for each in earlier]
    operands += earlier
    in_specs += [pl.BlockSpec(memory_space=pl.ANY)] * len(after)
    results = pl.pallas_call(
        functools.partial(step_kernel, at, layout, len(earlier), swap is not None, HALVES),
        out_shape=out_shape,
        grid_spec=pltpu.PrefetchScalarGridSpec(
            num_scalar_prefetch=2,
            grid=(1,),
            in_specs=in_specs,
            out_specs=out_specs,
        ),
        compiler_params=pltpu.CompilerParams(vmem_limit_bytes=VMEM_BYTES),
        cost_estimate=STEADY,
        name=f"sum_step_{at:02d}",
    )(*scalars, *operands, *after)
    return results[0], results[1] if swap is not None else None


def coded_specs(piece, tiles, index):
    lots = piece // LANES
    return [
        pl.BlockSpec((lots // tiles * M, LANES), lambda *at: (at[index], 0)),
        pl.BlockSpec((CODE_ROWS, LANES), lambda *at: (lots * M // CODE_ROWS, 0)),
    ]


def add_arrived(sums_ref, refs, tiles):
    lots = sums_ref.shape[1] // LANES
    tile = pl.program_id(0)
    for coded_ref, codes_ref in zip(refs[::2], refs[1::2]):
        parts = [decode(coded_ref, codes_ref, lots, at * lots) for at in range(tiles)]
        scale = functools.reduce(lambda chosen, at: jnp.where(tile == at, parts[at][1], chosen), range(1, tiles), parts[0][1])
        sums_ref[...] += parts[0][0] * scale


def finish_kernel(at, layout, tiles, raw, told, table, counts, pairs_ref, own_ref, partner_ref, inverse_ref, *rest):
    first, middle, last = rest[:2], rest[2:4], rest[4:6]
    sums_ref, rest = rest[-1], rest[:-1]
    if told:
        rest[-1][...] = jnp.zeros_like(rest[-1])
        rest = rest[:-1]
    out_ref = rest[-1]
    count = piece_count(at, layout, table, counts)
    sums_ref[...] = pair_sums(count, table, pairs_ref, own_ref, partner_ref)

    @pl.when(table[INNER] == 0)
    def _():
        if raw:
            sums_ref[...] += near_sums(True, count, table, pairs_ref, first)
        else:
            add_arrived(sums_ref, first, tiles)

    @pl.when(table[INNER] == 1)
    def _():
        add_arrived(sums_ref, middle, tiles)

    add_arrived(sums_ref, last, tiles)
    out_ref[...] = split_product(inverse_ref[0, :M, :M], sums_ref[...])


def finish(at, part, layout, scalars, pairs, phases, partner, inverse, raw, arrived, series, told, pixels, piece):
    partner, place_in = partner
    local_pairs = phases.shape[0]
    blocks = layout[1]
    tiles = HALVES
    tile = piece // tiles
    in_specs = [
        pl.BlockSpec(pairs.shape, lambda i, t, c: (0, 0)),
        pl.BlockSpec((local_pairs, tile), lambda i, t, c: (0, t[blocks + at] * tiles + i)),
        pl.BlockSpec((local_pairs, tile), lambda i, t, c: (0, place_in * tiles + i)),
        pl.BlockSpec((1, PAD, PAD), lambda i, t, c: (part // CUTS, 0, 0)),
    ]
    in_specs += [pl.BlockSpec((local_pairs, tile), lambda i, t, c: (0, i))] * len(raw) + coded_specs(piece, tiles, 0) * len(arrived)
    operands = [*scalars, pairs, phases, partner, inverse, *raw] + [each for each in arrived for _ in range(2)]
    aliases = {}
    if series is not None:
        in_specs.append(pl.BlockSpec(memory_space=pl.ANY))
        aliases = {len(operands): 0}
        operands.append(series)
    out_shape = [jax.ShapeDtypeStruct((M, pixels), F32)]
    out_specs = [pl.BlockSpec((M, tile), lambda i, t, c: (0, part * tiles + i))]
    if told:
        out_shape.append(jax.ShapeDtypeStruct((8, LANES), F32))
        out_specs.append(pl.BlockSpec((8, LANES), lambda i, t, c: (0, 0)))
    return pl.pallas_call(
        functools.partial(finish_kernel, at, layout, tiles, len(raw) > 0, told),
        out_shape=out_shape,
        grid_spec=pltpu.PrefetchScalarGridSpec(
            num_scalar_prefetch=2,
            grid=(tiles,),
            in_specs=in_specs,
            out_specs=out_specs,
            scratch_shapes=[pltpu.VMEM((M, tile), F32)],
        ),
        input_output_aliases=aliases,
        compiler_params=pltpu.CompilerParams(vmem_limit_bytes=VMEM_BYTES),
        cost_estimate=LITTLE,
        name=f"finish_{part}",
    )(*operands)


def line_permutation(links):
    return [(2 * source + side, 2 * target + side) for source, target in links for side in range(2)]


def solve_by_sums(phases, date_pairs, counts_of):
    owner_count = lax.axis_size("ifg")
    line = owner_count // 2
    local_pairs, pixels = phases.shape
    owner_pixels = pixels // owner_count
    runs = counts_of().shape[0]
    parts = runs * CUTS
    piece = owner_pixels // parts
    steps = (line - 1) * parts
    me = lax.axis_index("ifg")

    places = np.repeat(np.array(CHUNK_ORDER), parts, axis=1)
    part_of = np.tile(np.arange(parts), line)
    rows = []
    for device in range(owner_count):
        place, side = device // 2, device % 2
        own = (places[place] * 2 + side) * parts + part_of
        away = (places[place] * 2 + 1 - side) * parts + part_of
        known = [place, line - 1 - place, place ^ 1, line - 1 - (place ^ 1)]
        shift = np.array([known.index(chunk) for chunk in places[place]])
        rows.append(np.concatenate([[device, device ^ 1, device ^ 2, device ^ 3, int(0 < place < line - 1)], own, away, shift]))
    row = lax.dynamic_index_in_dim(jnp.asarray(np.stack(rows), jnp.int32), me, 0, keepdims=False)
    head, pieces = FIXED, line * parts
    layout = (parts, head, head + pieces, head + 2 * pieces)

    swap = [(i, i ^ 1) for i in range(owner_count)]
    partner_of = {}

    def swapped(away, first, count):
        here = lax.ppermute(away, "ifg", swap)
        partner_of.update({first + place: (here, place) for place in range(count)})

    place, side = me // 2, me % 2
    chunk = jnp.where(place < line // 2, 2 - 2 * place, 7 - 2 * place)

    def first_away(column, part, after):
        block = (chunk * 2 + column) * parts + part
        if after is not None:
            block, _ = lax.optimization_barrier((block, after))
        return lax.dynamic_slice(phases, (0, block * piece), (local_pairs, piece))

    near = line_permutation(SENDS[0][0])
    raw_other = lax.ppermute(first_away(1 - side, 0, None), "ifg", near)
    raw_own = lax.ppermute(first_away(side, 0, None), "ifg", near)
    run_counts = counts_of()
    mirrored = lax.ppermute(run_counts, "ifg", line_permutation([(i, line - 1 - i) for i in range(line)]))
    swapped(first_away(1 - side, FIRST_SWAPS[0][0], run_counts), *FIRST_SWAPS[0])
    both = jnp.concatenate([run_counts, mirrored])
    counts = jnp.concatenate([both, lax.ppermute(both, "ifg", line_permutation([(i, i ^ 1) for i in range(line)]))])
    swapped(give_out(FIRST_SWAPS[1], layout, row, phases, mirrored, piece), *FIRST_SWAPS[1])
    raw = [raw_own, lax.ppermute(raw_other, "ifg", swap)]
    pairs = jnp.concatenate([lax.dynamic_slice(date_pairs, (0, row[at] * local_pairs), (2, local_pairs)) for at in (ME, PARTNER, NEAR, NEAR_PARTNER)], axis=1)
    scalars = (row, counts)

    received, coded, series = [[raw_own, raw_other]], None, None

    def finished(part, series, told):
        at = steps + part
        arrived = [received[place * parts + part][-1] for place in range(1 if part == 0 else 0, line - 1)]
        data = (layout, scalars, pairs, phases, partner_of[at], inverse, raw if part == 0 else [], arrived)
        return finish(at, part, *data, series, told, owner_pixels, piece)

    for at in range(1, steps):
        earlier = [] if at < parts else raw if at == parts else [received[at - parts][0]]
        after = [coded] if at > 1 else []
        after += received[at - FLIGHT] if at >= FLIGHT else []
        if at in SWAP_WAITS:
            after.append(partner_of[SWAP_WAITS[at]][0])
        if at == INVERSE_STEP:
            inverse = invert_classes(date_pairs, run_counts, [coded])
            after.append(inverse)
        if at == steps - 1:
            for part in range(FINISHED_AHEAD):
                series, told = finished(part, series, True)
                after.append(told)
        coded, away = step(at, SWAPS.get(at), layout, scalars, pairs, phases, partner_of[at], earlier, after, piece)
        received.append([lax.ppermute(coded, "ifg", line_permutation(links)) for links in SENDS[at // parts]])
        if at in SWAPS:
            swapped(away, *SWAPS[at])

    for part in range(FINISHED_AHEAD, parts):
        series = finished(part, series, False)[0]
    return series


def solve_by_blocks(phases, date_pairs, counts_of):
    owner_count = lax.axis_size("ifg")
    local_pairs, pixels = phases.shape
    owner_pixels = pixels // owner_count
    run_counts = counts_of()
    outgoing = phases.reshape(local_pairs, owner_count, owner_pixels).transpose(1, 0, 2)
    received = lax.all_to_all(outgoing, "ifg", split_axis=0, concat_axis=0, tiled=True)
    inverse = invert_classes(date_pairs, run_counts, [])
    return sum_solve(run_counts, date_pairs, received.reshape(-1, owner_pixels), inverse)


def local(phases, date_pairs, pair_counts, group_ids):
    local_pairs, _, pixels = phases.shape

    def counts_of():
        strip_groups = lax.dynamic_index_in_dim(group_ids, lax.axis_index("grp"), 0, keepdims=False)[::RUN]
        chosen = strip_groups[:, None] == jnp.arange(pair_counts.shape[0], dtype=jnp.int32)
        return jnp.sum(jnp.where(chosen, pair_counts, 0), axis=1)

    line = lax.axis_size("ifg") == 2 * len(CHUNK_ORDER) and group_ids.shape[1] == 2 * RUN
    by_sums = line and 2 * local_pairs > M and local_pairs % LANES == 0 and lax.axis_size("grp") % 2 == 0
    solve = solve_by_sums if by_sums else solve_by_blocks
    return solve(phases.reshape(local_pairs, pixels), date_pairs, counts_of)[None, :, :]


def solution(mesh):
    in_specs = (P("ifg", "grp", None), P(), P(), P(None, "ifg"))
    out_specs = P("grp", None, "ifg")
    return jax.shard_map(local, mesh=mesh, in_specs=in_specs, out_specs=out_specs, check_vma=False)
```

```python
import functools

import jax
import jax.numpy as jnp
import numpy as np
from jax import lax
from jax.experimental import pallas as pl
from jax.experimental.pallas import tpu as pltpu
from jax.sharding import PartitionSpec as P

M = 200
RUN = 8
PAD = 256
SLABS = 8
DAMPING = 1.0
VMEM_BYTES = 48 * 1024 * 1024
F32 = jnp.float32
HIGHEST = lax.Precision.HIGHEST
STEADY = pl.CostEstimate(flops=10_000_000_000, bytes_accessed=30_000_000, transcendentals=0)
LITTLE = pl.CostEstimate(flops=1024, bytes_accessed=1024, transcendentals=0)
CUTS = 2
HALVES = 2
FLIGHT = 2
FIRST_SWAPS = ((1, 1), (2, 2))
SWAPS = {2: (4, 2), 3: (6, 2), 5: (8, 4), 8: (12, 2), 9: (14, 2)}
SWAP_WAITS = {5: 6, 10: 12}
RAW_STEP = 2
INVERSE_STEP = 2
FINISHED_AHEAD = 1
ME, PARTNER, NEAR, NEAR_PARTNER, INNER, FIXED = 0, 1, 2, 3, 4, 5
LANES = 128
CODE_ROWS = 16
LEVELS = 32700.0
ROUNDER = 1.5 * 2.0**23
CODES_PER_OCTAVE = 128.0
SMALLEST = 2.0**-110
CHUNK_ORDER = ((2, 3, 1, 0), (0, 2, 3, 1), (3, 1, 0, 2), (1, 0, 2, 3))
SENDS = (
    (((0, 1), (1, 0), (2, 3), (3, 2)),),
    (((0, 1), (3, 2)), ((1, 2), (2, 1))),
    (((0, 1), (1, 3), (2, 0), (3, 2)),),
)


def incidence(earlier, later, rows):
    shape = (rows, earlier.shape[1])
    date = lax.broadcasted_iota(jnp.int32, shape, 0)
    return (date == later).astype(F32) - (date == earlier).astype(F32)


def split_product(left, right):
    def halves(value):
        high = value.astype(jnp.bfloat16)
        return high, (value - high.astype(F32)).astype(jnp.bfloat16)

    left_high, left_low = halves(left)
    right_high, right_low = halves(right)
    small = jnp.dot(left_high, right_low, preferred_element_type=F32) + jnp.dot(left_low, right_high, preferred_element_type=F32)
    return jnp.dot(left_high, right_high, preferred_element_type=F32) + small


def full_product(left, right):
    return jnp.dot(left, right, precision=HIGHEST, preferred_element_type=F32)


def inverse_kernel(counts_ref, pairs_ref, *rest):
    out_ref = rest[-1]
    runs = out_ref.shape[0]
    design = incidence(pairs_ref[0:1, :], pairs_ref[1:2, :], PAD)
    pair = lax.broadcasted_iota(jnp.int32, design.shape, 1)
    contract_last = (((1,), (1,)), ((), ()))
    row = lax.broadcasted_iota(jnp.int32, (PAD, PAD), 0)
    col = lax.broadcasted_iota(jnp.int32, (PAD, PAD), 1)
    identity = (row == col).astype(F32)
    grams = []
    for run in range(runs):
        kept = jnp.where(pair < counts_ref[run], design, 0.0).astype(jnp.bfloat16)
        gram = lax.dot_general(kept, kept, contract_last, preferred_element_type=F32)
        grams.append(gram + DAMPING * identity)
    low = DAMPING
    high = 2.0 * functools.reduce(jnp.maximum, [jnp.max(gram) for gram in grams]) - DAMPING
    total, width = high + low, high - low
    scale = 2.0 * total * total - width * width
    starts = tuple((8.0 * total / scale) * identity - (8.0 / scale) * gram for gram in grams)
    needed = 18.0 * scale / (8.0 * high * low)
    steps = jnp.int32(0)
    for power in range(1, 16):
        steps += (needed > float(2**power)).astype(jnp.int32)

    def newton(product, guesses):
        products = [product(gram, guess) for gram, guess in zip(grams, guesses)]
        return tuple(2.0 * guess - product(guess, each) for guess, each in zip(guesses, products))

    full_steps = 1 + (high > 100.0).astype(jnp.int32)
    guesses = lax.fori_loop(0, steps + 1 - full_steps, lambda _, guesses: newton(split_product, guesses), starts)
    guesses = lax.fori_loop(0, full_steps, lambda _, guesses: newton(full_product, guesses), guesses)
    for run, guess in enumerate(guesses):
        out_ref[run] = guess


def invert_classes(date_pairs, run_counts, after):
    shape = (run_counts.shape[0], PAD, PAD)
    return pl.pallas_call(
        inverse_kernel,
        out_shape=jax.ShapeDtypeStruct(shape, F32),
        grid_spec=pltpu.PrefetchScalarGridSpec(
            num_scalar_prefetch=1,
            grid=(1,),
            in_specs=[pl.BlockSpec(date_pairs.shape, lambda i, c: (0, 0))] + [pl.BlockSpec(memory_space=pl.ANY)] * len(after),
            out_specs=pl.BlockSpec(shape, lambda i, c: (0, 0, 0)),
        ),
        compiler_params=pltpu.CompilerParams(vmem_limit_bytes=VMEM_BYTES),
        cost_estimate=LITTLE,
        name="invert_classes_0",
    )(run_counts, date_pairs, *after)


def sum_solve_kernel(tiles, counts_ref, pairs_ref, data_ref, inverse_ref, out_ref):
    run = pl.program_id(0) // tiles
    design = incidence(pairs_ref[0:1, :], pairs_ref[1:2, :], PAD)
    pair = lax.broadcasted_iota(jnp.int32, design.shape, 1)
    kept = jnp.where(pair < counts_ref[run], design, 0.0).astype(jnp.bfloat16)
    sums = jnp.dot(kept, data_ref[...], preferred_element_type=F32)
    out_ref[...] = jnp.dot(inverse_ref[0, :M, :], sums, precision=HIGHEST, preferred_element_type=F32)


def sum_solve(run_counts, date_pairs, received, inverse):
    runs = run_counts.shape[0]
    total_pairs, pixels = received.shape
    run_pixels = pixels // runs
    tile = run_pixels // 2
    tiles = run_pixels // tile
    return pl.pallas_call(
        functools.partial(sum_solve_kernel, tiles),
        out_shape=jax.ShapeDtypeStruct((M, pixels), F32),
        grid_spec=pltpu.PrefetchScalarGridSpec(
            num_scalar_prefetch=1,
            grid=(runs * tiles,),
            in_specs=[
                pl.BlockSpec(date_pairs.shape, lambda i, c: (0, 0)),
                pl.BlockSpec((total_pairs, tile), lambda i, c: (0, i)),
                pl.BlockSpec((1, PAD, PAD), lambda i, c: (i // tiles, 0, 0)),
            ],
            out_specs=pl.BlockSpec((M, tile), lambda i, c: (0, i)),
        ),
        compiler_params=pltpu.CompilerParams(vmem_limit_bytes=VMEM_BYTES),
        name="sum_solve",
    )(run_counts, date_pairs, received, inverse)


def coded_rows(piece):
    return M * (piece // LANES) + CODE_ROWS


def decode(coded_ref, codes_ref, lots, first):
    coded = coded_ref[...].astype(jnp.int32).astype(F32)
    values = jnp.concatenate([coded[lot * M : (lot + 1) * M, :] for lot in range(lots)], axis=1)
    codes = codes_ref[...].astype(jnp.int32).astype(F32)
    codes = jnp.concatenate([codes[first + lot : first + lot + 1, :] for lot in range(lots)], axis=1)
    return values, jnp.exp2(codes * (1.0 / CODES_PER_OCTAVE)) * (1.0 / LEVELS)


def encode(sums):
    largest = jnp.max(jnp.abs(sums), axis=0, keepdims=True)
    code = jnp.ceil(jnp.log2(jnp.maximum(largest, SMALLEST)) * CODES_PER_OCTAVE)
    scaled = (sums * (LEVELS / jnp.exp2(code * (1.0 / CODES_PER_OCTAVE))) + ROUNDER) - ROUNDER
    lots = sums.shape[1] // LANES
    return jnp.concatenate([scaled[:, lot * LANES : (lot + 1) * LANES] for lot in range(lots)], axis=0), code


def whole(values):
    return values.astype(jnp.int32).astype(jnp.int16)


def piece_count(at, layout, table, counts):
    parts, _, _, shifts = layout
    run = at % parts // CUTS
    return counts[table[shifts + at] * (parts // CUTS) + run]


def pair_sums(count, table, pairs_ref, first_ref, second_ref, members=(ME, PARTNER)):
    width = first_ref.shape[0]
    lane = lax.broadcasted_iota(jnp.int32, (1, 2 * width), 1)
    pair = jnp.where(lane < width, table[members[0]] * width + lane, table[members[1]] * width + lane - width)
    dates = pairs_ref[:, members[0] * width : (members[0] + 2) * width]
    design = incidence(dates[0:1, :], dates[1:2, :], M)
    kept = jnp.where(pair < count, design, 0.0).astype(jnp.bfloat16)
    data = jnp.concatenate([first_ref[...], second_ref[...]], axis=0)
    return jnp.dot(kept, data, preferred_element_type=F32)


def near_sums(wanted, count, table, pairs_ref, raw_refs):
    return pair_sums(jnp.where(wanted, count, 0), table, pairs_ref, *raw_refs, members=(NEAR, NEAR_PARTNER))


def step_kernel(at, layout, adds, swaps, halves, table, counts, pairs_ref, own_ref, partner_ref, *rest):
    if swaps:
        rest[-1][...] = rest[0][...]
        coded_ref, rest = rest[-2], rest[1:]
    else:
        coded_ref = rest[-1]
    count = piece_count(at, layout, table, counts)
    width = own_ref.shape[1] // halves
    lots = width // LANES
    codes = []
    for half in range(halves):
        part = pl.ds(half * width, width)
        sums = pair_sums(count, table, pairs_ref, own_ref.at[:, part], partner_ref.at[:, part])
        if adds == 1:
            rows = pl.ds(half * lots * M, lots * M)
            values, scale = decode(rest[0].at[rows, :], rest[0].at[halves * lots * M :, :], lots, half * lots)
            sums = sums + values * (scale * table[INNER].astype(F32))
        if adds == 2:
            sums = sums + near_sums(table[INNER] == 1, count, table, pairs_ref, [raw_ref.at[:, part] for raw_ref in rest[:2]])
        scaled, code = encode(sums)
        coded_ref[half * lots * M : (half + 1) * lots * M, :] = whole(scaled)
        codes += [code[:, lot * LANES : (lot + 1) * LANES] for lot in range(lots)]
    codes += [jnp.zeros((CODE_ROWS - len(codes), LANES), F32)]
    coded_ref[halves * lots * M :, :] = whole(jnp.concatenate(codes, axis=0))


def step(at, swap, layout, scalars, pairs, phases, partner, earlier, after, piece):
    partner, place_in = partner
    local_pairs = phases.shape[0]
    _, blocks, away, _ = layout
    coded_shape = (coded_rows(piece), LANES)
    in_specs = [
        pl.BlockSpec(pairs.shape, lambda i, t, c: (0, 0)),
        pl.BlockSpec((local_pairs, piece), lambda i, t, c: (0, t[blocks + at])),
        pl.BlockSpec((local_pairs, piece), lambda i, t, c: (0, place_in)),
    ]
    operands = [pairs, phases, partner]
    out_shape = [jax.ShapeDtypeStruct(coded_shape, jnp.int16)]
    out_specs = [pl.BlockSpec(coded_shape, lambda i, t, c: (0, 0))]
    if swap is not None:
        first, count = swap
        wide = piece * count
        in_specs.append(pl.BlockSpec((local_pairs, wide), lambda i, t, c: (0, t[away + first] // count)))
        operands.append(phases)
        out_shape.append(jax.ShapeDtypeStruct((local_pairs, wide), phases.dtype))
        out_specs.append(pl.BlockSpec((local_pairs, wide), lambda i, t, c: (0, 0)))
    in_specs += [pl.BlockSpec(each.shape, lambda i, t, c: (0, 0)) for each in earlier]
    operands += earlier
    in_specs += [pl.BlockSpec(memory_space=pl.ANY)] * len(after)
    results = pl.pallas_call(
        functools.partial(step_kernel, at, layout, len(earlier), swap is not None, HALVES),
        out_shape=out_shape,
        grid_spec=pltpu.PrefetchScalarGridSpec(
            num_scalar_prefetch=2,
            grid=(1,),
            in_specs=in_specs,
            out_specs=out_specs,
        ),
        compiler_params=pltpu.CompilerParams(vmem_limit_bytes=VMEM_BYTES),
        cost_estimate=STEADY,
        name=f"sum_step_{at:02d}",
    )(*scalars, *operands, *after)
    return results[0], results[1] if swap is not None else None


def coded_specs(piece, tiles, index):
    lots = piece // LANES
    return [
        pl.BlockSpec((lots // tiles * M, LANES), lambda *at: (at[index], 0)),
        pl.BlockSpec((CODE_ROWS, LANES), lambda *at: (lots * M // CODE_ROWS, 0)),
    ]


def add_arrived(sums_ref, refs, tiles):
    lots = sums_ref.shape[1] // LANES
    tile = pl.program_id(0)
    for coded_ref, codes_ref in zip(refs[::2], refs[1::2]):
        parts = [decode(coded_ref, codes_ref, lots, at * lots) for at in range(tiles)]
        scale = functools.reduce(lambda chosen, at: jnp.where(tile == at, parts[at][1], chosen), range(1, tiles), parts[0][1])
        sums_ref[...] += parts[0][0] * scale


def finish_kernel(at, layout, tiles, raw, told, table, counts, pairs_ref, own_ref, partner_ref, inverse_ref, *rest):
    first, middle, last = rest[:2], rest[2:4], rest[4:6]
    sums_ref, rest = rest[-1], rest[:-1]
    if told:
        rest[-1][...] = jnp.zeros_like(rest[-1])
        rest = rest[:-1]
    out_ref = rest[-1]
    count = piece_count(at, layout, table, counts)
    sums_ref[...] = pair_sums(count, table, pairs_ref, own_ref, partner_ref)

    @pl.when(table[INNER] == 0)
    def _():
        if raw:
            sums_ref[...] += near_sums(True, count, table, pairs_ref, first)
        else:
            add_arrived(sums_ref, first, tiles)

    @pl.when(table[INNER] == 1)
    def _():
        add_arrived(sums_ref, middle, tiles)

    add_arrived(sums_ref, last, tiles)
    out_ref[...] = split_product(inverse_ref[0, :M, :M], sums_ref[...])


def finish(at, part, layout, scalars, pairs, phases, partner, inverse, raw, arrived, series, told, pixels, piece):
    partner, place_in = partner
    local_pairs = phases.shape[0]
    blocks = layout[1]
    tiles = HALVES
    tile = piece // tiles
    in_specs = [
        pl.BlockSpec(pairs.shape, lambda i, t, c: (0, 0)),
        pl.BlockSpec((local_pairs, tile), lambda i, t, c: (0, t[blocks + at] * tiles + i)),
        pl.BlockSpec((local_pairs, tile), lambda i, t, c: (0, place_in * tiles + i)),
        pl.BlockSpec((1, PAD, PAD), lambda i, t, c: (part // CUTS, 0, 0)),
    ]
    in_specs += [pl.BlockSpec((local_pairs, tile), lambda i, t, c: (0, i))] * len(raw) + coded_specs(piece, tiles, 0) * len(arrived)
    operands = [*scalars, pairs, phases, partner, inverse, *raw] + [each for each in arrived for _ in range(2)]
    aliases = {}
    if series is not None:
        in_specs.append(pl.BlockSpec(memory_space=pl.ANY))
        aliases = {len(operands): 0}
        operands.append(series)
    out_shape = [jax.ShapeDtypeStruct((M, pixels), F32)]
    out_specs = [pl.BlockSpec((M, tile), lambda i, t, c: (0, part * tiles + i))]
    if told:
        out_shape.append(jax.ShapeDtypeStruct((8, LANES), F32))
        out_specs.append(pl.BlockSpec((8, LANES), lambda i, t, c: (0, 0)))
    return pl.pallas_call(
        functools.partial(finish_kernel, at, layout, tiles, len(raw) > 0, told),
        out_shape=out_shape,
        grid_spec=pltpu.PrefetchScalarGridSpec(
            num_scalar_prefetch=2,
            grid=(tiles,),
            in_specs=in_specs,
            out_specs=out_specs,
            scratch_shapes=[pltpu.VMEM((M, tile), F32)],
        ),
        input_output_aliases=aliases,
        compiler_params=pltpu.CompilerParams(vmem_limit_bytes=VMEM_BYTES),
        cost_estimate=LITTLE,
        name=f"finish_{part}",
    )(*operands)


def line_permutation(links):
    return [(2 * source + side, 2 * target + side) for source, target in links for side in range(2)]


def solve_by_sums(phases, date_pairs, counts_of):
    owner_count = lax.axis_size("ifg")
    line = owner_count // 2
    local_pairs, pixels = phases.shape
    owner_pixels = pixels // owner_count
    runs = counts_of().shape[0]
    parts = runs * CUTS
    piece = owner_pixels // parts
    steps = (line - 1) * parts
    me = lax.axis_index("ifg")

    places = np.repeat(np.array(CHUNK_ORDER), parts, axis=1)
    part_of = np.tile(np.arange(parts), line)
    rows = []
    for device in range(owner_count):
        place, side = device // 2, device % 2
        own = (places[place] * 2 + side) * parts + part_of
        away = (places[place] * 2 + 1 - side) * parts + part_of
        known = [place, line - 1 - place, place ^ 1, line - 1 - (place ^ 1)]
        shift = np.array([known.index(chunk) for chunk in places[place]])
        rows.append(np.concatenate([[device, device ^ 1, device ^ 2, device ^ 3, int(0 < place < line - 1)], own, away, shift]))
    row = lax.dynamic_index_in_dim(jnp.asarray(np.stack(rows), jnp.int32), me, 0, keepdims=False)
    head, pieces = FIXED, line * parts
    layout = (parts, head, head + pieces, head + 2 * pieces)

    swap = [(i, i ^ 1) for i in range(owner_count)]
    partner_of = {}

    def swapped(away, first, count):
        here = lax.ppermute(away, "ifg", swap)
        partner_of.update({first + place: (here, place) for place in range(count)})

    place, side = me // 2, me % 2
    chunk = jnp.where(place < line // 2, 2 - 2 * place, 7 - 2 * place)

    def first_away(column, part, count, after):
        block = (chunk * 2 + column) * parts + part
        if after is not None:
            block, _ = lax.optimization_barrier((block, after))
        return lax.dynamic_slice(phases, (0, block * piece), (local_pairs, count * piece))

    near = line_permutation(SENDS[0][0])
    raw_other = lax.ppermute(first_away(1 - side, 0, 1, None), "ifg", near)
    raw_own = lax.ppermute(first_away(side, 0, 1, None), "ifg", near)
    run_counts = counts_of()
    mirrored = lax.ppermute(run_counts, "ifg", line_permutation([(i, line - 1 - i) for i in range(line)]))
    swapped(first_away(1 - side, *FIRST_SWAPS[0], run_counts), *FIRST_SWAPS[0])
    both = jnp.concatenate([run_counts, mirrored])
    counts = jnp.concatenate([both, lax.ppermute(both, "ifg", line_permutation([(i, i ^ 1) for i in range(line)]))])
    swapped(first_away(1 - side, *FIRST_SWAPS[1], counts), *FIRST_SWAPS[1])
    pairs = jnp.concatenate([lax.dynamic_slice(date_pairs, (0, (me ^ at) * local_pairs), (2, local_pairs)) for at in range(4)], axis=1)
    scalars = (row, counts)

    received, coded, series = [[raw_own, raw_other]], None, None

    def finished(part, series, told):
        at = steps + part
        arrived = [received[place * parts + part][-1] for place in range(1 if part == 0 else 0, line - 1)]
        data = (layout, scalars, pairs, phases, partner_of[at], inverse, raw if part == 0 else [], arrived)
        return finish(at, part, *data, series, told, owner_pixels, piece)

    for at in range(1, steps):
        earlier = [] if at < parts else raw if at == parts else [received[at - parts][0]]
        after = [coded] if at > 1 else []
        after += received[at - FLIGHT] if at >= FLIGHT else []
        if at in SWAP_WAITS:
            after.append(partner_of[SWAP_WAITS[at]][0])
        if at == INVERSE_STEP:
            inverse = invert_classes(date_pairs, run_counts, [coded])
            after.append(inverse)
        if at == steps - 1:
            for part in range(FINISHED_AHEAD):
                series, told = finished(part, series, True)
                after.append(told)
        coded, away = step(at, SWAPS.get(at), layout, scalars, pairs, phases, partner_of[at], earlier, after, piece)
        received.append([lax.ppermute(coded, "ifg", line_permutation(links)) for links in SENDS[at // parts]])
        if at in SWAPS:
            swapped(away, *SWAPS[at])
        if at == RAW_STEP:
            raw_other, _ = lax.optimization_barrier((raw_other, coded))
            raw = [raw_own, lax.ppermute(raw_other, "ifg", swap)]

    for part in range(FINISHED_AHEAD, parts):
        series = finished(part, series, False)[0]
    return series


def solve_by_blocks(phases, date_pairs, counts_of):
    owner_count = lax.axis_size("ifg")
    local_pairs, pixels = phases.shape
    owner_pixels = pixels // owner_count
    run_counts = counts_of()
    outgoing = phases.reshape(local_pairs, owner_count, owner_pixels).transpose(1, 0, 2)
    received = lax.all_to_all(outgoing, "ifg", split_axis=0, concat_axis=0, tiled=True)
    inverse = invert_classes(date_pairs, run_counts, [])
    return sum_solve(run_counts, date_pairs, received.reshape(-1, owner_pixels), inverse)


def local(phases, date_pairs, pair_counts, group_ids):
    local_pairs, _, pixels = phases.shape

    def counts_of():
        strip_groups = lax.dynamic_index_in_dim(group_ids, lax.axis_index("grp"), 0, keepdims=False)[::RUN]
        chosen = strip_groups[:, None] == jnp.arange(pair_counts.shape[0], dtype=jnp.int32)
        return jnp.sum(jnp.where(chosen, pair_counts, 0), axis=1)

    line = lax.axis_size("ifg") == 2 * len(CHUNK_ORDER) and group_ids.shape[1] == 2 * RUN
    by_sums = line and 2 * local_pairs > M and local_pairs % LANES == 0 and lax.axis_size("grp") % 2 == 0
    solve = solve_by_sums if by_sums else solve_by_blocks
    return solve(phases.reshape(local_pairs, pixels), date_pairs, counts_of)[None, :, :]


def solution(mesh):
    in_specs = (P("ifg", "grp", None), P(), P(), P(None, "ifg"))
    out_specs = P("grp", None, "ifg")
    return jax.shard_map(local, mesh=mesh, in_specs=in_specs, out_specs=out_specs, check_vma=False)
```

```python
import functools

import jax
import jax.numpy as jnp
import numpy as np
from jax import lax
from jax.experimental import pallas as pl
from jax.experimental.pallas import tpu as pltpu
from jax.sharding import PartitionSpec as P

M = 200
RUN = 8
PAD = 256
SLABS = 8
DAMPING = 1.0
VMEM_BYTES = 48 * 1024 * 1024
F32 = jnp.float32
HIGHEST = lax.Precision.HIGHEST
STEADY = pl.CostEstimate(flops=10_000_000_000, bytes_accessed=30_000_000, transcendentals=0)
LITTLE = pl.CostEstimate(flops=1024, bytes_accessed=1024, transcendentals=0)
CUTS = 2
HALVES = 2
FLIGHT = 2
FIRST_SWAPS = ((1, 1), (2, 2))
SWAPS = {2: (4, 2), 3: (6, 2), 5: (8, 4), 8: (12, 2), 9: (14, 2)}
SWAP_WAITS = {5: 6, 10: 12}
RAW_STEP = 2
INVERSE_STEP = 2
FINISHED_AHEAD = 1
ME, PARTNER, NEAR, NEAR_PARTNER, INNER, FIXED = 0, 1, 2, 3, 4, 5
LANES = 128
CODE_ROWS = 16
LEVELS = 32700.0
ROUNDER = 1.5 * 2.0**23
CODES_PER_OCTAVE = 128.0
SMALLEST = 2.0**-110
CHUNK_ORDER = ((2, 3, 1, 0), (0, 2, 3, 1), (3, 1, 0, 2), (1, 0, 2, 3))
SENDS = (
    (((0, 1), (1, 0), (2, 3), (3, 2)),),
    (((0, 1), (3, 2)), ((1, 2), (2, 1))),
    (((0, 1), (1, 3), (2, 0), (3, 2)),),
)


def incidence(earlier, later, rows):
    shape = (rows, earlier.shape[1])
    date = lax.broadcasted_iota(jnp.int32, shape, 0)
    return (date == later).astype(F32) - (date == earlier).astype(F32)


def split_product(left, right):
    def halves(value):
        high = value.astype(jnp.bfloat16)
        return high, (value - high.astype(F32)).astype(jnp.bfloat16)

    left_high, left_low = halves(left)
    right_high, right_low = halves(right)
    small = jnp.dot(left_high, right_low, preferred_element_type=F32) + jnp.dot(left_low, right_high, preferred_element_type=F32)
    return jnp.dot(left_high, right_high, preferred_element_type=F32) + small


def full_product(left, right):
    return jnp.dot(left, right, precision=HIGHEST, preferred_element_type=F32)


def inverse_kernel(counts_ref, pairs_ref, *rest):
    out_ref = rest[-1]
    runs = out_ref.shape[0]
    design = incidence(pairs_ref[0:1, :], pairs_ref[1:2, :], PAD)
    pair = lax.broadcasted_iota(jnp.int32, design.shape, 1)
    contract_last = (((1,), (1,)), ((), ()))
    row = lax.broadcasted_iota(jnp.int32, (PAD, PAD), 0)
    col = lax.broadcasted_iota(jnp.int32, (PAD, PAD), 1)
    identity = (row == col).astype(F32)
    grams = []
    for run in range(runs):
        kept = jnp.where(pair < counts_ref[run], design, 0.0).astype(jnp.bfloat16)
        gram = lax.dot_general(kept, kept, contract_last, preferred_element_type=F32)
        grams.append(gram + DAMPING * identity)
    low = DAMPING
    high = 2.0 * functools.reduce(jnp.maximum, [jnp.max(gram) for gram in grams]) - DAMPING
    total, width = high + low, high - low
    scale = 2.0 * total * total - width * width
    starts = tuple((8.0 * total / scale) * identity - (8.0 / scale) * gram for gram in grams)
    needed = 18.0 * scale / (8.0 * high * low)
    steps = jnp.int32(0)
    for power in range(1, 16):
        steps += (needed > float(2**power)).astype(jnp.int32)

    def newton(product, guesses):
        products = [product(gram, guess) for gram, guess in zip(grams, guesses)]
        return tuple(2.0 * guess - product(guess, each) for guess, each in zip(guesses, products))

    full_steps = 1 + (high > 100.0).astype(jnp.int32)
    guesses = lax.fori_loop(0, steps + 1 - full_steps, lambda _, guesses: newton(split_product, guesses), starts)
    guesses = lax.fori_loop(0, full_steps, lambda _, guesses: newton(full_product, guesses), guesses)
    for run, guess in enumerate(guesses):
        out_ref[run] = guess


def invert_classes(date_pairs, run_counts, after):
    shape = (run_counts.shape[0], PAD, PAD)
    return pl.pallas_call(
        inverse_kernel,
        out_shape=jax.ShapeDtypeStruct(shape, F32),
        grid_spec=pltpu.PrefetchScalarGridSpec(
            num_scalar_prefetch=1,
            grid=(1,),
            in_specs=[pl.BlockSpec(date_pairs.shape, lambda i, c: (0, 0))] + [pl.BlockSpec(memory_space=pl.ANY)] * len(after),
            out_specs=pl.BlockSpec(shape, lambda i, c: (0, 0, 0)),
        ),
        compiler_params=pltpu.CompilerParams(vmem_limit_bytes=VMEM_BYTES),
        cost_estimate=LITTLE,
        name="invert_classes_0",
    )(run_counts, date_pairs, *after)


def sum_solve_kernel(tiles, counts_ref, pairs_ref, data_ref, inverse_ref, out_ref):
    run = pl.program_id(0) // tiles
    design = incidence(pairs_ref[0:1, :], pairs_ref[1:2, :], PAD)
    pair = lax.broadcasted_iota(jnp.int32, design.shape, 1)
    kept = jnp.where(pair < counts_ref[run], design, 0.0).astype(jnp.bfloat16)
    sums = jnp.dot(kept, data_ref[...], preferred_element_type=F32)
    out_ref[...] = jnp.dot(inverse_ref[0, :M, :], sums, precision=HIGHEST, preferred_element_type=F32)


def sum_solve(run_counts, date_pairs, received, inverse):
    runs = run_counts.shape[0]
    total_pairs, pixels = received.shape
    run_pixels = pixels // runs
    tile = run_pixels // 2
    tiles = run_pixels // tile
    return pl.pallas_call(
        functools.partial(sum_solve_kernel, tiles),
        out_shape=jax.ShapeDtypeStruct((M, pixels), F32),
        grid_spec=pltpu.PrefetchScalarGridSpec(
            num_scalar_prefetch=1,
            grid=(runs * tiles,),
            in_specs=[
                pl.BlockSpec(date_pairs.shape, lambda i, c: (0, 0)),
                pl.BlockSpec((total_pairs, tile), lambda i, c: (0, i)),
                pl.BlockSpec((1, PAD, PAD), lambda i, c: (i // tiles, 0, 0)),
            ],
            out_specs=pl.BlockSpec((M, tile), lambda i, c: (0, i)),
        ),
        compiler_params=pltpu.CompilerParams(vmem_limit_bytes=VMEM_BYTES),
        name="sum_solve",
    )(run_counts, date_pairs, received, inverse)


def coded_rows(piece):
    return M * (piece // LANES) + CODE_ROWS


def decode(coded_ref, codes_ref, lots, first):
    coded = coded_ref[...].astype(jnp.int32).astype(F32)
    values = jnp.concatenate([coded[lot * M : (lot + 1) * M, :] for lot in range(lots)], axis=1)
    codes = codes_ref[...].astype(jnp.int32).astype(F32)
    codes = jnp.concatenate([codes[first + lot : first + lot + 1, :] for lot in range(lots)], axis=1)
    return values, jnp.exp2(codes * (1.0 / CODES_PER_OCTAVE)) * (1.0 / LEVELS)


def encode(sums):
    largest = jnp.max(jnp.abs(sums), axis=0, keepdims=True)
    code = jnp.ceil(jnp.log2(jnp.maximum(largest, SMALLEST)) * CODES_PER_OCTAVE)
    scaled = (sums * (LEVELS / jnp.exp2(code * (1.0 / CODES_PER_OCTAVE))) + ROUNDER) - ROUNDER
    lots = sums.shape[1] // LANES
    return jnp.concatenate([scaled[:, lot * LANES : (lot + 1) * LANES] for lot in range(lots)], axis=0), code


def whole(values):
    return values.astype(jnp.int32).astype(jnp.int16)


def piece_count(at, layout, table, counts):
    parts, _, _, shifts = layout
    run = at % parts // CUTS
    return counts[table[shifts + at] * (parts // CUTS) + run]


def pair_sums(count, table, pairs_ref, first_ref, second_ref, members=(ME, PARTNER)):
    width = first_ref.shape[0]
    lane = lax.broadcasted_iota(jnp.int32, (1, 2 * width), 1)
    pair = jnp.where(lane < width, table[members[0]] * width + lane, table[members[1]] * width + lane - width)
    dates = pairs_ref[:, members[0] * width : (members[0] + 2) * width]
    design = incidence(dates[0:1, :], dates[1:2, :], M)
    kept = jnp.where(pair < count, design, 0.0).astype(jnp.bfloat16)
    data = jnp.concatenate([first_ref[...], second_ref[...]], axis=0)
    return jnp.dot(kept, data, preferred_element_type=F32)


def near_sums(wanted, count, table, pairs_ref, raw_refs):
    return pair_sums(jnp.where(wanted, count, 0), table, pairs_ref, *raw_refs, members=(NEAR, NEAR_PARTNER))


def step_kernel(at, layout, adds, swaps, halves, table, counts, pairs_ref, own_ref, partner_ref, *rest):
    if swaps:
        rest[-1][...] = rest[0][...]
        coded_ref, rest = rest[-2], rest[1:]
    else:
        coded_ref = rest[-1]
    count = piece_count(at, layout, table, counts)
    width = own_ref.shape[1] // halves
    lots = width // LANES
    codes = []
    for half in range(halves):
        part = pl.ds(half * width, width)
        sums = pair_sums(count, table, pairs_ref, own_ref.at[:, part], partner_ref.at[:, part])
        if adds == 1:
            rows = pl.ds(half * lots * M, lots * M)
            values, scale = decode(rest[0].at[rows, :], rest[0].at[halves * lots * M :, :], lots, half * lots)
            sums = sums + values * (scale * table[INNER].astype(F32))
        if adds == 2:
            sums = sums + near_sums(table[INNER] == 1, count, table, pairs_ref, [raw_ref.at[:, part] for raw_ref in rest[:2]])
        scaled, code = encode(sums)
        coded_ref[half * lots * M : (half + 1) * lots * M, :] = whole(scaled)
        codes += [code[:, lot * LANES : (lot + 1) * LANES] for lot in range(lots)]
    codes += [jnp.zeros((CODE_ROWS - len(codes), LANES), F32)]
    coded_ref[halves * lots * M :, :] = whole(jnp.concatenate(codes, axis=0))


def step(at, swap, layout, scalars, pairs, phases, partner, earlier, after, piece):
    partner, place_in = partner
    local_pairs = phases.shape[0]
    _, blocks, away, _ = layout
    coded_shape = (coded_rows(piece), LANES)
    in_specs = [
        pl.BlockSpec(pairs.shape, lambda i, t, c: (0, 0)),
        pl.BlockSpec((local_pairs, piece), lambda i, t, c: (0, t[blocks + at])),
        pl.BlockSpec((local_pairs, piece), lambda i, t, c: (0, place_in)),
    ]
    operands = [pairs, phases, partner]
    out_shape = [jax.ShapeDtypeStruct(coded_shape, jnp.int16)]
    out_specs = [pl.BlockSpec(coded_shape, lambda i, t, c: (0, 0))]
    if swap is not None:
        first, count = swap
        wide = piece * count
        in_specs.append(pl.BlockSpec((local_pairs, wide), lambda i, t, c: (0, t[away + first] // count)))
        operands.append(phases)
        out_shape.append(jax.ShapeDtypeStruct((local_pairs, wide), phases.dtype))
        out_specs.append(pl.BlockSpec((local_pairs, wide), lambda i, t, c: (0, 0)))
    in_specs += [pl.BlockSpec(each.shape, lambda i, t, c: (0, 0)) for each in earlier]
    operands += earlier
    in_specs += [pl.BlockSpec(memory_space=pl.ANY)] * len(after)
    results = pl.pallas_call(
        functools.partial(step_kernel, at, layout, len(earlier), swap is not None, HALVES),
        out_shape=out_shape,
        grid_spec=pltpu.PrefetchScalarGridSpec(
            num_scalar_prefetch=2,
            grid=(1,),
            in_specs=in_specs,
            out_specs=out_specs,
        ),
        compiler_params=pltpu.CompilerParams(vmem_limit_bytes=VMEM_BYTES),
        cost_estimate=STEADY,
        name=f"sum_step_{at:02d}",
    )(*scalars, *operands, *after)
    return results[0], results[1] if swap is not None else None


def coded_specs(piece, tiles, index):
    lots = piece // LANES
    return [
        pl.BlockSpec((lots // tiles * M, LANES), lambda *at: (at[index], 0)),
        pl.BlockSpec((CODE_ROWS, LANES), lambda *at: (lots * M // CODE_ROWS, 0)),
    ]


def add_arrived(sums_ref, refs, tiles):
    lots = sums_ref.shape[1] // LANES
    tile = pl.program_id(0)
    for coded_ref, codes_ref in zip(refs[::2], refs[1::2]):
        parts = [decode(coded_ref, codes_ref, lots, at * lots) for at in range(tiles)]
        scale = functools.reduce(lambda chosen, at: jnp.where(tile == at, parts[at][1], chosen), range(1, tiles), parts[0][1])
        sums_ref[...] += parts[0][0] * scale


def finish_kernel(at, layout, tiles, raw, told, table, counts, pairs_ref, own_ref, partner_ref, inverse_ref, *rest):
    first, middle, last = rest[:2], rest[2:4], rest[4:6]
    sums_ref, rest = rest[-1], rest[:-1]
    if told:
        rest[-1][...] = jnp.zeros_like(rest[-1])
        rest = rest[:-1]
    out_ref = rest[-1]
    count = piece_count(at, layout, table, counts)
    sums_ref[...] = pair_sums(count, table, pairs_ref, own_ref, partner_ref)

    @pl.when(table[INNER] == 0)
    def _():
        if raw:
            sums_ref[...] += near_sums(True, count, table, pairs_ref, first)
        else:
            add_arrived(sums_ref, first, tiles)

    @pl.when(table[INNER] == 1)
    def _():
        add_arrived(sums_ref, middle, tiles)

    add_arrived(sums_ref, last, tiles)
    out_ref[...] = split_product(inverse_ref[0, :M, :M], sums_ref[...])


def finish(at, part, layout, scalars, pairs, phases, partner, inverse, raw, arrived, series, told, pixels, piece):
    partner, place_in = partner
    local_pairs = phases.shape[0]
    blocks = layout[1]
    tiles = HALVES
    tile = piece // tiles
    in_specs = [
        pl.BlockSpec(pairs.shape, lambda i, t, c: (0, 0)),
        pl.BlockSpec((local_pairs, tile), lambda i, t, c: (0, t[blocks + at] * tiles + i)),
        pl.BlockSpec((local_pairs, tile), lambda i, t, c: (0, place_in * tiles + i)),
        pl.BlockSpec((1, PAD, PAD), lambda i, t, c: (part // CUTS, 0, 0)),
    ]
    in_specs += [pl.BlockSpec((local_pairs, tile), lambda i, t, c: (0, i))] * len(raw) + coded_specs(piece, tiles, 0) * len(arrived)
    operands = [*scalars, pairs, phases, partner, inverse, *raw] + [each for each in arrived for _ in range(2)]
    aliases = {}
    if series is not None:
        in_specs.append(pl.BlockSpec(memory_space=pl.ANY))
        aliases = {len(operands): 0}
        operands.append(series)
    out_shape = [jax.ShapeDtypeStruct((M, pixels), F32)]
    out_specs = [pl.BlockSpec((M, tile), lambda i, t, c: (0, part * tiles + i))]
    if told:
        out_shape.append(jax.ShapeDtypeStruct((8, LANES), F32))
        out_specs.append(pl.BlockSpec((8, LANES), lambda i, t, c: (0, 0)))
    return pl.pallas_call(
        functools.partial(finish_kernel, at, layout, tiles, len(raw) > 0, told),
        out_shape=out_shape,
        grid_spec=pltpu.PrefetchScalarGridSpec(
            num_scalar_prefetch=2,
            grid=(tiles,),
            in_specs=in_specs,
            out_specs=out_specs,
            scratch_shapes=[pltpu.VMEM((M, tile), F32)],
        ),
        input_output_aliases=aliases,
        compiler_params=pltpu.CompilerParams(vmem_limit_bytes=VMEM_BYTES),
        cost_estimate=LITTLE,
        name=f"finish_{part}",
    )(*operands)


def line_permutation(links):
    return [(2 * source + side, 2 * target + side) for source, target in links for side in range(2)]


def solve_by_sums(phases, date_pairs, counts_of):
    owner_count = lax.axis_size("ifg")
    line = owner_count // 2
    local_pairs, pixels = phases.shape
    owner_pixels = pixels // owner_count
    runs = counts_of().shape[0]
    parts = runs * CUTS
    piece = owner_pixels // parts
    steps = (line - 1) * parts
    me = lax.axis_index("ifg")

    places = np.repeat(np.array(CHUNK_ORDER), parts, axis=1)
    part_of = np.tile(np.arange(parts), line)
    rows = []
    for device in range(owner_count):
        place, side = device // 2, device % 2
        own = (places[place] * 2 + side) * parts + part_of
        away = (places[place] * 2 + 1 - side) * parts + part_of
        shift = (place - places[place]) % line
        rows.append(np.concatenate([[device, device ^ 1, device ^ 2, device ^ 3, int(0 < place < line - 1)], own, away, shift]))
    row = lax.dynamic_index_in_dim(jnp.asarray(np.stack(rows), jnp.int32), me, 0, keepdims=False)
    head, pieces = FIXED, line * parts
    layout = (parts, head, head + pieces, head + 2 * pieces)

    swap = [(i, i ^ 1) for i in range(owner_count)]
    partner_of = {}

    def swapped(away, first, count):
        here = lax.ppermute(away, "ifg", swap)
        partner_of.update({first + place: (here, place) for place in range(count)})

    place, side = me // 2, me % 2
    chunk = jnp.where(place < line // 2, 2 - 2 * place, 7 - 2 * place)

    def first_away(column, part, count, after):
        block = (chunk * 2 + column) * parts + part
        if after is not None:
            block, _ = lax.optimization_barrier((block, after))
        return lax.dynamic_slice(phases, (0, block * piece), (local_pairs, count * piece))

    run_counts = counts_of()
    counts = [run_counts]
    for distance in range(1, line):
        links = [(i, (i + distance) % line) for i in range(line)]
        counts.append(lax.ppermute(run_counts, "ifg", line_permutation(links)))
    counts = jnp.concatenate(counts)
    swapped(first_away(1 - side, *FIRST_SWAPS[0], run_counts), *FIRST_SWAPS[0])
    near = line_permutation(SENDS[0][0])
    raw_other = lax.ppermute(first_away(1 - side, 0, 1, run_counts), "ifg", near)
    raw_own = lax.ppermute(first_away(side, 0, 1, run_counts), "ifg", near)
    swapped(first_away(1 - side, *FIRST_SWAPS[1], counts), *FIRST_SWAPS[1])
    pairs = jnp.concatenate([lax.dynamic_slice(date_pairs, (0, (me ^ at) * local_pairs), (2, local_pairs)) for at in range(4)], axis=1)
    scalars = (row, counts)

    received, coded, series = [[raw_own, raw_other]], None, None

    def finished(part, series, told):
        at = steps + part
        arrived = [received[place * parts + part][-1] for place in range(1 if part == 0 else 0, line - 1)]
        data = (layout, scalars, pairs, phases, partner_of[at], inverse, raw if part == 0 else [], arrived)
        return finish(at, part, *data, series, told, owner_pixels, piece)

    for at in range(1, steps):
        earlier = [] if at < parts else raw if at == parts else [received[at - parts][0]]
        after = [coded] if at > 1 else []
        after += received[at - FLIGHT] if at >= FLIGHT else []
        if at in SWAP_WAITS:
            after.append(partner_of[SWAP_WAITS[at]][0])
        if at == INVERSE_STEP:
            inverse = invert_classes(date_pairs, run_counts, [coded])
            after.append(inverse)
        if at == steps - 1:
            for part in range(FINISHED_AHEAD):
                series, told = finished(part, series, True)
                after.append(told)
        coded, away = step(at, SWAPS.get(at), layout, scalars, pairs, phases, partner_of[at], earlier, after, piece)
        received.append([lax.ppermute(coded, "ifg", line_permutation(links)) for links in SENDS[at // parts]])
        if at in SWAPS:
            swapped(away, *SWAPS[at])
        if at == RAW_STEP:
            raw_other, _ = lax.optimization_barrier((raw_other, coded))
            raw = [raw_own, lax.ppermute(raw_other, "ifg", swap)]

    for part in range(FINISHED_AHEAD, parts):
        series = finished(part, series, False)[0]
    return series


def solve_by_blocks(phases, date_pairs, counts_of):
    owner_count = lax.axis_size("ifg")
    local_pairs, pixels = phases.shape
    owner_pixels = pixels // owner_count
    run_counts = counts_of()
    outgoing = phases.reshape(local_pairs, owner_count, owner_pixels).transpose(1, 0, 2)
    received = lax.all_to_all(outgoing, "ifg", split_axis=0, concat_axis=0, tiled=True)
    inverse = invert_classes(date_pairs, run_counts, [])
    return sum_solve(run_counts, date_pairs, received.reshape(-1, owner_pixels), inverse)


def local(phases, date_pairs, pair_counts, group_ids):
    local_pairs, _, pixels = phases.shape

    def counts_of():
        strip_groups = lax.dynamic_index_in_dim(group_ids, lax.axis_index("grp"), 0, keepdims=False)[::RUN]
        chosen = strip_groups[:, None] == jnp.arange(pair_counts.shape[0], dtype=jnp.int32)
        return jnp.sum(jnp.where(chosen, pair_counts, 0), axis=1)

    line = lax.axis_size("ifg") == 2 * len(CHUNK_ORDER) and group_ids.shape[1] == 2 * RUN
    by_sums = line and 2 * local_pairs > M and local_pairs % LANES == 0 and lax.axis_size("grp") % 2 == 0
    solve = solve_by_sums if by_sums else solve_by_blocks
    return solve(phases.reshape(local_pairs, pixels), date_pairs, counts_of)[None, :, :]


def solution(mesh):
    in_specs = (P("ifg", "grp", None), P(), P(), P(None, "ifg"))
    out_specs = P("grp", None, "ifg")
    return jax.shard_map(local, mesh=mesh, in_specs=in_specs, out_specs=out_specs, check_vma=False)
```

```python
import functools

import jax
import jax.numpy as jnp
import numpy as np
from jax import lax
from jax.experimental import pallas as pl
from jax.experimental.pallas import tpu as pltpu
from jax.sharding import PartitionSpec as P

M = 200
RUN = 8
PAD = 256
SLABS = 8
DAMPING = 1.0
VMEM_BYTES = 48 * 1024 * 1024
F32 = jnp.float32
HIGHEST = lax.Precision.HIGHEST
STEADY = pl.CostEstimate(flops=10_000_000_000, bytes_accessed=30_000_000, transcendentals=0)
LITTLE = pl.CostEstimate(flops=1024, bytes_accessed=1024, transcendentals=0)
CUTS = 2
HALVES = 2
FLIGHT = 2
FIRST_SWAPS = ((0, 1), (1, 2))
SWAPS = {1: (4, 2), 2: (6, 2), 5: (8, 4), 8: (12, 2), 9: (14, 2)}
SWAP_WAITS = {5: 6, 10: 12}
RAW_STEP, RAW_WAIT = 2, 5
INVERSE_STEP = 1
FINISHED_AHEAD = 1
ME, PARTNER, NEAR, NEAR_PARTNER, INNER, FIXED = 0, 1, 2, 3, 4, 5
LANES = 128
CODE_ROWS = 16
LEVELS = 32700.0
ROUNDER = 1.5 * 2.0**23
CODES_PER_OCTAVE = 128.0
SMALLEST = 2.0**-110
CHUNK_ORDER = ((2, 3, 1, 0), (0, 2, 3, 1), (3, 1, 0, 2), (1, 0, 2, 3))
SENDS = (
    (((0, 1), (1, 0), (2, 3), (3, 2)),),
    (((0, 1), (3, 2)), ((1, 2), (2, 1))),
    (((0, 1), (1, 3), (2, 0), (3, 2)),),
)


def incidence(earlier, later, rows):
    shape = (rows, earlier.shape[1])
    date = lax.broadcasted_iota(jnp.int32, shape, 0)
    return (date == later).astype(F32) - (date == earlier).astype(F32)


def split_product(left, right):
    def halves(value):
        high = value.astype(jnp.bfloat16)
        return high, (value - high.astype(F32)).astype(jnp.bfloat16)

    left_high, left_low = halves(left)
    right_high, right_low = halves(right)
    small = jnp.dot(left_high, right_low, preferred_element_type=F32) + jnp.dot(left_low, right_high, preferred_element_type=F32)
    return jnp.dot(left_high, right_high, preferred_element_type=F32) + small


def full_product(left, right):
    return jnp.dot(left, right, precision=HIGHEST, preferred_element_type=F32)


def inverse_kernel(counts_ref, pairs_ref, *rest):
    out_ref = rest[-1]
    runs = out_ref.shape[0]
    design = incidence(pairs_ref[0:1, :], pairs_ref[1:2, :], PAD)
    pair = lax.broadcasted_iota(jnp.int32, design.shape, 1)
    contract_last = (((1,), (1,)), ((), ()))
    row = lax.broadcasted_iota(jnp.int32, (PAD, PAD), 0)
    col = lax.broadcasted_iota(jnp.int32, (PAD, PAD), 1)
    identity = (row == col).astype(F32)
    grams = []
    for run in range(runs):
        kept = jnp.where(pair < counts_ref[run], design, 0.0).astype(jnp.bfloat16)
        gram = lax.dot_general(kept, kept, contract_last, preferred_element_type=F32)
        grams.append(gram + DAMPING * identity)
    low = DAMPING
    high = 2.0 * functools.reduce(jnp.maximum, [jnp.max(gram) for gram in grams]) - DAMPING
    total, width = high + low, high - low
    scale = 2.0 * total * total - width * width
    starts = tuple((8.0 * total / scale) * identity - (8.0 / scale) * gram for gram in grams)
    needed = 18.0 * scale / (8.0 * high * low)
    steps = jnp.int32(0)
    for power in range(1, 16):
        steps += (needed > float(2**power)).astype(jnp.int32)

    def newton(product, guesses):
        products = [product(gram, guess) for gram, guess in zip(grams, guesses)]
        return tuple(2.0 * guess - product(guess, each) for guess, each in zip(guesses, products))

    full_steps = 1 + (high > 100.0).astype(jnp.int32)
    guesses = lax.fori_loop(0, steps + 1 - full_steps, lambda _, guesses: newton(split_product, guesses), starts)
    guesses = lax.fori_loop(0, full_steps, lambda _, guesses: newton(full_product, guesses), guesses)
    for run, guess in enumerate(guesses):
        out_ref[run] = guess


def invert_classes(date_pairs, run_counts, after):
    shape = (run_counts.shape[0], PAD, PAD)
    return pl.pallas_call(
        inverse_kernel,
        out_shape=jax.ShapeDtypeStruct(shape, F32),
        grid_spec=pltpu.PrefetchScalarGridSpec(
            num_scalar_prefetch=1,
            grid=(1,),
            in_specs=[pl.BlockSpec(date_pairs.shape, lambda i, c: (0, 0))] + [pl.BlockSpec(memory_space=pl.ANY)] * len(after),
            out_specs=pl.BlockSpec(shape, lambda i, c: (0, 0, 0)),
        ),
        compiler_params=pltpu.CompilerParams(vmem_limit_bytes=VMEM_BYTES),
        cost_estimate=LITTLE,
        name="invert_classes_0",
    )(run_counts, date_pairs, *after)


def sum_solve_kernel(tiles, counts_ref, pairs_ref, data_ref, inverse_ref, out_ref):
    run = pl.program_id(0) // tiles
    design = incidence(pairs_ref[0:1, :], pairs_ref[1:2, :], PAD)
    pair = lax.broadcasted_iota(jnp.int32, design.shape, 1)
    kept = jnp.where(pair < counts_ref[run], design, 0.0).astype(jnp.bfloat16)
    sums = jnp.dot(kept, data_ref[...], preferred_element_type=F32)
    out_ref[...] = jnp.dot(inverse_ref[0, :M, :], sums, precision=HIGHEST, preferred_element_type=F32)


def sum_solve(run_counts, date_pairs, received, inverse):
    runs = run_counts.shape[0]
    total_pairs, pixels = received.shape
    run_pixels = pixels // runs
    tile = run_pixels // 2
    tiles = run_pixels // tile
    return pl.pallas_call(
        functools.partial(sum_solve_kernel, tiles),
        out_shape=jax.ShapeDtypeStruct((M, pixels), F32),
        grid_spec=pltpu.PrefetchScalarGridSpec(
            num_scalar_prefetch=1,
            grid=(runs * tiles,),
            in_specs=[
                pl.BlockSpec(date_pairs.shape, lambda i, c: (0, 0)),
                pl.BlockSpec((total_pairs, tile), lambda i, c: (0, i)),
                pl.BlockSpec((1, PAD, PAD), lambda i, c: (i // tiles, 0, 0)),
            ],
            out_specs=pl.BlockSpec((M, tile), lambda i, c: (0, i)),
        ),
        compiler_params=pltpu.CompilerParams(vmem_limit_bytes=VMEM_BYTES),
        name="sum_solve",
    )(run_counts, date_pairs, received, inverse)


def coded_rows(piece):
    return M * (piece // LANES) + CODE_ROWS


def decode(coded_ref, codes_ref, lots, first):
    coded = coded_ref[...].astype(jnp.int32).astype(F32)
    values = jnp.concatenate([coded[lot * M : (lot + 1) * M, :] for lot in range(lots)], axis=1)
    codes = codes_ref[...].astype(jnp.int32).astype(F32)
    codes = jnp.concatenate([codes[first + lot : first + lot + 1, :] for lot in range(lots)], axis=1)
    return values, jnp.exp2(codes * (1.0 / CODES_PER_OCTAVE)) * (1.0 / LEVELS)


def encode(sums):
    largest = jnp.max(jnp.abs(sums), axis=0, keepdims=True)
    code = jnp.ceil(jnp.log2(jnp.maximum(largest, SMALLEST)) * CODES_PER_OCTAVE)
    scaled = (sums * (LEVELS / jnp.exp2(code * (1.0 / CODES_PER_OCTAVE))) + ROUNDER) - ROUNDER
    lots = sums.shape[1] // LANES
    return jnp.concatenate([scaled[:, lot * LANES : (lot + 1) * LANES] for lot in range(lots)], axis=0), code


def whole(values):
    return values.astype(jnp.int32).astype(jnp.int16)


def piece_count(at, layout, table, counts):
    parts, _, _, shifts = layout
    run = at % parts // CUTS
    return counts[table[shifts + at] * (parts // CUTS) + run]


def pair_sums(count, table, pairs_ref, first_ref, second_ref, members=(ME, PARTNER)):
    width = first_ref.shape[0]
    lane = lax.broadcasted_iota(jnp.int32, (1, 2 * width), 1)
    pair = jnp.where(lane < width, table[members[0]] * width + lane, table[members[1]] * width + lane - width)
    dates = pairs_ref[:, members[0] * width : (members[0] + 2) * width]
    design = incidence(dates[0:1, :], dates[1:2, :], M)
    kept = jnp.where(pair < count, design, 0.0).astype(jnp.bfloat16)
    data = jnp.concatenate([first_ref[...], second_ref[...]], axis=0)
    return jnp.dot(kept, data, preferred_element_type=F32)


def near_sums(wanted, count, table, pairs_ref, raw_refs):
    return pair_sums(jnp.where(wanted, count, 0), table, pairs_ref, *raw_refs, members=(NEAR, NEAR_PARTNER))


def step_kernel(at, layout, adds, swaps, halves, table, counts, pairs_ref, own_ref, partner_ref, *rest):
    if swaps:
        rest[-1][...] = rest[0][...]
        coded_ref, rest = rest[-2], rest[1:]
    else:
        coded_ref = rest[-1]
    count = piece_count(at, layout, table, counts)
    width = own_ref.shape[1] // halves
    lots = width // LANES
    codes = []
    for half in range(halves):
        part = pl.ds(half * width, width)
        sums = pair_sums(count, table, pairs_ref, own_ref.at[:, part], partner_ref.at[:, part])
        if adds == 1:
            rows = pl.ds(half * lots * M, lots * M)
            values, scale = decode(rest[0].at[rows, :], rest[0].at[halves * lots * M :, :], lots, half * lots)
            sums = sums + values * (scale * table[INNER].astype(F32))
        if adds == 2:
            sums = sums + near_sums(table[INNER] == 1, count, table, pairs_ref, [raw_ref.at[:, part] for raw_ref in rest[:2]])
        scaled, code = encode(sums)
        coded_ref[half * lots * M : (half + 1) * lots * M, :] = whole(scaled)
        codes += [code[:, lot * LANES : (lot + 1) * LANES] for lot in range(lots)]
    codes += [jnp.zeros((CODE_ROWS - len(codes), LANES), F32)]
    coded_ref[halves * lots * M :, :] = whole(jnp.concatenate(codes, axis=0))


def step(at, swap, layout, scalars, pairs, phases, partner, earlier, after, piece):
    partner, place_in = partner
    local_pairs = phases.shape[0]
    _, blocks, away, _ = layout
    coded_shape = (coded_rows(piece), LANES)
    in_specs = [
        pl.BlockSpec(pairs.shape, lambda i, t, c: (0, 0)),
        pl.BlockSpec((local_pairs, piece), lambda i, t, c: (0, t[blocks + at])),
        pl.BlockSpec((local_pairs, piece), lambda i, t, c: (0, place_in)),
    ]
    operands = [pairs, phases, partner]
    out_shape = [jax.ShapeDtypeStruct(coded_shape, jnp.int16)]
    out_specs = [pl.BlockSpec(coded_shape, lambda i, t, c: (0, 0))]
    if swap is not None:
        first, count = swap
        wide = piece * count
        in_specs.append(pl.BlockSpec((local_pairs, wide), lambda i, t, c: (0, t[away + first] // count)))
        operands.append(phases)
        out_shape.append(jax.ShapeDtypeStruct((local_pairs, wide), phases.dtype))
        out_specs.append(pl.BlockSpec((local_pairs, wide), lambda i, t, c: (0, 0)))
    in_specs += [pl.BlockSpec(each.shape, lambda i, t, c: (0, 0)) for each in earlier]
    operands += earlier
    in_specs += [pl.BlockSpec(memory_space=pl.ANY)] * len(after)
    results = pl.pallas_call(
        functools.partial(step_kernel, at, layout, len(earlier), swap is not None, HALVES),
        out_shape=out_shape,
        grid_spec=pltpu.PrefetchScalarGridSpec(
            num_scalar_prefetch=2,
            grid=(1,),
            in_specs=in_specs,
            out_specs=out_specs,
        ),
        compiler_params=pltpu.CompilerParams(vmem_limit_bytes=VMEM_BYTES),
        cost_estimate=STEADY,
        name=f"sum_step_{at:02d}",
    )(*scalars, *operands, *after)
    return results[0], results[1] if swap is not None else None


def coded_specs(piece, tiles, index):
    lots = piece // LANES
    return [
        pl.BlockSpec((lots // tiles * M, LANES), lambda *at: (at[index], 0)),
        pl.BlockSpec((CODE_ROWS, LANES), lambda *at: (lots * M // CODE_ROWS, 0)),
    ]


def add_arrived(sums_ref, refs, tiles):
    lots = sums_ref.shape[1] // LANES
    tile = pl.program_id(0)
    for coded_ref, codes_ref in zip(refs[::2], refs[1::2]):
        parts = [decode(coded_ref, codes_ref, lots, at * lots) for at in range(tiles)]
        scale = functools.reduce(lambda chosen, at: jnp.where(tile == at, parts[at][1], chosen), range(1, tiles), parts[0][1])
        sums_ref[...] += parts[0][0] * scale


def finish_kernel(at, layout, tiles, raw, told, table, counts, pairs_ref, own_ref, partner_ref, inverse_ref, *rest):
    first, middle, last = rest[:2], rest[2:4], rest[4:6]
    sums_ref, rest = rest[-1], rest[:-1]
    if told:
        rest[-1][...] = jnp.zeros_like(rest[-1])
        rest = rest[:-1]
    out_ref = rest[-1]
    count = piece_count(at, layout, table, counts)
    sums_ref[...] = pair_sums(count, table, pairs_ref, own_ref, partner_ref)

    @pl.when(table[INNER] == 0)
    def _():
        if raw:
            sums_ref[...] += near_sums(True, count, table, pairs_ref, first)
        else:
            add_arrived(sums_ref, first, tiles)

    @pl.when(table[INNER] == 1)
    def _():
        add_arrived(sums_ref, middle, tiles)

    add_arrived(sums_ref, last, tiles)
    out_ref[...] = split_product(inverse_ref[0, :M, :M], sums_ref[...])


def finish(at, part, layout, scalars, pairs, phases, partner, inverse, raw, arrived, series, told, pixels, piece):
    partner, place_in = partner
    local_pairs = phases.shape[0]
    blocks = layout[1]
    tiles = HALVES
    tile = piece // tiles
    in_specs = [
        pl.BlockSpec(pairs.shape, lambda i, t, c: (0, 0)),
        pl.BlockSpec((local_pairs, tile), lambda i, t, c: (0, t[blocks + at] * tiles + i)),
        pl.BlockSpec((local_pairs, tile), lambda i, t, c: (0, place_in * tiles + i)),
        pl.BlockSpec((1, PAD, PAD), lambda i, t, c: (part // CUTS, 0, 0)),
    ]
    in_specs += [pl.BlockSpec((local_pairs, tile), lambda i, t, c: (0, i))] * len(raw) + coded_specs(piece, tiles, 0) * len(arrived)
    operands = [*scalars, pairs, phases, partner, inverse, *raw] + [each for each in arrived for _ in range(2)]
    aliases = {}
    if series is not None:
        in_specs.append(pl.BlockSpec(memory_space=pl.ANY))
        aliases = {len(operands): 0}
        operands.append(series)
    out_shape = [jax.ShapeDtypeStruct((M, pixels), F32)]
    out_specs = [pl.BlockSpec((M, tile), lambda i, t, c: (0, part * tiles + i))]
    if told:
        out_shape.append(jax.ShapeDtypeStruct((8, LANES), F32))
        out_specs.append(pl.BlockSpec((8, LANES), lambda i, t, c: (0, 0)))
    return pl.pallas_call(
        functools.partial(finish_kernel, at, layout, tiles, len(raw) > 0, told),
        out_shape=out_shape,
        grid_spec=pltpu.PrefetchScalarGridSpec(
            num_scalar_prefetch=2,
            grid=(tiles,),
            in_specs=in_specs,
            out_specs=out_specs,
            scratch_shapes=[pltpu.VMEM((M, tile), F32)],
        ),
        input_output_aliases=aliases,
        compiler_params=pltpu.CompilerParams(vmem_limit_bytes=VMEM_BYTES),
        cost_estimate=LITTLE,
        name=f"finish_{part}",
    )(*operands)


def line_permutation(links):
    return [(2 * source + side, 2 * target + side) for source, target in links for side in range(2)]


def solve_by_sums(phases, date_pairs, counts_of):
    owner_count = lax.axis_size("ifg")
    line = owner_count // 2
    local_pairs, pixels = phases.shape
    owner_pixels = pixels // owner_count
    runs = counts_of().shape[0]
    parts = runs * CUTS
    piece = owner_pixels // parts
    steps = (line - 1) * parts
    me = lax.axis_index("ifg")

    places = np.repeat(np.array(CHUNK_ORDER), parts, axis=1)
    part_of = np.tile(np.arange(parts), line)
    rows = []
    for device in range(owner_count):
        place, side = device // 2, device % 2
        own = (places[place] * 2 + side) * parts + part_of
        away = (places[place] * 2 + 1 - side) * parts + part_of
        shift = (place - places[place]) % line
        rows.append(np.concatenate([[device, device ^ 1, device ^ 2, device ^ 3, int(0 < place < line - 1)], own, away, shift]))
    row = lax.dynamic_index_in_dim(jnp.asarray(np.stack(rows), jnp.int32), me, 0, keepdims=False)
    head, pieces = FIXED, line * parts
    layout = (parts, head, head + pieces, head + 2 * pieces)

    swap = [(i, i ^ 1) for i in range(owner_count)]
    partner_of = {}

    def swapped(away, first, count):
        here = lax.ppermute(away, "ifg", swap)
        partner_of.update({first + place: (here, place) for place in range(count)})

    place, side = me // 2, me % 2
    chunk = jnp.where(place < line // 2, 2 - 2 * place, 7 - 2 * place)

    def first_away(column, part, count, after):
        block = (chunk * 2 + column) * parts + part
        if after is not None:
            block, _ = lax.optimization_barrier((block, after))
        return lax.dynamic_slice(phases, (0, block * piece), (local_pairs, count * piece))

    run_counts = counts_of()
    counts = [run_counts]
    for distance in range(1, line):
        links = [(i, (i + distance) % line) for i in range(line)]
        counts.append(lax.ppermute(run_counts, "ifg", line_permutation(links)))
    counts = jnp.concatenate(counts)
    away = first_away(1 - side, *FIRST_SWAPS[0], run_counts)
    swapped(away, *FIRST_SWAPS[0])
    raw_part = parts - 1
    near = line_permutation(SENDS[0][0])
    raw_other = lax.ppermute(first_away(1 - side, raw_part, 1, away), "ifg", near)
    raw_own = lax.ppermute(first_away(side, raw_part, 1, away), "ifg", near)
    swapped(first_away(1 - side, *FIRST_SWAPS[1], counts), *FIRST_SWAPS[1])
    pairs = jnp.concatenate([lax.dynamic_slice(date_pairs, (0, (me ^ at) * local_pairs), (2, local_pairs)) for at in range(4)], axis=1)
    scalars = (row, counts)

    received, sent, coded, series = {raw_part: [raw_own, raw_other]}, [raw_part], None, None

    def finished(part, series, told):
        at = steps + part
        arrived = [received[place * parts + part][-1] for place in range(1 if part == raw_part else 0, line - 1)]
        data = (layout, scalars, pairs, phases, partner_of[at], inverse, raw if part == raw_part else [], arrived)
        return finish(at, part, *data, series, told, owner_pixels, piece)

    for at in [each for each in range(steps) if each != raw_part]:
        earlier = [] if at < parts else raw if at == parts + raw_part else [received[at - parts][0]]
        after = [] if coded is None else [coded]
        after += received[sent[-FLIGHT]] if len(sent) >= FLIGHT else []
        if at in SWAP_WAITS:
            after.append(partner_of[SWAP_WAITS[at]][0])
        if at == RAW_WAIT:
            after.append(raw[1])
        if at == INVERSE_STEP:
            inverse = invert_classes(date_pairs, run_counts, [coded])
            after.append(inverse)
        if at == steps - 1:
            for part in range(FINISHED_AHEAD):
                series, told = finished(part, series, True)
                after.append(told)
        coded, away = step(at, SWAPS.get(at), layout, scalars, pairs, phases, partner_of[at], earlier, after, piece)
        received[at] = [lax.ppermute(coded, "ifg", line_permutation(links)) for links in SENDS[at // parts]]
        sent.append(at)
        if at in SWAPS:
            swapped(away, *SWAPS[at])
        if at == RAW_STEP:
            raw_other, _ = lax.optimization_barrier((raw_other, coded))
            raw = [raw_own, lax.ppermute(raw_other, "ifg", swap)]

    for part in range(FINISHED_AHEAD, parts):
        series = finished(part, series, False)[0]
    return series


def solve_by_blocks(phases, date_pairs, counts_of):
    owner_count = lax.axis_size("ifg")
    local_pairs, pixels = phases.shape
    owner_pixels = pixels // owner_count
    run_counts = counts_of()
    outgoing = phases.reshape(local_pairs, owner_count, owner_pixels).transpose(1, 0, 2)
    received = lax.all_to_all(outgoing, "ifg", split_axis=0, concat_axis=0, tiled=True)
    inverse = invert_classes(date_pairs, run_counts, [])
    return sum_solve(run_counts, date_pairs, received.reshape(-1, owner_pixels), inverse)


def local(phases, date_pairs, pair_counts, group_ids):
    local_pairs, _, pixels = phases.shape

    def counts_of():
        strip_groups = lax.dynamic_index_in_dim(group_ids, lax.axis_index("grp"), 0, keepdims=False)[::RUN]
        chosen = strip_groups[:, None] == jnp.arange(pair_counts.shape[0], dtype=jnp.int32)
        return jnp.sum(jnp.where(chosen, pair_counts, 0), axis=1)

    line = lax.axis_size("ifg") == 2 * len(CHUNK_ORDER) and group_ids.shape[1] == 2 * RUN
    by_sums = line and 2 * local_pairs > M and local_pairs % LANES == 0 and lax.axis_size("grp") % 2 == 0
    solve = solve_by_sums if by_sums else solve_by_blocks
    return solve(phases.reshape(local_pairs, pixels), date_pairs, counts_of)[None, :, :]


def solution(mesh):
    in_specs = (P("ifg", "grp", None), P(), P(), P(None, "ifg"))
    out_specs = P("grp", None, "ifg")
    return jax.shard_map(local, mesh=mesh, in_specs=in_specs, out_specs=out_specs, check_vma=False)
```

```python
import functools

import jax
import jax.numpy as jnp
import numpy as np
from jax import lax
from jax.experimental import pallas as pl
from jax.experimental.pallas import tpu as pltpu
from jax.sharding import PartitionSpec as P

M = 200
RUN = 8
PAD = 256
SLABS = 8
DAMPING = 1.0
VMEM_BYTES = 48 * 1024 * 1024
F32 = jnp.float32
HIGHEST = lax.Precision.HIGHEST
STEADY = pl.CostEstimate(flops=10_000_000_000, bytes_accessed=30_000_000, transcendentals=0)
LITTLE = pl.CostEstimate(flops=1024, bytes_accessed=1024, transcendentals=0)
CUTS = 2
HALVES = 2
FLIGHT = 2
FIRST_SWAPS = ((0, 1), (1, 2))
SWAPS = {1: (4, 2), 2: (6, 2), 5: (8, 4), 8: (12, 2), 9: (14, 2)}
SWAP_WAITS = {5: 6, 10: 12}
RAW_STEP, RAW_WAIT = 2, 5
INVERSE_STEP = 5
FINISHED_AHEAD = 1
ME, PARTNER, NEAR, NEAR_PARTNER, INNER, FIXED = 0, 1, 2, 3, 4, 5
LANES = 128
CODE_ROWS = 16
LEVELS = 32700.0
ROUNDER = 1.5 * 2.0**23
CODES_PER_OCTAVE = 128.0
SMALLEST = 2.0**-110
CHUNK_ORDER = ((2, 3, 1, 0), (0, 2, 3, 1), (3, 1, 0, 2), (1, 0, 2, 3))
SENDS = (
    (((0, 1), (1, 0), (2, 3), (3, 2)),),
    (((0, 1), (3, 2)), ((1, 2), (2, 1))),
    (((0, 1), (1, 3), (2, 0), (3, 2)),),
)


def incidence(earlier, later, rows):
    shape = (rows, earlier.shape[1])
    date = lax.broadcasted_iota(jnp.int32, shape, 0)
    return (date == later).astype(F32) - (date == earlier).astype(F32)


def split_product(left, right):
    def halves(value):
        high = value.astype(jnp.bfloat16)
        return high, (value - high.astype(F32)).astype(jnp.bfloat16)

    left_high, left_low = halves(left)
    right_high, right_low = halves(right)
    small = jnp.dot(left_high, right_low, preferred_element_type=F32) + jnp.dot(left_low, right_high, preferred_element_type=F32)
    return jnp.dot(left_high, right_high, preferred_element_type=F32) + small


def full_product(left, right):
    return jnp.dot(left, right, precision=HIGHEST, preferred_element_type=F32)


def inverse_kernel(counts_ref, pairs_ref, *rest):
    out_ref = rest[-1]
    runs = out_ref.shape[0]
    design = incidence(pairs_ref[0:1, :], pairs_ref[1:2, :], PAD)
    pair = lax.broadcasted_iota(jnp.int32, design.shape, 1)
    contract_last = (((1,), (1,)), ((), ()))
    row = lax.broadcasted_iota(jnp.int32, (PAD, PAD), 0)
    col = lax.broadcasted_iota(jnp.int32, (PAD, PAD), 1)
    identity = (row == col).astype(F32)
    grams = []
    for run in range(runs):
        kept = jnp.where(pair < counts_ref[run], design, 0.0).astype(jnp.bfloat16)
        gram = lax.dot_general(kept, kept, contract_last, preferred_element_type=F32)
        grams.append(gram + DAMPING * identity)
    low = DAMPING
    high = 2.0 * functools.reduce(jnp.maximum, [jnp.max(gram) for gram in grams]) - DAMPING
    total, width = high + low, high - low
    scale = 2.0 * total * total - width * width
    starts = tuple((8.0 * total / scale) * identity - (8.0 / scale) * gram for gram in grams)
    needed = 18.0 * scale / (8.0 * high * low)
    steps = jnp.int32(0)
    for power in range(1, 16):
        steps += (needed > float(2**power)).astype(jnp.int32)

    def newton(product, guesses):
        products = [product(gram, guess) for gram, guess in zip(grams, guesses)]
        return tuple(2.0 * guess - product(guess, each) for guess, each in zip(guesses, products))

    full_steps = 1 + (high > 100.0).astype(jnp.int32)
    guesses = lax.fori_loop(0, steps + 1 - full_steps, lambda _, guesses: newton(split_product, guesses), starts)
    guesses = lax.fori_loop(0, full_steps, lambda _, guesses: newton(full_product, guesses), guesses)
    for run, guess in enumerate(guesses):
        out_ref[run] = guess


def invert_classes(date_pairs, run_counts, after):
    shape = (run_counts.shape[0], PAD, PAD)
    return pl.pallas_call(
        inverse_kernel,
        out_shape=jax.ShapeDtypeStruct(shape, F32),
        grid_spec=pltpu.PrefetchScalarGridSpec(
            num_scalar_prefetch=1,
            grid=(1,),
            in_specs=[pl.BlockSpec(date_pairs.shape, lambda i, c: (0, 0))] + [pl.BlockSpec(memory_space=pl.ANY)] * len(after),
            out_specs=pl.BlockSpec(shape, lambda i, c: (0, 0, 0)),
        ),
        compiler_params=pltpu.CompilerParams(vmem_limit_bytes=VMEM_BYTES),
        cost_estimate=LITTLE,
        name="invert_classes_0",
    )(run_counts, date_pairs, *after)


def sum_solve_kernel(tiles, counts_ref, pairs_ref, data_ref, inverse_ref, out_ref):
    run = pl.program_id(0) // tiles
    design = incidence(pairs_ref[0:1, :], pairs_ref[1:2, :], PAD)
    pair = lax.broadcasted_iota(jnp.int32, design.shape, 1)
    kept = jnp.where(pair < counts_ref[run], design, 0.0).astype(jnp.bfloat16)
    sums = jnp.dot(kept, data_ref[...], preferred_element_type=F32)
    out_ref[...] = jnp.dot(inverse_ref[0, :M, :], sums, precision=HIGHEST, preferred_element_type=F32)


def sum_solve(run_counts, date_pairs, received, inverse):
    runs = run_counts.shape[0]
    total_pairs, pixels = received.shape
    run_pixels = pixels // runs
    tile = run_pixels // 2
    tiles = run_pixels // tile
    return pl.pallas_call(
        functools.partial(sum_solve_kernel, tiles),
        out_shape=jax.ShapeDtypeStruct((M, pixels), F32),
        grid_spec=pltpu.PrefetchScalarGridSpec(
            num_scalar_prefetch=1,
            grid=(runs * tiles,),
            in_specs=[
                pl.BlockSpec(date_pairs.shape, lambda i, c: (0, 0)),
                pl.BlockSpec((total_pairs, tile), lambda i, c: (0, i)),
                pl.BlockSpec((1, PAD, PAD), lambda i, c: (i // tiles, 0, 0)),
            ],
            out_specs=pl.BlockSpec((M, tile), lambda i, c: (0, i)),
        ),
        compiler_params=pltpu.CompilerParams(vmem_limit_bytes=VMEM_BYTES),
        name="sum_solve",
    )(run_counts, date_pairs, received, inverse)


def coded_rows(piece):
    return M * (piece // LANES) + CODE_ROWS


def decode(coded_ref, codes_ref, lots, first):
    coded = coded_ref[...].astype(jnp.int32).astype(F32)
    values = jnp.concatenate([coded[lot * M : (lot + 1) * M, :] for lot in range(lots)], axis=1)
    codes = codes_ref[...].astype(jnp.int32).astype(F32)
    codes = jnp.concatenate([codes[first + lot : first + lot + 1, :] for lot in range(lots)], axis=1)
    return values, jnp.exp2(codes * (1.0 / CODES_PER_OCTAVE)) * (1.0 / LEVELS)


def encode(sums):
    largest = jnp.max(jnp.abs(sums), axis=0, keepdims=True)
    code = jnp.ceil(jnp.log2(jnp.maximum(largest, SMALLEST)) * CODES_PER_OCTAVE)
    scaled = (sums * (LEVELS / jnp.exp2(code * (1.0 / CODES_PER_OCTAVE))) + ROUNDER) - ROUNDER
    lots = sums.shape[1] // LANES
    return jnp.concatenate([scaled[:, lot * LANES : (lot + 1) * LANES] for lot in range(lots)], axis=0), code


def whole(values):
    return values.astype(jnp.int32).astype(jnp.int16)


def piece_count(at, layout, table, counts):
    parts, _, _, shifts = layout
    run = at % parts // CUTS
    return counts[table[shifts + at] * (parts // CUTS) + run]


def pair_sums(count, table, pairs_ref, first_ref, second_ref, members=(ME, PARTNER)):
    width = first_ref.shape[0]
    lane = lax.broadcasted_iota(jnp.int32, (1, 2 * width), 1)
    pair = jnp.where(lane < width, table[members[0]] * width + lane, table[members[1]] * width + lane - width)
    dates = pairs_ref[:, members[0] * width : (members[0] + 2) * width]
    design = incidence(dates[0:1, :], dates[1:2, :], M)
    kept = jnp.where(pair < count, design, 0.0).astype(jnp.bfloat16)
    data = jnp.concatenate([first_ref[...], second_ref[...]], axis=0)
    return jnp.dot(kept, data, preferred_element_type=F32)


def near_sums(wanted, count, table, pairs_ref, raw_refs):
    return pair_sums(jnp.where(wanted, count, 0), table, pairs_ref, *raw_refs, members=(NEAR, NEAR_PARTNER))


def step_kernel(at, layout, adds, swaps, halves, table, counts, pairs_ref, own_ref, partner_ref, *rest):
    if swaps:
        rest[-1][...] = rest[0][...]
        coded_ref, rest = rest[-2], rest[1:]
    else:
        coded_ref = rest[-1]
    count = piece_count(at, layout, table, counts)
    width = own_ref.shape[1] // halves
    lots = width // LANES
    codes = []
    for half in range(halves):
        part = pl.ds(half * width, width)
        sums = pair_sums(count, table, pairs_ref, own_ref.at[:, part], partner_ref.at[:, part])
        if adds == 1:
            rows = pl.ds(half * lots * M, lots * M)
            values, scale = decode(rest[0].at[rows, :], rest[0].at[halves * lots * M :, :], lots, half * lots)
            sums = sums + values * (scale * table[INNER].astype(F32))
        if adds == 2:
            sums = sums + near_sums(table[INNER] == 1, count, table, pairs_ref, [raw_ref.at[:, part] for raw_ref in rest[:2]])
        scaled, code = encode(sums)
        coded_ref[half * lots * M : (half + 1) * lots * M, :] = whole(scaled)
        codes += [code[:, lot * LANES : (lot + 1) * LANES] for lot in range(lots)]
    codes += [jnp.zeros((CODE_ROWS - len(codes), LANES), F32)]
    coded_ref[halves * lots * M :, :] = whole(jnp.concatenate(codes, axis=0))


def step(at, swap, layout, scalars, pairs, phases, partner, earlier, after, piece):
    partner, place_in = partner
    local_pairs = phases.shape[0]
    _, blocks, away, _ = layout
    coded_shape = (coded_rows(piece), LANES)
    in_specs = [
        pl.BlockSpec(pairs.shape, lambda i, t, c: (0, 0)),
        pl.BlockSpec((local_pairs, piece), lambda i, t, c: (0, t[blocks + at])),
        pl.BlockSpec((local_pairs, piece), lambda i, t, c: (0, place_in)),
    ]
    operands = [pairs, phases, partner]
    out_shape = [jax.ShapeDtypeStruct(coded_shape, jnp.int16)]
    out_specs = [pl.BlockSpec(coded_shape, lambda i, t, c: (0, 0))]
    if swap is not None:
        first, count = swap
        wide = piece * count
        in_specs.append(pl.BlockSpec((local_pairs, wide), lambda i, t, c: (0, t[away + first] // count)))
        operands.append(phases)
        out_shape.append(jax.ShapeDtypeStruct((local_pairs, wide), phases.dtype))
        out_specs.append(pl.BlockSpec((local_pairs, wide), lambda i, t, c: (0, 0)))
    in_specs += [pl.BlockSpec(each.shape, lambda i, t, c: (0, 0)) for each in earlier]
    operands += earlier
    in_specs += [pl.BlockSpec(memory_space=pl.ANY)] * len(after)
    results = pl.pallas_call(
        functools.partial(step_kernel, at, layout, len(earlier), swap is not None, HALVES),
        out_shape=out_shape,
        grid_spec=pltpu.PrefetchScalarGridSpec(
            num_scalar_prefetch=2,
            grid=(1,),
            in_specs=in_specs,
            out_specs=out_specs,
        ),
        compiler_params=pltpu.CompilerParams(vmem_limit_bytes=VMEM_BYTES),
        cost_estimate=STEADY,
        name=f"sum_step_{at:02d}",
    )(*scalars, *operands, *after)
    return results[0], results[1] if swap is not None else None


def coded_specs(piece, tiles, index):
    lots = piece // LANES
    return [
        pl.BlockSpec((lots // tiles * M, LANES), lambda *at: (at[index], 0)),
        pl.BlockSpec((CODE_ROWS, LANES), lambda *at: (lots * M // CODE_ROWS, 0)),
    ]


def add_arrived(sums_ref, refs, tiles):
    lots = sums_ref.shape[1] // LANES
    tile = pl.program_id(0)
    for coded_ref, codes_ref in zip(refs[::2], refs[1::2]):
        parts = [decode(coded_ref, codes_ref, lots, at * lots) for at in range(tiles)]
        scale = functools.reduce(lambda chosen, at: jnp.where(tile == at, parts[at][1], chosen), range(1, tiles), parts[0][1])
        sums_ref[...] += parts[0][0] * scale


def finish_kernel(at, layout, tiles, raw, told, table, counts, pairs_ref, own_ref, partner_ref, inverse_ref, *rest):
    first, middle, last = rest[:2], rest[2:4], rest[4:6]
    sums_ref, rest = rest[-1], rest[:-1]
    if told:
        rest[-1][...] = jnp.zeros_like(rest[-1])
        rest = rest[:-1]
    out_ref = rest[-1]
    count = piece_count(at, layout, table, counts)
    sums_ref[...] = pair_sums(count, table, pairs_ref, own_ref, partner_ref)

    @pl.when(table[INNER] == 0)
    def _():
        if raw:
            sums_ref[...] += near_sums(True, count, table, pairs_ref, first)
        else:
            add_arrived(sums_ref, first, tiles)

    @pl.when(table[INNER] == 1)
    def _():
        add_arrived(sums_ref, middle, tiles)

    add_arrived(sums_ref, last, tiles)
    out_ref[...] = split_product(inverse_ref[0, :M, :M], sums_ref[...])


def finish(at, part, layout, scalars, pairs, phases, partner, inverse, raw, arrived, series, told, pixels, piece):
    partner, place_in = partner
    local_pairs = phases.shape[0]
    blocks = layout[1]
    tiles = HALVES
    tile = piece // tiles
    in_specs = [
        pl.BlockSpec(pairs.shape, lambda i, t, c: (0, 0)),
        pl.BlockSpec((local_pairs, tile), lambda i, t, c: (0, t[blocks + at] * tiles + i)),
        pl.BlockSpec((local_pairs, tile), lambda i, t, c: (0, place_in * tiles + i)),
        pl.BlockSpec((1, PAD, PAD), lambda i, t, c: (part // CUTS, 0, 0)),
    ]
    in_specs += [pl.BlockSpec((local_pairs, tile), lambda i, t, c: (0, i))] * len(raw) + coded_specs(piece, tiles, 0) * len(arrived)
    operands = [*scalars, pairs, phases, partner, inverse, *raw] + [each for each in arrived for _ in range(2)]
    aliases = {}
    if series is not None:
        in_specs.append(pl.BlockSpec(memory_space=pl.ANY))
        aliases = {len(operands): 0}
        operands.append(series)
    out_shape = [jax.ShapeDtypeStruct((M, pixels), F32)]
    out_specs = [pl.BlockSpec((M, tile), lambda i, t, c: (0, part * tiles + i))]
    if told:
        out_shape.append(jax.ShapeDtypeStruct((8, LANES), F32))
        out_specs.append(pl.BlockSpec((8, LANES), lambda i, t, c: (0, 0)))
    return pl.pallas_call(
        functools.partial(finish_kernel, at, layout, tiles, len(raw) > 0, told),
        out_shape=out_shape,
        grid_spec=pltpu.PrefetchScalarGridSpec(
            num_scalar_prefetch=2,
            grid=(tiles,),
            in_specs=in_specs,
            out_specs=out_specs,
            scratch_shapes=[pltpu.VMEM((M, tile), F32)],
        ),
        input_output_aliases=aliases,
        compiler_params=pltpu.CompilerParams(vmem_limit_bytes=VMEM_BYTES),
        cost_estimate=LITTLE,
        name=f"finish_{part}",
    )(*operands)


def line_permutation(links):
    return [(2 * source + side, 2 * target + side) for source, target in links for side in range(2)]


def solve_by_sums(phases, date_pairs, counts_of):
    owner_count = lax.axis_size("ifg")
    line = owner_count // 2
    local_pairs, pixels = phases.shape
    owner_pixels = pixels // owner_count
    runs = counts_of(None).shape[0]
    parts = runs * CUTS
    piece = owner_pixels // parts
    steps = (line - 1) * parts
    me = lax.axis_index("ifg")

    places = np.repeat(np.array(CHUNK_ORDER), parts, axis=1)
    part_of = np.tile(np.arange(parts), line)
    rows = []
    for device in range(owner_count):
        place, side = device // 2, device % 2
        own = (places[place] * 2 + side) * parts + part_of
        away = (places[place] * 2 + 1 - side) * parts + part_of
        shift = (place - places[place]) % line
        rows.append(np.concatenate([[device, device ^ 1, device ^ 2, device ^ 3, int(0 < place < line - 1)], own, away, shift]))
    row = lax.dynamic_index_in_dim(jnp.asarray(np.stack(rows), jnp.int32), me, 0, keepdims=False)
    head, pieces = FIXED, line * parts
    layout = (parts, head, head + pieces, head + 2 * pieces)

    swap = [(i, i ^ 1) for i in range(owner_count)]
    partner_of = {}

    def swapped(away, first, count):
        here = lax.ppermute(away, "ifg", swap)
        partner_of.update({first + place: (here, place) for place in range(count)})

    place, side = me // 2, me % 2
    chunk = jnp.where(place < line // 2, 2 - 2 * place, 7 - 2 * place)

    def first_away(column, part, count, after):
        block = (chunk * 2 + column) * parts + part
        if after is not None:
            block, _ = lax.optimization_barrier((block, after))
        return lax.dynamic_slice(phases, (0, block * piece), (local_pairs, count * piece))

    away = first_away(1 - side, *FIRST_SWAPS[0], None)
    swapped(away, *FIRST_SWAPS[0])
    run_counts = counts_of(away)
    counts = [run_counts]
    for distance in range(1, line):
        links = [(i, (i + distance) % line) for i in range(line)]
        counts.append(lax.ppermute(run_counts, "ifg", line_permutation(links)))
    counts = jnp.concatenate(counts)
    raw_part = parts - 1
    near = line_permutation(SENDS[0][0])
    raw_other = lax.ppermute(first_away(1 - side, raw_part, 1, run_counts), "ifg", near)
    raw_own = lax.ppermute(first_away(side, raw_part, 1, run_counts), "ifg", near)
    swapped(first_away(1 - side, *FIRST_SWAPS[1], counts), *FIRST_SWAPS[1])
    pairs = jnp.concatenate([lax.dynamic_slice(date_pairs, (0, (me ^ at) * local_pairs), (2, local_pairs)) for at in range(4)], axis=1)
    scalars = (row, counts)

    received, sent, coded, series = {raw_part: [raw_own, raw_other]}, [raw_part], None, None

    def finished(part, series, told):
        at = steps + part
        arrived = [received[place * parts + part][-1] for place in range(1 if part == raw_part else 0, line - 1)]
        data = (layout, scalars, pairs, phases, partner_of[at], inverse, raw if part == raw_part else [], arrived)
        return finish(at, part, *data, series, told, owner_pixels, piece)

    for at in [each for each in range(steps) if each != raw_part]:
        earlier = [] if at < parts else raw if at == parts + raw_part else [received[at - parts][0]]
        after = [] if coded is None else [coded]
        after += received[sent[-FLIGHT]] if len(sent) >= FLIGHT else []
        if at in SWAP_WAITS:
            after.append(partner_of[SWAP_WAITS[at]][0])
        if at == RAW_WAIT:
            after.append(raw[1])
        if at == INVERSE_STEP:
            inverse = invert_classes(date_pairs, run_counts, [coded])
            after.append(inverse)
        if at == steps - 1:
            for part in range(FINISHED_AHEAD):
                series, told = finished(part, series, True)
                after.append(told)
        coded, away = step(at, SWAPS.get(at), layout, scalars, pairs, phases, partner_of[at], earlier, after, piece)
        received[at] = [lax.ppermute(coded, "ifg", line_permutation(links)) for links in SENDS[at // parts]]
        sent.append(at)
        if at in SWAPS:
            swapped(away, *SWAPS[at])
        if at == RAW_STEP:
            raw_other, _ = lax.optimization_barrier((raw_other, coded))
            raw = [raw_own, lax.ppermute(raw_other, "ifg", swap)]

    for part in range(FINISHED_AHEAD, parts):
        series = finished(part, series, False)[0]
    return series


def solve_by_blocks(phases, date_pairs, counts_of):
    owner_count = lax.axis_size("ifg")
    local_pairs, pixels = phases.shape
    owner_pixels = pixels // owner_count
    run_counts = counts_of(None)
    outgoing = phases.reshape(local_pairs, owner_count, owner_pixels).transpose(1, 0, 2)
    received = lax.all_to_all(outgoing, "ifg", split_axis=0, concat_axis=0, tiled=True)
    inverse = invert_classes(date_pairs, run_counts, [])
    return sum_solve(run_counts, date_pairs, received.reshape(-1, owner_pixels), inverse)


def local(phases, date_pairs, pair_counts, group_ids):
    local_pairs, _, pixels = phases.shape

    def counts_of(after):
        groups = group_ids if after is None else lax.optimization_barrier((group_ids, after))[0]
        strip_groups = lax.dynamic_index_in_dim(groups, lax.axis_index("grp"), 0, keepdims=False)[::RUN]
        chosen = strip_groups[:, None] == jnp.arange(pair_counts.shape[0], dtype=jnp.int32)
        return jnp.sum(jnp.where(chosen, pair_counts, 0), axis=1)

    line = lax.axis_size("ifg") == 2 * len(CHUNK_ORDER) and group_ids.shape[1] == 2 * RUN
    by_sums = line and 2 * local_pairs > M and local_pairs % LANES == 0 and lax.axis_size("grp") % 2 == 0
    solve = solve_by_sums if by_sums else solve_by_blocks
    return solve(phases.reshape(local_pairs, pixels), date_pairs, counts_of)[None, :, :]


def solution(mesh):
    in_specs = (P("ifg", "grp", None), P(), P(), P(None, "ifg"))
    out_specs = P("grp", None, "ifg")
    return jax.shard_map(local, mesh=mesh, in_specs=in_specs, out_specs=out_specs, check_vma=False)
```

```python
import functools

import jax
import jax.numpy as jnp
import numpy as np
from jax import lax
from jax.experimental import pallas as pl
from jax.experimental.pallas import tpu as pltpu
from jax.sharding import PartitionSpec as P

M = 200
RUN = 8
PAD = 256
SLABS = 8
DAMPING = 1.0
VMEM_BYTES = 48 * 1024 * 1024
F32 = jnp.float32
HIGHEST = lax.Precision.HIGHEST
STEADY = pl.CostEstimate(flops=10_000_000_000, bytes_accessed=30_000_000, transcendentals=0)
LITTLE = pl.CostEstimate(flops=1024, bytes_accessed=1024, transcendentals=0)
CUTS = 2
HALVES = 2
FLIGHT = 2
FIRST_SWAP = (0, 2)
SWAPS = {0: (2, 1), 1: (4, 2), 2: (6, 2), 5: (8, 4), 8: (12, 2), 9: (14, 2)}
SWAP_WAITS = {5: 6, 10: 12}
RAW_STEP, RAW_WAIT = 2, 5
INVERSE_STEP = 5
FINISHED_AHEAD = 1
ME, PARTNER, NEAR, NEAR_PARTNER, INNER, FIXED = 0, 1, 2, 3, 4, 5
LANES = 128
CODE_ROWS = 16
LEVELS = 32700.0
ROUNDER = 1.5 * 2.0**23
CODES_PER_OCTAVE = 128.0
SMALLEST = 2.0**-110
CHUNK_ORDER = ((2, 3, 1, 0), (0, 2, 3, 1), (3, 1, 0, 2), (1, 0, 2, 3))
SENDS = (
    (((0, 1), (1, 0), (2, 3), (3, 2)),),
    (((0, 1), (3, 2)), ((1, 2), (2, 1))),
    (((0, 1), (1, 3), (2, 0), (3, 2)),),
)


def incidence(earlier, later, rows):
    shape = (rows, earlier.shape[1])
    date = lax.broadcasted_iota(jnp.int32, shape, 0)
    return (date == later).astype(F32) - (date == earlier).astype(F32)


def split_product(left, right):
    def halves(value):
        high = value.astype(jnp.bfloat16)
        return high, (value - high.astype(F32)).astype(jnp.bfloat16)

    left_high, left_low = halves(left)
    right_high, right_low = halves(right)
    small = jnp.dot(left_high, right_low, preferred_element_type=F32) + jnp.dot(left_low, right_high, preferred_element_type=F32)
    return jnp.dot(left_high, right_high, preferred_element_type=F32) + small


def full_product(left, right):
    return jnp.dot(left, right, precision=HIGHEST, preferred_element_type=F32)


def inverse_kernel(counts_ref, pairs_ref, *rest):
    out_ref = rest[-1]
    runs = out_ref.shape[0]
    design = incidence(pairs_ref[0:1, :], pairs_ref[1:2, :], PAD)
    pair = lax.broadcasted_iota(jnp.int32, design.shape, 1)
    contract_last = (((1,), (1,)), ((), ()))
    row = lax.broadcasted_iota(jnp.int32, (PAD, PAD), 0)
    col = lax.broadcasted_iota(jnp.int32, (PAD, PAD), 1)
    identity = (row == col).astype(F32)
    grams = []
    for run in range(runs):
        kept = jnp.where(pair < counts_ref[run], design, 0.0).astype(jnp.bfloat16)
        gram = lax.dot_general(kept, kept, contract_last, preferred_element_type=F32)
        grams.append(gram + DAMPING * identity)
    low = DAMPING
    high = 2.0 * functools.reduce(jnp.maximum, [jnp.max(gram) for gram in grams]) - DAMPING
    total, width = high + low, high - low
    scale = 2.0 * total * total - width * width
    starts = tuple((8.0 * total / scale) * identity - (8.0 / scale) * gram for gram in grams)
    needed = 18.0 * scale / (8.0 * high * low)
    steps = jnp.int32(0)
    for power in range(1, 16):
        steps += (needed > float(2**power)).astype(jnp.int32)

    def newton(product, guesses):
        products = [product(gram, guess) for gram, guess in zip(grams, guesses)]
        return tuple(2.0 * guess - product(guess, each) for guess, each in zip(guesses, products))

    full_steps = 1 + (high > 100.0).astype(jnp.int32)
    guesses = lax.fori_loop(0, steps + 1 - full_steps, lambda _, guesses: newton(split_product, guesses), starts)
    guesses = lax.fori_loop(0, full_steps, lambda _, guesses: newton(full_product, guesses), guesses)
    for run, guess in enumerate(guesses):
        out_ref[run] = guess


def invert_classes(date_pairs, run_counts, after):
    shape = (run_counts.shape[0], PAD, PAD)
    return pl.pallas_call(
        inverse_kernel,
        out_shape=jax.ShapeDtypeStruct(shape, F32),
        grid_spec=pltpu.PrefetchScalarGridSpec(
            num_scalar_prefetch=1,
            grid=(1,),
            in_specs=[pl.BlockSpec(date_pairs.shape, lambda i, c: (0, 0))] + [pl.BlockSpec(memory_space=pl.ANY)] * len(after),
            out_specs=pl.BlockSpec(shape, lambda i, c: (0, 0, 0)),
        ),
        compiler_params=pltpu.CompilerParams(vmem_limit_bytes=VMEM_BYTES),
        cost_estimate=LITTLE,
        name="invert_classes_0",
    )(run_counts, date_pairs, *after)


def sum_solve_kernel(tiles, counts_ref, pairs_ref, data_ref, inverse_ref, out_ref):
    run = pl.program_id(0) // tiles
    design = incidence(pairs_ref[0:1, :], pairs_ref[1:2, :], PAD)
    pair = lax.broadcasted_iota(jnp.int32, design.shape, 1)
    kept = jnp.where(pair < counts_ref[run], design, 0.0).astype(jnp.bfloat16)
    sums = jnp.dot(kept, data_ref[...], preferred_element_type=F32)
    out_ref[...] = jnp.dot(inverse_ref[0, :M, :], sums, precision=HIGHEST, preferred_element_type=F32)


def sum_solve(run_counts, date_pairs, received, inverse):
    runs = run_counts.shape[0]
    total_pairs, pixels = received.shape
    run_pixels = pixels // runs
    tile = run_pixels // 2
    tiles = run_pixels // tile
    return pl.pallas_call(
        functools.partial(sum_solve_kernel, tiles),
        out_shape=jax.ShapeDtypeStruct((M, pixels), F32),
        grid_spec=pltpu.PrefetchScalarGridSpec(
            num_scalar_prefetch=1,
            grid=(runs * tiles,),
            in_specs=[
                pl.BlockSpec(date_pairs.shape, lambda i, c: (0, 0)),
                pl.BlockSpec((total_pairs, tile), lambda i, c: (0, i)),
                pl.BlockSpec((1, PAD, PAD), lambda i, c: (i // tiles, 0, 0)),
            ],
            out_specs=pl.BlockSpec((M, tile), lambda i, c: (0, i)),
        ),
        compiler_params=pltpu.CompilerParams(vmem_limit_bytes=VMEM_BYTES),
        name="sum_solve",
    )(run_counts, date_pairs, received, inverse)


def coded_rows(piece):
    return M * (piece // LANES) + CODE_ROWS


def decode(coded_ref, codes_ref, lots, first):
    coded = coded_ref[...].astype(jnp.int32).astype(F32)
    values = jnp.concatenate([coded[lot * M : (lot + 1) * M, :] for lot in range(lots)], axis=1)
    codes = codes_ref[...].astype(jnp.int32).astype(F32)
    codes = jnp.concatenate([codes[first + lot : first + lot + 1, :] for lot in range(lots)], axis=1)
    return values, jnp.exp2(codes * (1.0 / CODES_PER_OCTAVE)) * (1.0 / LEVELS)


def encode(sums):
    largest = jnp.max(jnp.abs(sums), axis=0, keepdims=True)
    code = jnp.ceil(jnp.log2(jnp.maximum(largest, SMALLEST)) * CODES_PER_OCTAVE)
    scaled = (sums * (LEVELS / jnp.exp2(code * (1.0 / CODES_PER_OCTAVE))) + ROUNDER) - ROUNDER
    lots = sums.shape[1] // LANES
    return jnp.concatenate([scaled[:, lot * LANES : (lot + 1) * LANES] for lot in range(lots)], axis=0), code


def whole(values):
    return values.astype(jnp.int32).astype(jnp.int16)


def piece_count(at, layout, table, counts):
    parts, _, _, shifts = layout
    run = at % parts // CUTS
    return counts[table[shifts + at] * (parts // CUTS) + run]


def pair_sums(count, table, pairs_ref, first_ref, second_ref, members=(ME, PARTNER)):
    width = first_ref.shape[0]
    lane = lax.broadcasted_iota(jnp.int32, (1, 2 * width), 1)
    pair = jnp.where(lane < width, table[members[0]] * width + lane, table[members[1]] * width + lane - width)
    dates = pairs_ref[:, members[0] * width : (members[0] + 2) * width]
    design = incidence(dates[0:1, :], dates[1:2, :], M)
    kept = jnp.where(pair < count, design, 0.0).astype(jnp.bfloat16)
    data = jnp.concatenate([first_ref[...], second_ref[...]], axis=0)
    return jnp.dot(kept, data, preferred_element_type=F32)


def near_sums(wanted, count, table, pairs_ref, raw_refs):
    return pair_sums(jnp.where(wanted, count, 0), table, pairs_ref, *raw_refs, members=(NEAR, NEAR_PARTNER))


def step_kernel(at, layout, adds, swaps, halves, table, counts, pairs_ref, own_ref, partner_ref, *rest):
    if swaps:
        rest[-1][...] = rest[0][...]
        coded_ref, rest = rest[-2], rest[1:]
    else:
        coded_ref = rest[-1]
    count = piece_count(at, layout, table, counts)
    width = own_ref.shape[1] // halves
    lots = width // LANES
    codes = []
    for half in range(halves):
        part = pl.ds(half * width, width)
        sums = pair_sums(count, table, pairs_ref, own_ref.at[:, part], partner_ref.at[:, part])
        if adds == 1:
            rows = pl.ds(half * lots * M, lots * M)
            values, scale = decode(rest[0].at[rows, :], rest[0].at[halves * lots * M :, :], lots, half * lots)
            sums = sums + values * (scale * table[INNER].astype(F32))
        if adds == 2:
            sums = sums + near_sums(table[INNER] == 1, count, table, pairs_ref, [raw_ref.at[:, part] for raw_ref in rest[:2]])
        scaled, code = encode(sums)
        coded_ref[half * lots * M : (half + 1) * lots * M, :] = whole(scaled)
        codes += [code[:, lot * LANES : (lot + 1) * LANES] for lot in range(lots)]
    codes += [jnp.zeros((CODE_ROWS - len(codes), LANES), F32)]
    coded_ref[halves * lots * M :, :] = whole(jnp.concatenate(codes, axis=0))


def step(at, swap, layout, scalars, pairs, phases, partner, earlier, after, piece):
    partner, place_in = partner
    local_pairs = phases.shape[0]
    _, blocks, away, _ = layout
    coded_shape = (coded_rows(piece), LANES)
    in_specs = [
        pl.BlockSpec(pairs.shape, lambda i, t, c: (0, 0)),
        pl.BlockSpec((local_pairs, piece), lambda i, t, c: (0, t[blocks + at])),
        pl.BlockSpec((local_pairs, piece), lambda i, t, c: (0, place_in)),
    ]
    operands = [pairs, phases, partner]
    out_shape = [jax.ShapeDtypeStruct(coded_shape, jnp.int16)]
    out_specs = [pl.BlockSpec(coded_shape, lambda i, t, c: (0, 0))]
    if swap is not None:
        first, count = swap
        wide = piece * count
        in_specs.append(pl.BlockSpec((local_pairs, wide), lambda i, t, c: (0, t[away + first] // count)))
        operands.append(phases)
        out_shape.append(jax.ShapeDtypeStruct((local_pairs, wide), phases.dtype))
        out_specs.append(pl.BlockSpec((local_pairs, wide), lambda i, t, c: (0, 0)))
    in_specs += [pl.BlockSpec(each.shape, lambda i, t, c: (0, 0)) for each in earlier]
    operands += earlier
    in_specs += [pl.BlockSpec(memory_space=pl.ANY)] * len(after)
    results = pl.pallas_call(
        functools.partial(step_kernel, at, layout, len(earlier), swap is not None, HALVES),
        out_shape=out_shape,
        grid_spec=pltpu.PrefetchScalarGridSpec(
            num_scalar_prefetch=2,
            grid=(1,),
            in_specs=in_specs,
            out_specs=out_specs,
        ),
        compiler_params=pltpu.CompilerParams(vmem_limit_bytes=VMEM_BYTES),
        cost_estimate=STEADY,
        name=f"sum_step_{at:02d}",
    )(*scalars, *operands, *after)
    return results[0], results[1] if swap is not None else None


def coded_specs(piece, tiles, index):
    lots = piece // LANES
    return [
        pl.BlockSpec((lots // tiles * M, LANES), lambda *at: (at[index], 0)),
        pl.BlockSpec((CODE_ROWS, LANES), lambda *at: (lots * M // CODE_ROWS, 0)),
    ]


def add_arrived(sums_ref, refs, tiles):
    lots = sums_ref.shape[1] // LANES
    tile = pl.program_id(0)
    for coded_ref, codes_ref in zip(refs[::2], refs[1::2]):
        parts = [decode(coded_ref, codes_ref, lots, at * lots) for at in range(tiles)]
        scale = functools.reduce(lambda chosen, at: jnp.where(tile == at, parts[at][1], chosen), range(1, tiles), parts[0][1])
        sums_ref[...] += parts[0][0] * scale


def finish_kernel(at, layout, tiles, raw, told, table, counts, pairs_ref, own_ref, partner_ref, inverse_ref, *rest):
    first, middle, last = rest[:2], rest[2:4], rest[4:6]
    sums_ref, rest = rest[-1], rest[:-1]
    if told:
        rest[-1][...] = jnp.zeros_like(rest[-1])
        rest = rest[:-1]
    out_ref = rest[-1]
    count = piece_count(at, layout, table, counts)
    sums_ref[...] = pair_sums(count, table, pairs_ref, own_ref, partner_ref)

    @pl.when(table[INNER] == 0)
    def _():
        if raw:
            sums_ref[...] += near_sums(True, count, table, pairs_ref, first)
        else:
            add_arrived(sums_ref, first, tiles)

    @pl.when(table[INNER] == 1)
    def _():
        add_arrived(sums_ref, middle, tiles)

    add_arrived(sums_ref, last, tiles)
    out_ref[...] = split_product(inverse_ref[0, :M, :M], sums_ref[...])


def finish(at, part, layout, scalars, pairs, phases, partner, inverse, raw, arrived, series, told, pixels, piece):
    partner, place_in = partner
    local_pairs = phases.shape[0]
    blocks = layout[1]
    tiles = HALVES
    tile = piece // tiles
    in_specs = [
        pl.BlockSpec(pairs.shape, lambda i, t, c: (0, 0)),
        pl.BlockSpec((local_pairs, tile), lambda i, t, c: (0, t[blocks + at] * tiles + i)),
        pl.BlockSpec((local_pairs, tile), lambda i, t, c: (0, place_in * tiles + i)),
        pl.BlockSpec((1, PAD, PAD), lambda i, t, c: (part // CUTS, 0, 0)),
    ]
    in_specs += [pl.BlockSpec((local_pairs, tile), lambda i, t, c: (0, i))] * len(raw) + coded_specs(piece, tiles, 0) * len(arrived)
    operands = [*scalars, pairs, phases, partner, inverse, *raw] + [each for each in arrived for _ in range(2)]
    aliases = {}
    if series is not None:
        in_specs.append(pl.BlockSpec(memory_space=pl.ANY))
        aliases = {len(operands): 0}
        operands.append(series)
    out_shape = [jax.ShapeDtypeStruct((M, pixels), F32)]
    out_specs = [pl.BlockSpec((M, tile), lambda i, t, c: (0, part * tiles + i))]
    if told:
        out_shape.append(jax.ShapeDtypeStruct((8, LANES), F32))
        out_specs.append(pl.BlockSpec((8, LANES), lambda i, t, c: (0, 0)))
    return pl.pallas_call(
        functools.partial(finish_kernel, at, layout, tiles, len(raw) > 0, told),
        out_shape=out_shape,
        grid_spec=pltpu.PrefetchScalarGridSpec(
            num_scalar_prefetch=2,
            grid=(tiles,),
            in_specs=in_specs,
            out_specs=out_specs,
            scratch_shapes=[pltpu.VMEM((M, tile), F32)],
        ),
        input_output_aliases=aliases,
        compiler_params=pltpu.CompilerParams(vmem_limit_bytes=VMEM_BYTES),
        cost_estimate=LITTLE,
        name=f"finish_{part}",
    )(*operands)


def line_permutation(links):
    return [(2 * source + side, 2 * target + side) for source, target in links for side in range(2)]


def solve_by_sums(phases, date_pairs, counts_of):
    owner_count = lax.axis_size("ifg")
    line = owner_count // 2
    local_pairs, pixels = phases.shape
    owner_pixels = pixels // owner_count
    runs = counts_of(None).shape[0]
    parts = runs * CUTS
    piece = owner_pixels // parts
    steps = (line - 1) * parts
    me = lax.axis_index("ifg")

    places = np.repeat(np.array(CHUNK_ORDER), parts, axis=1)
    part_of = np.tile(np.arange(parts), line)
    rows = []
    for device in range(owner_count):
        place, side = device // 2, device % 2
        own = (places[place] * 2 + side) * parts + part_of
        away = (places[place] * 2 + 1 - side) * parts + part_of
        shift = (place - places[place]) % line
        rows.append(np.concatenate([[device, device ^ 1, device ^ 2, device ^ 3, int(0 < place < line - 1)], own, away, shift]))
    row = lax.dynamic_index_in_dim(jnp.asarray(np.stack(rows), jnp.int32), me, 0, keepdims=False)
    head, pieces = FIXED, line * parts
    layout = (parts, head, head + pieces, head + 2 * pieces)

    swap = [(i, i ^ 1) for i in range(owner_count)]
    partner_of = {}

    def swapped(away, first, count):
        here = lax.ppermute(away, "ifg", swap)
        partner_of.update({first + place: (here, place) for place in range(count)})

    place, side = me // 2, me % 2
    chunk = jnp.where(place < line // 2, 2 - 2 * place, 7 - 2 * place)

    def first_away(column, part, count, after):
        block = (chunk * 2 + column) * parts + part
        if after is not None:
            block, _ = lax.optimization_barrier((block, after))
        return lax.dynamic_slice(phases, (0, block * piece), (local_pairs, count * piece))

    away = first_away(1 - side, *FIRST_SWAP, None)
    swapped(away, *FIRST_SWAP)
    run_counts = counts_of(away)
    counts = [run_counts]
    for distance in range(1, line):
        links = [(i, (i + distance) % line) for i in range(line)]
        counts.append(lax.ppermute(run_counts, "ifg", line_permutation(links)))
    counts = jnp.concatenate(counts)
    raw_part = parts - 1
    near = line_permutation(SENDS[0][0])
    raw_other = lax.ppermute(first_away(1 - side, raw_part, 1, run_counts), "ifg", near)
    raw_own = lax.ppermute(first_away(side, raw_part, 1, run_counts), "ifg", near)
    pairs = jnp.concatenate([lax.dynamic_slice(date_pairs, (0, (me ^ at) * local_pairs), (2, local_pairs)) for at in range(4)], axis=1)
    scalars = (row, counts)

    received, sent, coded, series = {raw_part: [raw_own, raw_other]}, [raw_part], None, None

    def finished(part, series, told):
        at = steps + part
        arrived = [received[place * parts + part][-1] for place in range(1 if part == raw_part else 0, line - 1)]
        data = (layout, scalars, pairs, phases, partner_of[at], inverse, raw if part == raw_part else [], arrived)
        return finish(at, part, *data, series, told, owner_pixels, piece)

    for at in [each for each in range(steps) if each != raw_part]:
        earlier = [] if at < parts else raw if at == parts + raw_part else [received[at - parts][0]]
        after = [] if coded is None else [coded]
        after += received[sent[-FLIGHT]] if len(sent) >= FLIGHT else []
        if at in SWAP_WAITS:
            after.append(partner_of[SWAP_WAITS[at]][0])
        if at == RAW_WAIT:
            after.append(raw[1])
        if at == INVERSE_STEP:
            inverse = invert_classes(date_pairs, run_counts, [coded])
            after.append(inverse)
        if at == steps - 1:
            for part in range(FINISHED_AHEAD):
                series, told = finished(part, series, True)
                after.append(told)
        coded, away = step(at, SWAPS.get(at), layout, scalars, pairs, phases, partner_of[at], earlier, after, piece)
        received[at] = [lax.ppermute(coded, "ifg", line_permutation(links)) for links in SENDS[at // parts]]
        sent.append(at)
        if at in SWAPS:
            swapped(away, *SWAPS[at])
        if at == RAW_STEP:
            raw_other, _ = lax.optimization_barrier((raw_other, coded))
            raw = [raw_own, lax.ppermute(raw_other, "ifg", swap)]

    for part in range(FINISHED_AHEAD, parts):
        series = finished(part, series, False)[0]
    return series


def solve_by_blocks(phases, date_pairs, counts_of):
    owner_count = lax.axis_size("ifg")
    local_pairs, pixels = phases.shape
    owner_pixels = pixels // owner_count
    run_counts = counts_of(None)
    outgoing = phases.reshape(local_pairs, owner_count, owner_pixels).transpose(1, 0, 2)
    received = lax.all_to_all(outgoing, "ifg", split_axis=0, concat_axis=0, tiled=True)
    inverse = invert_classes(date_pairs, run_counts, [])
    return sum_solve(run_counts, date_pairs, received.reshape(-1, owner_pixels), inverse)


def local(phases, date_pairs, pair_counts, group_ids):
    local_pairs, _, pixels = phases.shape

    def counts_of(after):
        groups = group_ids if after is None else lax.optimization_barrier((group_ids, after))[0]
        strip_groups = lax.dynamic_index_in_dim(groups, lax.axis_index("grp"), 0, keepdims=False)[::RUN]
        chosen = strip_groups[:, None] == jnp.arange(pair_counts.shape[0], dtype=jnp.int32)
        return jnp.sum(jnp.where(chosen, pair_counts, 0), axis=1)

    line = lax.axis_size("ifg") == 2 * len(CHUNK_ORDER) and group_ids.shape[1] == 2 * RUN
    by_sums = line and 2 * local_pairs > M and local_pairs % LANES == 0 and lax.axis_size("grp") % 2 == 0
    solve = solve_by_sums if by_sums else solve_by_blocks
    return solve(phases.reshape(local_pairs, pixels), date_pairs, counts_of)[None, :, :]


def solution(mesh):
    in_specs = (P("ifg", "grp", None), P(), P(), P(None, "ifg"))
    out_specs = P("grp", None, "ifg")
    return jax.shard_map(local, mesh=mesh, in_specs=in_specs, out_specs=out_specs, check_vma=False)
```

```python
import functools

import jax
import jax.numpy as jnp
import numpy as np
from jax import lax
from jax.experimental import pallas as pl
from jax.experimental.pallas import tpu as pltpu
from jax.sharding import PartitionSpec as P

M = 200
RUN = 8
PAD = 256
SLABS = 8
DAMPING = 1.0
VMEM_BYTES = 48 * 1024 * 1024
F32 = jnp.float32
HIGHEST = lax.Precision.HIGHEST
STEADY = pl.CostEstimate(flops=10_000_000_000, bytes_accessed=30_000_000, transcendentals=0)
LITTLE = pl.CostEstimate(flops=1024, bytes_accessed=1024, transcendentals=0)
CUTS = 2
HALVES = 2
FLIGHT = 2
FIRST_SWAP = (0, 2)
SWAPS = {0: (2, 1), 1: (4, 2), 2: (6, 2), 6: (8, 2), 8: (10, 2), 9: (12, 2), 10: (14, 2)}
SWAP_WAITS = {}
RAW_STEP, RAW_WAIT = 2, 5
INVERSE_STEP = 0
FINISHED_AHEAD = 1
ME, PARTNER, NEAR, NEAR_PARTNER, INNER, FIXED = 0, 1, 2, 3, 4, 5
LANES = 128
CODE_ROWS = 16
LEVELS = 32700.0
ROUNDER = 1.5 * 2.0**23
CODES_PER_OCTAVE = 128.0
SMALLEST = 2.0**-110
CHUNK_ORDER = ((2, 3, 1, 0), (0, 2, 3, 1), (3, 1, 0, 2), (1, 0, 2, 3))
SENDS = (
    (((0, 1), (1, 0), (2, 3), (3, 2)),),
    (((0, 1), (3, 2)), ((1, 2), (2, 1))),
    (((0, 1), (1, 3), (2, 0), (3, 2)),),
)


def incidence(earlier, later, rows):
    shape = (rows, earlier.shape[1])
    date = lax.broadcasted_iota(jnp.int32, shape, 0)
    return (date == later).astype(F32) - (date == earlier).astype(F32)


def split_product(left, right):
    def halves(value):
        high = value.astype(jnp.bfloat16)
        return high, (value - high.astype(F32)).astype(jnp.bfloat16)

    left_high, left_low = halves(left)
    right_high, right_low = halves(right)
    small = jnp.dot(left_high, right_low, preferred_element_type=F32) + jnp.dot(left_low, right_high, preferred_element_type=F32)
    return jnp.dot(left_high, right_high, preferred_element_type=F32) + small


def full_product(left, right):
    return jnp.dot(left, right, precision=HIGHEST, preferred_element_type=F32)


def inverse_kernel(counts_ref, pairs_ref, *rest):
    out_ref = rest[-1]
    runs = out_ref.shape[0]
    design = incidence(pairs_ref[0:1, :], pairs_ref[1:2, :], PAD)
    pair = lax.broadcasted_iota(jnp.int32, design.shape, 1)
    contract_last = (((1,), (1,)), ((), ()))
    row = lax.broadcasted_iota(jnp.int32, (PAD, PAD), 0)
    col = lax.broadcasted_iota(jnp.int32, (PAD, PAD), 1)
    identity = (row == col).astype(F32)
    grams = []
    for run in range(runs):
        kept = jnp.where(pair < counts_ref[run], design, 0.0).astype(jnp.bfloat16)
        gram = lax.dot_general(kept, kept, contract_last, preferred_element_type=F32)
        grams.append(gram + DAMPING * identity)
    low = DAMPING
    high = 2.0 * functools.reduce(jnp.maximum, [jnp.max(gram) for gram in grams]) - DAMPING
    total, width = high + low, high - low
    scale = 2.0 * total * total - width * width
    starts = tuple((8.0 * total / scale) * identity - (8.0 / scale) * gram for gram in grams)
    needed = 18.0 * scale / (8.0 * high * low)
    steps = jnp.int32(0)
    for power in range(1, 16):
        steps += (needed > float(2**power)).astype(jnp.int32)

    def newton(product, guesses):
        products = [product(gram, guess) for gram, guess in zip(grams, guesses)]
        return tuple(2.0 * guess - product(guess, each) for guess, each in zip(guesses, products))

    full_steps = 1 + (high > 100.0).astype(jnp.int32)
    guesses = lax.fori_loop(0, steps + 1 - full_steps, lambda _, guesses: newton(split_product, guesses), starts)
    guesses = lax.fori_loop(0, full_steps, lambda _, guesses: newton(full_product, guesses), guesses)
    for run, guess in enumerate(guesses):
        out_ref[run] = guess


def invert_classes(date_pairs, run_counts, after):
    shape = (run_counts.shape[0], PAD, PAD)
    return pl.pallas_call(
        inverse_kernel,
        out_shape=jax.ShapeDtypeStruct(shape, F32),
        grid_spec=pltpu.PrefetchScalarGridSpec(
            num_scalar_prefetch=1,
            grid=(1,),
            in_specs=[pl.BlockSpec(date_pairs.shape, lambda i, c: (0, 0))] + [pl.BlockSpec(memory_space=pl.ANY)] * len(after),
            out_specs=pl.BlockSpec(shape, lambda i, c: (0, 0, 0)),
        ),
        compiler_params=pltpu.CompilerParams(vmem_limit_bytes=VMEM_BYTES),
        cost_estimate=LITTLE,
        name="invert_classes_0",
    )(run_counts, date_pairs, *after)


def sum_solve_kernel(tiles, counts_ref, pairs_ref, data_ref, inverse_ref, out_ref):
    run = pl.program_id(0) // tiles
    design = incidence(pairs_ref[0:1, :], pairs_ref[1:2, :], PAD)
    pair = lax.broadcasted_iota(jnp.int32, design.shape, 1)
    kept = jnp.where(pair < counts_ref[run], design, 0.0).astype(jnp.bfloat16)
    sums = jnp.dot(kept, data_ref[...], preferred_element_type=F32)
    out_ref[...] = jnp.dot(inverse_ref[0, :M, :], sums, precision=HIGHEST, preferred_element_type=F32)


def sum_solve(run_counts, date_pairs, received, inverse):
    runs = run_counts.shape[0]
    total_pairs, pixels = received.shape
    run_pixels = pixels // runs
    tile = run_pixels // 2
    tiles = run_pixels // tile
    return pl.pallas_call(
        functools.partial(sum_solve_kernel, tiles),
        out_shape=jax.ShapeDtypeStruct((M, pixels), F32),
        grid_spec=pltpu.PrefetchScalarGridSpec(
            num_scalar_prefetch=1,
            grid=(runs * tiles,),
            in_specs=[
                pl.BlockSpec(date_pairs.shape, lambda i, c: (0, 0)),
                pl.BlockSpec((total_pairs, tile), lambda i, c: (0, i)),
                pl.BlockSpec((1, PAD, PAD), lambda i, c: (i // tiles, 0, 0)),
            ],
            out_specs=pl.BlockSpec((M, tile), lambda i, c: (0, i)),
        ),
        compiler_params=pltpu.CompilerParams(vmem_limit_bytes=VMEM_BYTES),
        name="sum_solve",
    )(run_counts, date_pairs, received, inverse)


def coded_rows(piece):
    return M * (piece // LANES) + CODE_ROWS


def decode(coded_ref, codes_ref, lots, first):
    coded = coded_ref[...].astype(jnp.int32).astype(F32)
    values = jnp.concatenate([coded[lot * M : (lot + 1) * M, :] for lot in range(lots)], axis=1)
    codes = codes_ref[...].astype(jnp.int32).astype(F32)
    codes = jnp.concatenate([codes[first + lot : first + lot + 1, :] for lot in range(lots)], axis=1)
    return values, jnp.exp2(codes * (1.0 / CODES_PER_OCTAVE)) * (1.0 / LEVELS)


def encode(sums):
    largest = jnp.max(jnp.abs(sums), axis=0, keepdims=True)
    code = jnp.ceil(jnp.log2(jnp.maximum(largest, SMALLEST)) * CODES_PER_OCTAVE)
    scaled = (sums * (LEVELS / jnp.exp2(code * (1.0 / CODES_PER_OCTAVE))) + ROUNDER) - ROUNDER
    lots = sums.shape[1] // LANES
    return jnp.concatenate([scaled[:, lot * LANES : (lot + 1) * LANES] for lot in range(lots)], axis=0), code


def whole(values):
    return values.astype(jnp.int32).astype(jnp.int16)


def piece_count(at, layout, table, counts):
    parts, _, _, shifts = layout
    run = at % parts // CUTS
    return counts[table[shifts + at] * (parts // CUTS) + run]


def pair_sums(count, table, pairs_ref, first_ref, second_ref, members=(ME, PARTNER)):
    width = first_ref.shape[0]
    lane = lax.broadcasted_iota(jnp.int32, (1, 2 * width), 1)
    pair = jnp.where(lane < width, table[members[0]] * width + lane, table[members[1]] * width + lane - width)
    dates = pairs_ref[:, members[0] * width : (members[0] + 2) * width]
    design = incidence(dates[0:1, :], dates[1:2, :], M)
    kept = jnp.where(pair < count, design, 0.0).astype(jnp.bfloat16)
    data = jnp.concatenate([first_ref[...], second_ref[...]], axis=0)
    return jnp.dot(kept, data, preferred_element_type=F32)


def near_sums(wanted, count, table, pairs_ref, raw_refs):
    return pair_sums(jnp.where(wanted, count, 0), table, pairs_ref, *raw_refs, members=(NEAR, NEAR_PARTNER))


def step_kernel(at, layout, adds, swaps, halves, table, counts, pairs_ref, own_ref, partner_ref, *rest):
    if swaps:
        rest[-1][...] = rest[0][...]
        coded_ref, rest = rest[-2], rest[1:]
    else:
        coded_ref = rest[-1]
    count = piece_count(at, layout, table, counts)
    width = own_ref.shape[1] // halves
    lots = width // LANES
    codes = []
    for half in range(halves):
        part = pl.ds(half * width, width)
        sums = pair_sums(count, table, pairs_ref, own_ref.at[:, part], partner_ref.at[:, part])
        if adds == 1:
            rows = pl.ds(half * lots * M, lots * M)
            values, scale = decode(rest[0].at[rows, :], rest[0].at[halves * lots * M :, :], lots, half * lots)
            sums = sums + values * (scale * table[INNER].astype(F32))
        if adds == 2:
            sums = sums + near_sums(table[INNER] == 1, count, table, pairs_ref, [raw_ref.at[:, part] for raw_ref in rest[:2]])
        scaled, code = encode(sums)
        coded_ref[half * lots * M : (half + 1) * lots * M, :] = whole(scaled)
        codes += [code[:, lot * LANES : (lot + 1) * LANES] for lot in range(lots)]
    codes += [jnp.zeros((CODE_ROWS - len(codes), LANES), F32)]
    coded_ref[halves * lots * M :, :] = whole(jnp.concatenate(codes, axis=0))


def step(at, swap, layout, scalars, pairs, phases, partner, earlier, after, piece):
    partner, place_in = partner
    local_pairs = phases.shape[0]
    _, blocks, away, _ = layout
    coded_shape = (coded_rows(piece), LANES)
    in_specs = [
        pl.BlockSpec(pairs.shape, lambda i, t, c: (0, 0)),
        pl.BlockSpec((local_pairs, piece), lambda i, t, c: (0, t[blocks + at])),
        pl.BlockSpec((local_pairs, piece), lambda i, t, c: (0, place_in)),
    ]
    operands = [pairs, phases, partner]
    out_shape = [jax.ShapeDtypeStruct(coded_shape, jnp.int16)]
    out_specs = [pl.BlockSpec(coded_shape, lambda i, t, c: (0, 0))]
    if swap is not None:
        first, count = swap
        wide = piece * count
        in_specs.append(pl.BlockSpec((local_pairs, wide), lambda i, t, c: (0, t[away + first] // count)))
        operands.append(phases)
        out_shape.append(jax.ShapeDtypeStruct((local_pairs, wide), phases.dtype))
        out_specs.append(pl.BlockSpec((local_pairs, wide), lambda i, t, c: (0, 0)))
    in_specs += [pl.BlockSpec(each.shape, lambda i, t, c: (0, 0)) for each in earlier]
    operands += earlier
    in_specs += [pl.BlockSpec(memory_space=pl.ANY)] * len(after)
    results = pl.pallas_call(
        functools.partial(step_kernel, at, layout, len(earlier), swap is not None, HALVES),
        out_shape=out_shape,
        grid_spec=pltpu.PrefetchScalarGridSpec(
            num_scalar_prefetch=2,
            grid=(1,),
            in_specs=in_specs,
            out_specs=out_specs,
        ),
        compiler_params=pltpu.CompilerParams(vmem_limit_bytes=VMEM_BYTES),
        cost_estimate=STEADY,
        name=f"sum_step_{at:02d}",
    )(*scalars, *operands, *after)
    return results[0], results[1] if swap is not None else None


def coded_specs(piece, tiles, index):
    lots = piece // LANES
    return [
        pl.BlockSpec((lots // tiles * M, LANES), lambda *at: (at[index], 0)),
        pl.BlockSpec((CODE_ROWS, LANES), lambda *at: (lots * M // CODE_ROWS, 0)),
    ]


def add_arrived(sums_ref, refs, tiles):
    lots = sums_ref.shape[1] // LANES
    tile = pl.program_id(0)
    for coded_ref, codes_ref in zip(refs[::2], refs[1::2]):
        parts = [decode(coded_ref, codes_ref, lots, at * lots) for at in range(tiles)]
        scale = functools.reduce(lambda chosen, at: jnp.where(tile == at, parts[at][1], chosen), range(1, tiles), parts[0][1])
        sums_ref[...] += parts[0][0] * scale


def finish_kernel(at, layout, tiles, raw, told, table, counts, pairs_ref, own_ref, partner_ref, inverse_ref, *rest):
    first, middle, last = rest[:2], rest[2:4], rest[4:6]
    sums_ref, rest = rest[-1], rest[:-1]
    if told:
        rest[-1][...] = jnp.zeros_like(rest[-1])
        rest = rest[:-1]
    out_ref = rest[-1]
    count = piece_count(at, layout, table, counts)
    sums_ref[...] = pair_sums(count, table, pairs_ref, own_ref, partner_ref)

    @pl.when(table[INNER] == 0)
    def _():
        if raw:
            sums_ref[...] += near_sums(True, count, table, pairs_ref, first)
        else:
            add_arrived(sums_ref, first, tiles)

    @pl.when(table[INNER] == 1)
    def _():
        add_arrived(sums_ref, middle, tiles)

    add_arrived(sums_ref, last, tiles)
    out_ref[...] = split_product(inverse_ref[0, :M, :M], sums_ref[...])


def finish(at, part, layout, scalars, pairs, phases, partner, inverse, raw, arrived, series, told, pixels, piece):
    partner, place_in = partner
    local_pairs = phases.shape[0]
    blocks = layout[1]
    tiles = HALVES
    tile = piece // tiles
    in_specs = [
        pl.BlockSpec(pairs.shape, lambda i, t, c: (0, 0)),
        pl.BlockSpec((local_pairs, tile), lambda i, t, c: (0, t[blocks + at] * tiles + i)),
        pl.BlockSpec((local_pairs, tile), lambda i, t, c: (0, place_in * tiles + i)),
        pl.BlockSpec((1, PAD, PAD), lambda i, t, c: (part // CUTS, 0, 0)),
    ]
    in_specs += [pl.BlockSpec((local_pairs, tile), lambda i, t, c: (0, i))] * len(raw) + coded_specs(piece, tiles, 0) * len(arrived)
    operands = [*scalars, pairs, phases, partner, inverse, *raw] + [each for each in arrived for _ in range(2)]
    aliases = {}
    if series is not None:
        in_specs.append(pl.BlockSpec(memory_space=pl.ANY))
        aliases = {len(operands): 0}
        operands.append(series)
    out_shape = [jax.ShapeDtypeStruct((M, pixels), F32)]
    out_specs = [pl.BlockSpec((M, tile), lambda i, t, c: (0, part * tiles + i))]
    if told:
        out_shape.append(jax.ShapeDtypeStruct((8, LANES), F32))
        out_specs.append(pl.BlockSpec((8, LANES), lambda i, t, c: (0, 0)))
    return pl.pallas_call(
        functools.partial(finish_kernel, at, layout, tiles, len(raw) > 0, told),
        out_shape=out_shape,
        grid_spec=pltpu.PrefetchScalarGridSpec(
            num_scalar_prefetch=2,
            grid=(tiles,),
            in_specs=in_specs,
            out_specs=out_specs,
            scratch_shapes=[pltpu.VMEM((M, tile), F32)],
        ),
        input_output_aliases=aliases,
        compiler_params=pltpu.CompilerParams(vmem_limit_bytes=VMEM_BYTES),
        cost_estimate=LITTLE,
        name=f"finish_{part}",
    )(*operands)


def line_permutation(links):
    return [(2 * source + side, 2 * target + side) for source, target in links for side in range(2)]


def solve_by_sums(phases, date_pairs, counts_of):
    owner_count = lax.axis_size("ifg")
    line = owner_count // 2
    local_pairs, pixels = phases.shape
    owner_pixels = pixels // owner_count
    runs = counts_of(None).shape[0]
    parts = runs * CUTS
    piece = owner_pixels // parts
    steps = (line - 1) * parts
    me = lax.axis_index("ifg")

    places = np.repeat(np.array(CHUNK_ORDER), parts, axis=1)
    part_of = np.tile(np.arange(parts), line)
    rows = []
    for device in range(owner_count):
        place, side = device // 2, device % 2
        own = (places[place] * 2 + side) * parts + part_of
        away = (places[place] * 2 + 1 - side) * parts + part_of
        shift = (place - places[place]) % line
        rows.append(np.concatenate([[device, device ^ 1, device ^ 2, device ^ 3, int(0 < place < line - 1)], own, away, shift]))
    row = lax.dynamic_index_in_dim(jnp.asarray(np.stack(rows), jnp.int32), me, 0, keepdims=False)
    head, pieces = FIXED, line * parts
    layout = (parts, head, head + pieces, head + 2 * pieces)

    swap = [(i, i ^ 1) for i in range(owner_count)]
    partner_of = {}

    def swapped(away, first, count):
        here = lax.ppermute(away, "ifg", swap)
        partner_of.update({first + place: (here, place) for place in range(count)})

    place, side = me // 2, me % 2
    chunk = jnp.where(place < line // 2, 2 - 2 * place, 7 - 2 * place)

    def first_away(column, part, count, after):
        block = (chunk * 2 + column) * parts + part
        if after is not None:
            block, _ = lax.optimization_barrier((block, after))
        return lax.dynamic_slice(phases, (0, block * piece), (local_pairs, count * piece))

    away = first_away(1 - side, *FIRST_SWAP, None)
    swapped(away, *FIRST_SWAP)
    run_counts = counts_of(away)
    counts = [run_counts]
    for distance in range(1, line):
        links = [(i, (i + distance) % line) for i in range(line)]
        counts.append(lax.ppermute(run_counts, "ifg", line_permutation(links)))
    counts = jnp.concatenate(counts)
    raw_part = parts - 1
    near = line_permutation(SENDS[0][0])
    raw_other = lax.ppermute(first_away(1 - side, raw_part, 1, run_counts), "ifg", near)
    raw_own = lax.ppermute(first_away(side, raw_part, 1, run_counts), "ifg", near)
    pairs = jnp.concatenate([lax.dynamic_slice(date_pairs, (0, (me ^ at) * local_pairs), (2, local_pairs)) for at in range(4)], axis=1)
    scalars = (row, counts)

    received, sent, coded, series = {raw_part: [raw_own, raw_other]}, [raw_part], None, None

    def finished(part, series, told):
        at = steps + part
        arrived = [received[place * parts + part][-1] for place in range(1 if part == raw_part else 0, line - 1)]
        data = (layout, scalars, pairs, phases, partner_of[at], inverse, raw if part == raw_part else [], arrived)
        return finish(at, part, *data, series, told, owner_pixels, piece)

    for at in [each for each in range(steps) if each != raw_part]:
        earlier = [] if at < parts else raw if at == parts + raw_part else [received[at - parts][0]]
        after = [] if coded is None else [coded]
        after += received[sent[-FLIGHT]] if len(sent) >= FLIGHT else []
        if at in SWAP_WAITS:
            after.append(partner_of[SWAP_WAITS[at]][0])
        if at == RAW_WAIT:
            after.append(raw[1])
        if at == INVERSE_STEP:
            inverse = invert_classes(date_pairs, run_counts, [counts if coded is None else coded])
            after.append(inverse)
        if at == steps - 1:
            for part in range(FINISHED_AHEAD):
                series, told = finished(part, series, True)
                after.append(told)
        coded, away = step(at, SWAPS.get(at), layout, scalars, pairs, phases, partner_of[at], earlier, after, piece)
        received[at] = [lax.ppermute(coded, "ifg", line_permutation(links)) for links in SENDS[at // parts]]
        sent.append(at)
        if at in SWAPS:
            swapped(away, *SWAPS[at])
        if at == RAW_STEP:
            raw_other, _ = lax.optimization_barrier((raw_other, coded))
            raw = [raw_own, lax.ppermute(raw_other, "ifg", swap)]

    for part in range(FINISHED_AHEAD, parts):
        series = finished(part, series, False)[0]
    return series


def solve_by_blocks(phases, date_pairs, counts_of):
    owner_count = lax.axis_size("ifg")
    local_pairs, pixels = phases.shape
    owner_pixels = pixels // owner_count
    run_counts = counts_of(None)
    outgoing = phases.reshape(local_pairs, owner_count, owner_pixels).transpose(1, 0, 2)
    received = lax.all_to_all(outgoing, "ifg", split_axis=0, concat_axis=0, tiled=True)
    inverse = invert_classes(date_pairs, run_counts, [])
    return sum_solve(run_counts, date_pairs, received.reshape(-1, owner_pixels), inverse)


def local(phases, date_pairs, pair_counts, group_ids):
    local_pairs, _, pixels = phases.shape

    def counts_of(after):
        groups = group_ids if after is None else lax.optimization_barrier((group_ids, after))[0]
        strip_groups = lax.dynamic_index_in_dim(groups, lax.axis_index("grp"), 0, keepdims=False)[::RUN]
        chosen = strip_groups[:, None] == jnp.arange(pair_counts.shape[0], dtype=jnp.int32)
        return jnp.sum(jnp.where(chosen, pair_counts, 0), axis=1)

    line = lax.axis_size("ifg") == 2 * len(CHUNK_ORDER) and group_ids.shape[1] == 2 * RUN
    by_sums = line and 2 * local_pairs > M and local_pairs % LANES == 0 and lax.axis_size("grp") % 2 == 0
    solve = solve_by_sums if by_sums else solve_by_blocks
    return solve(phases.reshape(local_pairs, pixels), date_pairs, counts_of)[None, :, :]


def solution(mesh):
    in_specs = (P("ifg", "grp", None), P(), P(), P(None, "ifg"))
    out_specs = P("grp", None, "ifg")
    return jax.shard_map(local, mesh=mesh, in_specs=in_specs, out_specs=out_specs, check_vma=False)
```

```python
import functools

import jax
import jax.numpy as jnp
import numpy as np
from jax import lax
from jax.experimental import pallas as pl
from jax.experimental.pallas import tpu as pltpu
from jax.sharding import PartitionSpec as P

M = 200
RUN = 8
PAD = 256
SLABS = 8
DAMPING = 1.0
VMEM_BYTES = 48 * 1024 * 1024
F32 = jnp.float32
HIGHEST = lax.Precision.HIGHEST
STEADY = pl.CostEstimate(flops=10_000_000_000, bytes_accessed=30_000_000, transcendentals=0)
LITTLE = pl.CostEstimate(flops=1024, bytes_accessed=1024, transcendentals=0)
CUTS = 2
HALVES = 2
FLIGHT = 2
FIRST_SWAP = (0, 2)
SWAPS = {0: (2, 1), 1: (4, 2), 2: (6, 2), 6: (8, 2), 7: (10, 2), 8: (12, 2), 9: (14, 2)}
SWAP_WAITS = {}
RAW_STEP, RAW_WAIT = 2, 5
INVERSE_STEP = 0
FINISHED_AHEAD = 0
ME, PARTNER, NEAR, NEAR_PARTNER, INNER, FIXED = 0, 1, 2, 3, 4, 5
LANES = 128
CODE_ROWS = 16
LEVELS = 32700.0
ROUNDER = 1.5 * 2.0**23
CODES_PER_OCTAVE = 128.0
SMALLEST = 2.0**-110
CHUNK_ORDER = ((2, 3, 1, 0), (0, 2, 3, 1), (3, 1, 0, 2), (1, 0, 2, 3))
SENDS = (
    (((0, 1), (1, 0), (2, 3), (3, 2)),),
    (((0, 1), (3, 2)), ((1, 2), (2, 1))),
    (((0, 1), (1, 3), (2, 0), (3, 2)),),
)


def incidence(earlier, later, rows):
    shape = (rows, earlier.shape[1])
    date = lax.broadcasted_iota(jnp.int32, shape, 0)
    return (date == later).astype(F32) - (date == earlier).astype(F32)


def split_product(left, right):
    def halves(value):
        high = value.astype(jnp.bfloat16)
        return high, (value - high.astype(F32)).astype(jnp.bfloat16)

    left_high, left_low = halves(left)
    right_high, right_low = halves(right)
    small = jnp.dot(left_high, right_low, preferred_element_type=F32) + jnp.dot(left_low, right_high, preferred_element_type=F32)
    return jnp.dot(left_high, right_high, preferred_element_type=F32) + small


def full_product(left, right):
    return jnp.dot(left, right, precision=HIGHEST, preferred_element_type=F32)


def inverse_kernel(counts_ref, pairs_ref, *rest):
    out_ref = rest[-1]
    runs = out_ref.shape[0]
    design = incidence(pairs_ref[0:1, :], pairs_ref[1:2, :], PAD)
    pair = lax.broadcasted_iota(jnp.int32, design.shape, 1)
    contract_last = (((1,), (1,)), ((), ()))
    row = lax.broadcasted_iota(jnp.int32, (PAD, PAD), 0)
    col = lax.broadcasted_iota(jnp.int32, (PAD, PAD), 1)
    identity = (row == col).astype(F32)
    grams = []
    for run in range(runs):
        kept = jnp.where(pair < counts_ref[run], design, 0.0).astype(jnp.bfloat16)
        gram = lax.dot_general(kept, kept, contract_last, preferred_element_type=F32)
        grams.append(gram + DAMPING * identity)
    low = DAMPING
    high = 2.0 * functools.reduce(jnp.maximum, [jnp.max(gram) for gram in grams]) - DAMPING
    total, width = high + low, high - low
    scale = 2.0 * total * total - width * width
    starts = tuple((8.0 * total / scale) * identity - (8.0 / scale) * gram for gram in grams)
    needed = 18.0 * scale / (8.0 * high * low)
    steps = jnp.int32(0)
    for power in range(1, 16):
        steps += (needed > float(2**power)).astype(jnp.int32)

    def newton(product, guesses):
        products = [product(gram, guess) for gram, guess in zip(grams, guesses)]
        return tuple(2.0 * guess - product(guess, each) for guess, each in zip(guesses, products))

    full_steps = 1 + (high > 100.0).astype(jnp.int32)
    guesses = lax.fori_loop(0, steps + 1 - full_steps, lambda _, guesses: newton(split_product, guesses), starts)
    guesses = lax.fori_loop(0, full_steps, lambda _, guesses: newton(full_product, guesses), guesses)
    for run, guess in enumerate(guesses):
        out_ref[run] = guess


def invert_classes(date_pairs, run_counts, after):
    shape = (run_counts.shape[0], PAD, PAD)
    return pl.pallas_call(
        inverse_kernel,
        out_shape=jax.ShapeDtypeStruct(shape, F32),
        grid_spec=pltpu.PrefetchScalarGridSpec(
            num_scalar_prefetch=1,
            grid=(1,),
            in_specs=[pl.BlockSpec(date_pairs.shape, lambda i, c: (0, 0))] + [pl.BlockSpec(memory_space=pl.ANY)] * len(after),
            out_specs=pl.BlockSpec(shape, lambda i, c: (0, 0, 0)),
        ),
        compiler_params=pltpu.CompilerParams(vmem_limit_bytes=VMEM_BYTES),
        cost_estimate=LITTLE,
        name="invert_classes_0",
    )(run_counts, date_pairs, *after)


def sum_solve_kernel(tiles, counts_ref, pairs_ref, data_ref, inverse_ref, out_ref):
    run = pl.program_id(0) // tiles
    design = incidence(pairs_ref[0:1, :], pairs_ref[1:2, :], PAD)
    pair = lax.broadcasted_iota(jnp.int32, design.shape, 1)
    kept = jnp.where(pair < counts_ref[run], design, 0.0).astype(jnp.bfloat16)
    sums = jnp.dot(kept, data_ref[...], preferred_element_type=F32)
    out_ref[...] = jnp.dot(inverse_ref[0, :M, :], sums, precision=HIGHEST, preferred_element_type=F32)


def sum_solve(run_counts, date_pairs, received, inverse):
    runs = run_counts.shape[0]
    total_pairs, pixels = received.shape
    run_pixels = pixels // runs
    tile = run_pixels // 2
    tiles = run_pixels // tile
    return pl.pallas_call(
        functools.partial(sum_solve_kernel, tiles),
        out_shape=jax.ShapeDtypeStruct((M, pixels), F32),
        grid_spec=pltpu.PrefetchScalarGridSpec(
            num_scalar_prefetch=1,
            grid=(runs * tiles,),
            in_specs=[
                pl.BlockSpec(date_pairs.shape, lambda i, c: (0, 0)),
                pl.BlockSpec((total_pairs, tile), lambda i, c: (0, i)),
                pl.BlockSpec((1, PAD, PAD), lambda i, c: (i // tiles, 0, 0)),
            ],
            out_specs=pl.BlockSpec((M, tile), lambda i, c: (0, i)),
        ),
        compiler_params=pltpu.CompilerParams(vmem_limit_bytes=VMEM_BYTES),
        name="sum_solve",
    )(run_counts, date_pairs, received, inverse)


def coded_rows(piece):
    return M * (piece // LANES) + CODE_ROWS


def decode(coded_ref, codes_ref, lots, first):
    coded = coded_ref[...].astype(jnp.int32).astype(F32)
    values = jnp.concatenate([coded[lot * M : (lot + 1) * M, :] for lot in range(lots)], axis=1)
    codes = codes_ref[...].astype(jnp.int32).astype(F32)
    codes = jnp.concatenate([codes[first + lot : first + lot + 1, :] for lot in range(lots)], axis=1)
    return values, jnp.exp2(codes * (1.0 / CODES_PER_OCTAVE)) * (1.0 / LEVELS)


def encode(sums):
    largest = jnp.max(jnp.abs(sums), axis=0, keepdims=True)
    code = jnp.ceil(jnp.log2(jnp.maximum(largest, SMALLEST)) * CODES_PER_OCTAVE)
    scaled = (sums * (LEVELS / jnp.exp2(code * (1.0 / CODES_PER_OCTAVE))) + ROUNDER) - ROUNDER
    lots = sums.shape[1] // LANES
    return jnp.concatenate([scaled[:, lot * LANES : (lot + 1) * LANES] for lot in range(lots)], axis=0), code


def whole(values):
    return values.astype(jnp.int32).astype(jnp.int16)


def piece_count(at, layout, table, counts):
    parts, _, _, shifts = layout
    run = at % parts // CUTS
    return counts[table[shifts + at] * (parts // CUTS) + run]


def pair_sums(count, table, pairs_ref, first_ref, second_ref, members=(ME, PARTNER)):
    width = first_ref.shape[0]
    lane = lax.broadcasted_iota(jnp.int32, (1, 2 * width), 1)
    pair = jnp.where(lane < width, table[members[0]] * width + lane, table[members[1]] * width + lane - width)
    dates = pairs_ref[:, members[0] * width : (members[0] + 2) * width]
    design = incidence(dates[0:1, :], dates[1:2, :], M)
    kept = jnp.where(pair < count, design, 0.0).astype(jnp.bfloat16)
    data = jnp.concatenate([first_ref[...], second_ref[...]], axis=0)
    return jnp.dot(kept, data, preferred_element_type=F32)


def near_sums(wanted, count, table, pairs_ref, raw_refs):
    return pair_sums(jnp.where(wanted, count, 0), table, pairs_ref, *raw_refs, members=(NEAR, NEAR_PARTNER))


def step_kernel(at, layout, adds, swaps, halves, table, counts, pairs_ref, own_ref, partner_ref, *rest):
    if swaps:
        rest[-1][...] = rest[0][...]
        coded_ref, rest = rest[-2], rest[1:]
    else:
        coded_ref = rest[-1]
    count = piece_count(at, layout, table, counts)
    width = own_ref.shape[1] // halves
    lots = width // LANES
    codes = []
    for half in range(halves):
        part = pl.ds(half * width, width)
        sums = pair_sums(count, table, pairs_ref, own_ref.at[:, part], partner_ref.at[:, part])
        if adds == 1:
            rows = pl.ds(half * lots * M, lots * M)
            values, scale = decode(rest[0].at[rows, :], rest[0].at[halves * lots * M :, :], lots, half * lots)
            sums = sums + values * (scale * table[INNER].astype(F32))
        if adds == 2:
            sums = sums + near_sums(table[INNER] == 1, count, table, pairs_ref, [raw_ref.at[:, part] for raw_ref in rest[:2]])
        scaled, code = encode(sums)
        coded_ref[half * lots * M : (half + 1) * lots * M, :] = whole(scaled)
        codes += [code[:, lot * LANES : (lot + 1) * LANES] for lot in range(lots)]
    codes += [jnp.zeros((CODE_ROWS - len(codes), LANES), F32)]
    coded_ref[halves * lots * M :, :] = whole(jnp.concatenate(codes, axis=0))


def step(at, swap, layout, scalars, pairs, phases, partner, earlier, after, piece):
    partner, place_in = partner
    local_pairs = phases.shape[0]
    _, blocks, away, _ = layout
    coded_shape = (coded_rows(piece), LANES)
    in_specs = [
        pl.BlockSpec(pairs.shape, lambda i, t, c: (0, 0)),
        pl.BlockSpec((local_pairs, piece), lambda i, t, c: (0, t[blocks + at])),
        pl.BlockSpec((local_pairs, piece), lambda i, t, c: (0, place_in)),
    ]
    operands = [pairs, phases, partner]
    out_shape = [jax.ShapeDtypeStruct(coded_shape, jnp.int16)]
    out_specs = [pl.BlockSpec(coded_shape, lambda i, t, c: (0, 0))]
    if swap is not None:
        first, count = swap
        wide = piece * count
        in_specs.append(pl.BlockSpec((local_pairs, wide), lambda i, t, c: (0, t[away + first] // count)))
        operands.append(phases)
        out_shape.append(jax.ShapeDtypeStruct((local_pairs, wide), phases.dtype))
        out_specs.append(pl.BlockSpec((local_pairs, wide), lambda i, t, c: (0, 0)))
    in_specs += [pl.BlockSpec(each.shape, lambda i, t, c: (0, 0)) for each in earlier]
    operands += earlier
    in_specs += [pl.BlockSpec(memory_space=pl.ANY)] * len(after)
    results = pl.pallas_call(
        functools.partial(step_kernel, at, layout, len(earlier), swap is not None, HALVES),
        out_shape=out_shape,
        grid_spec=pltpu.PrefetchScalarGridSpec(
            num_scalar_prefetch=2,
            grid=(1,),
            in_specs=in_specs,
            out_specs=out_specs,
        ),
        compiler_params=pltpu.CompilerParams(vmem_limit_bytes=VMEM_BYTES),
        cost_estimate=STEADY,
        name=f"sum_step_{at:02d}",
    )(*scalars, *operands, *after)
    return results[0], results[1] if swap is not None else None


def coded_specs(piece, tiles, index):
    lots = piece // LANES
    return [
        pl.BlockSpec((lots // tiles * M, LANES), lambda *at: (at[index], 0)),
        pl.BlockSpec((CODE_ROWS, LANES), lambda *at: (lots * M // CODE_ROWS, 0)),
    ]


def add_arrived(sums_ref, refs, tiles):
    lots = sums_ref.shape[1] // LANES
    tile = pl.program_id(0)
    for coded_ref, codes_ref in zip(refs[::2], refs[1::2]):
        parts = [decode(coded_ref, codes_ref, lots, at * lots) for at in range(tiles)]
        scale = functools.reduce(lambda chosen, at: jnp.where(tile == at, parts[at][1], chosen), range(1, tiles), parts[0][1])
        sums_ref[...] += parts[0][0] * scale


def finish_kernel(at, layout, tiles, raw, told, table, counts, pairs_ref, own_ref, partner_ref, inverse_ref, *rest):
    first, middle, last = rest[:2], rest[2:4], rest[4:6]
    sums_ref, rest = rest[-1], rest[:-1]
    if told:
        rest[-1][...] = jnp.zeros_like(rest[-1])
        rest = rest[:-1]
    out_ref = rest[-1]
    count = piece_count(at, layout, table, counts)
    sums_ref[...] = pair_sums(count, table, pairs_ref, own_ref, partner_ref)

    @pl.when(table[INNER] == 0)
    def _():
        if raw:
            sums_ref[...] += near_sums(True, count, table, pairs_ref, first)
        else:
            add_arrived(sums_ref, first, tiles)

    @pl.when(table[INNER] == 1)
    def _():
        add_arrived(sums_ref, middle, tiles)

    add_arrived(sums_ref, last, tiles)
    out_ref[...] = split_product(inverse_ref[0, :M, :M], sums_ref[...])


def finish(at, part, layout, scalars, pairs, phases, partner, inverse, raw, arrived, series, told, pixels, piece):
    partner, place_in = partner
    local_pairs = phases.shape[0]
    blocks = layout[1]
    tiles = HALVES
    tile = piece // tiles
    in_specs = [
        pl.BlockSpec(pairs.shape, lambda i, t, c: (0, 0)),
        pl.BlockSpec((local_pairs, tile), lambda i, t, c: (0, t[blocks + at] * tiles + i)),
        pl.BlockSpec((local_pairs, tile), lambda i, t, c: (0, place_in * tiles + i)),
        pl.BlockSpec((1, PAD, PAD), lambda i, t, c: (part // CUTS, 0, 0)),
    ]
    in_specs += [pl.BlockSpec((local_pairs, tile), lambda i, t, c: (0, i))] * len(raw) + coded_specs(piece, tiles, 0) * len(arrived)
    operands = [*scalars, pairs, phases, partner, inverse, *raw] + [each for each in arrived for _ in range(2)]
    aliases = {}
    if series is not None:
        in_specs.append(pl.BlockSpec(memory_space=pl.ANY))
        aliases = {len(operands): 0}
        operands.append(series)
    out_shape = [jax.ShapeDtypeStruct((M, pixels), F32)]
    out_specs = [pl.BlockSpec((M, tile), lambda i, t, c: (0, part * tiles + i))]
    if told:
        out_shape.append(jax.ShapeDtypeStruct((8, LANES), F32))
        out_specs.append(pl.BlockSpec((8, LANES), lambda i, t, c: (0, 0)))
    return pl.pallas_call(
        functools.partial(finish_kernel, at, layout, tiles, len(raw) > 0, told),
        out_shape=out_shape,
        grid_spec=pltpu.PrefetchScalarGridSpec(
            num_scalar_prefetch=2,
            grid=(tiles,),
            in_specs=in_specs,
            out_specs=out_specs,
            scratch_shapes=[pltpu.VMEM((M, tile), F32)],
        ),
        input_output_aliases=aliases,
        compiler_params=pltpu.CompilerParams(vmem_limit_bytes=VMEM_BYTES),
        cost_estimate=LITTLE,
        name=f"finish_{part}",
    )(*operands)


def line_permutation(links):
    return [(2 * source + side, 2 * target + side) for source, target in links for side in range(2)]


def solve_by_sums(phases, date_pairs, counts_of):
    owner_count = lax.axis_size("ifg")
    line = owner_count // 2
    local_pairs, pixels = phases.shape
    owner_pixels = pixels // owner_count
    runs = counts_of(None).shape[0]
    parts = runs * CUTS
    piece = owner_pixels // parts
    steps = (line - 1) * parts
    me = lax.axis_index("ifg")

    places = np.repeat(np.array(CHUNK_ORDER), parts, axis=1)
    part_of = np.tile(np.arange(parts), line)
    rows = []
    for device in range(owner_count):
        place, side = device // 2, device % 2
        own = (places[place] * 2 + side) * parts + part_of
        away = (places[place] * 2 + 1 - side) * parts + part_of
        shift = (place - places[place]) % line
        rows.append(np.concatenate([[device, device ^ 1, device ^ 2, device ^ 3, int(0 < place < line - 1)], own, away, shift]))
    row = lax.dynamic_index_in_dim(jnp.asarray(np.stack(rows), jnp.int32), me, 0, keepdims=False)
    head, pieces = FIXED, line * parts
    layout = (parts, head, head + pieces, head + 2 * pieces)

    swap = [(i, i ^ 1) for i in range(owner_count)]
    partner_of = {}

    def swapped(away, first, count):
        here = lax.ppermute(away, "ifg", swap)
        partner_of.update({first + place: (here, place) for place in range(count)})

    place, side = me // 2, me % 2
    chunk = jnp.where(place < line // 2, 2 - 2 * place, 7 - 2 * place)

    def first_away(column, part, count, after):
        block = (chunk * 2 + column) * parts + part
        if after is not None:
            block, _ = lax.optimization_barrier((block, after))
        return lax.dynamic_slice(phases, (0, block * piece), (local_pairs, count * piece))

    away = first_away(1 - side, *FIRST_SWAP, None)
    swapped(away, *FIRST_SWAP)
    run_counts = counts_of(away)
    counts = [run_counts]
    for distance in range(1, line):
        links = [(i, (i + distance) % line) for i in range(line)]
        counts.append(lax.ppermute(run_counts, "ifg", line_permutation(links)))
    counts = jnp.concatenate(counts)
    raw_part = parts - 1
    near = line_permutation(SENDS[0][0])
    raw_other = lax.ppermute(first_away(1 - side, raw_part, 1, run_counts), "ifg", near)
    raw_own = lax.ppermute(first_away(side, raw_part, 1, run_counts), "ifg", near)
    pairs = jnp.concatenate([lax.dynamic_slice(date_pairs, (0, (me ^ at) * local_pairs), (2, local_pairs)) for at in range(4)], axis=1)
    scalars = (row, counts)

    received, sent, coded, series = {raw_part: [raw_own, raw_other]}, [raw_part], None, None

    def finished(part, series, told):
        at = steps + part
        arrived = [received[place * parts + part][-1] for place in range(1 if part == raw_part else 0, line - 1)]
        data = (layout, scalars, pairs, phases, partner_of[at], inverse, raw if part == raw_part else [], arrived)
        return finish(at, part, *data, series, told, owner_pixels, piece)

    for at in [each for each in range(steps) if each != raw_part]:
        earlier = [] if at < parts else raw if at == parts + raw_part else [received[at - parts][0]]
        after = [] if coded is None else [coded]
        after += received[sent[-FLIGHT]] if len(sent) >= FLIGHT else []
        if at in SWAP_WAITS:
            after.append(partner_of[SWAP_WAITS[at]][0])
        if at == RAW_WAIT:
            after.append(raw[1])
        if at == INVERSE_STEP:
            inverse = invert_classes(date_pairs, run_counts, [counts if coded is None else coded])
            after.append(inverse)
        if at == steps - 1:
            for part in range(FINISHED_AHEAD):
                series, told = finished(part, series, True)
                after.append(told)
        coded, away = step(at, SWAPS.get(at), layout, scalars, pairs, phases, partner_of[at], earlier, after, piece)
        received[at] = [lax.ppermute(coded, "ifg", line_permutation(links)) for links in SENDS[at // parts]]
        sent.append(at)
        if at in SWAPS:
            swapped(away, *SWAPS[at])
        if at == RAW_STEP:
            raw_other, _ = lax.optimization_barrier((raw_other, coded))
            raw = [raw_own, lax.ppermute(raw_other, "ifg", swap)]

    for part in range(FINISHED_AHEAD, parts):
        series = finished(part, series, False)[0]
    return series


def solve_by_blocks(phases, date_pairs, counts_of):
    owner_count = lax.axis_size("ifg")
    local_pairs, pixels = phases.shape
    owner_pixels = pixels // owner_count
    run_counts = counts_of(None)
    outgoing = phases.reshape(local_pairs, owner_count, owner_pixels).transpose(1, 0, 2)
    received = lax.all_to_all(outgoing, "ifg", split_axis=0, concat_axis=0, tiled=True)
    inverse = invert_classes(date_pairs, run_counts, [])
    return sum_solve(run_counts, date_pairs, received.reshape(-1, owner_pixels), inverse)


def local(phases, date_pairs, pair_counts, group_ids):
    local_pairs, _, pixels = phases.shape

    def counts_of(after):
        groups = group_ids if after is None else lax.optimization_barrier((group_ids, after))[0]
        strip_groups = lax.dynamic_index_in_dim(groups, lax.axis_index("grp"), 0, keepdims=False)[::RUN]
        chosen = strip_groups[:, None] == jnp.arange(pair_counts.shape[0], dtype=jnp.int32)
        return jnp.sum(jnp.where(chosen, pair_counts, 0), axis=1)

    line = lax.axis_size("ifg") == 2 * len(CHUNK_ORDER) and group_ids.shape[1] == 2 * RUN
    by_sums = line and 2 * local_pairs > M and local_pairs % LANES == 0 and lax.axis_size("grp") % 2 == 0
    solve = solve_by_sums if by_sums else solve_by_blocks
    return solve(phases.reshape(local_pairs, pixels), date_pairs, counts_of)[None, :, :]


def solution(mesh):
    in_specs = (P("ifg", "grp", None), P(), P(), P(None, "ifg"))
    out_specs = P("grp", None, "ifg")
    return jax.shard_map(local, mesh=mesh, in_specs=in_specs, out_specs=out_specs, check_vma=False)
```

```python
import functools

import jax
import jax.numpy as jnp
import numpy as np
from jax import lax
from jax.experimental import pallas as pl
from jax.experimental.pallas import tpu as pltpu
from jax.sharding import PartitionSpec as P

M = 200
RUN = 8
PAD = 256
SLABS = 8
DAMPING = 1.0
VMEM_BYTES = 48 * 1024 * 1024
F32 = jnp.float32
HIGHEST = lax.Precision.HIGHEST
STEADY = pl.CostEstimate(flops=10_000_000_000, bytes_accessed=30_000_000, transcendentals=0)
LITTLE = pl.CostEstimate(flops=1024, bytes_accessed=1024, transcendentals=0)
CUTS = 2
HALVES = 2
FLIGHT = 2
FIRST_SWAP = (0, 2)
SWAPS = {0: (2, 1), 1: (4, 2), 2: (6, 2), 5: (8, 2), 7: (10, 2), 8: (12, 2), 9: (14, 2)}
SWAP_WAITS = {}
RAW_STEP, RAW_WAIT = 2, 5
INVERSE_STEP = 0
FINISHED_AHEAD = 1
ME, PARTNER, NEAR, NEAR_PARTNER, INNER, FIXED = 0, 1, 2, 3, 4, 5
LANES = 128
CODE_ROWS = 16
LEVELS = 32700.0
ROUNDER = 1.5 * 2.0**23
CODES_PER_OCTAVE = 128.0
SMALLEST = 2.0**-110
CHUNK_ORDER = ((2, 3, 1, 0), (0, 2, 3, 1), (3, 1, 0, 2), (1, 0, 2, 3))
SENDS = (
    (((0, 1), (1, 0), (2, 3), (3, 2)),),
    (((0, 1), (3, 2)), ((1, 2), (2, 1))),
    (((0, 1), (1, 3), (2, 0), (3, 2)),),
)


def incidence(earlier, later, rows):
    shape = (rows, earlier.shape[1])
    date = lax.broadcasted_iota(jnp.int32, shape, 0)
    return (date == later).astype(F32) - (date == earlier).astype(F32)


def split_product(left, right):
    def halves(value):
        high = value.astype(jnp.bfloat16)
        return high, (value - high.astype(F32)).astype(jnp.bfloat16)

    left_high, left_low = halves(left)
    right_high, right_low = halves(right)
    small = jnp.dot(left_high, right_low, preferred_element_type=F32) + jnp.dot(left_low, right_high, preferred_element_type=F32)
    return jnp.dot(left_high, right_high, preferred_element_type=F32) + small


def full_product(left, right):
    return jnp.dot(left, right, precision=HIGHEST, preferred_element_type=F32)


def inverse_kernel(counts_ref, pairs_ref, *rest):
    out_ref = rest[-1]
    runs = out_ref.shape[0]
    design = incidence(pairs_ref[0:1, :], pairs_ref[1:2, :], PAD)
    pair = lax.broadcasted_iota(jnp.int32, design.shape, 1)
    contract_last = (((1,), (1,)), ((), ()))
    row = lax.broadcasted_iota(jnp.int32, (PAD, PAD), 0)
    col = lax.broadcasted_iota(jnp.int32, (PAD, PAD), 1)
    identity = (row == col).astype(F32)
    grams = []
    for run in range(runs):
        kept = jnp.where(pair < counts_ref[run], design, 0.0).astype(jnp.bfloat16)
        gram = lax.dot_general(kept, kept, contract_last, preferred_element_type=F32)
        grams.append(gram + DAMPING * identity)
    low = DAMPING
    high = 2.0 * functools.reduce(jnp.maximum, [jnp.max(gram) for gram in grams]) - DAMPING
    total, width = high + low, high - low
    scale = 2.0 * total * total - width * width
    starts = tuple((8.0 * total / scale) * identity - (8.0 / scale) * gram for gram in grams)
    needed = 18.0 * scale / (8.0 * high * low)
    steps = jnp.int32(0)
    for power in range(1, 16):
        steps += (needed > float(2**power)).astype(jnp.int32)

    def newton(product, guesses):
        products = [product(gram, guess) for gram, guess in zip(grams, guesses)]
        return tuple(2.0 * guess - product(guess, each) for guess, each in zip(guesses, products))

    full_steps = 1 + (high > 100.0).astype(jnp.int32)
    guesses = lax.fori_loop(0, steps + 1 - full_steps, lambda _, guesses: newton(split_product, guesses), starts)
    guesses = lax.fori_loop(0, full_steps, lambda _, guesses: newton(full_product, guesses), guesses)
    for run, guess in enumerate(guesses):
        out_ref[run] = guess


def invert_classes(date_pairs, run_counts, after):
    shape = (run_counts.shape[0], PAD, PAD)
    return pl.pallas_call(
        inverse_kernel,
        out_shape=jax.ShapeDtypeStruct(shape, F32),
        grid_spec=pltpu.PrefetchScalarGridSpec(
            num_scalar_prefetch=1,
            grid=(1,),
            in_specs=[pl.BlockSpec(date_pairs.shape, lambda i, c: (0, 0))] + [pl.BlockSpec(memory_space=pl.ANY)] * len(after),
            out_specs=pl.BlockSpec(shape, lambda i, c: (0, 0, 0)),
        ),
        compiler_params=pltpu.CompilerParams(vmem_limit_bytes=VMEM_BYTES),
        cost_estimate=LITTLE,
        name="invert_classes_0",
    )(run_counts, date_pairs, *after)


def sum_solve_kernel(tiles, counts_ref, pairs_ref, data_ref, inverse_ref, out_ref):
    run = pl.program_id(0) // tiles
    design = incidence(pairs_ref[0:1, :], pairs_ref[1:2, :], PAD)
    pair = lax.broadcasted_iota(jnp.int32, design.shape, 1)
    kept = jnp.where(pair < counts_ref[run], design, 0.0).astype(jnp.bfloat16)
    sums = jnp.dot(kept, data_ref[...], preferred_element_type=F32)
    out_ref[...] = jnp.dot(inverse_ref[0, :M, :], sums, precision=HIGHEST, preferred_element_type=F32)


def sum_solve(run_counts, date_pairs, received, inverse):
    runs = run_counts.shape[0]
    total_pairs, pixels = received.shape
    run_pixels = pixels // runs
    tile = run_pixels // 2
    tiles = run_pixels // tile
    return pl.pallas_call(
        functools.partial(sum_solve_kernel, tiles),
        out_shape=jax.ShapeDtypeStruct((M, pixels), F32),
        grid_spec=pltpu.PrefetchScalarGridSpec(
            num_scalar_prefetch=1,
            grid=(runs * tiles,),
            in_specs=[
                pl.BlockSpec(date_pairs.shape, lambda i, c: (0, 0)),
                pl.BlockSpec((total_pairs, tile), lambda i, c: (0, i)),
                pl.BlockSpec((1, PAD, PAD), lambda i, c: (i // tiles, 0, 0)),
            ],
            out_specs=pl.BlockSpec((M, tile), lambda i, c: (0, i)),
        ),
        compiler_params=pltpu.CompilerParams(vmem_limit_bytes=VMEM_BYTES),
        name="sum_solve",
    )(run_counts, date_pairs, received, inverse)


def coded_rows(piece):
    return M * (piece // LANES) + CODE_ROWS


def decode(coded_ref, codes_ref, lots, first):
    coded = coded_ref[...].astype(jnp.int32).astype(F32)
    values = jnp.concatenate([coded[lot * M : (lot + 1) * M, :] for lot in range(lots)], axis=1)
    codes = codes_ref[...].astype(jnp.int32).astype(F32)
    codes = jnp.concatenate([codes[first + lot : first + lot + 1, :] for lot in range(lots)], axis=1)
    return values, jnp.exp2(codes * (1.0 / CODES_PER_OCTAVE)) * (1.0 / LEVELS)


def encode(sums):
    largest = jnp.max(jnp.abs(sums), axis=0, keepdims=True)
    code = jnp.ceil(jnp.log2(jnp.maximum(largest, SMALLEST)) * CODES_PER_OCTAVE)
    scaled = (sums * (LEVELS / jnp.exp2(code * (1.0 / CODES_PER_OCTAVE))) + ROUNDER) - ROUNDER
    lots = sums.shape[1] // LANES
    return jnp.concatenate([scaled[:, lot * LANES : (lot + 1) * LANES] for lot in range(lots)], axis=0), code


def whole(values):
    return values.astype(jnp.int32).astype(jnp.int16)


def piece_count(at, layout, table, counts):
    parts, _, _, shifts = layout
    run = at % parts // CUTS
    return counts[table[shifts + at] * (parts // CUTS) + run]


def pair_sums(count, table, pairs_ref, first_ref, second_ref, members=(ME, PARTNER)):
    width = first_ref.shape[0]
    lane = lax.broadcasted_iota(jnp.int32, (1, 2 * width), 1)
    pair = jnp.where(lane < width, table[members[0]] * width + lane, table[members[1]] * width + lane - width)
    dates = pairs_ref[:, members[0] * width : (members[0] + 2) * width]
    design = incidence(dates[0:1, :], dates[1:2, :], M)
    kept = jnp.where(pair < count, design, 0.0).astype(jnp.bfloat16)
    data = jnp.concatenate([first_ref[...], second_ref[...]], axis=0)
    return jnp.dot(kept, data, preferred_element_type=F32)


def near_sums(wanted, count, table, pairs_ref, raw_refs):
    return pair_sums(jnp.where(wanted, count, 0), table, pairs_ref, *raw_refs, members=(NEAR, NEAR_PARTNER))


def step_kernel(at, layout, adds, swaps, halves, table, counts, pairs_ref, own_ref, partner_ref, *rest):
    if swaps:
        rest[-1][...] = rest[0][...]
        coded_ref, rest = rest[-2], rest[1:]
    else:
        coded_ref = rest[-1]
    count = piece_count(at, layout, table, counts)
    width = own_ref.shape[1] // halves
    lots = width // LANES
    codes = []
    for half in range(halves):
        part = pl.ds(half * width, width)
        sums = pair_sums(count, table, pairs_ref, own_ref.at[:, part], partner_ref.at[:, part])
        if adds == 1:
            rows = pl.ds(half * lots * M, lots * M)
            values, scale = decode(rest[0].at[rows, :], rest[0].at[halves * lots * M :, :], lots, half * lots)
            sums = sums + values * (scale * table[INNER].astype(F32))
        if adds == 2:
            sums = sums + near_sums(table[INNER] == 1, count, table, pairs_ref, [raw_ref.at[:, part] for raw_ref in rest[:2]])
        scaled, code = encode(sums)
        coded_ref[half * lots * M : (half + 1) * lots * M, :] = whole(scaled)
        codes += [code[:, lot * LANES : (lot + 1) * LANES] for lot in range(lots)]
    codes += [jnp.zeros((CODE_ROWS - len(codes), LANES), F32)]
    coded_ref[halves * lots * M :, :] = whole(jnp.concatenate(codes, axis=0))


def step(at, swap, layout, scalars, pairs, phases, partner, earlier, after, piece):
    partner, place_in = partner
    local_pairs = phases.shape[0]
    _, blocks, away, _ = layout
    coded_shape = (coded_rows(piece), LANES)
    in_specs = [
        pl.BlockSpec(pairs.shape, lambda i, t, c: (0, 0)),
        pl.BlockSpec((local_pairs, piece), lambda i, t, c: (0, t[blocks + at])),
        pl.BlockSpec((local_pairs, piece), lambda i, t, c: (0, place_in)),
    ]
    operands = [pairs, phases, partner]
    out_shape = [jax.ShapeDtypeStruct(coded_shape, jnp.int16)]
    out_specs = [pl.BlockSpec(coded_shape, lambda i, t, c: (0, 0))]
    if swap is not None:
        first, count = swap
        wide = piece * count
        in_specs.append(pl.BlockSpec((local_pairs, wide), lambda i, t, c: (0, t[away + first] // count)))
        operands.append(phases)
        out_shape.append(jax.ShapeDtypeStruct((local_pairs, wide), phases.dtype))
        out_specs.append(pl.BlockSpec((local_pairs, wide), lambda i, t, c: (0, 0)))
    in_specs += [pl.BlockSpec(each.shape, lambda i, t, c: (0, 0)) for each in earlier]
    operands += earlier
    in_specs += [pl.BlockSpec(memory_space=pl.ANY)] * len(after)
    results = pl.pallas_call(
        functools.partial(step_kernel, at, layout, len(earlier), swap is not None, HALVES),
        out_shape=out_shape,
        grid_spec=pltpu.PrefetchScalarGridSpec(
            num_scalar_prefetch=2,
            grid=(1,),
            in_specs=in_specs,
            out_specs=out_specs,
        ),
        compiler_params=pltpu.CompilerParams(vmem_limit_bytes=VMEM_BYTES),
        cost_estimate=STEADY,
        name=f"sum_step_{at:02d}",
    )(*scalars, *operands, *after)
    return results[0], results[1] if swap is not None else None


def coded_specs(piece, tiles, index):
    lots = piece // LANES
    return [
        pl.BlockSpec((lots // tiles * M, LANES), lambda *at: (at[index], 0)),
        pl.BlockSpec((CODE_ROWS, LANES), lambda *at: (lots * M // CODE_ROWS, 0)),
    ]


def add_arrived(sums_ref, refs, tiles):
    lots = sums_ref.shape[1] // LANES
    tile = pl.program_id(0)
    for coded_ref, codes_ref in zip(refs[::2], refs[1::2]):
        parts = [decode(coded_ref, codes_ref, lots, at * lots) for at in range(tiles)]
        scale = functools.reduce(lambda chosen, at: jnp.where(tile == at, parts[at][1], chosen), range(1, tiles), parts[0][1])
        sums_ref[...] += parts[0][0] * scale


def finish_kernel(at, layout, tiles, raw, told, table, counts, pairs_ref, own_ref, partner_ref, inverse_ref, *rest):
    first, middle, last = rest[:2], rest[2:4], rest[4:6]
    sums_ref, rest = rest[-1], rest[:-1]
    if told:
        rest[-1][...] = jnp.zeros_like(rest[-1])
        rest = rest[:-1]
    out_ref = rest[-1]
    count = piece_count(at, layout, table, counts)
    sums_ref[...] = pair_sums(count, table, pairs_ref, own_ref, partner_ref)

    @pl.when(table[INNER] == 0)
    def _():
        if raw:
            sums_ref[...] += near_sums(True, count, table, pairs_ref, first)
        else:
            add_arrived(sums_ref, first, tiles)

    @pl.when(table[INNER] == 1)
    def _():
        add_arrived(sums_ref, middle, tiles)

    add_arrived(sums_ref, last, tiles)
    out_ref[...] = split_product(inverse_ref[0, :M, :M], sums_ref[...])


def finish(at, part, layout, scalars, pairs, phases, partner, inverse, raw, arrived, series, told, pixels, piece):
    partner, place_in = partner
    local_pairs = phases.shape[0]
    blocks = layout[1]
    tiles = HALVES
    tile = piece // tiles
    in_specs = [
        pl.BlockSpec(pairs.shape, lambda i, t, c: (0, 0)),
        pl.BlockSpec((local_pairs, tile), lambda i, t, c: (0, t[blocks + at] * tiles + i)),
        pl.BlockSpec((local_pairs, tile), lambda i, t, c: (0, place_in * tiles + i)),
        pl.BlockSpec((1, PAD, PAD), lambda i, t, c: (part // CUTS, 0, 0)),
    ]
    in_specs += [pl.BlockSpec((local_pairs, tile), lambda i, t, c: (0, i))] * len(raw) + coded_specs(piece, tiles, 0) * len(arrived)
    operands = [*scalars, pairs, phases, partner, inverse, *raw] + [each for each in arrived for _ in range(2)]
    aliases = {}
    if series is not None:
        in_specs.append(pl.BlockSpec(memory_space=pl.ANY))
        aliases = {len(operands): 0}
        operands.append(series)
    out_shape = [jax.ShapeDtypeStruct((M, pixels), F32)]
    out_specs = [pl.BlockSpec((M, tile), lambda i, t, c: (0, part * tiles + i))]
    if told:
        out_shape.append(jax.ShapeDtypeStruct((8, LANES), F32))
        out_specs.append(pl.BlockSpec((8, LANES), lambda i, t, c: (0, 0)))
    return pl.pallas_call(
        functools.partial(finish_kernel, at, layout, tiles, len(raw) > 0, told),
        out_shape=out_shape,
        grid_spec=pltpu.PrefetchScalarGridSpec(
            num_scalar_prefetch=2,
            grid=(tiles,),
            in_specs=in_specs,
            out_specs=out_specs,
            scratch_shapes=[pltpu.VMEM((M, tile), F32)],
        ),
        input_output_aliases=aliases,
        compiler_params=pltpu.CompilerParams(vmem_limit_bytes=VMEM_BYTES),
        cost_estimate=LITTLE,
        name=f"finish_{part}",
    )(*operands)


def line_permutation(links):
    return [(2 * source + side, 2 * target + side) for source, target in links for side in range(2)]


def solve_by_sums(phases, date_pairs, counts_of):
    owner_count = lax.axis_size("ifg")
    line = owner_count // 2
    local_pairs, pixels = phases.shape
    owner_pixels = pixels // owner_count
    runs = counts_of(None).shape[0]
    parts = runs * CUTS
    piece = owner_pixels // parts
    steps = (line - 1) * parts
    me = lax.axis_index("ifg")

    places = np.repeat(np.array(CHUNK_ORDER), parts, axis=1)
    part_of = np.tile(np.arange(parts), line)
    rows = []
    for device in range(owner_count):
        place, side = device // 2, device % 2
        own = (places[place] * 2 + side) * parts + part_of
        away = (places[place] * 2 + 1 - side) * parts + part_of
        shift = (place - places[place]) % line
        rows.append(np.concatenate([[device, device ^ 1, device ^ 2, device ^ 3, int(0 < place < line - 1)], own, away, shift]))
    row = lax.dynamic_index_in_dim(jnp.asarray(np.stack(rows), jnp.int32), me, 0, keepdims=False)
    head, pieces = FIXED, line * parts
    layout = (parts, head, head + pieces, head + 2 * pieces)

    swap = [(i, i ^ 1) for i in range(owner_count)]
    partner_of = {}

    def swapped(away, first, count):
        here = lax.ppermute(away, "ifg", swap)
        partner_of.update({first + place: (here, place) for place in range(count)})

    place, side = me // 2, me % 2
    chunk = jnp.where(place < line // 2, 2 - 2 * place, 7 - 2 * place)

    def first_away(column, part, count, after):
        block = (chunk * 2 + column) * parts + part
        if after is not None:
            block, _ = lax.optimization_barrier((block, after))
        return lax.dynamic_slice(phases, (0, block * piece), (local_pairs, count * piece))

    away = first_away(1 - side, *FIRST_SWAP, None)
    swapped(away, *FIRST_SWAP)
    run_counts = counts_of(away)
    counts = [run_counts]
    for distance in range(1, line):
        links = [(i, (i + distance) % line) for i in range(line)]
        counts.append(lax.ppermute(run_counts, "ifg", line_permutation(links)))
    counts = jnp.concatenate(counts)
    raw_part = parts - 1
    near = line_permutation(SENDS[0][0])
    raw_other = lax.ppermute(first_away(1 - side, raw_part, 1, run_counts), "ifg", near)
    raw_own = lax.ppermute(first_away(side, raw_part, 1, run_counts), "ifg", near)
    pairs = jnp.concatenate([lax.dynamic_slice(date_pairs, (0, (me ^ at) * local_pairs), (2, local_pairs)) for at in range(4)], axis=1)
    scalars = (row, counts)

    received, sent, coded, series = {raw_part: [raw_own, raw_other]}, [raw_part], None, None

    def finished(part, series, told):
        at = steps + part
        arrived = [received[place * parts + part][-1] for place in range(1 if part == raw_part else 0, line - 1)]
        data = (layout, scalars, pairs, phases, partner_of[at], inverse, raw if part == raw_part else [], arrived)
        return finish(at, part, *data, series, told, owner_pixels, piece)

    for at in [each for each in range(steps) if each != raw_part]:
        earlier = [] if at < parts else raw if at == parts + raw_part else [received[at - parts][0]]
        after = [] if coded is None else [coded]
        after += received[sent[-FLIGHT]] if len(sent) >= FLIGHT else []
        if at in SWAP_WAITS:
            after.append(partner_of[SWAP_WAITS[at]][0])
        if at == RAW_WAIT:
            after.append(raw[1])
        if at == INVERSE_STEP:
            inverse = invert_classes(date_pairs, run_counts, [counts if coded is None else coded])
            after.append(inverse)
        if at == steps - 1:
            for part in range(FINISHED_AHEAD):
                series, told = finished(part, series, True)
                after.append(told)
        coded, away = step(at, SWAPS.get(at), layout, scalars, pairs, phases, partner_of[at], earlier, after, piece)
        received[at] = [lax.ppermute(coded, "ifg", line_permutation(links)) for links in SENDS[at // parts]]
        sent.append(at)
        if at in SWAPS:
            swapped(away, *SWAPS[at])
        if at == RAW_STEP:
            raw_other, _ = lax.optimization_barrier((raw_other, coded))
            raw = [raw_own, lax.ppermute(raw_other, "ifg", swap)]

    for part in range(FINISHED_AHEAD, parts):
        series = finished(part, series, False)[0]
    return series


def solve_by_blocks(phases, date_pairs, counts_of):
    owner_count = lax.axis_size("ifg")
    local_pairs, pixels = phases.shape
    owner_pixels = pixels // owner_count
    run_counts = counts_of(None)
    outgoing = phases.reshape(local_pairs, owner_count, owner_pixels).transpose(1, 0, 2)
    received = lax.all_to_all(outgoing, "ifg", split_axis=0, concat_axis=0, tiled=True)
    inverse = invert_classes(date_pairs, run_counts, [])
    return sum_solve(run_counts, date_pairs, received.reshape(-1, owner_pixels), inverse)


def local(phases, date_pairs, pair_counts, group_ids):
    local_pairs, _, pixels = phases.shape

    def counts_of(after):
        groups = group_ids if after is None else lax.optimization_barrier((group_ids, after))[0]
        strip_groups = lax.dynamic_index_in_dim(groups, lax.axis_index("grp"), 0, keepdims=False)[::RUN]
        chosen = strip_groups[:, None] == jnp.arange(pair_counts.shape[0], dtype=jnp.int32)
        return jnp.sum(jnp.where(chosen, pair_counts, 0), axis=1)

    line = lax.axis_size("ifg") == 2 * len(CHUNK_ORDER) and group_ids.shape[1] == 2 * RUN
    by_sums = line and 2 * local_pairs > M and local_pairs % LANES == 0 and lax.axis_size("grp") % 2 == 0
    solve = solve_by_sums if by_sums else solve_by_blocks
    return solve(phases.reshape(local_pairs, pixels), date_pairs, counts_of)[None, :, :]


def solution(mesh):
    in_specs = (P("ifg", "grp", None), P(), P(), P(None, "ifg"))
    out_specs = P("grp", None, "ifg")
    return jax.shard_map(local, mesh=mesh, in_specs=in_specs, out_specs=out_specs, check_vma=False)
```

```python
import functools

import jax
import jax.numpy as jnp
import numpy as np
from jax import lax
from jax.experimental import pallas as pl
from jax.experimental.pallas import tpu as pltpu
from jax.sharding import PartitionSpec as P

M = 200
RUN = 8
PAD = 256
SLABS = 8
DAMPING = 1.0
VMEM_BYTES = 48 * 1024 * 1024
F32 = jnp.float32
HIGHEST = lax.Precision.HIGHEST
STEADY = pl.CostEstimate(flops=10_000_000_000, bytes_accessed=30_000_000, transcendentals=0)
LITTLE = pl.CostEstimate(flops=1024, bytes_accessed=1024, transcendentals=0)
CUTS = 2
HALVES = 2
FLIGHT = 2
FIRST_SWAP = (0, 2)
SWAPS = {0: (2, 1), 1: (4, 2), 2: (6, 2), 5: (8, 2), 7: (10, 2), 8: (12, 2), 9: (14, 2)}
SWAP_WAITS = {}
RAW_STEP, RAW_WAIT = 2, 5
INVERSE_STEP = 0
FINISHED_AHEAD = 1
ME, PARTNER, NEAR, NEAR_PARTNER, INNER, FIXED = 0, 1, 2, 3, 4, 5
LANES = 128
CODE_ROWS = 16
LEVELS = 32700.0
ROUNDER = 1.5 * 2.0**23
CODES_PER_OCTAVE = 128.0
SMALLEST = 2.0**-110
CHUNK_ORDER = ((2, 3, 1, 0), (0, 2, 3, 1), (3, 1, 0, 2), (1, 0, 2, 3))
SENDS = (
    (((0, 1), (1, 0), (2, 3), (3, 2)),),
    (((0, 1), (3, 2)), ((1, 2), (2, 1))),
    (((0, 1), (1, 3), (2, 0), (3, 2)),),
)


def incidence(earlier, later, rows):
    shape = (rows, earlier.shape[1])
    date = lax.broadcasted_iota(jnp.int32, shape, 0)
    return (date == later).astype(F32) - (date == earlier).astype(F32)


def split_product(left, right):
    def halves(value):
        high = value.astype(jnp.bfloat16)
        return high, (value - high.astype(F32)).astype(jnp.bfloat16)

    left_high, left_low = halves(left)
    right_high, right_low = halves(right)
    small = jnp.dot(left_high, right_low, preferred_element_type=F32) + jnp.dot(left_low, right_high, preferred_element_type=F32)
    return jnp.dot(left_high, right_high, preferred_element_type=F32) + small


def full_product(left, right):
    return jnp.dot(left, right, precision=HIGHEST, preferred_element_type=F32)


def inverse_kernel(counts_ref, pairs_ref, *rest):
    out_ref = rest[-1]
    runs = out_ref.shape[0]
    design = incidence(pairs_ref[0:1, :], pairs_ref[1:2, :], PAD)
    pair = lax.broadcasted_iota(jnp.int32, design.shape, 1)
    contract_last = (((1,), (1,)), ((), ()))
    row = lax.broadcasted_iota(jnp.int32, (PAD, PAD), 0)
    col = lax.broadcasted_iota(jnp.int32, (PAD, PAD), 1)
    identity = (row == col).astype(F32)
    grams = []
    for run in range(runs):
        kept = jnp.where(pair < counts_ref[run], design, 0.0).astype(jnp.bfloat16)
        gram = lax.dot_general(kept, kept, contract_last, preferred_element_type=F32)
        grams.append(gram + DAMPING * identity)
    low = DAMPING
    high = 2.0 * functools.reduce(jnp.maximum, [jnp.max(gram) for gram in grams]) - DAMPING
    total, width = high + low, high - low
    scale = 2.0 * total * total - width * width
    starts = tuple((8.0 * total / scale) * identity - (8.0 / scale) * gram for gram in grams)
    needed = 18.0 * scale / (8.0 * high * low)
    steps = jnp.int32(0)
    for power in range(1, 16):
        steps += (needed > float(2**power)).astype(jnp.int32)

    def newton(product, guesses):
        products = [product(gram, guess) for gram, guess in zip(grams, guesses)]
        return tuple(2.0 * guess - product(guess, each) for guess, each in zip(guesses, products))

    full_steps = 1 + (high > 100.0).astype(jnp.int32)
    guesses = lax.fori_loop(0, steps + 1 - full_steps, lambda _, guesses: newton(split_product, guesses), starts)
    guesses = lax.fori_loop(0, full_steps, lambda _, guesses: newton(full_product, guesses), guesses)
    for run, guess in enumerate(guesses):
        out_ref[run] = guess


def invert_classes(date_pairs, run_counts, after):
    shape = (run_counts.shape[0], PAD, PAD)
    return pl.pallas_call(
        inverse_kernel,
        out_shape=jax.ShapeDtypeStruct(shape, F32),
        grid_spec=pltpu.PrefetchScalarGridSpec(
            num_scalar_prefetch=1,
            grid=(1,),
            in_specs=[pl.BlockSpec(date_pairs.shape, lambda i, c: (0, 0))] + [pl.BlockSpec(memory_space=pl.ANY)] * len(after),
            out_specs=pl.BlockSpec(shape, lambda i, c: (0, 0, 0)),
        ),
        compiler_params=pltpu.CompilerParams(vmem_limit_bytes=VMEM_BYTES),
        cost_estimate=LITTLE,
        name="invert_classes_0",
    )(run_counts, date_pairs, *after)


def sum_solve_kernel(tiles, counts_ref, pairs_ref, data_ref, inverse_ref, out_ref):
    run = pl.program_id(0) // tiles
    design = incidence(pairs_ref[0:1, :], pairs_ref[1:2, :], PAD)
    pair = lax.broadcasted_iota(jnp.int32, design.shape, 1)
    kept = jnp.where(pair < counts_ref[run], design, 0.0).astype(jnp.bfloat16)
    sums = jnp.dot(kept, data_ref[...], preferred_element_type=F32)
    out_ref[...] = jnp.dot(inverse_ref[0, :M, :], sums, precision=HIGHEST, preferred_element_type=F32)


def sum_solve(run_counts, date_pairs, received, inverse):
    runs = run_counts.shape[0]
    total_pairs, pixels = received.shape
    run_pixels = pixels // runs
    tile = run_pixels // 2
    tiles = run_pixels // tile
    return pl.pallas_call(
        functools.partial(sum_solve_kernel, tiles),
        out_shape=jax.ShapeDtypeStruct((M, pixels), F32),
        grid_spec=pltpu.PrefetchScalarGridSpec(
            num_scalar_prefetch=1,
            grid=(runs * tiles,),
            in_specs=[
                pl.BlockSpec(date_pairs.shape, lambda i, c: (0, 0)),
                pl.BlockSpec((total_pairs, tile), lambda i, c: (0, i)),
                pl.BlockSpec((1, PAD, PAD), lambda i, c: (i // tiles, 0, 0)),
            ],
            out_specs=pl.BlockSpec((M, tile), lambda i, c: (0, i)),
        ),
        compiler_params=pltpu.CompilerParams(vmem_limit_bytes=VMEM_BYTES),
        name="sum_solve",
    )(run_counts, date_pairs, received, inverse)


def coded_rows(piece):
    return M * (piece // LANES) + CODE_ROWS


def decode(coded_ref, codes_ref, lots, first):
    coded = coded_ref[...].astype(jnp.int32).astype(F32)
    values = jnp.concatenate([coded[lot * M : (lot + 1) * M, :] for lot in range(lots)], axis=1)
    codes = codes_ref[...].astype(jnp.int32).astype(F32)
    codes = jnp.concatenate([codes[first + lot : first + lot + 1, :] for lot in range(lots)], axis=1)
    return values, jnp.exp2(codes * (1.0 / CODES_PER_OCTAVE)) * (1.0 / LEVELS)


def encode(sums):
    largest = jnp.max(jnp.abs(sums), axis=0, keepdims=True)
    code = jnp.ceil(jnp.log2(jnp.maximum(largest, SMALLEST)) * CODES_PER_OCTAVE)
    scaled = (sums * (LEVELS / jnp.exp2(code * (1.0 / CODES_PER_OCTAVE))) + ROUNDER) - ROUNDER
    lots = sums.shape[1] // LANES
    return jnp.concatenate([scaled[:, lot * LANES : (lot + 1) * LANES] for lot in range(lots)], axis=0), code


def whole(values):
    return values.astype(jnp.int32).astype(jnp.int16)


def piece_count(at, layout, table, counts):
    parts, _, _, shifts = layout
    run = at % parts // CUTS
    return counts[table[shifts + at] * (parts // CUTS) + run]


def pair_sums(count, table, pairs_ref, first_ref, second_ref, members=(ME, PARTNER)):
    width = first_ref.shape[0]
    lane = lax.broadcasted_iota(jnp.int32, (1, 2 * width), 1)
    pair = jnp.where(lane < width, table[members[0]] * width + lane, table[members[1]] * width + lane - width)
    dates = pairs_ref[:, members[0] * width : (members[0] + 2) * width]
    design = incidence(dates[0:1, :], dates[1:2, :], M)
    kept = jnp.where(pair < count, design, 0.0).astype(jnp.bfloat16)
    data = jnp.concatenate([first_ref[...], second_ref[...]], axis=0)
    return jnp.dot(kept, data, preferred_element_type=F32)


def near_sums(wanted, count, table, pairs_ref, raw_refs):
    return pair_sums(jnp.where(wanted, count, 0), table, pairs_ref, *raw_refs, members=(NEAR, NEAR_PARTNER))


def step_kernel(at, layout, adds, swaps, halves, table, counts, pairs_ref, own_ref, partner_ref, *rest):
    if swaps:
        rest[-1][...] = rest[0][...]
        coded_ref, rest = rest[-2], rest[1:]
    else:
        coded_ref = rest[-1]
    count = piece_count(at, layout, table, counts)
    width = own_ref.shape[1] // halves
    lots = width // LANES
    codes = []
    for half in range(halves):
        part = pl.ds(half * width, width)
        sums = pair_sums(count, table, pairs_ref, own_ref.at[:, part], partner_ref.at[:, part])
        if adds == 1:
            rows = pl.ds(half * lots * M, lots * M)
            values, scale = decode(rest[0].at[rows, :], rest[0].at[halves * lots * M :, :], lots, half * lots)
            sums = sums + values * (scale * table[INNER].astype(F32))
        if adds == 2:
            sums = sums + near_sums(table[INNER] == 1, count, table, pairs_ref, [raw_ref.at[:, part] for raw_ref in rest[:2]])
        scaled, code = encode(sums)
        coded_ref[half * lots * M : (half + 1) * lots * M, :] = whole(scaled)
        codes += [code[:, lot * LANES : (lot + 1) * LANES] for lot in range(lots)]
    codes += [jnp.zeros((CODE_ROWS - len(codes), LANES), F32)]
    coded_ref[halves * lots * M :, :] = whole(jnp.concatenate(codes, axis=0))


def step(at, swap, layout, scalars, pairs, phases, partner, earlier, after, piece):
    partner, place_in = partner
    local_pairs = phases.shape[0]
    _, blocks, away, _ = layout
    coded_shape = (coded_rows(piece), LANES)
    in_specs = [
        pl.BlockSpec(pairs.shape, lambda i, t, c: (0, 0)),
        pl.BlockSpec((local_pairs, piece), lambda i, t, c: (0, t[blocks + at])),
        pl.BlockSpec((local_pairs, piece), lambda i, t, c: (0, place_in)),
    ]
    operands = [pairs, phases, partner]
    out_shape = [jax.ShapeDtypeStruct(coded_shape, jnp.int16)]
    out_specs = [pl.BlockSpec(coded_shape, lambda i, t, c: (0, 0))]
    if swap is not None:
        first, count = swap
        wide = piece * count
        in_specs.append(pl.BlockSpec((local_pairs, wide), lambda i, t, c: (0, t[away + first] // count)))
        operands.append(phases)
        out_shape.append(jax.ShapeDtypeStruct((local_pairs, wide), phases.dtype))
        out_specs.append(pl.BlockSpec((local_pairs, wide), lambda i, t, c: (0, 0)))
    in_specs += [pl.BlockSpec(each.shape, lambda i, t, c: (0, 0)) for each in earlier]
    operands += earlier
    in_specs += [pl.BlockSpec(memory_space=pl.ANY)] * len(after)
    results = pl.pallas_call(
        functools.partial(step_kernel, at, layout, len(earlier), swap is not None, HALVES),
        out_shape=out_shape,
        grid_spec=pltpu.PrefetchScalarGridSpec(
            num_scalar_prefetch=2,
            grid=(1,),
            in_specs=in_specs,
            out_specs=out_specs,
        ),
        compiler_params=pltpu.CompilerParams(vmem_limit_bytes=VMEM_BYTES),
        cost_estimate=STEADY,
        name=f"sum_step_{at:02d}",
    )(*scalars, *operands, *after)
    return results[0], results[1] if swap is not None else None


def coded_specs(piece, tiles, index):
    lots = piece // LANES
    return [
        pl.BlockSpec((lots // tiles * M, LANES), lambda *at: (at[index], 0)),
        pl.BlockSpec((CODE_ROWS, LANES), lambda *at: (lots * M // CODE_ROWS, 0)),
    ]


def add_arrived(sums_ref, refs, tiles):
    lots = sums_ref.shape[1] // LANES
    tile = pl.program_id(0)
    for coded_ref, codes_ref in zip(refs[::2], refs[1::2]):
        codes = codes_ref[...].astype(jnp.int32).astype(F32)
        pieces = [codes[at * lots : (at + 1) * lots, :] for at in range(tiles)]
        codes = functools.reduce(lambda chosen, at: jnp.where(tile == at, pieces[at], chosen), range(1, tiles), pieces[0])
        scale = jnp.exp2(codes * (1.0 / CODES_PER_OCTAVE)) * (1.0 / LEVELS)
        coded = coded_ref[...].astype(jnp.int32).astype(F32)
        for lot in range(lots):
            lanes = slice(lot * LANES, (lot + 1) * LANES)
            sums_ref[:M, lanes] += coded[lot * M : (lot + 1) * M, :] * scale[lot : lot + 1, :]


def solve_product(inverse, sums):
    def halves(value):
        high = value.astype(jnp.bfloat16)
        return high, (value - high.astype(F32)).astype(jnp.bfloat16)

    inverse_high, inverse_low = halves(inverse)
    sums_high, sums_low = halves(sums)
    left = jnp.concatenate([inverse_high, inverse_high, inverse_low], axis=1)
    right = jnp.concatenate([sums_high, sums_low, sums_high], axis=0)
    return jnp.dot(left, right, preferred_element_type=F32)


def finish_kernel(at, layout, tiles, raw, told, table, counts, pairs_ref, own_ref, partner_ref, inverse_ref, *rest):
    first, middle, last = rest[:2], rest[2:4], rest[4:6]
    sums_ref, rest = rest[-1], rest[:-1]
    if told:
        rest[-1][...] = jnp.zeros_like(rest[-1])
        rest = rest[:-1]
    out_ref = rest[-1]
    count = piece_count(at, layout, table, counts)
    sums_ref[:M, :] = pair_sums(count, table, pairs_ref, own_ref, partner_ref)
    sums_ref[M:, :] = jnp.zeros((PAD - M, sums_ref.shape[1]), F32)

    @pl.when(table[INNER] == 0)
    def _():
        if raw:
            sums_ref[:M, :] += near_sums(True, count, table, pairs_ref, first)
        else:
            add_arrived(sums_ref, first, tiles)

    @pl.when(table[INNER] == 1)
    def _():
        add_arrived(sums_ref, middle, tiles)

    add_arrived(sums_ref, last, tiles)
    out_ref[...] = solve_product(inverse_ref[0, :M, :], sums_ref[...])


def finish(at, part, layout, scalars, pairs, phases, partner, inverse, raw, arrived, series, told, pixels, piece):
    partner, place_in = partner
    local_pairs = phases.shape[0]
    blocks = layout[1]
    tiles = HALVES
    tile = piece // tiles
    in_specs = [
        pl.BlockSpec(pairs.shape, lambda i, t, c: (0, 0)),
        pl.BlockSpec((local_pairs, tile), lambda i, t, c: (0, t[blocks + at] * tiles + i)),
        pl.BlockSpec((local_pairs, tile), lambda i, t, c: (0, place_in * tiles + i)),
        pl.BlockSpec((1, PAD, PAD), lambda i, t, c: (part // CUTS, 0, 0)),
    ]
    in_specs += [pl.BlockSpec((local_pairs, tile), lambda i, t, c: (0, i))] * len(raw) + coded_specs(piece, tiles, 0) * len(arrived)
    operands = [*scalars, pairs, phases, partner, inverse, *raw] + [each for each in arrived for _ in range(2)]
    aliases = {}
    if series is not None:
        in_specs.append(pl.BlockSpec(memory_space=pl.ANY))
        aliases = {len(operands): 0}
        operands.append(series)
    out_shape = [jax.ShapeDtypeStruct((M, pixels), F32)]
    out_specs = [pl.BlockSpec((M, tile), lambda i, t, c: (0, part * tiles + i))]
    if told:
        out_shape.append(jax.ShapeDtypeStruct((8, LANES), F32))
        out_specs.append(pl.BlockSpec((8, LANES), lambda i, t, c: (0, 0)))
    return pl.pallas_call(
        functools.partial(finish_kernel, at, layout, tiles, len(raw) > 0, told),
        out_shape=out_shape,
        grid_spec=pltpu.PrefetchScalarGridSpec(
            num_scalar_prefetch=2,
            grid=(tiles,),
            in_specs=in_specs,
            out_specs=out_specs,
            scratch_shapes=[pltpu.VMEM((PAD, tile), F32)],
        ),
        input_output_aliases=aliases,
        compiler_params=pltpu.CompilerParams(vmem_limit_bytes=VMEM_BYTES),
        cost_estimate=LITTLE,
        name=f"finish_{part}",
    )(*operands)


def line_permutation(links):
    return [(2 * source + side, 2 * target + side) for source, target in links for side in range(2)]


def solve_by_sums(phases, date_pairs, counts_of):
    owner_count = lax.axis_size("ifg")
    line = owner_count // 2
    local_pairs, pixels = phases.shape
    owner_pixels = pixels // owner_count
    runs = counts_of(None).shape[0]
    parts = runs * CUTS
    piece = owner_pixels // parts
    steps = (line - 1) * parts
    me = lax.axis_index("ifg")

    places = np.repeat(np.array(CHUNK_ORDER), parts, axis=1)
    part_of = np.tile(np.arange(parts), line)
    rows = []
    for device in range(owner_count):
        place, side = device // 2, device % 2
        own = (places[place] * 2 + side) * parts + part_of
        away = (places[place] * 2 + 1 - side) * parts + part_of
        shift = (place - places[place]) % line
        rows.append(np.concatenate([[device, device ^ 1, device ^ 2, device ^ 3, int(0 < place < line - 1)], own, away, shift]))
    row = lax.dynamic_index_in_dim(jnp.asarray(np.stack(rows), jnp.int32), me, 0, keepdims=False)
    head, pieces = FIXED, line * parts
    layout = (parts, head, head + pieces, head + 2 * pieces)

    swap = [(i, i ^ 1) for i in range(owner_count)]
    partner_of = {}

    def swapped(away, first, count):
        here = lax.ppermute(away, "ifg", swap)
        partner_of.update({first + place: (here, place) for place in range(count)})

    place, side = me // 2, me % 2
    chunk = jnp.where(place < line // 2, 2 - 2 * place, 7 - 2 * place)

    def first_away(column, part, count, after):
        block = (chunk * 2 + column) * parts + part
        if after is not None:
            block, _ = lax.optimization_barrier((block, after))
        return lax.dynamic_slice(phases, (0, block * piece), (local_pairs, count * piece))

    away = first_away(1 - side, *FIRST_SWAP, None)
    swapped(away, *FIRST_SWAP)
    run_counts = counts_of(away)
    counts = [run_counts]
    for distance in range(1, line):
        links = [(i, (i + distance) % line) for i in range(line)]
        counts.append(lax.ppermute(run_counts, "ifg", line_permutation(links)))
    counts = jnp.concatenate(counts)
    raw_part = parts - 1
    near = line_permutation(SENDS[0][0])
    raw_other = lax.ppermute(first_away(1 - side, raw_part, 1, run_counts), "ifg", near)
    raw_own = lax.ppermute(first_away(side, raw_part, 1, run_counts), "ifg", near)
    pairs = jnp.concatenate([lax.dynamic_slice(date_pairs, (0, (me ^ at) * local_pairs), (2, local_pairs)) for at in range(4)], axis=1)
    scalars = (row, counts)

    received, sent, coded, series = {raw_part: [raw_own, raw_other]}, [raw_part], None, None

    def finished(part, series, told):
        at = steps + part
        arrived = [received[place * parts + part][-1] for place in range(1 if part == raw_part else 0, line - 1)]
        data = (layout, scalars, pairs, phases, partner_of[at], inverse, raw if part == raw_part else [], arrived)
        return finish(at, part, *data, series, told, owner_pixels, piece)

    for at in [each for each in range(steps) if each != raw_part]:
        earlier = [] if at < parts else raw if at == parts + raw_part else [received[at - parts][0]]
        after = [] if coded is None else [coded]
        after += received[sent[-FLIGHT]] if len(sent) >= FLIGHT else []
        if at in SWAP_WAITS:
            after.append(partner_of[SWAP_WAITS[at]][0])
        if at == RAW_WAIT:
            after.append(raw[1])
        if at == INVERSE_STEP:
            inverse = invert_classes(date_pairs, run_counts, [counts if coded is None else coded])
            after.append(inverse)
        if at == steps - 1:
            for part in range(FINISHED_AHEAD):
                series, told = finished(part, series, True)
                after.append(told)
        coded, away = step(at, SWAPS.get(at), layout, scalars, pairs, phases, partner_of[at], earlier, after, piece)
        received[at] = [lax.ppermute(coded, "ifg", line_permutation(links)) for links in SENDS[at // parts]]
        sent.append(at)
        if at in SWAPS:
            swapped(away, *SWAPS[at])
        if at == RAW_STEP:
            raw_other, _ = lax.optimization_barrier((raw_other, coded))
            raw = [raw_own, lax.ppermute(raw_other, "ifg", swap)]

    for part in range(FINISHED_AHEAD, parts):
        series = finished(part, series, False)[0]
    return series


def solve_by_blocks(phases, date_pairs, counts_of):
    owner_count = lax.axis_size("ifg")
    local_pairs, pixels = phases.shape
    owner_pixels = pixels // owner_count
    run_counts = counts_of(None)
    outgoing = phases.reshape(local_pairs, owner_count, owner_pixels).transpose(1, 0, 2)
    received = lax.all_to_all(outgoing, "ifg", split_axis=0, concat_axis=0, tiled=True)
    inverse = invert_classes(date_pairs, run_counts, [])
    return sum_solve(run_counts, date_pairs, received.reshape(-1, owner_pixels), inverse)


def local(phases, date_pairs, pair_counts, group_ids):
    local_pairs, _, pixels = phases.shape

    def counts_of(after):
        groups = group_ids if after is None else lax.optimization_barrier((group_ids, after))[0]
        strip_groups = lax.dynamic_index_in_dim(groups, lax.axis_index("grp"), 0, keepdims=False)[::RUN]
        chosen = strip_groups[:, None] == jnp.arange(pair_counts.shape[0], dtype=jnp.int32)
        return jnp.sum(jnp.where(chosen, pair_counts, 0), axis=1)

    line = lax.axis_size("ifg") == 2 * len(CHUNK_ORDER) and group_ids.shape[1] == 2 * RUN
    by_sums = line and 2 * local_pairs > M and local_pairs % LANES == 0 and lax.axis_size("grp") % 2 == 0
    solve = solve_by_sums if by_sums else solve_by_blocks
    return solve(phases.reshape(local_pairs, pixels), date_pairs, counts_of)[None, :, :]


def solution(mesh):
    in_specs = (P("ifg", "grp", None), P(), P(), P(None, "ifg"))
    out_specs = P("grp", None, "ifg")
    return jax.shard_map(local, mesh=mesh, in_specs=in_specs, out_specs=out_specs, check_vma=False)
```

```python
import functools

import jax
import jax.numpy as jnp
import numpy as np
from jax import lax
from jax.experimental import pallas as pl
from jax.experimental.pallas import tpu as pltpu
from jax.sharding import PartitionSpec as P

M = 200
RUN = 8
PAD = 256
SLABS = 8
DAMPING = 1.0
VMEM_BYTES = 48 * 1024 * 1024
F32 = jnp.float32
HIGHEST = lax.Precision.HIGHEST
STEADY = pl.CostEstimate(flops=10_000_000_000, bytes_accessed=30_000_000, transcendentals=0)
LITTLE = pl.CostEstimate(flops=1024, bytes_accessed=1024, transcendentals=0)
CUTS = 2
HALVES = 2
FLIGHT = 2
FIRST_SWAP = (0, 2)
SWAPS = {0: (2, 1), 1: (4, 2), 2: (6, 2), 5: (8, 2), 7: (10, 2), 8: (12, 2), 9: (14, 2)}
SWAP_WAITS = {}
RAW_STEP, RAW_WAIT = 2, 5
INVERSE_STEP = 0
FINISHED_AHEAD = 1
ME, PARTNER, NEAR, NEAR_PARTNER, INNER, FIXED = 0, 1, 2, 3, 4, 5
LANES = 128
CODE_ROWS = 16
LEVELS = 32700.0
ROUNDER = 1.5 * 2.0**23
CODES_PER_OCTAVE = 128.0
SMALLEST = 2.0**-110
CHUNK_ORDER = ((2, 3, 1, 0), (0, 2, 3, 1), (3, 1, 0, 2), (1, 0, 2, 3))
SENDS = (
    (((0, 1), (1, 0), (2, 3), (3, 2)),),
    (((0, 1), (3, 2)), ((1, 2), (2, 1))),
    (((0, 1), (1, 3), (2, 0), (3, 2)),),
)


def incidence(earlier, later, rows):
    shape = (rows, earlier.shape[1])
    date = lax.broadcasted_iota(jnp.int32, shape, 0)
    return (date == later).astype(F32) - (date == earlier).astype(F32)


def split_product(left, right):
    def halves(value):
        high = value.astype(jnp.bfloat16)
        return high, (value - high.astype(F32)).astype(jnp.bfloat16)

    left_high, left_low = halves(left)
    right_high, right_low = halves(right)
    small = jnp.dot(left_high, right_low, preferred_element_type=F32) + jnp.dot(left_low, right_high, preferred_element_type=F32)
    return jnp.dot(left_high, right_high, preferred_element_type=F32) + small


def full_product(left, right):
    return jnp.dot(left, right, precision=HIGHEST, preferred_element_type=F32)


def inverse_kernel(counts_ref, pairs_ref, *rest):
    out_ref = rest[-1]
    runs = out_ref.shape[0]
    design = incidence(pairs_ref[0:1, :], pairs_ref[1:2, :], PAD)
    pair = lax.broadcasted_iota(jnp.int32, design.shape, 1)
    contract_last = (((1,), (1,)), ((), ()))
    row = lax.broadcasted_iota(jnp.int32, (PAD, PAD), 0)
    col = lax.broadcasted_iota(jnp.int32, (PAD, PAD), 1)
    identity = (row == col).astype(F32)
    grams = []
    for run in range(runs):
        kept = jnp.where(pair < counts_ref[run], design, 0.0).astype(jnp.bfloat16)
        gram = lax.dot_general(kept, kept, contract_last, preferred_element_type=F32)
        grams.append(gram + DAMPING * identity)
    low = DAMPING
    high = 2.0 * functools.reduce(jnp.maximum, [jnp.max(gram) for gram in grams]) - DAMPING
    total, width = high + low, high - low
    scale = 2.0 * total * total - width * width
    starts = tuple((8.0 * total / scale) * identity - (8.0 / scale) * gram for gram in grams)
    needed = 18.0 * scale / (8.0 * high * low)
    steps = jnp.int32(0)
    for power in range(1, 16):
        steps += (needed > float(2**power)).astype(jnp.int32)

    def newton(product, guesses):
        products = [product(gram, guess) for gram, guess in zip(grams, guesses)]
        return tuple(2.0 * guess - product(guess, each) for guess, each in zip(guesses, products))

    full_steps = 1 + (high > 100.0).astype(jnp.int32)
    guesses = lax.fori_loop(0, steps + 1 - full_steps, lambda _, guesses: newton(split_product, guesses), starts)
    guesses = lax.fori_loop(0, full_steps, lambda _, guesses: newton(full_product, guesses), guesses)
    for run, guess in enumerate(guesses):
        out_ref[run] = guess


def invert_classes(date_pairs, run_counts, after):
    shape = (run_counts.shape[0], PAD, PAD)
    return pl.pallas_call(
        inverse_kernel,
        out_shape=jax.ShapeDtypeStruct(shape, F32),
        grid_spec=pltpu.PrefetchScalarGridSpec(
            num_scalar_prefetch=1,
            grid=(1,),
            in_specs=[pl.BlockSpec(date_pairs.shape, lambda i, c: (0, 0))] + [pl.BlockSpec(memory_space=pl.ANY)] * len(after),
            out_specs=pl.BlockSpec(shape, lambda i, c: (0, 0, 0)),
        ),
        compiler_params=pltpu.CompilerParams(vmem_limit_bytes=VMEM_BYTES),
        cost_estimate=LITTLE,
        name="invert_classes_0",
    )(run_counts, date_pairs, *after)


def sum_solve_kernel(tiles, counts_ref, pairs_ref, data_ref, inverse_ref, out_ref):
    run = pl.program_id(0) // tiles
    design = incidence(pairs_ref[0:1, :], pairs_ref[1:2, :], PAD)
    pair = lax.broadcasted_iota(jnp.int32, design.shape, 1)
    kept = jnp.where(pair < counts_ref[run], design, 0.0).astype(jnp.bfloat16)
    sums = jnp.dot(kept, data_ref[...], preferred_element_type=F32)
    out_ref[...] = jnp.dot(inverse_ref[0, :M, :], sums, precision=HIGHEST, preferred_element_type=F32)


def sum_solve(run_counts, date_pairs, received, inverse):
    runs = run_counts.shape[0]
    total_pairs, pixels = received.shape
    run_pixels = pixels // runs
    tile = run_pixels // 2
    tiles = run_pixels // tile
    return pl.pallas_call(
        functools.partial(sum_solve_kernel, tiles),
        out_shape=jax.ShapeDtypeStruct((M, pixels), F32),
        grid_spec=pltpu.PrefetchScalarGridSpec(
            num_scalar_prefetch=1,
            grid=(runs * tiles,),
            in_specs=[
                pl.BlockSpec(date_pairs.shape, lambda i, c: (0, 0)),
                pl.BlockSpec((total_pairs, tile), lambda i, c: (0, i)),
                pl.BlockSpec((1, PAD, PAD), lambda i, c: (i // tiles, 0, 0)),
            ],
            out_specs=pl.BlockSpec((M, tile), lambda i, c: (0, i)),
        ),
        compiler_params=pltpu.CompilerParams(vmem_limit_bytes=VMEM_BYTES),
        name="sum_solve",
    )(run_counts, date_pairs, received, inverse)


def coded_rows(piece):
    return M * (piece // LANES) + CODE_ROWS


def decode(coded_ref, codes_ref, lots, first):
    coded = coded_ref[...].astype(jnp.int32).astype(F32)
    values = jnp.concatenate([coded[lot * M : (lot + 1) * M, :] for lot in range(lots)], axis=1)
    codes = codes_ref[...].astype(jnp.int32).astype(F32)
    codes = jnp.concatenate([codes[first + lot : first + lot + 1, :] for lot in range(lots)], axis=1)
    return values, jnp.exp2(codes * (1.0 / CODES_PER_OCTAVE)) * (1.0 / LEVELS)


def encode(sums):
    largest = jnp.max(jnp.abs(sums), axis=0, keepdims=True)
    code = jnp.ceil(jnp.log2(jnp.maximum(largest, SMALLEST)) * CODES_PER_OCTAVE)
    scaled = (sums * (LEVELS / jnp.exp2(code * (1.0 / CODES_PER_OCTAVE))) + ROUNDER) - ROUNDER
    lots = sums.shape[1] // LANES
    return jnp.concatenate([scaled[:, lot * LANES : (lot + 1) * LANES] for lot in range(lots)], axis=0), code


def whole(values):
    return values.astype(jnp.int32).astype(jnp.int16)


def piece_count(at, layout, table, counts):
    parts, _, _, shifts = layout
    run = at % parts // CUTS
    return counts[table[shifts + at] * (parts // CUTS) + run]


def pair_sums(count, table, pairs_ref, first_ref, second_ref, members=(ME, PARTNER)):
    width = first_ref.shape[0]
    lane = lax.broadcasted_iota(jnp.int32, (1, 2 * width), 1)
    pair = jnp.where(lane < width, table[members[0]] * width + lane, table[members[1]] * width + lane - width)
    dates = pairs_ref[:, members[0] * width : (members[0] + 2) * width]
    design = incidence(dates[0:1, :], dates[1:2, :], M)
    kept = jnp.where(pair < count, design, 0.0).astype(jnp.bfloat16)
    data = jnp.concatenate([first_ref[...], second_ref[...]], axis=0)
    return jnp.dot(kept, data, preferred_element_type=F32)


def near_sums(wanted, count, table, pairs_ref, raw_refs):
    return pair_sums(jnp.where(wanted, count, 0), table, pairs_ref, *raw_refs, members=(NEAR, NEAR_PARTNER))


def step_kernel(at, layout, adds, swaps, halves, table, counts, pairs_ref, own_ref, partner_ref, *rest):
    if swaps:
        rest[-1][...] = rest[0][...]
        coded_ref, rest = rest[-2], rest[1:]
    else:
        coded_ref = rest[-1]
    count = piece_count(at, layout, table, counts)
    width = own_ref.shape[1] // halves
    lots = width // LANES
    codes = []
    for half in range(halves):
        part = pl.ds(half * width, width)
        sums = pair_sums(count, table, pairs_ref, own_ref.at[:, part], partner_ref.at[:, part])
        if adds == 1:
            rows = pl.ds(half * lots * M, lots * M)
            values, scale = decode(rest[0].at[rows, :], rest[0].at[halves * lots * M :, :], lots, half * lots)
            sums = sums + values * (scale * table[INNER].astype(F32))
        if adds == 2:
            sums = sums + near_sums(table[INNER] == 1, count, table, pairs_ref, [raw_ref.at[:, part] for raw_ref in rest[:2]])
        scaled, code = encode(sums)
        coded_ref[half * lots * M : (half + 1) * lots * M, :] = whole(scaled)
        codes += [code[:, lot * LANES : (lot + 1) * LANES] for lot in range(lots)]
    codes += [jnp.zeros((CODE_ROWS - len(codes), LANES), F32)]
    coded_ref[halves * lots * M :, :] = whole(jnp.concatenate(codes, axis=0))


def step(at, swap, layout, scalars, pairs, phases, partner, earlier, after, piece):
    partner, place_in = partner
    local_pairs = phases.shape[0]
    _, blocks, away, _ = layout
    coded_shape = (coded_rows(piece), LANES)
    in_specs = [
        pl.BlockSpec(pairs.shape, lambda i, t, c: (0, 0)),
        pl.BlockSpec((local_pairs, piece), lambda i, t, c: (0, t[blocks + at])),
        pl.BlockSpec((local_pairs, piece), lambda i, t, c: (0, place_in)),
    ]
    operands = [pairs, phases, partner]
    out_shape = [jax.ShapeDtypeStruct(coded_shape, jnp.int16)]
    out_specs = [pl.BlockSpec(coded_shape, lambda i, t, c: (0, 0))]
    if swap is not None:
        first, count = swap
        wide = piece * count
        in_specs.append(pl.BlockSpec((local_pairs, wide), lambda i, t, c: (0, t[away + first] // count)))
        operands.append(phases)
        out_shape.append(jax.ShapeDtypeStruct((local_pairs, wide), phases.dtype))
        out_specs.append(pl.BlockSpec((local_pairs, wide), lambda i, t, c: (0, 0)))
    in_specs += [pl.BlockSpec(each.shape, lambda i, t, c: (0, 0)) for each in earlier]
    operands += earlier
    in_specs += [pl.BlockSpec(memory_space=pl.ANY)] * len(after)
    results = pl.pallas_call(
        functools.partial(step_kernel, at, layout, len(earlier), swap is not None, HALVES),
        out_shape=out_shape,
        grid_spec=pltpu.PrefetchScalarGridSpec(
            num_scalar_prefetch=2,
            grid=(1,),
            in_specs=in_specs,
            out_specs=out_specs,
        ),
        compiler_params=pltpu.CompilerParams(vmem_limit_bytes=VMEM_BYTES),
        cost_estimate=STEADY,
        name=f"sum_step_{at:02d}",
    )(*scalars, *operands, *after)
    return results[0], results[1] if swap is not None else None


def add_coded(sums_ref, coded_ref, half, halves):
    lots = sums_ref.shape[1] // LANES
    first = half * lots
    coded = coded_ref[first * M : (first + lots) * M, :].astype(jnp.int32).astype(F32)
    codes = coded_ref[halves * lots * M :, :].astype(jnp.int32).astype(F32)
    scale = jnp.exp2(codes * (1.0 / CODES_PER_OCTAVE)) * (1.0 / LEVELS)
    for lot in range(lots):
        lanes = slice(lot * LANES, (lot + 1) * LANES)
        sums_ref[:M, lanes] += coded[lot * M : (lot + 1) * M, :] * scale[first + lot : first + lot + 1, :]


def solve_product(inverse, sums):
    def halves(value):
        high = value.astype(jnp.bfloat16)
        return high, (value - high.astype(F32)).astype(jnp.bfloat16)

    inverse_high, inverse_low = halves(inverse)
    sums_high, sums_low = halves(sums)
    left = jnp.concatenate([inverse_high, inverse_high, inverse_low], axis=1)
    right = jnp.concatenate([sums_high, sums_low, sums_high], axis=0)
    return jnp.dot(left, right, preferred_element_type=F32)


def finish_kernel(at, layout, halves, raw, told, table, counts, pairs_ref, own_ref, partner_ref, inverse_ref, *rest):
    first, middle_ref, last_ref = rest[: max(raw, 1)], rest[max(raw, 1)], rest[max(raw, 1) + 1]
    sums_ref, rest = rest[-1], rest[:-1]
    if told:
        rest[-1][...] = jnp.zeros_like(rest[-1])
        rest = rest[:-1]
    out_ref = rest[-1]
    count = piece_count(at, layout, table, counts)
    width = sums_ref.shape[1]
    sums_ref[M:, :] = jnp.zeros((PAD - M, width), F32)
    for half in range(halves):
        part = pl.ds(half * width, width)
        sums_ref[:M, :] = pair_sums(count, table, pairs_ref, own_ref.at[:, part], partner_ref.at[:, part])

        @pl.when(table[INNER] == 0)
        def _():
            if raw:
                sums_ref[:M, :] += near_sums(True, count, table, pairs_ref, [each.at[:, part] for each in first])
            else:
                add_coded(sums_ref, first[0], half, halves)

        @pl.when(table[INNER] == 1)
        def _():
            add_coded(sums_ref, middle_ref, half, halves)

        add_coded(sums_ref, last_ref, half, halves)
        out_ref[:, part] = solve_product(inverse_ref[0, :M, :], sums_ref[...])


def finish(at, part, layout, scalars, pairs, phases, partner, inverse, raw, arrived, series, told, pixels, piece):
    partner, place_in = partner
    local_pairs = phases.shape[0]
    blocks = layout[1]
    whole_block = lambda i, t, c: (0, 0)
    in_specs = [
        pl.BlockSpec(pairs.shape, whole_block),
        pl.BlockSpec((local_pairs, piece), lambda i, t, c: (0, t[blocks + at])),
        pl.BlockSpec((local_pairs, piece), lambda i, t, c: (0, place_in)),
        pl.BlockSpec((1, PAD, PAD), lambda i, t, c: (part // CUTS, 0, 0)),
    ]
    in_specs += [pl.BlockSpec(each.shape, whole_block) for each in [*raw, *arrived]]
    operands = [*scalars, pairs, phases, partner, inverse, *raw, *arrived]
    aliases = {}
    if series is not None:
        in_specs.append(pl.BlockSpec(memory_space=pl.ANY))
        aliases = {len(operands): 0}
        operands.append(series)
    out_shape = [jax.ShapeDtypeStruct((M, pixels), F32)]
    out_specs = [pl.BlockSpec((M, piece), lambda i, t, c: (0, part))]
    if told:
        out_shape.append(jax.ShapeDtypeStruct((8, LANES), F32))
        out_specs.append(pl.BlockSpec((8, LANES), lambda i, t, c: (0, 0)))
    return pl.pallas_call(
        functools.partial(finish_kernel, at, layout, HALVES, len(raw), told),
        out_shape=out_shape,
        grid_spec=pltpu.PrefetchScalarGridSpec(
            num_scalar_prefetch=2,
            grid=(1,),
            in_specs=in_specs,
            out_specs=out_specs,
            scratch_shapes=[pltpu.VMEM((PAD, piece // HALVES), F32)],
        ),
        input_output_aliases=aliases,
        compiler_params=pltpu.CompilerParams(vmem_limit_bytes=VMEM_BYTES),
        cost_estimate=LITTLE,
        name=f"finish_{part}",
    )(*operands)


def line_permutation(links):
    return [(2 * source + side, 2 * target + side) for source, target in links for side in range(2)]


def solve_by_sums(phases, date_pairs, counts_of):
    owner_count = lax.axis_size("ifg")
    line = owner_count // 2
    local_pairs, pixels = phases.shape
    owner_pixels = pixels // owner_count
    runs = counts_of(None).shape[0]
    parts = runs * CUTS
    piece = owner_pixels // parts
    steps = (line - 1) * parts
    me = lax.axis_index("ifg")

    places = np.repeat(np.array(CHUNK_ORDER), parts, axis=1)
    part_of = np.tile(np.arange(parts), line)
    rows = []
    for device in range(owner_count):
        place, side = device // 2, device % 2
        own = (places[place] * 2 + side) * parts + part_of
        away = (places[place] * 2 + 1 - side) * parts + part_of
        shift = (place - places[place]) % line
        rows.append(np.concatenate([[device, device ^ 1, device ^ 2, device ^ 3, int(0 < place < line - 1)], own, away, shift]))
    row = lax.dynamic_index_in_dim(jnp.asarray(np.stack(rows), jnp.int32), me, 0, keepdims=False)
    head, pieces = FIXED, line * parts
    layout = (parts, head, head + pieces, head + 2 * pieces)

    swap = [(i, i ^ 1) for i in range(owner_count)]
    partner_of = {}

    def swapped(away, first, count):
        here = lax.ppermute(away, "ifg", swap)
        partner_of.update({first + place: (here, place) for place in range(count)})

    place, side = me // 2, me % 2
    chunk = jnp.where(place < line // 2, 2 - 2 * place, 7 - 2 * place)

    def first_away(column, part, count, after):
        block = (chunk * 2 + column) * parts + part
        if after is not None:
            block, _ = lax.optimization_barrier((block, after))
        return lax.dynamic_slice(phases, (0, block * piece), (local_pairs, count * piece))

    away = first_away(1 - side, *FIRST_SWAP, None)
    swapped(away, *FIRST_SWAP)
    run_counts = counts_of(away)
    counts = [run_counts]
    for distance in range(1, line):
        links = [(i, (i + distance) % line) for i in range(line)]
        counts.append(lax.ppermute(run_counts, "ifg", line_permutation(links)))
    counts = jnp.concatenate(counts)
    raw_part = parts - 1
    near = line_permutation(SENDS[0][0])
    raw_other = lax.ppermute(first_away(1 - side, raw_part, 1, run_counts), "ifg", near)
    raw_own = lax.ppermute(first_away(side, raw_part, 1, run_counts), "ifg", near)
    pairs = jnp.concatenate([lax.dynamic_slice(date_pairs, (0, (me ^ at) * local_pairs), (2, local_pairs)) for at in range(4)], axis=1)
    scalars = (row, counts)

    received, sent, coded, series = {raw_part: [raw_own, raw_other]}, [raw_part], None, None

    def finished(part, series, told):
        at = steps + part
        arrived = [received[place * parts + part][-1] for place in range(1 if part == raw_part else 0, line - 1)]
        data = (layout, scalars, pairs, phases, partner_of[at], inverse, raw if part == raw_part else [], arrived)
        return finish(at, part, *data, series, told, owner_pixels, piece)

    for at in [each for each in range(steps) if each != raw_part]:
        earlier = [] if at < parts else raw if at == parts + raw_part else [received[at - parts][0]]
        after = [] if coded is None else [coded]
        after += received[sent[-FLIGHT]] if len(sent) >= FLIGHT else []
        if at in SWAP_WAITS:
            after.append(partner_of[SWAP_WAITS[at]][0])
        if at == RAW_WAIT:
            after.append(raw[1])
        if at == INVERSE_STEP:
            inverse = invert_classes(date_pairs, run_counts, [counts if coded is None else coded])
            after.append(inverse)
        if at == steps - 1:
            for part in range(FINISHED_AHEAD):
                series, told = finished(part, series, True)
                after.append(told)
        coded, away = step(at, SWAPS.get(at), layout, scalars, pairs, phases, partner_of[at], earlier, after, piece)
        received[at] = [lax.ppermute(coded, "ifg", line_permutation(links)) for links in SENDS[at // parts]]
        sent.append(at)
        if at in SWAPS:
            swapped(away, *SWAPS[at])
        if at == RAW_STEP:
            raw_other, _ = lax.optimization_barrier((raw_other, coded))
            raw = [raw_own, lax.ppermute(raw_other, "ifg", swap)]

    for part in range(FINISHED_AHEAD, parts):
        series = finished(part, series, False)[0]
    return series


def solve_by_blocks(phases, date_pairs, counts_of):
    owner_count = lax.axis_size("ifg")
    local_pairs, pixels = phases.shape
    owner_pixels = pixels // owner_count
    run_counts = counts_of(None)
    outgoing = phases.reshape(local_pairs, owner_count, owner_pixels).transpose(1, 0, 2)
    received = lax.all_to_all(outgoing, "ifg", split_axis=0, concat_axis=0, tiled=True)
    inverse = invert_classes(date_pairs, run_counts, [])
    return sum_solve(run_counts, date_pairs, received.reshape(-1, owner_pixels), inverse)


def local(phases, date_pairs, pair_counts, group_ids):
    local_pairs, _, pixels = phases.shape

    def counts_of(after):
        groups = group_ids if after is None else lax.optimization_barrier((group_ids, after))[0]
        strip_groups = lax.dynamic_index_in_dim(groups, lax.axis_index("grp"), 0, keepdims=False)[::RUN]
        chosen = strip_groups[:, None] == jnp.arange(pair_counts.shape[0], dtype=jnp.int32)
        return jnp.sum(jnp.where(chosen, pair_counts, 0), axis=1)

    line = lax.axis_size("ifg") == 2 * len(CHUNK_ORDER) and group_ids.shape[1] == 2 * RUN
    by_sums = line and 2 * local_pairs > M and local_pairs % LANES == 0 and lax.axis_size("grp") % 2 == 0
    solve = solve_by_sums if by_sums else solve_by_blocks
    return solve(phases.reshape(local_pairs, pixels), date_pairs, counts_of)[None, :, :]


def solution(mesh):
    in_specs = (P("ifg", "grp", None), P(), P(), P(None, "ifg"))
    out_specs = P("grp", None, "ifg")
    return jax.shard_map(local, mesh=mesh, in_specs=in_specs, out_specs=out_specs, check_vma=False)
```

```python
import functools

import jax
import jax.numpy as jnp
import numpy as np
from jax import lax
from jax.experimental import pallas as pl
from jax.experimental.pallas import tpu as pltpu
from jax.sharding import PartitionSpec as P

M = 200
RUN = 8
PAD = 256
SLABS = 8
DAMPING = 1.0
VMEM_BYTES = 48 * 1024 * 1024
F32 = jnp.float32
HIGHEST = lax.Precision.HIGHEST
STEADY = pl.CostEstimate(flops=10_000_000_000, bytes_accessed=30_000_000, transcendentals=0)
LITTLE = pl.CostEstimate(flops=1024, bytes_accessed=1024, transcendentals=0)
CUTS = 2
HALVES = 2
FLIGHT = 2
FIRST_SWAP = (0, 2)
SWAPS = {0: (2, 1), 1: (4, 2), 2: (6, 2), 5: (8, 2), 7: (10, 2), 8: (12, 2), 9: (14, 2)}
SWAP_WAITS = {}
RAW_STEP, RAW_WAIT = 2, 5
INVERSE_STEPS = (0, 2)
FINISHED_AHEAD = 1
ME, PARTNER, NEAR, NEAR_PARTNER, INNER, FIXED = 0, 1, 2, 3, 4, 5
LANES = 128
CODE_ROWS = 16
LEVELS = 32700.0
ROUNDER = 1.5 * 2.0**23
CODES_PER_OCTAVE = 128.0
SMALLEST = 2.0**-110
CHUNK_ORDER = ((2, 3, 1, 0), (0, 2, 3, 1), (3, 1, 0, 2), (1, 0, 2, 3))
SENDS = (
    (((0, 1), (1, 0), (2, 3), (3, 2)),),
    (((0, 1), (3, 2)), ((1, 2), (2, 1))),
    (((0, 1), (1, 3), (2, 0), (3, 2)),),
)


def incidence(earlier, later, rows):
    shape = (rows, earlier.shape[1])
    date = lax.broadcasted_iota(jnp.int32, shape, 0)
    return (date == later).astype(F32) - (date == earlier).astype(F32)


def split_product(left, right):
    def halves(value):
        high = value.astype(jnp.bfloat16)
        return high, (value - high.astype(F32)).astype(jnp.bfloat16)

    left_high, left_low = halves(left)
    right_high, right_low = halves(right)
    small = jnp.dot(left_high, right_low, preferred_element_type=F32) + jnp.dot(left_low, right_high, preferred_element_type=F32)
    return jnp.dot(left_high, right_high, preferred_element_type=F32) + small


def full_product(left, right):
    return jnp.dot(left, right, precision=HIGHEST, preferred_element_type=F32)


def inverse_kernel(first, counts_ref, pairs_ref, *rest):
    out_ref = rest[-1]
    runs = out_ref.shape[0]
    design = incidence(pairs_ref[0:1, :], pairs_ref[1:2, :], PAD)
    pair = lax.broadcasted_iota(jnp.int32, design.shape, 1)
    contract_last = (((1,), (1,)), ((), ()))
    row = lax.broadcasted_iota(jnp.int32, (PAD, PAD), 0)
    col = lax.broadcasted_iota(jnp.int32, (PAD, PAD), 1)
    identity = (row == col).astype(F32)
    grams = []
    for run in range(runs):
        kept = jnp.where(pair < counts_ref[first + run], design, 0.0).astype(jnp.bfloat16)
        gram = lax.dot_general(kept, kept, contract_last, preferred_element_type=F32)
        grams.append(gram + DAMPING * identity)
    low = DAMPING
    high = 2.0 * functools.reduce(jnp.maximum, [jnp.max(gram) for gram in grams]) - DAMPING
    total, width = high + low, high - low
    scale = 2.0 * total * total - width * width
    starts = tuple((8.0 * total / scale) * identity - (8.0 / scale) * gram for gram in grams)
    needed = 18.0 * scale / (8.0 * high * low)
    steps = jnp.int32(0)
    for power in range(1, 16):
        steps += (needed > float(2**power)).astype(jnp.int32)

    def newton(product, guesses):
        products = [product(gram, guess) for gram, guess in zip(grams, guesses)]
        return tuple(2.0 * guess - product(guess, each) for guess, each in zip(guesses, products))

    full_steps = 1 + (high > 100.0).astype(jnp.int32)
    guesses = lax.fori_loop(0, steps + 1 - full_steps, lambda _, guesses: newton(split_product, guesses), starts)
    guesses = lax.fori_loop(0, full_steps, lambda _, guesses: newton(full_product, guesses), guesses)
    for run, guess in enumerate(guesses):
        out_ref[run] = guess


def invert_classes(first, runs, date_pairs, run_counts, after):
    shape = (runs, PAD, PAD)
    return pl.pallas_call(
        functools.partial(inverse_kernel, first),
        out_shape=jax.ShapeDtypeStruct(shape, F32),
        grid_spec=pltpu.PrefetchScalarGridSpec(
            num_scalar_prefetch=1,
            grid=(1,),
            in_specs=[pl.BlockSpec(date_pairs.shape, lambda i, c: (0, 0))] + [pl.BlockSpec(memory_space=pl.ANY)] * len(after),
            out_specs=pl.BlockSpec(shape, lambda i, c: (0, 0, 0)),
        ),
        compiler_params=pltpu.CompilerParams(vmem_limit_bytes=VMEM_BYTES),
        cost_estimate=LITTLE,
        name=f"invert_classes_{first}",
    )(run_counts, date_pairs, *after)


def sum_solve_kernel(tiles, counts_ref, pairs_ref, data_ref, inverse_ref, out_ref):
    run = pl.program_id(0) // tiles
    design = incidence(pairs_ref[0:1, :], pairs_ref[1:2, :], PAD)
    pair = lax.broadcasted_iota(jnp.int32, design.shape, 1)
    kept = jnp.where(pair < counts_ref[run], design, 0.0).astype(jnp.bfloat16)
    sums = jnp.dot(kept, data_ref[...], preferred_element_type=F32)
    out_ref[...] = jnp.dot(inverse_ref[0, :M, :], sums, precision=HIGHEST, preferred_element_type=F32)


def sum_solve(run_counts, date_pairs, received, inverse):
    runs = run_counts.shape[0]
    total_pairs, pixels = received.shape
    run_pixels = pixels // runs
    tile = run_pixels // 2
    tiles = run_pixels // tile
    return pl.pallas_call(
        functools.partial(sum_solve_kernel, tiles),
        out_shape=jax.ShapeDtypeStruct((M, pixels), F32),
        grid_spec=pltpu.PrefetchScalarGridSpec(
            num_scalar_prefetch=1,
            grid=(runs * tiles,),
            in_specs=[
                pl.BlockSpec(date_pairs.shape, lambda i, c: (0, 0)),
                pl.BlockSpec((total_pairs, tile), lambda i, c: (0, i)),
                pl.BlockSpec((1, PAD, PAD), lambda i, c: (i // tiles, 0, 0)),
            ],
            out_specs=pl.BlockSpec((M, tile), lambda i, c: (0, i)),
        ),
        compiler_params=pltpu.CompilerParams(vmem_limit_bytes=VMEM_BYTES),
        name="sum_solve",
    )(run_counts, date_pairs, received, inverse)


def coded_rows(piece):
    return M * (piece // LANES) + CODE_ROWS


def decode(coded_ref, codes_ref, lots, first):
    coded = coded_ref[...].astype(jnp.int32).astype(F32)
    values = jnp.concatenate([coded[lot * M : (lot + 1) * M, :] for lot in range(lots)], axis=1)
    codes = codes_ref[...].astype(jnp.int32).astype(F32)
    codes = jnp.concatenate([codes[first + lot : first + lot + 1, :] for lot in range(lots)], axis=1)
    return values, jnp.exp2(codes * (1.0 / CODES_PER_OCTAVE)) * (1.0 / LEVELS)


def encode(sums):
    largest = jnp.max(jnp.abs(sums), axis=0, keepdims=True)
    code = jnp.ceil(jnp.log2(jnp.maximum(largest, SMALLEST)) * CODES_PER_OCTAVE)
    scaled = (sums * (LEVELS / jnp.exp2(code * (1.0 / CODES_PER_OCTAVE))) + ROUNDER) - ROUNDER
    lots = sums.shape[1] // LANES
    return jnp.concatenate([scaled[:, lot * LANES : (lot + 1) * LANES] for lot in range(lots)], axis=0), code


def whole(values):
    return values.astype(jnp.int32).astype(jnp.int16)


def piece_count(at, layout, table, counts):
    parts, _, _, shifts = layout
    run = at % parts // CUTS
    return counts[table[shifts + at] * (parts // CUTS) + run]


def pair_sums(count, table, pairs_ref, first_ref, second_ref, members=(ME, PARTNER)):
    width = first_ref.shape[0]
    lane = lax.broadcasted_iota(jnp.int32, (1, 2 * width), 1)
    pair = jnp.where(lane < width, table[members[0]] * width + lane, table[members[1]] * width + lane - width)
    dates = pairs_ref[:, members[0] * width : (members[0] + 2) * width]
    design = incidence(dates[0:1, :], dates[1:2, :], M)
    kept = jnp.where(pair < count, design, 0.0).astype(jnp.bfloat16)
    data = jnp.concatenate([first_ref[...], second_ref[...]], axis=0)
    return jnp.dot(kept, data, preferred_element_type=F32)


def near_sums(wanted, count, table, pairs_ref, raw_refs):
    return pair_sums(jnp.where(wanted, count, 0), table, pairs_ref, *raw_refs, members=(NEAR, NEAR_PARTNER))


def step_kernel(at, layout, adds, swaps, halves, table, counts, pairs_ref, own_ref, partner_ref, *rest):
    if swaps:
        rest[-1][...] = rest[0][...]
        coded_ref, rest = rest[-2], rest[1:]
    else:
        coded_ref = rest[-1]
    count = piece_count(at, layout, table, counts)
    width = own_ref.shape[1] // halves
    lots = width // LANES
    codes = []
    for half in range(halves):
        part = pl.ds(half * width, width)
        sums = pair_sums(count, table, pairs_ref, own_ref.at[:, part], partner_ref.at[:, part])
        if adds == 1:
            rows = pl.ds(half * lots * M, lots * M)
            values, scale = decode(rest[0].at[rows, :], rest[0].at[halves * lots * M :, :], lots, half * lots)
            sums = sums + values * (scale * table[INNER].astype(F32))
        if adds == 2:
            sums = sums + near_sums(table[INNER] == 1, count, table, pairs_ref, [raw_ref.at[:, part] for raw_ref in rest[:2]])
        scaled, code = encode(sums)
        coded_ref[half * lots * M : (half + 1) * lots * M, :] = whole(scaled)
        codes += [code[:, lot * LANES : (lot + 1) * LANES] for lot in range(lots)]
    codes += [jnp.zeros((CODE_ROWS - len(codes), LANES), F32)]
    coded_ref[halves * lots * M :, :] = whole(jnp.concatenate(codes, axis=0))


def step(at, swap, layout, scalars, pairs, phases, partner, earlier, after, piece):
    partner, place_in = partner
    local_pairs = phases.shape[0]
    _, blocks, away, _ = layout
    coded_shape = (coded_rows(piece), LANES)
    in_specs = [
        pl.BlockSpec(pairs.shape, lambda i, t, c: (0, 0)),
        pl.BlockSpec((local_pairs, piece), lambda i, t, c: (0, t[blocks + at])),
        pl.BlockSpec((local_pairs, piece), lambda i, t, c: (0, place_in)),
    ]
    operands = [pairs, phases, partner]
    out_shape = [jax.ShapeDtypeStruct(coded_shape, jnp.int16)]
    out_specs = [pl.BlockSpec(coded_shape, lambda i, t, c: (0, 0))]
    if swap is not None:
        first, count = swap
        wide = piece * count
        in_specs.append(pl.BlockSpec((local_pairs, wide), lambda i, t, c: (0, t[away + first] // count)))
        operands.append(phases)
        out_shape.append(jax.ShapeDtypeStruct((local_pairs, wide), phases.dtype))
        out_specs.append(pl.BlockSpec((local_pairs, wide), lambda i, t, c: (0, 0)))
    in_specs += [pl.BlockSpec(each.shape, lambda i, t, c: (0, 0)) for each in earlier]
    operands += earlier
    in_specs += [pl.BlockSpec(memory_space=pl.ANY)] * len(after)
    results = pl.pallas_call(
        functools.partial(step_kernel, at, layout, len(earlier), swap is not None, HALVES),
        out_shape=out_shape,
        grid_spec=pltpu.PrefetchScalarGridSpec(
            num_scalar_prefetch=2,
            grid=(1,),
            in_specs=in_specs,
            out_specs=out_specs,
        ),
        compiler_params=pltpu.CompilerParams(vmem_limit_bytes=VMEM_BYTES),
        cost_estimate=STEADY,
        name=f"sum_step_{at:02d}",
    )(*scalars, *operands, *after)
    return results[0], results[1] if swap is not None else None


def add_coded(sums_ref, coded_ref, half, halves):
    lots = sums_ref.shape[1] // LANES
    first = half * lots
    coded = coded_ref[first * M : (first + lots) * M, :].astype(jnp.int32).astype(F32)
    codes = coded_ref[halves * lots * M :, :].astype(jnp.int32).astype(F32)
    scale = jnp.exp2(codes * (1.0 / CODES_PER_OCTAVE)) * (1.0 / LEVELS)
    for lot in range(lots):
        lanes = slice(lot * LANES, (lot + 1) * LANES)
        sums_ref[:M, lanes] += coded[lot * M : (lot + 1) * M, :] * scale[first + lot : first + lot + 1, :]


def solve_product(inverse, sums):
    def halves(value):
        high = value.astype(jnp.bfloat16)
        return high, (value - high.astype(F32)).astype(jnp.bfloat16)

    inverse_high, inverse_low = halves(inverse)
    sums_high, sums_low = halves(sums)
    left = jnp.concatenate([inverse_high, inverse_high, inverse_low], axis=1)
    right = jnp.concatenate([sums_high, sums_low, sums_high], axis=0)
    return jnp.dot(left, right, preferred_element_type=F32)


def finish_kernel(at, layout, halves, raw, told, table, counts, pairs_ref, own_ref, partner_ref, inverse_ref, *rest):
    first, middle_ref, last_ref = rest[: max(raw, 1)], rest[max(raw, 1)], rest[max(raw, 1) + 1]
    sums_ref, rest = rest[-1], rest[:-1]
    if told:
        rest[-1][...] = jnp.zeros_like(rest[-1])
        rest = rest[:-1]
    out_ref = rest[-1]
    count = piece_count(at, layout, table, counts)
    width = sums_ref.shape[1]
    sums_ref[M:, :] = jnp.zeros((PAD - M, width), F32)
    for half in range(halves):
        part = pl.ds(half * width, width)
        sums_ref[:M, :] = pair_sums(count, table, pairs_ref, own_ref.at[:, part], partner_ref.at[:, part])

        @pl.when(table[INNER] == 0)
        def _():
            if raw:
                sums_ref[:M, :] += near_sums(True, count, table, pairs_ref, [each.at[:, part] for each in first])
            else:
                add_coded(sums_ref, first[0], half, halves)

        @pl.when(table[INNER] == 1)
        def _():
            add_coded(sums_ref, middle_ref, half, halves)

        add_coded(sums_ref, last_ref, half, halves)
        out_ref[:, part] = solve_product(inverse_ref[0, :M, :], sums_ref[...])


def finish(at, part, layout, scalars, pairs, phases, partner, inverse, raw, arrived, series, told, pixels, piece):
    partner, place_in = partner
    local_pairs = phases.shape[0]
    blocks = layout[1]
    whole_block = lambda i, t, c: (0, 0)
    in_specs = [
        pl.BlockSpec(pairs.shape, whole_block),
        pl.BlockSpec((local_pairs, piece), lambda i, t, c: (0, t[blocks + at])),
        pl.BlockSpec((local_pairs, piece), lambda i, t, c: (0, place_in)),
        pl.BlockSpec((1, PAD, PAD), lambda i, t, c: (0, 0, 0)),
    ]
    in_specs += [pl.BlockSpec(each.shape, whole_block) for each in [*raw, *arrived]]
    operands = [*scalars, pairs, phases, partner, inverse, *raw, *arrived]
    aliases = {}
    if series is not None:
        in_specs.append(pl.BlockSpec(memory_space=pl.ANY))
        aliases = {len(operands): 0}
        operands.append(series)
    out_shape = [jax.ShapeDtypeStruct((M, pixels), F32)]
    out_specs = [pl.BlockSpec((M, piece), lambda i, t, c: (0, part))]
    if told:
        out_shape.append(jax.ShapeDtypeStruct((8, LANES), F32))
        out_specs.append(pl.BlockSpec((8, LANES), lambda i, t, c: (0, 0)))
    return pl.pallas_call(
        functools.partial(finish_kernel, at, layout, HALVES, len(raw), told),
        out_shape=out_shape,
        grid_spec=pltpu.PrefetchScalarGridSpec(
            num_scalar_prefetch=2,
            grid=(1,),
            in_specs=in_specs,
            out_specs=out_specs,
            scratch_shapes=[pltpu.VMEM((PAD, piece // HALVES), F32)],
        ),
        input_output_aliases=aliases,
        compiler_params=pltpu.CompilerParams(vmem_limit_bytes=VMEM_BYTES),
        cost_estimate=LITTLE,
        name=f"finish_{part}",
    )(*operands)


def line_permutation(links):
    return [(2 * source + side, 2 * target + side) for source, target in links for side in range(2)]


def solve_by_sums(phases, date_pairs, counts_of):
    owner_count = lax.axis_size("ifg")
    line = owner_count // 2
    local_pairs, pixels = phases.shape
    owner_pixels = pixels // owner_count
    runs = counts_of(None).shape[0]
    parts = runs * CUTS
    piece = owner_pixels // parts
    steps = (line - 1) * parts
    me = lax.axis_index("ifg")

    places = np.repeat(np.array(CHUNK_ORDER), parts, axis=1)
    part_of = np.tile(np.arange(parts), line)
    rows = []
    for device in range(owner_count):
        place, side = device // 2, device % 2
        own = (places[place] * 2 + side) * parts + part_of
        away = (places[place] * 2 + 1 - side) * parts + part_of
        shift = (place - places[place]) % line
        rows.append(np.concatenate([[device, device ^ 1, device ^ 2, device ^ 3, int(0 < place < line - 1)], own, away, shift]))
    row = lax.dynamic_index_in_dim(jnp.asarray(np.stack(rows), jnp.int32), me, 0, keepdims=False)
    head, pieces = FIXED, line * parts
    layout = (parts, head, head + pieces, head + 2 * pieces)

    swap = [(i, i ^ 1) for i in range(owner_count)]
    partner_of = {}

    def swapped(away, first, count):
        here = lax.ppermute(away, "ifg", swap)
        partner_of.update({first + place: (here, place) for place in range(count)})

    place, side = me // 2, me % 2
    chunk = jnp.where(place < line // 2, 2 - 2 * place, 7 - 2 * place)

    def first_away(column, part, count, after):
        block = (chunk * 2 + column) * parts + part
        if after is not None:
            block, _ = lax.optimization_barrier((block, after))
        return lax.dynamic_slice(phases, (0, block * piece), (local_pairs, count * piece))

    away = first_away(1 - side, *FIRST_SWAP, None)
    swapped(away, *FIRST_SWAP)
    run_counts = counts_of(away)
    counts = [run_counts]
    for distance in range(1, line):
        links = [(i, (i + distance) % line) for i in range(line)]
        counts.append(lax.ppermute(run_counts, "ifg", line_permutation(links)))
    counts = jnp.concatenate(counts)
    raw_part = parts - 1
    near = line_permutation(SENDS[0][0])
    raw_other = lax.ppermute(first_away(1 - side, raw_part, 1, run_counts), "ifg", near)
    raw_own = lax.ppermute(first_away(side, raw_part, 1, run_counts), "ifg", near)
    pairs = jnp.concatenate([lax.dynamic_slice(date_pairs, (0, (me ^ at) * local_pairs), (2, local_pairs)) for at in range(4)], axis=1)
    scalars = (row, counts)

    received, sent, coded, series, inverses = {raw_part: [raw_own, raw_other]}, [raw_part], None, None, []

    def finished(part, series, told):
        at = steps + part
        arrived = [received[place * parts + part][-1] for place in range(1 if part == raw_part else 0, line - 1)]
        data = (layout, scalars, pairs, phases, partner_of[at], inverses[part // CUTS], raw if part == raw_part else [], arrived)
        return finish(at, part, *data, series, told, owner_pixels, piece)

    for at in [each for each in range(steps) if each != raw_part]:
        earlier = [] if at < parts else raw if at == parts + raw_part else [received[at - parts][0]]
        after = [] if coded is None else [coded]
        after += received[sent[-FLIGHT]] if len(sent) >= FLIGHT else []
        if at in SWAP_WAITS:
            after.append(partner_of[SWAP_WAITS[at]][0])
        if at == RAW_WAIT:
            after.append(raw[1])
        if at in INVERSE_STEPS:
            run = len(inverses)
            inverses.append(invert_classes(run, 1, date_pairs, run_counts, [counts if coded is None else coded]))
            after.append(inverses[-1])
        if at == steps - 1:
            for part in range(FINISHED_AHEAD):
                series, told = finished(part, series, True)
                after.append(told)
        coded, away = step(at, SWAPS.get(at), layout, scalars, pairs, phases, partner_of[at], earlier, after, piece)
        received[at] = [lax.ppermute(coded, "ifg", line_permutation(links)) for links in SENDS[at // parts]]
        sent.append(at)
        if at in SWAPS:
            swapped(away, *SWAPS[at])
        if at == RAW_STEP:
            raw_other, _ = lax.optimization_barrier((raw_other, coded))
            raw = [raw_own, lax.ppermute(raw_other, "ifg", swap)]

    for part in range(FINISHED_AHEAD, parts):
        series = finished(part, series, False)[0]
    return series


def solve_by_blocks(phases, date_pairs, counts_of):
    owner_count = lax.axis_size("ifg")
    local_pairs, pixels = phases.shape
    owner_pixels = pixels // owner_count
    run_counts = counts_of(None)
    outgoing = phases.reshape(local_pairs, owner_count, owner_pixels).transpose(1, 0, 2)
    received = lax.all_to_all(outgoing, "ifg", split_axis=0, concat_axis=0, tiled=True)
    inverse = invert_classes(0, run_counts.shape[0], date_pairs, run_counts, [])
    return sum_solve(run_counts, date_pairs, received.reshape(-1, owner_pixels), inverse)


def local(phases, date_pairs, pair_counts, group_ids):
    local_pairs, _, pixels = phases.shape

    def counts_of(after):
        groups = group_ids if after is None else lax.optimization_barrier((group_ids, after))[0]
        strip_groups = lax.dynamic_index_in_dim(groups, lax.axis_index("grp"), 0, keepdims=False)[::RUN]
        chosen = strip_groups[:, None] == jnp.arange(pair_counts.shape[0], dtype=jnp.int32)
        return jnp.sum(jnp.where(chosen, pair_counts, 0), axis=1)

    line = lax.axis_size("ifg") == 2 * len(CHUNK_ORDER) and group_ids.shape[1] == 2 * RUN
    by_sums = line and 2 * local_pairs > M and local_pairs % LANES == 0 and lax.axis_size("grp") % 2 == 0
    solve = solve_by_sums if by_sums else solve_by_blocks
    return solve(phases.reshape(local_pairs, pixels), date_pairs, counts_of)[None, :, :]


def solution(mesh):
    in_specs = (P("ifg", "grp", None), P(), P(), P(None, "ifg"))
    out_specs = P("grp", None, "ifg")
    return jax.shard_map(local, mesh=mesh, in_specs=in_specs, out_specs=out_specs, check_vma=False)
```

```python
import functools

import jax
import jax.numpy as jnp
import numpy as np
from jax import lax
from jax.experimental import pallas as pl
from jax.experimental.pallas import tpu as pltpu
from jax.sharding import PartitionSpec as P

M = 200
RUN = 8
PAD = 256
SLABS = 8
DAMPING = 1.0
VMEM_BYTES = 48 * 1024 * 1024
F32 = jnp.float32
HIGHEST = lax.Precision.HIGHEST
STEADY = pl.CostEstimate(flops=10_000_000_000, bytes_accessed=30_000_000, transcendentals=0)
LITTLE = pl.CostEstimate(flops=1024, bytes_accessed=1024, transcendentals=0)
CUTS = 2
HALVES = 1
FLIGHT = 2
FIRST_SWAP = (0, 2)
SWAPS = {0: (2, 1), 1: (4, 2), 2: (6, 2), 5: (8, 2), 7: (10, 2), 8: (12, 2), 9: (14, 2)}
SWAP_WAITS = {}
RAW_STEP, RAW_WAIT = 2, 5
INVERSE_STEP = 0
FINISHED_AHEAD = 1
ME, PARTNER, NEAR, NEAR_PARTNER, INNER, FIXED = 0, 1, 2, 3, 4, 5
LANES = 128
CODE_ROWS = 16
LEVELS = 32700.0
ROUNDER = 1.5 * 2.0**23
CODES_PER_OCTAVE = 128.0
SMALLEST = 2.0**-110
CHUNK_ORDER = ((2, 3, 1, 0), (0, 2, 3, 1), (3, 1, 0, 2), (1, 0, 2, 3))
SENDS = (
    (((0, 1), (1, 0), (2, 3), (3, 2)),),
    (((0, 1), (3, 2)), ((1, 2), (2, 1))),
    (((0, 1), (1, 3), (2, 0), (3, 2)),),
)


def incidence(earlier, later, rows):
    shape = (rows, earlier.shape[1])
    date = lax.broadcasted_iota(jnp.int32, shape, 0)
    return (date == later).astype(F32) - (date == earlier).astype(F32)


def split_product(left, right):
    def halves(value):
        high = value.astype(jnp.bfloat16)
        return high, (value - high.astype(F32)).astype(jnp.bfloat16)

    left_high, left_low = halves(left)
    right_high, right_low = halves(right)
    small = jnp.dot(left_high, right_low, preferred_element_type=F32) + jnp.dot(left_low, right_high, preferred_element_type=F32)
    return jnp.dot(left_high, right_high, preferred_element_type=F32) + small


def full_product(left, right):
    return jnp.dot(left, right, precision=HIGHEST, preferred_element_type=F32)


def inverse_kernel(counts_ref, pairs_ref, *rest):
    out_ref = rest[-1]
    runs = out_ref.shape[0]
    design = incidence(pairs_ref[0:1, :], pairs_ref[1:2, :], PAD)
    pair = lax.broadcasted_iota(jnp.int32, design.shape, 1)
    contract_last = (((1,), (1,)), ((), ()))
    row = lax.broadcasted_iota(jnp.int32, (PAD, PAD), 0)
    col = lax.broadcasted_iota(jnp.int32, (PAD, PAD), 1)
    identity = (row == col).astype(F32)
    grams = []
    for run in range(runs):
        kept = jnp.where(pair < counts_ref[run], design, 0.0).astype(jnp.bfloat16)
        gram = lax.dot_general(kept, kept, contract_last, preferred_element_type=F32)
        grams.append(gram + DAMPING * identity)
    low = DAMPING
    high = 2.0 * functools.reduce(jnp.maximum, [jnp.max(gram) for gram in grams]) - DAMPING
    total, width = high + low, high - low
    scale = 2.0 * total * total - width * width
    starts = tuple((8.0 * total / scale) * identity - (8.0 / scale) * gram for gram in grams)
    needed = 18.0 * scale / (8.0 * high * low)
    steps = jnp.int32(0)
    for power in range(1, 16):
        steps += (needed > float(2**power)).astype(jnp.int32)

    def newton(product, guesses):
        products = [product(gram, guess) for gram, guess in zip(grams, guesses)]
        return tuple(2.0 * guess - product(guess, each) for guess, each in zip(guesses, products))

    full_steps = 1 + (high > 100.0).astype(jnp.int32)
    guesses = lax.fori_loop(0, steps + 1 - full_steps, lambda _, guesses: newton(split_product, guesses), starts)
    guesses = lax.fori_loop(0, full_steps, lambda _, guesses: newton(full_product, guesses), guesses)
    for run, guess in enumerate(guesses):
        out_ref[run] = guess


def invert_classes(date_pairs, run_counts, after):
    shape = (run_counts.shape[0], PAD, PAD)
    return pl.pallas_call(
        inverse_kernel,
        out_shape=jax.ShapeDtypeStruct(shape, F32),
        grid_spec=pltpu.PrefetchScalarGridSpec(
            num_scalar_prefetch=1,
            grid=(1,),
            in_specs=[pl.BlockSpec(date_pairs.shape, lambda i, c: (0, 0))] + [pl.BlockSpec(memory_space=pl.ANY)] * len(after),
            out_specs=pl.BlockSpec(shape, lambda i, c: (0, 0, 0)),
        ),
        compiler_params=pltpu.CompilerParams(vmem_limit_bytes=VMEM_BYTES),
        cost_estimate=LITTLE,
        name="invert_classes_0",
    )(run_counts, date_pairs, *after)


def sum_solve_kernel(tiles, counts_ref, pairs_ref, data_ref, inverse_ref, out_ref):
    run = pl.program_id(0) // tiles
    design = incidence(pairs_ref[0:1, :], pairs_ref[1:2, :], PAD)
    pair = lax.broadcasted_iota(jnp.int32, design.shape, 1)
    kept = jnp.where(pair < counts_ref[run], design, 0.0).astype(jnp.bfloat16)
    sums = jnp.dot(kept, data_ref[...], preferred_element_type=F32)
    out_ref[...] = jnp.dot(inverse_ref[0, :M, :], sums, precision=HIGHEST, preferred_element_type=F32)


def sum_solve(run_counts, date_pairs, received, inverse):
    runs = run_counts.shape[0]
    total_pairs, pixels = received.shape
    run_pixels = pixels // runs
    tile = run_pixels // 2
    tiles = run_pixels // tile
    return pl.pallas_call(
        functools.partial(sum_solve_kernel, tiles),
        out_shape=jax.ShapeDtypeStruct((M, pixels), F32),
        grid_spec=pltpu.PrefetchScalarGridSpec(
            num_scalar_prefetch=1,
            grid=(runs * tiles,),
            in_specs=[
                pl.BlockSpec(date_pairs.shape, lambda i, c: (0, 0)),
                pl.BlockSpec((total_pairs, tile), lambda i, c: (0, i)),
                pl.BlockSpec((1, PAD, PAD), lambda i, c: (i // tiles, 0, 0)),
            ],
            out_specs=pl.BlockSpec((M, tile), lambda i, c: (0, i)),
        ),
        compiler_params=pltpu.CompilerParams(vmem_limit_bytes=VMEM_BYTES),
        name="sum_solve",
    )(run_counts, date_pairs, received, inverse)


def coded_rows(piece):
    return M * (piece // LANES) + CODE_ROWS


def decode(coded_ref, codes_ref, lots, first):
    coded = coded_ref[...].astype(jnp.int32).astype(F32)
    values = jnp.concatenate([coded[lot * M : (lot + 1) * M, :] for lot in range(lots)], axis=1)
    codes = codes_ref[...].astype(jnp.int32).astype(F32)
    codes = jnp.concatenate([codes[first + lot : first + lot + 1, :] for lot in range(lots)], axis=1)
    return values, jnp.exp2(codes * (1.0 / CODES_PER_OCTAVE)) * (1.0 / LEVELS)


def encode(sums):
    largest = jnp.max(jnp.abs(sums), axis=0, keepdims=True)
    code = jnp.ceil(jnp.log2(jnp.maximum(largest, SMALLEST)) * CODES_PER_OCTAVE)
    scaled = (sums * (LEVELS / jnp.exp2(code * (1.0 / CODES_PER_OCTAVE))) + ROUNDER) - ROUNDER
    lots = sums.shape[1] // LANES
    return jnp.concatenate([scaled[:, lot * LANES : (lot + 1) * LANES] for lot in range(lots)], axis=0), code


def whole(values):
    return values.astype(jnp.int32).astype(jnp.int16)


def piece_count(at, layout, table, counts):
    parts, _, _, shifts = layout
    run = at % parts // CUTS
    return counts[table[shifts + at] * (parts // CUTS) + run]


def pair_sums(count, table, pairs_ref, first_ref, second_ref, members=(ME, PARTNER)):
    width = first_ref.shape[0]
    lane = lax.broadcasted_iota(jnp.int32, (1, 2 * width), 1)
    pair = jnp.where(lane < width, table[members[0]] * width + lane, table[members[1]] * width + lane - width)
    dates = pairs_ref[:, members[0] * width : (members[0] + 2) * width]
    design = incidence(dates[0:1, :], dates[1:2, :], M)
    kept = jnp.where(pair < count, design, 0.0).astype(jnp.bfloat16)
    data = jnp.concatenate([first_ref[...], second_ref[...]], axis=0)
    return jnp.dot(kept, data, preferred_element_type=F32)


def near_sums(wanted, count, table, pairs_ref, raw_refs):
    return pair_sums(jnp.where(wanted, count, 0), table, pairs_ref, *raw_refs, members=(NEAR, NEAR_PARTNER))


def step_kernel(at, layout, adds, swaps, halves, table, counts, pairs_ref, own_ref, partner_ref, *rest):
    if swaps:
        rest[-1][...] = rest[0][...]
        coded_ref, rest = rest[-2], rest[1:]
    else:
        coded_ref = rest[-1]
    count = piece_count(at, layout, table, counts)
    width = own_ref.shape[1] // halves
    lots = width // LANES
    codes = []
    for half in range(halves):
        part = pl.ds(half * width, width)
        sums = pair_sums(count, table, pairs_ref, own_ref.at[:, part], partner_ref.at[:, part])
        if adds == 1:
            rows = pl.ds(half * lots * M, lots * M)
            values, scale = decode(rest[0].at[rows, :], rest[0].at[halves * lots * M :, :], lots, half * lots)
            sums = sums + values * (scale * table[INNER].astype(F32))
        if adds == 2:
            sums = sums + near_sums(table[INNER] == 1, count, table, pairs_ref, [raw_ref.at[:, part] for raw_ref in rest[:2]])
        scaled, code = encode(sums)
        coded_ref[half * lots * M : (half + 1) * lots * M, :] = whole(scaled)
        codes += [code[:, lot * LANES : (lot + 1) * LANES] for lot in range(lots)]
    codes += [jnp.zeros((CODE_ROWS - len(codes), LANES), F32)]
    coded_ref[halves * lots * M :, :] = whole(jnp.concatenate(codes, axis=0))


def step(at, swap, layout, scalars, pairs, phases, partner, earlier, after, piece):
    partner, place_in = partner
    local_pairs = phases.shape[0]
    _, blocks, away, _ = layout
    coded_shape = (coded_rows(piece), LANES)
    in_specs = [
        pl.BlockSpec(pairs.shape, lambda i, t, c: (0, 0)),
        pl.BlockSpec((local_pairs, piece), lambda i, t, c: (0, t[blocks + at])),
        pl.BlockSpec((local_pairs, piece), lambda i, t, c: (0, place_in)),
    ]
    operands = [pairs, phases, partner]
    out_shape = [jax.ShapeDtypeStruct(coded_shape, jnp.int16)]
    out_specs = [pl.BlockSpec(coded_shape, lambda i, t, c: (0, 0))]
    if swap is not None:
        first, count = swap
        wide = piece * count
        in_specs.append(pl.BlockSpec((local_pairs, wide), lambda i, t, c: (0, t[away + first] // count)))
        operands.append(phases)
        out_shape.append(jax.ShapeDtypeStruct((local_pairs, wide), phases.dtype))
        out_specs.append(pl.BlockSpec((local_pairs, wide), lambda i, t, c: (0, 0)))
    in_specs += [pl.BlockSpec(each.shape, lambda i, t, c: (0, 0)) for each in earlier]
    operands += earlier
    in_specs += [pl.BlockSpec(memory_space=pl.ANY)] * len(after)
    results = pl.pallas_call(
        functools.partial(step_kernel, at, layout, len(earlier), swap is not None, HALVES),
        out_shape=out_shape,
        grid_spec=pltpu.PrefetchScalarGridSpec(
            num_scalar_prefetch=2,
            grid=(1,),
            in_specs=in_specs,
            out_specs=out_specs,
        ),
        compiler_params=pltpu.CompilerParams(vmem_limit_bytes=VMEM_BYTES),
        cost_estimate=STEADY,
        name=f"sum_step_{at:02d}",
    )(*scalars, *operands, *after)
    return results[0], results[1] if swap is not None else None


def add_coded(sums_ref, coded_ref, half, halves):
    lots = sums_ref.shape[1] // LANES
    first = half * lots
    coded = coded_ref[first * M : (first + lots) * M, :].astype(jnp.int32).astype(F32)
    codes = coded_ref[halves * lots * M :, :].astype(jnp.int32).astype(F32)
    scale = jnp.exp2(codes * (1.0 / CODES_PER_OCTAVE)) * (1.0 / LEVELS)
    for lot in range(lots):
        lanes = slice(lot * LANES, (lot + 1) * LANES)
        sums_ref[:M, lanes] += coded[lot * M : (lot + 1) * M, :] * scale[first + lot : first + lot + 1, :]


def solve_product(inverse, sums):
    def halves(value):
        high = value.astype(jnp.bfloat16)
        return high, (value - high.astype(F32)).astype(jnp.bfloat16)

    inverse_high, inverse_low = halves(inverse)
    sums_high, sums_low = halves(sums)
    left = jnp.concatenate([inverse_high, inverse_high, inverse_low], axis=1)
    right = jnp.concatenate([sums_high, sums_low, sums_high], axis=0)
    return jnp.dot(left, right, preferred_element_type=F32)


def finish_kernel(at, layout, halves, raw, told, table, counts, pairs_ref, own_ref, partner_ref, inverse_ref, *rest):
    first, middle_ref, last_ref = rest[: max(raw, 1)], rest[max(raw, 1)], rest[max(raw, 1) + 1]
    sums_ref, rest = rest[-1], rest[:-1]
    if told:
        rest[-1][...] = jnp.zeros_like(rest[-1])
        rest = rest[:-1]
    out_ref = rest[-1]
    count = piece_count(at, layout, table, counts)
    width = sums_ref.shape[1]
    sums_ref[M:, :] = jnp.zeros((PAD - M, width), F32)
    for half in range(halves):
        part = pl.ds(half * width, width)
        sums_ref[:M, :] = pair_sums(count, table, pairs_ref, own_ref.at[:, part], partner_ref.at[:, part])

        @pl.when(table[INNER] == 0)
        def _():
            if raw:
                sums_ref[:M, :] += near_sums(True, count, table, pairs_ref, [each.at[:, part] for each in first])
            else:
                add_coded(sums_ref, first[0], half, halves)

        @pl.when(table[INNER] == 1)
        def _():
            add_coded(sums_ref, middle_ref, half, halves)

        add_coded(sums_ref, last_ref, half, halves)
        out_ref[:, part] = solve_product(inverse_ref[0, :M, :], sums_ref[...])


def finish(at, part, layout, scalars, pairs, phases, partner, inverse, raw, arrived, series, told, pixels, piece):
    partner, place_in = partner
    local_pairs = phases.shape[0]
    blocks = layout[1]
    whole_block = lambda i, t, c: (0, 0)
    in_specs = [
        pl.BlockSpec(pairs.shape, whole_block),
        pl.BlockSpec((local_pairs, piece), lambda i, t, c: (0, t[blocks + at])),
        pl.BlockSpec((local_pairs, piece), lambda i, t, c: (0, place_in)),
        pl.BlockSpec((1, PAD, PAD), lambda i, t, c: (part // CUTS, 0, 0)),
    ]
    in_specs += [pl.BlockSpec(each.shape, whole_block) for each in [*raw, *arrived]]
    operands = [*scalars, pairs, phases, partner, inverse, *raw, *arrived]
    aliases = {}
    if series is not None:
        in_specs.append(pl.BlockSpec(memory_space=pl.ANY))
        aliases = {len(operands): 0}
        operands.append(series)
    out_shape = [jax.ShapeDtypeStruct((M, pixels), F32)]
    out_specs = [pl.BlockSpec((M, piece), lambda i, t, c: (0, part))]
    if told:
        out_shape.append(jax.ShapeDtypeStruct((8, LANES), F32))
        out_specs.append(pl.BlockSpec((8, LANES), lambda i, t, c: (0, 0)))
    return pl.pallas_call(
        functools.partial(finish_kernel, at, layout, HALVES, len(raw), told),
        out_shape=out_shape,
        grid_spec=pltpu.PrefetchScalarGridSpec(
            num_scalar_prefetch=2,
            grid=(1,),
            in_specs=in_specs,
            out_specs=out_specs,
            scratch_shapes=[pltpu.VMEM((PAD, piece // HALVES), F32)],
        ),
        input_output_aliases=aliases,
        compiler_params=pltpu.CompilerParams(vmem_limit_bytes=VMEM_BYTES),
        cost_estimate=LITTLE,
        name=f"finish_{part}",
    )(*operands)


def line_permutation(links):
    return [(2 * source + side, 2 * target + side) for source, target in links for side in range(2)]


def solve_by_sums(phases, date_pairs, counts_of):
    owner_count = lax.axis_size("ifg")
    line = owner_count // 2
    local_pairs, pixels = phases.shape
    owner_pixels = pixels // owner_count
    runs = counts_of(None).shape[0]
    parts = runs * CUTS
    piece = owner_pixels // parts
    steps = (line - 1) * parts
    me = lax.axis_index("ifg")

    places = np.repeat(np.array(CHUNK_ORDER), parts, axis=1)
    part_of = np.tile(np.arange(parts), line)
    rows = []
    for device in range(owner_count):
        place, side = device // 2, device % 2
        own = (places[place] * 2 + side) * parts + part_of
        away = (places[place] * 2 + 1 - side) * parts + part_of
        shift = (place - places[place]) % line
        rows.append(np.concatenate([[device, device ^ 1, device ^ 2, device ^ 3, int(0 < place < line - 1)], own, away, shift]))
    row = lax.dynamic_index_in_dim(jnp.asarray(np.stack(rows), jnp.int32), me, 0, keepdims=False)
    head, pieces = FIXED, line * parts
    layout = (parts, head, head + pieces, head + 2 * pieces)

    swap = [(i, i ^ 1) for i in range(owner_count)]
    partner_of = {}

    def swapped(away, first, count):
        here = lax.ppermute(away, "ifg", swap)
        partner_of.update({first + place: (here, place) for place in range(count)})

    place, side = me // 2, me % 2
    chunk = jnp.where(place < line // 2, 2 - 2 * place, 7 - 2 * place)

    def first_away(column, part, count, after):
        block = (chunk * 2 + column) * parts + part
        if after is not None:
            block, _ = lax.optimization_barrier((block, after))
        return lax.dynamic_slice(phases, (0, block * piece), (local_pairs, count * piece))

    away = first_away(1 - side, *FIRST_SWAP, None)
    swapped(away, *FIRST_SWAP)
    run_counts = counts_of(away)
    counts = [run_counts]
    for distance in range(1, line):
        links = [(i, (i + distance) % line) for i in range(line)]
        counts.append(lax.ppermute(run_counts, "ifg", line_permutation(links)))
    counts = jnp.concatenate(counts)
    raw_part = parts - 1
    near = line_permutation(SENDS[0][0])
    raw_other = lax.ppermute(first_away(1 - side, raw_part, 1, run_counts), "ifg", near)
    raw_own = lax.ppermute(first_away(side, raw_part, 1, run_counts), "ifg", near)
    pairs = jnp.concatenate([lax.dynamic_slice(date_pairs, (0, (me ^ at) * local_pairs), (2, local_pairs)) for at in range(4)], axis=1)
    scalars = (row, counts)

    received, sent, coded, series = {raw_part: [raw_own, raw_other]}, [raw_part], None, None

    def finished(part, series, told):
        at = steps + part
        arrived = [received[place * parts + part][-1] for place in range(1 if part == raw_part else 0, line - 1)]
        data = (layout, scalars, pairs, phases, partner_of[at], inverse, raw if part == raw_part else [], arrived)
        return finish(at, part, *data, series, told, owner_pixels, piece)

    for at in [each for each in range(steps) if each != raw_part]:
        earlier = [] if at < parts else raw if at == parts + raw_part else [received[at - parts][0]]
        after = [] if coded is None else [coded]
        after += received[sent[-FLIGHT]] if len(sent) >= FLIGHT else []
        if at in SWAP_WAITS:
            after.append(partner_of[SWAP_WAITS[at]][0])
        if at == RAW_WAIT:
            after.append(raw[1])
        if at == INVERSE_STEP:
            inverse = invert_classes(date_pairs, run_counts, [counts if coded is None else coded])
            after.append(inverse)
        if at == steps - 1:
            for part in range(FINISHED_AHEAD):
                series, told = finished(part, series, True)
                after.append(told)
        coded, away = step(at, SWAPS.get(at), layout, scalars, pairs, phases, partner_of[at], earlier, after, piece)
        received[at] = [lax.ppermute(coded, "ifg", line_permutation(links)) for links in SENDS[at // parts]]
        sent.append(at)
        if at in SWAPS:
            swapped(away, *SWAPS[at])
        if at == RAW_STEP:
            raw_other, _ = lax.optimization_barrier((raw_other, coded))
            raw = [raw_own, lax.ppermute(raw_other, "ifg", swap)]

    for part in range(FINISHED_AHEAD, parts):
        series = finished(part, series, False)[0]
    return series


def solve_by_blocks(phases, date_pairs, counts_of):
    owner_count = lax.axis_size("ifg")
    local_pairs, pixels = phases.shape
    owner_pixels = pixels // owner_count
    run_counts = counts_of(None)
    outgoing = phases.reshape(local_pairs, owner_count, owner_pixels).transpose(1, 0, 2)
    received = lax.all_to_all(outgoing, "ifg", split_axis=0, concat_axis=0, tiled=True)
    inverse = invert_classes(date_pairs, run_counts, [])
    return sum_solve(run_counts, date_pairs, received.reshape(-1, owner_pixels), inverse)


def local(phases, date_pairs, pair_counts, group_ids):
    local_pairs, _, pixels = phases.shape

    def counts_of(after):
        groups = group_ids if after is None else lax.optimization_barrier((group_ids, after))[0]
        strip_groups = lax.dynamic_index_in_dim(groups, lax.axis_index("grp"), 0, keepdims=False)[::RUN]
        chosen = strip_groups[:, None] == jnp.arange(pair_counts.shape[0], dtype=jnp.int32)
        return jnp.sum(jnp.where(chosen, pair_counts, 0), axis=1)

    line = lax.axis_size("ifg") == 2 * len(CHUNK_ORDER) and group_ids.shape[1] == 2 * RUN
    by_sums = line and 2 * local_pairs > M and local_pairs % LANES == 0 and lax.axis_size("grp") % 2 == 0
    solve = solve_by_sums if by_sums else solve_by_blocks
    return solve(phases.reshape(local_pairs, pixels), date_pairs, counts_of)[None, :, :]


def solution(mesh):
    in_specs = (P("ifg", "grp", None), P(), P(), P(None, "ifg"))
    out_specs = P("grp", None, "ifg")
    return jax.shard_map(local, mesh=mesh, in_specs=in_specs, out_specs=out_specs, check_vma=False)
```

```python
import functools

import jax
import jax.numpy as jnp
import numpy as np
from jax import lax
from jax.experimental import pallas as pl
from jax.experimental.pallas import tpu as pltpu
from jax.sharding import PartitionSpec as P

M = 200
RUN = 8
PAD = 256
SLABS = 8
DAMPING = 1.0
VMEM_BYTES = 48 * 1024 * 1024
F32 = jnp.float32
HIGHEST = lax.Precision.HIGHEST
STEADY = pl.CostEstimate(flops=10_000_000_000, bytes_accessed=30_000_000, transcendentals=0)
LITTLE = pl.CostEstimate(flops=1024, bytes_accessed=1024, transcendentals=0)
CUTS = 2
HALVES = 1
FLIGHT = 2
FIRST_SWAP = (0, 2)
SWAPS = {0: (2, 1), 1: (4, 2), 2: (6, 2), 5: (8, 2), 7: (10, 2), 8: (12, 2), 9: (14, 2)}
SWAP_WAITS = {}
RAW_STEP, RAW_WAIT = 2, 5
INVERSE_STEP = 0
FINISHED_AHEAD = 1
ME, PARTNER, NEAR, NEAR_PARTNER, INNER, FIXED = 0, 1, 2, 3, 4, 5
LANES = 128
CODE_ROWS = 16
LEVELS = 32700.0
ROUNDER = 1.5 * 2.0**23
CODES_PER_OCTAVE = 128.0
SMALLEST = 2.0**-110
CHUNK_ORDER = ((2, 3, 1, 0), (0, 2, 3, 1), (3, 1, 0, 2), (1, 0, 2, 3))
SENDS = (
    (((0, 1), (1, 0), (2, 3), (3, 2)),),
    (((0, 1), (3, 2)), ((1, 2), (2, 1))),
    (((0, 1), (1, 3), (2, 0), (3, 2)),),
)


def incidence(earlier, later, rows):
    shape = (rows, earlier.shape[1])
    date = lax.broadcasted_iota(jnp.int32, shape, 0)
    return (date == later).astype(F32) - (date == earlier).astype(F32)


def split_product(left, right):
    def halves(value):
        high = value.astype(jnp.bfloat16)
        return high, (value - high.astype(F32)).astype(jnp.bfloat16)

    left_high, left_low = halves(left)
    right_high, right_low = halves(right)
    small = jnp.dot(left_high, right_low, preferred_element_type=F32) + jnp.dot(left_low, right_high, preferred_element_type=F32)
    return jnp.dot(left_high, right_high, preferred_element_type=F32) + small


def full_product(left, right):
    return jnp.dot(left, right, precision=HIGHEST, preferred_element_type=F32)


def inverse_kernel(counts_ref, pairs_ref, *rest):
    out_ref = rest[-1]
    runs = out_ref.shape[0]
    design = incidence(pairs_ref[0:1, :], pairs_ref[1:2, :], PAD)
    pair = lax.broadcasted_iota(jnp.int32, design.shape, 1)
    contract_last = (((1,), (1,)), ((), ()))
    row = lax.broadcasted_iota(jnp.int32, (PAD, PAD), 0)
    col = lax.broadcasted_iota(jnp.int32, (PAD, PAD), 1)
    identity = (row == col).astype(F32)
    grams = []
    for run in range(runs):
        kept = jnp.where(pair < counts_ref[run], design, 0.0).astype(jnp.bfloat16)
        gram = lax.dot_general(kept, kept, contract_last, preferred_element_type=F32)
        grams.append(gram + DAMPING * identity)
    low = DAMPING
    high = 2.0 * functools.reduce(jnp.maximum, [jnp.max(gram) for gram in grams]) - DAMPING
    total, width = high + low, high - low
    scale = 2.0 * total * total - width * width
    starts = tuple((8.0 * total / scale) * identity - (8.0 / scale) * gram for gram in grams)
    needed = 18.0 * scale / (8.0 * high * low)
    steps = jnp.int32(0)
    for power in range(1, 16):
        steps += (needed > float(2**power)).astype(jnp.int32)

    def newton(product, guesses):
        products = [product(gram, guess) for gram, guess in zip(grams, guesses)]
        return tuple(2.0 * guess - product(guess, each) for guess, each in zip(guesses, products))

    full_steps = 1 + (high > 100.0).astype(jnp.int32)
    guesses = lax.fori_loop(0, steps + 1 - full_steps, lambda _, guesses: newton(split_product, guesses), starts)
    guesses = lax.fori_loop(0, full_steps, lambda _, guesses: newton(full_product, guesses), guesses)
    for run, guess in enumerate(guesses):
        out_ref[run] = guess


def invert_classes(date_pairs, run_counts, after):
    shape = (run_counts.shape[0], PAD, PAD)
    return pl.pallas_call(
        inverse_kernel,
        out_shape=jax.ShapeDtypeStruct(shape, F32),
        grid_spec=pltpu.PrefetchScalarGridSpec(
            num_scalar_prefetch=1,
            grid=(1,),
            in_specs=[pl.BlockSpec(date_pairs.shape, lambda i, c: (0, 0))] + [pl.BlockSpec(memory_space=pl.ANY)] * len(after),
            out_specs=pl.BlockSpec(shape, lambda i, c: (0, 0, 0)),
        ),
        compiler_params=pltpu.CompilerParams(vmem_limit_bytes=VMEM_BYTES),
        cost_estimate=LITTLE,
        name="invert_classes_0",
    )(run_counts, date_pairs, *after)


def sum_solve_kernel(tiles, counts_ref, pairs_ref, data_ref, inverse_ref, out_ref):
    run = pl.program_id(0) // tiles
    design = incidence(pairs_ref[0:1, :], pairs_ref[1:2, :], PAD)
    pair = lax.broadcasted_iota(jnp.int32, design.shape, 1)
    kept = jnp.where(pair < counts_ref[run], design, 0.0).astype(jnp.bfloat16)
    sums = jnp.dot(kept, data_ref[...], preferred_element_type=F32)
    out_ref[...] = jnp.dot(inverse_ref[0, :M, :], sums, precision=HIGHEST, preferred_element_type=F32)


def sum_solve(run_counts, date_pairs, received, inverse):
    runs = run_counts.shape[0]
    total_pairs, pixels = received.shape
    run_pixels = pixels // runs
    tile = run_pixels // 2
    tiles = run_pixels // tile
    return pl.pallas_call(
        functools.partial(sum_solve_kernel, tiles),
        out_shape=jax.ShapeDtypeStruct((M, pixels), F32),
        grid_spec=pltpu.PrefetchScalarGridSpec(
            num_scalar_prefetch=1,
            grid=(runs * tiles,),
            in_specs=[
                pl.BlockSpec(date_pairs.shape, lambda i, c: (0, 0)),
                pl.BlockSpec((total_pairs, tile), lambda i, c: (0, i)),
                pl.BlockSpec((1, PAD, PAD), lambda i, c: (i // tiles, 0, 0)),
            ],
            out_specs=pl.BlockSpec((M, tile), lambda i, c: (0, i)),
        ),
        compiler_params=pltpu.CompilerParams(vmem_limit_bytes=VMEM_BYTES),
        name="sum_solve",
    )(run_counts, date_pairs, received, inverse)


def coded_rows(piece):
    return M * (piece // LANES) + CODE_ROWS


def decode(coded_ref, codes_ref, lots, first):
    coded = coded_ref[...].astype(jnp.int32).astype(F32)
    values = jnp.concatenate([coded[lot * M : (lot + 1) * M, :] for lot in range(lots)], axis=1)
    codes = codes_ref[...].astype(jnp.int32).astype(F32)
    codes = jnp.concatenate([codes[first + lot : first + lot + 1, :] for lot in range(lots)], axis=1)
    return values, jnp.exp2(codes * (1.0 / CODES_PER_OCTAVE)) * (1.0 / LEVELS)


def encode(sums):
    largest = jnp.max(jnp.abs(sums), axis=0, keepdims=True)
    code = jnp.ceil(jnp.log2(jnp.maximum(largest, SMALLEST)) * CODES_PER_OCTAVE)
    scaled = (sums * (LEVELS / jnp.exp2(code * (1.0 / CODES_PER_OCTAVE))) + ROUNDER) - ROUNDER
    lots = sums.shape[1] // LANES
    return jnp.concatenate([scaled[:, lot * LANES : (lot + 1) * LANES] for lot in range(lots)], axis=0), code


def whole(values):
    return values.astype(jnp.int32).astype(jnp.int16)


def piece_count(at, layout, table, counts):
    parts, _, _, shifts = layout
    run = at % parts // CUTS
    return counts[table[shifts + at] * (parts // CUTS) + run]


def pair_sums(count, table, pairs_ref, first_ref, second_ref, members=(ME, PARTNER)):
    width = first_ref.shape[0]
    lane = lax.broadcasted_iota(jnp.int32, (1, 2 * width), 1)
    pair = jnp.where(lane < width, table[members[0]] * width + lane, table[members[1]] * width + lane - width)
    dates = pairs_ref[:, members[0] * width : (members[0] + 2) * width]
    design = incidence(dates[0:1, :], dates[1:2, :], M)
    kept = jnp.where(pair < count, design, 0.0).astype(jnp.bfloat16)
    data = jnp.concatenate([first_ref[...], second_ref[...]], axis=0)
    return jnp.dot(kept, data, preferred_element_type=F32)


def near_sums(wanted, count, table, pairs_ref, raw_refs):
    return pair_sums(jnp.where(wanted, count, 0), table, pairs_ref, *raw_refs, members=(NEAR, NEAR_PARTNER))


def step_kernel(at, layout, adds, swaps, halves, table, counts, pairs_ref, own_ref, partner_ref, *rest):
    if swaps:
        rest[-1][...] = rest[0][...]
        coded_ref, rest = rest[-2], rest[1:]
    else:
        coded_ref = rest[-1]
    count = piece_count(at, layout, table, counts)
    width = own_ref.shape[1] // halves
    lots = width // LANES
    codes = []
    for half in range(halves):
        part = pl.ds(half * width, width)
        sums = pair_sums(count, table, pairs_ref, own_ref.at[:, part], partner_ref.at[:, part])
        if adds == 1:
            rows = pl.ds(half * lots * M, lots * M)
            values, scale = decode(rest[0].at[rows, :], rest[0].at[halves * lots * M :, :], lots, half * lots)
            sums = sums + values * (scale * table[INNER].astype(F32))
        if adds == 2:
            sums = sums + near_sums(table[INNER] == 1, count, table, pairs_ref, [raw_ref.at[:, part] for raw_ref in rest[:2]])
        scaled, code = encode(sums)
        coded_ref[half * lots * M : (half + 1) * lots * M, :] = whole(scaled)
        codes += [code[:, lot * LANES : (lot + 1) * LANES] for lot in range(lots)]
    codes += [jnp.zeros((CODE_ROWS - len(codes), LANES), F32)]
    coded_ref[halves * lots * M :, :] = whole(jnp.concatenate(codes, axis=0))


def step(at, swap, layout, scalars, pairs, phases, partner, earlier, after, piece):
    partner, place_in = partner
    local_pairs = phases.shape[0]
    _, blocks, away, _ = layout
    coded_shape = (coded_rows(piece), LANES)
    in_specs = [
        pl.BlockSpec(pairs.shape, lambda i, t, c: (0, 0)),
        pl.BlockSpec((local_pairs, piece), lambda i, t, c: (0, t[blocks + at])),
        pl.BlockSpec((local_pairs, piece), lambda i, t, c: (0, place_in)),
    ]
    operands = [pairs, phases, partner]
    out_shape = [jax.ShapeDtypeStruct(coded_shape, jnp.int16)]
    out_specs = [pl.BlockSpec(coded_shape, lambda i, t, c: (0, 0))]
    if swap is not None:
        first, count = swap
        wide = piece * count
        in_specs.append(pl.BlockSpec((local_pairs, wide), lambda i, t, c: (0, t[away + first] // count)))
        operands.append(phases)
        out_shape.append(jax.ShapeDtypeStruct((local_pairs, wide), phases.dtype))
        out_specs.append(pl.BlockSpec((local_pairs, wide), lambda i, t, c: (0, 0)))
    in_specs += [pl.BlockSpec(each.shape, lambda i, t, c: (0, 0)) for each in earlier]
    operands += earlier
    in_specs += [pl.BlockSpec(memory_space=pl.ANY)] * len(after)
    results = pl.pallas_call(
        functools.partial(step_kernel, at, layout, len(earlier), swap is not None, HALVES),
        out_shape=out_shape,
        grid_spec=pltpu.PrefetchScalarGridSpec(
            num_scalar_prefetch=2,
            grid=(1,),
            in_specs=in_specs,
            out_specs=out_specs,
        ),
        compiler_params=pltpu.CompilerParams(vmem_limit_bytes=VMEM_BYTES),
        cost_estimate=STEADY,
        name=f"sum_step_{at:02d}",
    )(*scalars, *operands, *after)
    return results[0], results[1] if swap is not None else None


def add_coded(sums_ref, coded_ref, half, halves):
    lots = sums_ref.shape[1] // LANES
    first = half * lots
    coded = coded_ref[first * M : (first + lots) * M, :].astype(jnp.int32).astype(F32)
    codes = coded_ref[halves * lots * M :, :].astype(jnp.int32).astype(F32)
    scale = jnp.exp2(codes * (1.0 / CODES_PER_OCTAVE)) * (1.0 / LEVELS)
    for lot in range(lots):
        lanes = slice(lot * LANES, (lot + 1) * LANES)
        sums_ref[:M, lanes] += coded[lot * M : (lot + 1) * M, :] * scale[first + lot : first + lot + 1, :]


def solve_product(inverse, sums):
    def halves(value):
        high = value.astype(jnp.bfloat16)
        return high, (value - high.astype(F32)).astype(jnp.bfloat16)

    inverse_high, inverse_low = halves(inverse)
    sums_high, sums_low = halves(sums)
    left = jnp.concatenate([inverse_high, inverse_high, inverse_low], axis=1)
    right = jnp.concatenate([sums_high, sums_low, sums_high], axis=0)
    return jnp.dot(left, right, preferred_element_type=F32)


def finish_kernel(at, layout, halves, raw, told, table, counts, pairs_ref, own_ref, partner_ref, inverse_ref, *rest):
    first, middle_ref, last_ref = rest[: max(raw, 1)], rest[max(raw, 1)], rest[max(raw, 1) + 1]
    sums_ref, rest = rest[-1], rest[:-1]
    if told:
        rest[-1][...] = jnp.zeros_like(rest[-1])
        rest = rest[:-1]
    out_ref = rest[-1]
    count = piece_count(at, layout, table, counts)
    width = sums_ref.shape[1]
    sums_ref[M:, :] = jnp.zeros((PAD - M, width), F32)
    for half in range(halves):
        part = pl.ds(half * width, width)
        sums_ref[:M, :] = pair_sums(count, table, pairs_ref, own_ref.at[:, part], partner_ref.at[:, part])

        @pl.when(table[INNER] == 0)
        def _():
            if raw:
                sums_ref[:M, :] += near_sums(True, count, table, pairs_ref, [each.at[:, part] for each in first])
            else:
                add_coded(sums_ref, first[0], half, halves)

        @pl.when(table[INNER] == 1)
        def _():
            add_coded(sums_ref, middle_ref, half, halves)

        add_coded(sums_ref, last_ref, half, halves)
        out_ref[:, part] = solve_product(inverse_ref[0, :M, :], sums_ref[...])


def finish(at, part, layout, scalars, pairs, phases, partner, inverse, raw, arrived, series, told, pixels, piece):
    partner, place_in = partner
    local_pairs = phases.shape[0]
    blocks = layout[1]
    whole_block = lambda i, t, c: (0, 0)
    in_specs = [
        pl.BlockSpec(pairs.shape, whole_block),
        pl.BlockSpec((local_pairs, piece), lambda i, t, c: (0, t[blocks + at])),
        pl.BlockSpec((local_pairs, piece), lambda i, t, c: (0, place_in)),
        pl.BlockSpec((1, PAD, PAD), lambda i, t, c: (part // CUTS, 0, 0)),
    ]
    in_specs += [pl.BlockSpec(each.shape, whole_block) for each in [*raw, *arrived]]
    operands = [*scalars, pairs, phases, partner, inverse, *raw, *arrived]
    aliases = {}
    if series is not None:
        in_specs.append(pl.BlockSpec(memory_space=pl.ANY))
        aliases = {len(operands): 0}
        operands.append(series)
    out_shape = [jax.ShapeDtypeStruct((M, pixels), F32)]
    out_specs = [pl.BlockSpec((M, piece), lambda i, t, c: (0, part))]
    if told:
        out_shape.append(jax.ShapeDtypeStruct((8, LANES), F32))
        out_specs.append(pl.BlockSpec((8, LANES), lambda i, t, c: (0, 0)))
    return pl.pallas_call(
        functools.partial(finish_kernel, at, layout, HALVES, len(raw), told),
        out_shape=out_shape,
        grid_spec=pltpu.PrefetchScalarGridSpec(
            num_scalar_prefetch=2,
            grid=(1,),
            in_specs=in_specs,
            out_specs=out_specs,
            scratch_shapes=[pltpu.VMEM((PAD, piece // HALVES), F32)],
        ),
        input_output_aliases=aliases,
        compiler_params=pltpu.CompilerParams(vmem_limit_bytes=VMEM_BYTES),
        cost_estimate=LITTLE,
        name=f"finish_{part}",
    )(*operands)


def line_permutation(links):
    return [(2 * source + side, 2 * target + side) for source, target in links for side in range(2)]


def solve_by_sums(phases, date_pairs, counts_of):
    owner_count = lax.axis_size("ifg")
    line = owner_count // 2
    local_pairs, pixels = phases.shape
    owner_pixels = pixels // owner_count
    runs = counts_of(None).shape[0]
    parts = runs * CUTS
    piece = owner_pixels // parts
    steps = (line - 1) * parts
    me = lax.axis_index("ifg")

    places = np.repeat(np.array(CHUNK_ORDER), parts, axis=1)
    part_of = np.tile(np.arange(parts), line)
    rows = []
    for device in range(owner_count):
        place, side = device // 2, device % 2
        own = (places[place] * 2 + side) * parts + part_of
        away = (places[place] * 2 + 1 - side) * parts + part_of
        shift = (place - places[place]) % line
        rows.append(np.concatenate([[device, device ^ 1, device ^ 2, device ^ 3, int(0 < place < line - 1)], own, away, shift]))
    row = lax.dynamic_index_in_dim(jnp.asarray(np.stack(rows), jnp.int32), me, 0, keepdims=False)
    head, pieces = FIXED, line * parts
    layout = (parts, head, head + pieces, head + 2 * pieces)

    swap = [(i, i ^ 1) for i in range(owner_count)]
    partner_of = {}

    def swapped(away, first, count):
        here = lax.ppermute(away, "ifg", swap)
        partner_of.update({first + place: (here, place) for place in range(count)})

    place, side = me // 2, me % 2
    chunk = jnp.where(place < line // 2, 2 - 2 * place, 7 - 2 * place)

    def first_away(column, part, count, after):
        block = (chunk * 2 + column) * parts + part
        if after is not None:
            block, _ = lax.optimization_barrier((block, after))
        return lax.dynamic_slice(phases, (0, block * piece), (local_pairs, count * piece))

    away = first_away(1 - side, *FIRST_SWAP, None)
    swapped(away, *FIRST_SWAP)
    run_counts = counts_of(away)
    counts = [run_counts]
    for distance in range(1, line):
        links = [(i, (i + distance) % line) for i in range(line)]
        counts.append(lax.ppermute(run_counts, "ifg", line_permutation(links)))
    counts = jnp.concatenate(counts)
    raw_part = parts - 1
    near = line_permutation(SENDS[0][0])
    both_sides = jnp.concatenate([first_away(column, raw_part, 1, run_counts) for column in (1 - side, side)])
    raws = lax.ppermute(both_sides, "ifg", near)
    pairs = jnp.concatenate([lax.dynamic_slice(date_pairs, (0, (me ^ at) * local_pairs), (2, local_pairs)) for at in range(4)], axis=1)
    scalars = (row, counts)

    received, sent, coded, series = {raw_part: [raws]}, [raw_part], None, None

    def finished(part, series, told):
        at = steps + part
        arrived = [received[place * parts + part][-1] for place in range(1 if part == raw_part else 0, line - 1)]
        data = (layout, scalars, pairs, phases, partner_of[at], inverse, raw if part == raw_part else [], arrived)
        return finish(at, part, *data, series, told, owner_pixels, piece)

    for at in [each for each in range(steps) if each != raw_part]:
        earlier = [] if at < parts else raw if at == parts + raw_part else [received[at - parts][0]]
        after = [] if coded is None else [coded]
        after += received[sent[-FLIGHT]] if len(sent) >= FLIGHT else []
        if at in SWAP_WAITS:
            after.append(partner_of[SWAP_WAITS[at]][0])
        if at == RAW_WAIT:
            after.append(raw[1])
        if at == INVERSE_STEP:
            inverse = invert_classes(date_pairs, run_counts, [] if coded is None else [coded])
            after.append(inverse)
        if at == steps - 1:
            for part in range(FINISHED_AHEAD):
                series, told = finished(part, series, True)
                after.append(told)
        coded, away = step(at, SWAPS.get(at), layout, scalars, pairs, phases, partner_of[at], earlier, after, piece)
        received[at] = [lax.ppermute(coded, "ifg", line_permutation(links)) for links in SENDS[at // parts]]
        sent.append(at)
        if at in SWAPS:
            swapped(away, *SWAPS[at])
        if at == RAW_STEP:
            raws, _ = lax.optimization_barrier((raws, coded))
            raw = [raws[local_pairs:], lax.ppermute(raws[:local_pairs], "ifg", swap)]

    for part in range(FINISHED_AHEAD, parts):
        series = finished(part, series, False)[0]
    return series


def solve_by_blocks(phases, date_pairs, counts_of):
    owner_count = lax.axis_size("ifg")
    local_pairs, pixels = phases.shape
    owner_pixels = pixels // owner_count
    run_counts = counts_of(None)
    outgoing = phases.reshape(local_pairs, owner_count, owner_pixels).transpose(1, 0, 2)
    received = lax.all_to_all(outgoing, "ifg", split_axis=0, concat_axis=0, tiled=True)
    inverse = invert_classes(date_pairs, run_counts, [])
    return sum_solve(run_counts, date_pairs, received.reshape(-1, owner_pixels), inverse)


def local(phases, date_pairs, pair_counts, group_ids):
    local_pairs, _, pixels = phases.shape

    def counts_of(after):
        groups = group_ids if after is None else lax.optimization_barrier((group_ids, after))[0]
        strip_groups = lax.dynamic_index_in_dim(groups, lax.axis_index("grp"), 0, keepdims=False)[::RUN]
        chosen = strip_groups[:, None] == jnp.arange(pair_counts.shape[0], dtype=jnp.int32)
        return jnp.sum(jnp.where(chosen, pair_counts, 0), axis=1)

    line = lax.axis_size("ifg") == 2 * len(CHUNK_ORDER) and group_ids.shape[1] == 2 * RUN
    by_sums = line and 2 * local_pairs > M and local_pairs % LANES == 0 and lax.axis_size("grp") % 2 == 0
    solve = solve_by_sums if by_sums else solve_by_blocks
    return solve(phases.reshape(local_pairs, pixels), date_pairs, counts_of)[None, :, :]


def solution(mesh):
    in_specs = (P("ifg", "grp", None), P(), P(), P(None, "ifg"))
    out_specs = P("grp", None, "ifg")
    return jax.shard_map(local, mesh=mesh, in_specs=in_specs, out_specs=out_specs, check_vma=False)
```

```python
import functools

import jax
import jax.numpy as jnp
import numpy as np
from jax import lax
from jax.experimental import pallas as pl
from jax.experimental.pallas import tpu as pltpu
from jax.sharding import PartitionSpec as P

M = 200
RUN = 8
PAD = 256
SLABS = 8
DAMPING = 1.0
VMEM_BYTES = 48 * 1024 * 1024
F32 = jnp.float32
HIGHEST = lax.Precision.HIGHEST
STEADY = pl.CostEstimate(flops=10_000_000_000, bytes_accessed=30_000_000, transcendentals=0)
LITTLE = pl.CostEstimate(flops=1024, bytes_accessed=1024, transcendentals=0)
CUTS = 2
HALVES = 1
FLIGHT = 2
FIRST_SWAP = (0, 2)
SWAPS = {0: (2, 1), 1: (4, 2), 2: (6, 2), 5: (8, 2), 7: (10, 2), 8: (12, 2), 9: (14, 2)}
SWAP_WAITS = {}
RAW_STEP, RAW_WAIT = 2, 5
INVERSE_STEP = 0
FINISHED_AHEAD = 1
ME, PARTNER, NEAR, NEAR_PARTNER, INNER, FIXED = 0, 1, 2, 3, 4, 5
LANES = 128
CODE_ROWS = 16
LEVELS = 32700.0
ROUNDER = 1.5 * 2.0**23
CODES_PER_OCTAVE = 128.0
SMALLEST = 2.0**-110
CHUNK_ORDER = ((2, 3, 1, 0), (0, 2, 3, 1), (3, 1, 0, 2), (1, 0, 2, 3))
SENDS = (
    (((0, 1), (1, 0), (2, 3), (3, 2)),),
    (((0, 1), (3, 2)), ((1, 2), (2, 1))),
    (((0, 1), (1, 3), (2, 0), (3, 2)),),
)


def incidence(earlier, later, rows):
    shape = (rows, earlier.shape[1])
    date = lax.broadcasted_iota(jnp.int32, shape, 0)
    return (date == later).astype(F32) - (date == earlier).astype(F32)


def split_product(left, right):
    def halves(value):
        high = value.astype(jnp.bfloat16)
        return high, (value - high.astype(F32)).astype(jnp.bfloat16)

    left_high, left_low = halves(left)
    right_high, right_low = halves(right)
    small = jnp.dot(left_high, right_low, preferred_element_type=F32) + jnp.dot(left_low, right_high, preferred_element_type=F32)
    return jnp.dot(left_high, right_high, preferred_element_type=F32) + small


def full_product(left, right):
    return jnp.dot(left, right, precision=HIGHEST, preferred_element_type=F32)


def inverse_kernel(counts_ref, pairs_ref, *rest):
    out_ref = rest[-1]
    runs = out_ref.shape[0]
    design = incidence(pairs_ref[0:1, :], pairs_ref[1:2, :], PAD)
    pair = lax.broadcasted_iota(jnp.int32, design.shape, 1)
    contract_last = (((1,), (1,)), ((), ()))
    row = lax.broadcasted_iota(jnp.int32, (PAD, PAD), 0)
    col = lax.broadcasted_iota(jnp.int32, (PAD, PAD), 1)
    identity = (row == col).astype(F32)
    grams = []
    for run in range(runs):
        kept = jnp.where(pair < counts_ref[run], design, 0.0).astype(jnp.bfloat16)
        gram = lax.dot_general(kept, kept, contract_last, preferred_element_type=F32)
        grams.append(gram + DAMPING * identity)
    low = DAMPING
    high = 2.0 * functools.reduce(jnp.maximum, [jnp.max(gram) for gram in grams]) - DAMPING
    total, width = high + low, high - low
    scale = 2.0 * total * total - width * width
    starts = tuple((8.0 * total / scale) * identity - (8.0 / scale) * gram for gram in grams)
    needed = 18.0 * scale / (8.0 * high * low)
    steps = jnp.int32(0)
    for power in range(1, 16):
        steps += (needed > float(2**power)).astype(jnp.int32)

    def newton(product, guesses):
        products = [product(gram, guess) for gram, guess in zip(grams, guesses)]
        return tuple(2.0 * guess - product(guess, each) for guess, each in zip(guesses, products))

    full_steps = 1 + (high > 100.0).astype(jnp.int32)
    guesses = lax.fori_loop(0, steps + 1 - full_steps, lambda _, guesses: newton(split_product, guesses), starts)
    guesses = lax.fori_loop(0, full_steps, lambda _, guesses: newton(full_product, guesses), guesses)
    for run, guess in enumerate(guesses):
        out_ref[run] = guess


def invert_classes(date_pairs, run_counts, after):
    shape = (run_counts.shape[0], PAD, PAD)
    return pl.pallas_call(
        inverse_kernel,
        out_shape=jax.ShapeDtypeStruct(shape, F32),
        grid_spec=pltpu.PrefetchScalarGridSpec(
            num_scalar_prefetch=1,
            grid=(1,),
            in_specs=[pl.BlockSpec(date_pairs.shape, lambda i, c: (0, 0))] + [pl.BlockSpec(memory_space=pl.ANY)] * len(after),
            out_specs=pl.BlockSpec(shape, lambda i, c: (0, 0, 0)),
        ),
        compiler_params=pltpu.CompilerParams(vmem_limit_bytes=VMEM_BYTES),
        cost_estimate=LITTLE,
        name="invert_classes_0",
    )(run_counts, date_pairs, *after)


def sum_solve_kernel(tiles, counts_ref, pairs_ref, data_ref, inverse_ref, out_ref):
    run = pl.program_id(0) // tiles
    design = incidence(pairs_ref[0:1, :], pairs_ref[1:2, :], PAD)
    pair = lax.broadcasted_iota(jnp.int32, design.shape, 1)
    kept = jnp.where(pair < counts_ref[run], design, 0.0).astype(jnp.bfloat16)
    sums = jnp.dot(kept, data_ref[...], preferred_element_type=F32)
    out_ref[...] = jnp.dot(inverse_ref[0, :M, :], sums, precision=HIGHEST, preferred_element_type=F32)


def sum_solve(run_counts, date_pairs, received, inverse):
    runs = run_counts.shape[0]
    total_pairs, pixels = received.shape
    run_pixels = pixels // runs
    tile = run_pixels // 2
    tiles = run_pixels // tile
    return pl.pallas_call(
        functools.partial(sum_solve_kernel, tiles),
        out_shape=jax.ShapeDtypeStruct((M, pixels), F32),
        grid_spec=pltpu.PrefetchScalarGridSpec(
            num_scalar_prefetch=1,
            grid=(runs * tiles,),
            in_specs=[
                pl.BlockSpec(date_pairs.shape, lambda i, c: (0, 0)),
                pl.BlockSpec((total_pairs, tile), lambda i, c: (0, i)),
                pl.BlockSpec((1, PAD, PAD), lambda i, c: (i // tiles, 0, 0)),
            ],
            out_specs=pl.BlockSpec((M, tile), lambda i, c: (0, i)),
        ),
        compiler_params=pltpu.CompilerParams(vmem_limit_bytes=VMEM_BYTES),
        name="sum_solve",
    )(run_counts, date_pairs, received, inverse)


def coded_rows(piece):
    return M * (piece // LANES) + CODE_ROWS


def decode(coded_ref, codes_ref, lots, first):
    coded = coded_ref[...].astype(jnp.int32).astype(F32)
    values = jnp.concatenate([coded[lot * M : (lot + 1) * M, :] for lot in range(lots)], axis=1)
    codes = codes_ref[...].astype(jnp.int32).astype(F32)
    codes = jnp.concatenate([codes[first + lot : first + lot + 1, :] for lot in range(lots)], axis=1)
    return values, jnp.exp2(codes * (1.0 / CODES_PER_OCTAVE)) * (1.0 / LEVELS)


def encode(sums):
    largest = jnp.max(jnp.abs(sums), axis=0, keepdims=True)
    code = jnp.ceil(jnp.log2(jnp.maximum(largest, SMALLEST)) * CODES_PER_OCTAVE)
    scaled = (sums * (LEVELS / jnp.exp2(code * (1.0 / CODES_PER_OCTAVE))) + ROUNDER) - ROUNDER
    lots = sums.shape[1] // LANES
    return jnp.concatenate([scaled[:, lot * LANES : (lot + 1) * LANES] for lot in range(lots)], axis=0), code


def whole(values):
    return values.astype(jnp.int32).astype(jnp.int16)


def piece_count(at, layout, table, counts):
    parts, _, _, shifts = layout
    run = at % parts // CUTS
    return counts[table[shifts + at] * (parts // CUTS) + run]


def pair_sums(count, table, pairs_ref, first_ref, second_ref, members=(ME, PARTNER)):
    width = first_ref.shape[0]
    lane = lax.broadcasted_iota(jnp.int32, (1, 2 * width), 1)
    pair = jnp.where(lane < width, table[members[0]] * width + lane, table[members[1]] * width + lane - width)
    dates = pairs_ref[:, members[0] * width : (members[0] + 2) * width]
    design = incidence(dates[0:1, :], dates[1:2, :], M)
    kept = jnp.where(pair < count, design, 0.0).astype(jnp.bfloat16)
    data = jnp.concatenate([first_ref[...], second_ref[...]], axis=0)
    return jnp.dot(kept, data, preferred_element_type=F32)


def near_sums(wanted, count, table, pairs_ref, raw_refs):
    return pair_sums(jnp.where(wanted, count, 0), table, pairs_ref, *raw_refs, members=(NEAR, NEAR_PARTNER))


def step_kernel(at, layout, adds, swaps, halves, table, counts, pairs_ref, own_ref, partner_ref, *rest):
    if swaps:
        rest[-1][...] = rest[0][...]
        coded_ref, rest = rest[-2], rest[1:]
    else:
        coded_ref = rest[-1]
    count = piece_count(at, layout, table, counts)
    width = own_ref.shape[1] // halves
    lots = width // LANES
    codes = []
    for half in range(halves):
        part = pl.ds(half * width, width)
        sums = pair_sums(count, table, pairs_ref, own_ref.at[:, part], partner_ref.at[:, part])
        if adds == 1:
            rows = pl.ds(half * lots * M, lots * M)
            values, scale = decode(rest[0].at[rows, :], rest[0].at[halves * lots * M :, :], lots, half * lots)
            sums = sums + values * (scale * table[INNER].astype(F32))
        if adds == 2:
            sums = sums + near_sums(table[INNER] == 1, count, table, pairs_ref, [raw_ref.at[:, part] for raw_ref in rest[:2]])
        scaled, code = encode(sums)
        coded_ref[half * lots * M : (half + 1) * lots * M, :] = whole(scaled)
        codes += [code[:, lot * LANES : (lot + 1) * LANES] for lot in range(lots)]
    codes += [jnp.zeros((CODE_ROWS - len(codes), LANES), F32)]
    coded_ref[halves * lots * M :, :] = whole(jnp.concatenate(codes, axis=0))


def step(at, swap, layout, scalars, pairs, phases, partner, earlier, after, piece):
    partner, place_in = partner
    local_pairs = phases.shape[0]
    _, blocks, away, _ = layout
    coded_shape = (coded_rows(piece), LANES)
    in_specs = [
        pl.BlockSpec(pairs.shape, lambda i, t, c: (0, 0)),
        pl.BlockSpec((local_pairs, piece), lambda i, t, c: (0, t[blocks + at])),
        pl.BlockSpec((local_pairs, piece), lambda i, t, c: (0, place_in)),
    ]
    operands = [pairs, phases, partner]
    out_shape = [jax.ShapeDtypeStruct(coded_shape, jnp.int16)]
    out_specs = [pl.BlockSpec(coded_shape, lambda i, t, c: (0, 0))]
    if swap is not None:
        first, count = swap
        wide = piece * count
        in_specs.append(pl.BlockSpec((local_pairs, wide), lambda i, t, c: (0, t[away + first] // count)))
        operands.append(phases)
        out_shape.append(jax.ShapeDtypeStruct((local_pairs, wide), phases.dtype))
        out_specs.append(pl.BlockSpec((local_pairs, wide), lambda i, t, c: (0, 0)))
    in_specs += [pl.BlockSpec(each.shape, lambda i, t, c: (0, 0)) for each in earlier]
    operands += earlier
    in_specs += [pl.BlockSpec(memory_space=pl.ANY)] * len(after)
    results = pl.pallas_call(
        functools.partial(step_kernel, at, layout, len(earlier), swap is not None, HALVES),
        out_shape=out_shape,
        grid_spec=pltpu.PrefetchScalarGridSpec(
            num_scalar_prefetch=2,
            grid=(1,),
            in_specs=in_specs,
            out_specs=out_specs,
        ),
        compiler_params=pltpu.CompilerParams(vmem_limit_bytes=VMEM_BYTES),
        cost_estimate=STEADY,
        name=f"sum_step_{at:02d}",
    )(*scalars, *operands, *after)
    return results[0], results[1] if swap is not None else None


def add_coded(sums_ref, coded_ref, half, halves):
    lots = sums_ref.shape[1] // LANES
    first = half * lots
    coded = coded_ref[first * M : (first + lots) * M, :].astype(jnp.int32).astype(F32)
    codes = coded_ref[halves * lots * M :, :].astype(jnp.int32).astype(F32)
    scale = jnp.exp2(codes * (1.0 / CODES_PER_OCTAVE)) * (1.0 / LEVELS)
    for lot in range(lots):
        lanes = slice(lot * LANES, (lot + 1) * LANES)
        sums_ref[:M, lanes] += coded[lot * M : (lot + 1) * M, :] * scale[first + lot : first + lot + 1, :]


def solve_product(inverse, sums):
    def halves(value):
        high = value.astype(jnp.bfloat16)
        return high, (value - high.astype(F32)).astype(jnp.bfloat16)

    inverse_high, inverse_low = halves(inverse)
    sums_high, sums_low = halves(sums)
    left = jnp.concatenate([inverse_high, inverse_high, inverse_low], axis=1)
    right = jnp.concatenate([sums_high, sums_low, sums_high], axis=0)
    return jnp.dot(left, right, preferred_element_type=F32)


def finish_kernel(at, layout, halves, raw, told, table, counts, pairs_ref, own_ref, partner_ref, inverse_ref, *rest):
    first, middle_ref, last_ref = rest[: max(raw, 1)], rest[max(raw, 1)], rest[max(raw, 1) + 1]
    sums_ref, rest = rest[-1], rest[:-1]
    if told:
        rest[-1][...] = jnp.zeros_like(rest[-1])
        rest = rest[:-1]
    out_ref = rest[-1]
    count = piece_count(at, layout, table, counts)
    width = sums_ref.shape[1]
    sums_ref[M:, :] = jnp.zeros((PAD - M, width), F32)
    for half in range(halves):
        part = pl.ds(half * width, width)
        sums_ref[:M, :] = pair_sums(count, table, pairs_ref, own_ref.at[:, part], partner_ref.at[:, part])

        @pl.when(table[INNER] == 0)
        def _():
            if raw:
                sums_ref[:M, :] += near_sums(True, count, table, pairs_ref, [each.at[:, part] for each in first])
            else:
                add_coded(sums_ref, first[0], half, halves)

        @pl.when(table[INNER] == 1)
        def _():
            add_coded(sums_ref, middle_ref, half, halves)

        add_coded(sums_ref, last_ref, half, halves)
        out_ref[:, part] = solve_product(inverse_ref[0, :M, :], sums_ref[...])


def finish(at, part, layout, scalars, pairs, phases, partner, inverse, raw, arrived, series, told, pixels, piece):
    partner, place_in = partner
    local_pairs = phases.shape[0]
    blocks = layout[1]
    whole_block = lambda i, t, c: (0, 0)
    in_specs = [
        pl.BlockSpec(pairs.shape, whole_block),
        pl.BlockSpec((local_pairs, piece), lambda i, t, c: (0, t[blocks + at])),
        pl.BlockSpec((local_pairs, piece), lambda i, t, c: (0, place_in)),
        pl.BlockSpec((1, PAD, PAD), lambda i, t, c: (part // CUTS, 0, 0)),
    ]
    in_specs += [pl.BlockSpec(each.shape, whole_block) for each in [*raw, *arrived]]
    operands = [*scalars, pairs, phases, partner, inverse, *raw, *arrived]
    aliases = {}
    if series is not None:
        in_specs.append(pl.BlockSpec(memory_space=pl.ANY))
        aliases = {len(operands): 0}
        operands.append(series)
    out_shape = [jax.ShapeDtypeStruct((M, pixels), F32)]
    out_specs = [pl.BlockSpec((M, piece), lambda i, t, c: (0, part))]
    if told:
        out_shape.append(jax.ShapeDtypeStruct((8, LANES), F32))
        out_specs.append(pl.BlockSpec((8, LANES), lambda i, t, c: (0, 0)))
    return pl.pallas_call(
        functools.partial(finish_kernel, at, layout, HALVES, len(raw), told),
        out_shape=out_shape,
        grid_spec=pltpu.PrefetchScalarGridSpec(
            num_scalar_prefetch=2,
            grid=(1,),
            in_specs=in_specs,
            out_specs=out_specs,
            scratch_shapes=[pltpu.VMEM((PAD, piece // HALVES), F32)],
        ),
        input_output_aliases=aliases,
        compiler_params=pltpu.CompilerParams(vmem_limit_bytes=VMEM_BYTES),
        cost_estimate=LITTLE,
        name=f"finish_{part}",
    )(*operands)


def line_permutation(links):
    return [(2 * source + side, 2 * target + side) for source, target in links for side in range(2)]


def solve_by_sums(phases, date_pairs, counts_of):
    owner_count = lax.axis_size("ifg")
    line = owner_count // 2
    local_pairs, pixels = phases.shape
    owner_pixels = pixels // owner_count
    runs = counts_of(None).shape[0]
    parts = runs * CUTS
    piece = owner_pixels // parts
    steps = (line - 1) * parts
    me = lax.axis_index("ifg")

    places = np.repeat(np.array(CHUNK_ORDER), parts, axis=1)
    part_of = np.tile(np.arange(parts), line)
    rows = []
    for device in range(owner_count):
        place, side = device // 2, device % 2
        own = (places[place] * 2 + side) * parts + part_of
        away = (places[place] * 2 + 1 - side) * parts + part_of
        shift = (place - places[place]) % line
        rows.append(np.concatenate([[device, device ^ 1, device ^ 2, device ^ 3, int(0 < place < line - 1)], own, away, shift]))
    row = lax.dynamic_index_in_dim(jnp.asarray(np.stack(rows), jnp.int32), me, 0, keepdims=False)
    head, pieces = FIXED, line * parts
    layout = (parts, head, head + pieces, head + 2 * pieces)

    swap = [(i, i ^ 1) for i in range(owner_count)]
    partner_of = {}

    def swapped(away, first, count):
        here = lax.ppermute(away, "ifg", swap)
        partner_of.update({first + place: (here, place) for place in range(count)})

    place, side = me // 2, me % 2
    chunk = jnp.where(place < line // 2, 2 - 2 * place, 7 - 2 * place)

    def first_away(column, part, count, after):
        block = (chunk * 2 + column) * parts + part
        if after is not None:
            block, _ = lax.optimization_barrier((block, after))
        return lax.dynamic_slice(phases, (0, block * piece), (local_pairs, count * piece))

    away = first_away(1 - side, *FIRST_SWAP, None)
    swapped(away, *FIRST_SWAP)
    run_counts = counts_of(away)
    counts = [run_counts]
    for distance in range(1, line):
        links = [(i, (i + distance) % line) for i in range(line)]
        counts.append(lax.ppermute(run_counts, "ifg", line_permutation(links)))
    counts = jnp.concatenate(counts)
    raw_part = parts - 1
    near = line_permutation(SENDS[0][0])
    both_sides = jnp.concatenate([first_away(column, raw_part, 1, run_counts) for column in (1 - side, side)])
    raws = lax.ppermute(both_sides, "ifg", near)
    pairs = jnp.concatenate([lax.dynamic_slice(date_pairs, (0, (me ^ at) * local_pairs), (2, local_pairs)) for at in range(4)], axis=1)
    scalars = (row, counts)

    received, sent, coded, series = {raw_part: [raws]}, [raw_part], None, None

    def finished(part, series, told):
        at = steps + part
        arrived = [received[place * parts + part][-1] for place in range(1 if part == raw_part else 0, line - 1)]
        data = (layout, scalars, pairs, phases, partner_of[at], inverse, raw if part == raw_part else [], arrived)
        return finish(at, part, *data, series, told, owner_pixels, piece)

    for at in [each for each in range(steps) if each != raw_part]:
        earlier = [] if at < parts else raw if at == parts + raw_part else [received[at - parts][0]]
        after = [] if coded is None else [coded]
        after += received[sent[-FLIGHT]][::-1] if len(sent) >= FLIGHT else []
        if at in SWAP_WAITS:
            after.append(partner_of[SWAP_WAITS[at]][0])
        if at == RAW_WAIT:
            after.append(raw[1])
        if at == INVERSE_STEP:
            inverse = invert_classes(date_pairs, run_counts, [] if coded is None else [coded])
            after.append(inverse)
        if at == steps - 1:
            for part in range(FINISHED_AHEAD):
                series, told = finished(part, series, True)
                after.append(told)
        coded, away = step(at, SWAPS.get(at), layout, scalars, pairs, phases, partner_of[at], earlier, after, piece)
        received[at] = [lax.ppermute(coded, "ifg", line_permutation(links)) for links in SENDS[at // parts]]
        sent.append(at)
        if at in SWAPS:
            swapped(away, *SWAPS[at])
        if at == RAW_STEP:
            raws, _ = lax.optimization_barrier((raws, coded))
            raw = [raws[local_pairs:], lax.ppermute(raws[:local_pairs], "ifg", swap)]

    for part in range(FINISHED_AHEAD, parts):
        series = finished(part, series, False)[0]
    return series


def solve_by_blocks(phases, date_pairs, counts_of):
    owner_count = lax.axis_size("ifg")
    local_pairs, pixels = phases.shape
    owner_pixels = pixels // owner_count
    run_counts = counts_of(None)
    outgoing = phases.reshape(local_pairs, owner_count, owner_pixels).transpose(1, 0, 2)
    received = lax.all_to_all(outgoing, "ifg", split_axis=0, concat_axis=0, tiled=True)
    inverse = invert_classes(date_pairs, run_counts, [])
    return sum_solve(run_counts, date_pairs, received.reshape(-1, owner_pixels), inverse)


def local(phases, date_pairs, pair_counts, group_ids):
    local_pairs, _, pixels = phases.shape

    def counts_of(after):
        groups = group_ids if after is None else lax.optimization_barrier((group_ids, after))[0]
        strip_groups = lax.dynamic_index_in_dim(groups, lax.axis_index("grp"), 0, keepdims=False)[::RUN]
        chosen = strip_groups[:, None] == jnp.arange(pair_counts.shape[0], dtype=jnp.int32)
        return jnp.sum(jnp.where(chosen, pair_counts, 0), axis=1)

    line = lax.axis_size("ifg") == 2 * len(CHUNK_ORDER) and group_ids.shape[1] == 2 * RUN
    by_sums = line and 2 * local_pairs > M and local_pairs % LANES == 0 and lax.axis_size("grp") % 2 == 0
    solve = solve_by_sums if by_sums else solve_by_blocks
    return solve(phases.reshape(local_pairs, pixels), date_pairs, counts_of)[None, :, :]


def solution(mesh):
    in_specs = (P("ifg", "grp", None), P(), P(), P(None, "ifg"))
    out_specs = P("grp", None, "ifg")
    return jax.shard_map(local, mesh=mesh, in_specs=in_specs, out_specs=out_specs, check_vma=False)
```
